32 devices in a mesh: grp: 2 (over core), dp: 16 (over z, y, x).
Axes of the slice: x: 2, y: 2, z: 4, core: 2. Of those that a mesh axis runs over, the one named last changes fastest.
Arguments:
- params: float32 [2, 8888320], P('grp', 'dp'), may hold values from -8 to 8
- first_moment: float32 [2, 8888320], P('grp', 'dp'), may hold values from -1 to 1
- second_moment: float32 [2, 8888320], P('grp', 'dp'), may hold values from 0 to 1, as said below
- average: float32 [2, 8888320], P('grp', 'dp'), may hold values from -8 to 8
- pixels: bfloat16 [25088, 768], P('dp'), may hold values from -6 to 6
- visible_index: int32 [128, 64], P('dp'), may hold values from 0 to 195, as said below
- visible_count: int32 [128], P('dp'), may hold values from 32 to 64, as said below
- gsd_id: int32 [128], P('dp'), may hold values from 0 to 6
Outputs:
- new_params: float32 [2, 8888320], P('grp', 'dp')
- new_first_moment: float32 [2, 8888320], P('grp', 'dp')
- new_second_moment: float32 [2, 8888320], P('grp', 'dp')
- new_average: float32 [2, 8888320], P('grp', 'dp')
- loss_sum: float32 [], replicated
- masked_total: float32 [], replicated
- grad_norm: float32 [], replicated
The draws below stay inside these ranges and needn't reach their ends.
Inputs may be any that keep to these rules, and one draw needn't show every extreme that they name: `visible_count`: the first image of every block of 8 images has 64 visible patches. `visible_index`: the entries of a row are different positions; the first visible_count entries are the visible patches, the others are not read. `second_moment`: positive.
All inputs are finite; a program needn't handle non-finite values.
Results may differ from the reference program's by a relative error of at most 0.00045.
The reference program's roundings to bfloat16 on the way count: a program that leaves them out, or rounds other values in their place, can miss the bound.
Values may be sent and summed in bfloat16 or wider, within the bound.
A program may use at most 448 MiB of HBM per device.

```python
import math
import jax
import jax.numpy as jnp
from jax import lax

DE = 1024
HE = 16
FE = 4096
DD = 512
HD = 16
FD = 2048
PSIDE = 16
GSIDE = 14
VMAX = 64
STEP = 10
IMG_DEV = 8
PIX = 768
LOWPIX = 192
GRID = 196
IMAGES = 128
NENC = 8662528
NDEC = 3644352
NBOR = 5242880
PG = 8888320
N_DP = 16


def encoder_row_layout_drawn():
    return [('pe_w', (PIX, DE)), ('pe_b', (DE,)), ('ln1_g', (DE,)), ('ln1_b', (DE,)), ('qkv_w', (DE, 3 * DE)), ('ln2_g', (DE,)), ('ln2_b', (DE,)), ('fc1_w', (DE, FE)), ('fc1_b', (FE,)), ('fc2_b', (DE,)), ('lnf_g', (DE,)), ('lnf_b', (DE,)), ('emb_w', (DE, DD)), ('emb_b', (DD,))]


def decoder_layout_drawn():
    return [('mask_tok', (DD,)), ('ln1_g', (DD,)), ('ln1_b', (DD,)), ('qkv_w', (DD, 3 * DD)), ('out_w', (DD, DD)), ('ln2_g', (DD,)), ('ln2_b', (DD,)), ('fc1_w', (DD, FD)), ('fc1_b', (FD,)), ('fc2_w', (FD, DD)), ('fc2_b', (DD,)), ('lnf_g', (DD,)), ('lnf_b', (DD,)), ('head_w', (DD, LOWPIX + PIX)), ('head_b', (LOWPIX + PIX,)), ('enc_out_w', (DE, DE)), ('enc_fc2_w', (FE, DE))]


def parameter_rows(key):
    rows_out = []
    for group_index, layout in enumerate((encoder_row_layout_drawn(), decoder_layout_drawn())):
        pieces = []
        for section_index, (section_name, section_shape) in enumerate(layout):
            extent = math.prod(section_shape)
            normal_draw = jax.random.normal(jax.random.fold_in(key, 100 * group_index + section_index), (extent,), jnp.float32)
            ending = section_name[-2:]
            if ending == '_g':
                pieces.append(1.0 + 0.1 * normal_draw)
            elif ending == '_w':
                factor = 1.0
                if section_name == 'out_w':
                    factor = 5.0
                elif section_name == 'enc_out_w':
                    factor = 3.0
                pieces.append(normal_draw * (factor / math.sqrt(section_shape[0])))
            elif section_name == 'mask_tok':
                pieces.append(normal_draw)
            else:
                pieces.append(0.1 * normal_draw)
        used = jnp.concatenate(pieces)
        tail = 0.02 * jax.random.normal(jax.random.fold_in(key, 100 * group_index + 99), (PG - used.shape[0],), jnp.float32)
        rows_out.append(jnp.concatenate([used, tail]))
    return jnp.stack(rows_out)


def draw_params(key, part):
    key = jax.random.fold_in(key, 1)
    return parameter_rows(key)


def draw_average(key, part):
    key = jax.random.fold_in(key, 2)
    return parameter_rows(key)


def draw_first_moment(key, part):
    key = jax.random.fold_in(key, 3)
    spread = 0.05 / math.sqrt(NENC + NDEC + NBOR)
    return spread * jax.random.normal(key, (2, PG), jnp.float32)


def draw_second_moment(key, part):
    key = jax.random.fold_in(key, 4)
    spread = 0.05 / math.sqrt(NENC + NDEC + NBOR)
    return spread * spread * jnp.exp(jax.random.uniform(key, (2, PG), jnp.float32, 0.0, math.log(4.0)))


def draw_visible_count(key, part):
    key = jax.random.fold_in(key, 5)
    counts = jax.random.randint(key, (IMAGES,), VMAX // 2, VMAX + 1)
    leaders = jnp.arange(IMAGES) % IMG_DEV == 0
    return jnp.where(leaders, VMAX, counts).astype(jnp.int32)


def draw_visible_index(key, part):
    key = jax.random.fold_in(key, 6)
    scores = jax.random.randint(key, (IMAGES, GRID), 0, 1 << 20) * GRID + jnp.arange(GRID)[None, :]
    return jnp.argsort(scores, axis=1, stable=True)[:, :VMAX].astype(jnp.int32)


def set_ends(result, own_key, low, largest):
    longest = result.shape.index(max(result.shape))
    spots = []
    for shift in (0, 1):
        where = [jax.random.randint(jax.random.fold_in(own_key, axis), (), 0, length) for axis, length in enumerate(result.shape)]
        where[longest] = (where[longest] + shift) % result.shape[longest]
        spots.append(tuple(where))
    return result.at[spots[0]].set(low).at[spots[1]].set(largest)


def block_levels(rng, dims, cuts, low, high):
    factor_of = 1.0
    for dim, blocks in cuts:
        draws = jax.random.uniform(jax.random.fold_in(jax.random.fold_in(rng, 6), dim), (blocks,), jnp.float32, low / len(cuts), high / len(cuts))
        factor_of = factor_of * jnp.repeat(jnp.exp(draws), dims[dim] // blocks).reshape((-1,) + (1,) * (len(dims) - 1 - dim))
    return factor_of


def normal_values(stream_key, shape, scale, limit, cuts=(), kind=jnp.bfloat16):
    entries = jax.random.normal(stream_key, shape, jnp.float32) * scale
    if len(cuts) > 0:
        entries = block_levels(stream_key, shape, cuts, -0.22, 0.18) * entries
    return jnp.clip(entries, min=-limit, max=limit).astype(kind)


def setup_inputs(seed: int = 0) -> dict:
    key_list = jax.random.split(jax.random.key(seed), 9)
    params = draw_params(jax.random.fold_in(key_list[8], 71), 0)
    first_moment = draw_first_moment(jax.random.fold_in(key_list[8], 71), 0)
    second_moment = draw_second_moment(jax.random.fold_in(key_list[8], 71), 0)
    average = draw_average(jax.random.fold_in(key_list[8], 71), 0)
    pixels = normal_values(key_list[4], (IMAGES * GRID, PIX), 1.0, 6.0, ((0, 16),))
    visible_index = draw_visible_index(jax.random.fold_in(key_list[8], 71), 0)
    visible_count = draw_visible_count(jax.random.fold_in(key_list[8], 71), 0)
    gsd_id = set_ends(jax.random.randint(key_list[7], (IMAGES,), 0, 7), jax.random.fold_in(key_list[7], 1), 0, 6).astype(jnp.int32)
    return {"params": params, "first_moment": first_moment, "second_moment": second_moment, "average": average, "pixels": pixels, "visible_index": visible_index, "visible_count": visible_count, "gsd_id": gsd_id}


@jax.custom_vjp
def low(v):
    return lax.optimization_barrier(v.astype(jnp.bfloat16)).astype(jnp.float32)

@jax.custom_vjp
def low_back(v):
    return v

def low_keep(v):
    return (low(v), None)

def low_pass(kept, grad):
    return (grad,)

def back_keep(v):
    return (v, None)

def back_low(kept, grad):
    return (low(grad),)
low.defvjp(low_keep, low_pass)
low_back.defvjp(back_keep, back_low)
HIGHEST = lax.Precision.HIGHEST
CLIP = 0.05
RATE = 0.01
BETA_ONE = 0.5
BETA_TWO = 0.5
ADAM_EPS = 1e-08
DECAY_WEIGHT = 0.05
AVERAGE_KEEP = 0.9
NORM_EPS = 1e-06
MASK_FILL = -1000000000.0

def encoder_row_layout():
    return [('pe_w', (PIX, DE)), ('pe_b', (DE,)), ('ln1_g', (DE,)), ('ln1_b', (DE,)), ('qkv_w', (DE, 3 * DE)), ('ln2_g', (DE,)), ('ln2_b', (DE,)), ('fc1_w', (DE, FE)), ('fc1_b', (FE,)), ('fc2_b', (DE,)), ('lnf_g', (DE,)), ('lnf_b', (DE,)), ('emb_w', (DE, DD)), ('emb_b', (DD,))]

def decoder_layout():
    return [('mask_tok', (DD,)), ('ln1_g', (DD,)), ('ln1_b', (DD,)), ('qkv_w', (DD, 3 * DD)), ('out_w', (DD, DD)), ('ln2_g', (DD,)), ('ln2_b', (DD,)), ('fc1_w', (DD, FD)), ('fc1_b', (FD,)), ('fc2_w', (FD, DD)), ('fc2_b', (DD,)), ('lnf_g', (DD,)), ('lnf_b', (DD,)), ('head_w', (DD, LOWPIX + PIX)), ('head_b', (LOWPIX + PIX,)), ('enc_out_w', (DE, DE)), ('enc_fc2_w', (FE, DE))]

def unpack(flat, layout):
    tensors = {}
    offset = 0
    for section_name, section_shape in layout:
        extent = math.prod(section_shape)
        tensors[section_name] = flat[offset:offset + extent].reshape(section_shape)
        offset += extent
    return tensors

def packing(counts, index_rows):
    images = counts.shape[0]
    starts = (jnp.cumsum(counts) - counts).astype(jnp.int32)
    row_ids = jnp.arange(images * VMAX, dtype=jnp.int32)
    owner_image = (lax.optimization_barrier(jnp.sum((row_ids[:, None] >= starts[None, :]).astype(jnp.int32), axis=1)) - 1).astype(jnp.int32)
    within = row_ids - starts[owner_image]
    is_valid = row_ids < jnp.sum(counts).astype(jnp.int32)
    position = index_rows[owner_image, jnp.clip(within, 0, VMAX - 1)].astype(jnp.int32)
    grid_row = jnp.where(is_valid, owner_image * GRID + position, images * GRID).astype(jnp.int32)
    segment = jnp.where(is_valid, owner_image, -1).astype(jnp.int32)
    return (grid_row, segment, is_valid, position)

def position_code(position, scales, width):
    quarter = width // 4
    frequency = jnp.exp(jnp.arange(quarter, dtype=jnp.float32) * (-math.log(10000.0) / quarter))
    row_angle = ((position // GSIDE).astype(jnp.float32) * scales)[:, None] * frequency[None, :]
    col_angle = ((position % GSIDE).astype(jnp.float32) * scales)[:, None] * frequency[None, :]
    return jnp.concatenate([jnp.sin(row_angle), jnp.cos(row_angle), jnp.sin(col_angle), jnp.cos(col_angle)], axis=1)

def bands(pixel_rows):
    pixel_ids = jnp.arange(PIX, dtype=jnp.int32)
    coarse = (pixel_ids // (3 * PSIDE) // 2 * (PSIDE // 2) + pixel_ids // 3 % PSIDE // 2) * 3 + pixel_ids % 3
    pool_table = (coarse[:, None] == jnp.arange(LOWPIX, dtype=jnp.int32)[None, :]).astype(jnp.float32)
    low_band = jnp.dot(pixel_rows, pool_table, precision=HIGHEST) * 0.25
    high_band = pixel_rows - jnp.dot(low_band, pool_table.T, precision=HIGHEST)
    return (low_band, high_band)

def product(left, right):
    return jnp.einsum('...k,kn->...n', left, right, precision=HIGHEST)

def layer_norm(state, gain, shift):
    centered = state - lax.optimization_barrier(jnp.mean(state, axis=-1, keepdims=True))
    return centered * lax.rsqrt(lax.optimization_barrier(jnp.mean(centered * centered, axis=-1, keepdims=True)) + NORM_EPS) * gain + shift

def attention(normed, qkv_w, out_w, heads, bias):
    batch, length, width = normed.shape
    head_dim = width // heads
    qkv = low(low_back(product(normed, qkv_w))).reshape(batch, length, 3, heads, head_dim)
    query_part, key_part, value_part = (qkv[:, :, 0], qkv[:, :, 1], qkv[:, :, 2])
    scores = low_back(jnp.einsum('blhd,bmhd->bhlm', query_part, key_part, precision=HIGHEST) * head_dim ** (-0.5))
    attend = low(jax.nn.softmax(scores + bias, axis=-1))
    mixed = low(low_back(jnp.einsum('bhlm,bmhd->blhd', attend, value_part, precision=HIGHEST)))
    return low_back(product(mixed.reshape(batch, length, width), out_w))

def block(state, weights, heads, bias):
    normed = low(layer_norm(state, weights['ln1_g'], weights['ln1_b']))
    state = state + attention(normed, weights['qkv_w'], weights['out_w'], heads, bias)
    normed = low(layer_norm(state, weights['ln2_g'], weights['ln2_b']))
    pre_act = low_back(product(normed, weights['fc1_w'])) + weights['fc1_b']
    active = low(jax.nn.gelu(pre_act, approximate=False))
    return state + low_back(product(active, weights['fc2_w'])) + weights['fc2_b']

def shard_loss(enc, dec, pixel_rows, index_shard, count_shard, gsd_shard):
    images = count_shard.shape[0]
    total_rows = images * GRID
    grid_row, segment, is_valid, position = packing(count_shard, index_shard)
    image_scale = 0.5 + 0.25 * gsd_shard.astype(jnp.float32)
    patches = jnp.where(is_valid[:, None], pixel_rows[jnp.minimum(grid_row, total_rows - 1)], 0.0)
    state = low_back(product(patches, enc['pe_w'])) + enc['pe_b'] + position_code(position, image_scale[jnp.maximum(segment, 0)], DE)
    mask_bias = jnp.where(segment[:, None] == segment[None, :], 0.0, MASK_FILL)
    state = block(state[None], enc, HE, mask_bias[None, None])[0]
    normed = low(layer_norm(state, enc['lnf_g'], enc['lnf_b']))
    sent = low(low_back(product(normed, enc['emb_w']) + enc['emb_b']))
    placed = jnp.zeros((total_rows, DD), jnp.float32).at[grid_row].set(sent, mode='drop')
    seen = jnp.zeros((total_rows,), jnp.float32).at[grid_row].set(1.0, mode='drop')
    grid_ids = jnp.arange(total_rows, dtype=jnp.int32)
    state = jnp.where(seen[:, None] > 0.5, placed, dec['mask_tok']) + position_code(grid_ids % GRID, image_scale[grid_ids // GRID], DD)
    state = block(state.reshape(images, GRID, DD), dec, HD, 0.0).reshape(total_rows, DD)
    normed = low(layer_norm(state, dec['lnf_g'], dec['lnf_b']))
    predicted = low_back(product(normed, dec['head_w']) + dec['head_b'])
    low_band, high_band = bands(pixel_rows)
    miss_low = predicted[:, :LOWPIX] - low_band
    miss_high = predicted[:, LOWPIX:] - high_band
    per_patch = lax.optimization_barrier(jnp.sum(miss_low * miss_low, axis=1)) + lax.optimization_barrier(jnp.sum(jnp.sqrt(miss_high * miss_high + 1.0) - 1.0, axis=1))
    return jnp.sum(per_patch * (1.0 - seen))

def reference(params, first_moment, second_moment, average, pixels, visible_index, visible_count, gsd_id):
    masked_total = jnp.sum(GRID - visible_count).astype(jnp.float32)
    pixel_rows = pixels.astype(jnp.float32)
    shards = (pixel_rows.reshape(N_DP, IMG_DEV * GRID, PIX), visible_index.reshape(N_DP, IMG_DEV, VMAX), visible_count.reshape(N_DP, IMG_DEV), gsd_id.reshape(N_DP, IMG_DEV))

    def objective(master):
        copies = low(master)
        enc = unpack(copies[0], encoder_row_layout())
        dec = unpack(copies[1], decoder_layout())
        enc['out_w'] = dec['enc_out_w']
        enc['fc2_w'] = dec['enc_fc2_w']
        checked = jax.checkpoint(shard_loss)

        def accumulate(running, shard):
            return (running + checked(enc, dec, shard[0], shard[1], shard[2], shard[3]), None)
        total_loss, _ = lax.scan(accumulate, jnp.zeros((), jnp.float32), shards)
        return (total_loss / masked_total, total_loss)
    _, pullback, loss_sum = jax.vjp(objective, params, has_aux=True)
    gradient = pullback(jnp.ones((), jnp.float32))[0]
    grad_norm = jnp.sqrt(jnp.sum(gradient * gradient))
    clipped = gradient * jnp.minimum(1.0, CLIP / grad_norm)
    new_first = BETA_ONE * first_moment + (1.0 - BETA_ONE) * clipped
    new_second = BETA_TWO * second_moment + (1.0 - BETA_TWO) * clipped * clipped
    direction = new_first / (1.0 - BETA_ONE ** STEP) / (jnp.sqrt(new_second / (1.0 - BETA_TWO ** STEP)) + ADAM_EPS)
    new_params = params - RATE * (direction + DECAY_WEIGHT * params)
    new_average = AVERAGE_KEEP * average + (1.0 - AVERAGE_KEEP) * new_params
    return (new_params, new_first, new_second, new_average, loss_sum, masked_total, grad_norm)
```

```python
import functools
import math
import types

import jax
import jax.numpy as jnp
from jax import lax
from jax.experimental import pallas as pl
from jax.experimental.pallas import tpu as pltpu
from jax.sharding import PartitionSpec as P

DE = 1024
HE = 16
FE = 4096
DD = 512
HD = 16
FD = 2048
PSIDE = 16
GSIDE = 14
VMAX = 64
STEP = 10
PIX = 768
LOWPIX = 192
GRID = 196
GPAD = 208
NENC = 8662528
NDEC = 3644352
LANES = 128
UNIT = 4 * LANES

HIGHEST = lax.Precision.HIGHEST
CLIP = 0.05
RATE = 0.01
BETA_ONE = 0.5
BETA_TWO = 0.5
ADAM_EPS = 1e-08
DECAY_WEIGHT = 0.05
AVERAGE_KEEP = 0.9
NORM_EPS = 1e-06
MASK_FILL = -1000000000.0
F32 = jnp.float32
BF16 = jnp.bfloat16
MESH = pl.DeviceIdType.MESH

WIDTH = 256
SUB = 64
PIECE = 8192
VEC_ROWS = 16
VEC_COLS = (FE, FD)
HEAD = LOWPIX + PIX

ENC_LAYOUT = [
    (PIX, DE),
    (DE,),
    (DE,),
    (DE,),
    (DE, 3 * DE),
    (DE,),
    (DE,),
    (DE, FE),
    (FE,),
    (DE,),
    (DE,),
    (DE,),
    (DE, DD),
    (DD,),
]
DEC_LAYOUT = [
    (DD,),
    (DD,),
    (DD,),
    (DD, 3 * DD),
    (DD, DD),
    (DD,),
    (DD,),
    (DD, FD),
    (FD,),
    (FD, DD),
    (DD,),
    (DD,),
    (DD,),
    (DD, HEAD),
    (HEAD,),
]
LENT = [(DE, DE), (FE, DE)]


DP_GRID = (4, 2, 2)
ORDERS = (("y", "z", "x"), ("x", "z", "y"), ("z", "x", "y"))
WAYS = ("x", "y", "up", "down")
CHUNK = 16
OPPOSITE = {"x": "x", "y": "y", "up": "down", "down": "up"}


def part_ranges(units):
    first = int(units * 0.41)
    second = int(units * 0.26)
    return [(0, first), (first, second), (first + second, units - first - second)]


def relatives():
    places = [(dz, dy, dx) for dz in range(-3, 4) for dy in (0, 1) for dx in (0, 1)]
    places.remove((0, 0, 0))
    return sorted(places, key=lambda r: abs(r[0]) + r[1] + r[2])


def last_axis(order, place):
    differs = {"z": place[0] != 0, "y": place[1] != 0, "x": place[2] != 0}
    return [axis for axis in order if differs[axis]][-1]


def onward(order, place):
    if place == (0, 0, 0):
        return ["up", "down", "x", "y"]
    axis = last_axis(order, place)
    ways = []
    if axis == "z":
        ways.append("up" if place[0] < 0 else "down")
    for later in order[order.index(axis) + 1 :]:
        ways += ["up", "down"] if later == "z" else [later]
    return ways


def when(condition, action):
    if condition is None:
        action()
    else:
        pl.when(condition)(action)


def both(left, right):
    if left is None:
        return right
    return left if right is None else left & right


class Spot:
    def __init__(self):
        self.grp = lax.axis_index("grp")
        self.dp = lax.axis_index("dp")
        self.x = self.dp % 2
        self.y = (self.dp // 2) % 2
        self.z = self.dp // 4
        self.neighbour = {
            "x": (self.grp, self.index(self.z, self.y, 1 - self.x)),
            "y": (self.grp, self.index(self.z, 1 - self.y, self.x)),
            "up": (self.grp, self.index(jnp.minimum(self.z + 1, 3), self.y, self.x)),
            "down": (self.grp, self.index(jnp.maximum(self.z - 1, 0), self.y, self.x)),
            "core": (1 - self.grp, self.dp),
        }
        self.exists = {"x": None, "y": None, "up": self.z < 3, "down": self.z > 0, "core": None}

    def index(self, z, y, x):
        return z * 4 + y * 2 + x

    def at(self, place):
        z = self.z + place[0]
        y = 1 - self.y if place[1] else self.y
        x = 1 - self.x if place[2] else self.x
        inside = None if place[0] == 0 else (z >= 0) & (z <= 3)
        return z, self.index(z, y, x), inside

    def greet(self):
        barrier = pltpu.get_barrier_semaphore()
        me = self.grp * 16 + self.dp

        def signal(step, carry):
            other = (me + step) % 32
            pl.semaphore_signal(
                barrier, inc=1, device_id=(other // 16, other % 16), device_id_type=MESH
            )
            return carry

        lax.fori_loop(1, 32, signal, 0)
        pl.semaphore_wait(barrier, 31)


def tell_all(spot, tiles, send_sem, recv_sem):
    me = spot.grp * 16 + spot.dp

    def copy(number, other):
        return pltpu.make_async_remote_copy(
            src_ref=tiles.at[number],
            dst_ref=tiles.at[number],
            send_sem=send_sem.at[other],
            recv_sem=recv_sem.at[number],
            device_id=(other // 16, other % 16),
            device_id_type=MESH,
        )

    def start(step, carry):
        copy(me, (me + step) % 32).start()
        return carry

    def finish(step, carry):
        other = (me + step) % 32
        copy(other, other).wait_recv()
        copy(me, other).wait_send()
        return carry

    return (
        lambda: lax.fori_loop(1, 32, start, 0),
        lambda: lax.fori_loop(1, 32, finish, 0),
    )


def gather_kernel(
    master_ref,
    masked_ref,
    out_ref,
    masked_out,
    master,
    own_ref,
    tiles,
    local_sem,
    send_sem,
    recv_sem,
    core_send,
    core_recv,
    tile_send,
    tile_recv,
):
    spot = Spot()
    read = pltpu.make_async_copy(master_ref, master, local_sem)
    read.start()
    tiles[spot.grp * 16 + spot.dp] = masked_ref[...]
    spot.greet()
    tell, told = tell_all(spot, tiles, tile_send, tile_recv)
    ranges = part_ranges(own_ref.shape[0])
    read.wait()

    def round_off(start, length):
        block = pl.ds(start, length)
        own_ref[block] = master[block].astype(BF16)

    def step(index, carry):
        round_off(index * CHUNK, CHUNK)
        return carry

    units = own_ref.shape[0]
    lax.fori_loop(0, units // CHUNK, step, 0)
    if units % CHUNK:
        round_off(units - units % CHUNK, units % CHUNK)

    def copy(part, source, way, from_own):
        target = out_ref.at[spot.grp, source, pl.ds(*ranges[part])]
        origin = own_ref.at[pl.ds(*ranges[part])] if from_own else target
        if way == "core":
            sems = (core_send.at[part, source], core_recv.at[part, source])
        else:
            sems = (send_sem.at[part, source, WAYS.index(way)], recv_sem.at[part, source])
        return pltpu.make_async_remote_copy(
            src_ref=origin,
            dst_ref=target,
            send_sem=sems[0],
            recv_sem=sems[1],
            device_id=spot.neighbour[way],
            device_id_type=MESH,
        )

    sent = []
    for part in (2, 0, 1):
        for way in onward(ORDERS[part], (0, 0, 0)):
            when(
                spot.exists[way],
                lambda part=part, way=way: copy(part, spot.dp, way, True).start(),
            )
            sent.append((part, spot.dp, way, spot.exists[way], True))
    local = pltpu.make_async_copy(own_ref, out_ref.at[spot.grp, spot.dp], local_sem)
    local.start()
    tell()
    for part in range(3):
        copy(part, spot.dp, "core", True).start()
        sent.append((part, spot.dp, "core", None, True))
    for place in relatives():
        _, source, inside = spot.at(place)
        for part in range(3):
            ways = onward(ORDERS[part], place)

            def pass_on(part=part, source=source, ways=ways):
                copy(part, source, "x", False).wait_recv()
                for way in ways:
                    when(
                        spot.exists[way],
                        lambda way=way: copy(part, source, way, False).start(),
                    )
                copy(part, source, "core", False).start()

            when(inside, pass_on)
            for way in ways + ["core"]:
                sent.append((part, source, way, both(inside, spot.exists[way]), False))
    for part, source, way, condition, from_own in sent:
        when(condition, lambda: copy(part, source, way, from_own).wait_send())

    def await_core(source, carry):
        for part in range(3):
            landed = out_ref.at[1 - spot.grp, source, pl.ds(*ranges[part])]
            pltpu.make_async_remote_copy(
                src_ref=landed,
                dst_ref=landed,
                send_sem=core_send.at[part, source],
                recv_sem=core_recv.at[part, source],
                device_id=spot.neighbour["core"],
                device_id_type=MESH,
            ).wait_recv()
        return carry

    lax.fori_loop(0, 16, await_core, 0)
    told()
    masked_out[...] = jnp.sum(tiles[pl.ds(0, 16)], axis=0)
    local.wait()


def gather_rows(master, masked):
    units = master.shape[0]
    dma = pltpu.SemaphoreType.DMA
    anywhere = pl.BlockSpec(memory_space=pl.ANY)
    vmem = pl.BlockSpec(memory_space=pltpu.VMEM)
    return pl.pallas_call(
        gather_kernel,
        out_shape=(
            jax.ShapeDtypeStruct((2, 16, units, 4, LANES), BF16),
            jax.ShapeDtypeStruct((8, LANES), F32),
        ),
        in_specs=[anywhere, vmem],
        out_specs=(anywhere, vmem),
        scratch_shapes=[
            pltpu.VMEM((units, 4, LANES), F32),
            pltpu.VMEM((units, 4, LANES), BF16),
            pltpu.VMEM((32, 8, LANES), F32),
            dma,
            dma((3, 16, 4)),
            dma((3, 16)),
            dma((3, 16)),
            dma((3, 16)),
            dma((32,)),
            dma((32,)),
        ],
        compiler_params=pltpu.CompilerParams(collective_id=0, has_side_effects=True),
        name="gather_rows",
    )(master, masked)


def slot_tables():
    tables = []
    for order in ORDERS:
        table = {}
        for way in WAYS:
            keys = []
            along = False
            for place in [(0, 0, 0)] + relatives():
                if way in onward(order, place):
                    if place[1:] not in keys:
                        keys.append(place[1:])
                    along = along or place[0] != 0
            table[way] = (keys, 3 if way in ("up", "down") else (4 if along else 1))
        tables.append(table)
    return tables


SLOTS = slot_tables()
STAGES = 4


def scatter_kernel(grad_ref, loss_ref, out_ref, sums_ref, *refs):
    ranges = part_ranges(grad_ref.shape[1])
    landing = {}
    for part in range(3):
        for number, way in enumerate(WAYS):
            landing[part, way] = refs[part * 4 + number]
    stage, total, tiles, send_sem, recv_sem, stage_sem, out_sem, tile_send, tile_recv = refs[12:]
    spot = Spot()
    spot.greet()

    def slot(part, way, place, z):
        keys, depth = SLOTS[part][way]
        base = keys.index(place[1:]) * depth
        if way == "up":
            return base + z
        if way == "down":
            return base + z - 1
        return base + (z if depth == 4 else 0)

    def parent(part, place):
        axis = last_axis(ORDERS[part], place)
        if axis == "z":
            return "up" if place[0] > 0 else "down"
        return axis

    def seen_from_parent(part, place):
        way = parent(part, place)
        dz, dy, dx = place
        if way == "x":
            return (dz, dy, 0)
        if way == "y":
            return (dz, 0, dx)
        return (dz - 1 if way == "up" else dz + 1, dy, dx)

    def send(part, place, origin):
        z, owner, _ = spot.at(place)
        way = parent(part, place)
        back = OPPOSITE[way]
        return pltpu.make_async_remote_copy(
            src_ref=origin,
            dst_ref=landing[part, back].at[slot(part, back, seen_from_parent(part, place), z)],
            send_sem=send_sem.at[part, owner],
            recv_sem=recv_sem.at[part, owner, WAYS.index(back)],
            device_id=spot.neighbour[way],
            device_id_type=MESH,
        )

    def own(part, owner):
        return grad_ref.at[owner, pl.ds(*ranges[part])]

    nodes = [((0, 0, 0), part) for part in (2, 0, 1)]
    nodes += [(place, part) for place in relatives() for part in range(3)]
    nodes.reverse()
    sent = []
    inner = []
    for place, part in nodes:
        ways = onward(ORDERS[part], place)
        z, owner, inside = spot.at(place)
        if ways:
            inner.append((part, place, ways, z, owner, inside))
        else:
            when(inside, lambda: send(part, place, own(part, owner)).start())
        if place != (0, 0, 0):
            sent.append((part, place, owner, inside))

    def staged(number):
        part, _, _, _, owner, _ = inner[number]
        return pltpu.make_async_copy(
            own(part, owner),
            stage.at[number % STAGES, pl.ds(0, ranges[part][1])],
            stage_sem.at[number % STAGES],
        )

    for number in range(STAGES - 1):
        when(inner[number][5], lambda: staged(number).start())
    for number, (part, place, ways, z, owner, inside) in enumerate(inner):
        ahead = number + STAGES - 1
        if ahead < len(inner):
            when(inner[ahead][5], lambda: staged(ahead).start())
        length = ranges[part][1]
        root = place == (0, 0, 0)

        def combine(arriving, number=number, part=part, place=place, z=z, owner=owner):
            slots = []
            for way in arriving:
                spot_of = landing[part, way].at[slot(part, way, place, z)]
                pltpu.make_async_remote_copy(
                    src_ref=spot_of,
                    dst_ref=spot_of,
                    send_sem=send_sem.at[part, owner],
                    recv_sem=recv_sem.at[part, owner, WAYS.index(way)],
                    device_id=spot.neighbour[way],
                    device_id_type=MESH,
                ).wait_recv()
                slots.append(spot_of)
            staged(number).wait()
            if slots:
                target = total.at[pl.ds(*ranges[part])] if root else slots[0]

                def add(start, count):
                    value = stage[number % STAGES, pl.ds(start, count)]
                    for item in slots:
                        value = value + item[pl.ds(start, count)]
                    target[pl.ds(start, count)] = value

                def step(index, carry):
                    add(index * CHUNK, CHUNK)
                    return carry

                lax.fori_loop(0, length // CHUNK, step, 0)
                if length % CHUNK:
                    add(length - length % CHUNK, length % CHUNK)
            if not root:
                send(part, place, slots[0] if slots else own(part, owner)).start()

        def choose(ways=ways, combine=combine):
            flat = [way for way in ways if way in ("x", "y")]
            along = [way for way in ways if way in ("up", "down")]
            if not along:
                combine(flat)
            elif len(along) == 1:
                there = spot.exists[along[0]]
                pl.when(there)(lambda: combine(flat + along))
                pl.when(jnp.logical_not(there))(lambda: combine(flat))
            else:
                up, down = spot.exists["up"], spot.exists["down"]
                pl.when(up & down)(lambda: combine(flat + ["up", "down"]))
                pl.when(jnp.logical_not(down))(lambda: combine(flat + ["up"]))
                pl.when(jnp.logical_not(up))(lambda: combine(flat + ["down"]))

        when(inside, choose)
    out = pltpu.make_async_copy(total, out_ref, out_sem)
    out.start()
    units = total.shape[0]

    def square(start, count, running):
        value = total[pl.ds(start, count)]
        return running + jnp.sum(value * value, axis=0)

    squares = lax.fori_loop(
        0,
        units // CHUNK,
        lambda index, running: square(index * CHUNK, CHUNK, running),
        jnp.zeros((4, LANES), F32),
    )
    if units % CHUNK:
        squares = square(units - units % CHUNK, units % CHUNK, squares)
    me = spot.grp * 16 + spot.dp
    tiles[me, pl.ds(0, 4)] = squares
    tiles[me, pl.ds(4, 4)] = loss_ref[pl.ds(4, 4)]
    tell, told = tell_all(spot, tiles, tile_send, tile_recv)
    tell()
    for part, place, owner, inside in sent:
        when(inside, lambda: send(part, place, own(part, owner)).wait_send())
    told()
    sums_ref[...] = jnp.sum(tiles[...], axis=0)
    out.wait()


def scatter_sums(grads, loss):
    units = grads.shape[1]
    ranges = part_ranges(units)
    scratch = []
    for part in range(3):
        for way in WAYS:
            keys, depth = SLOTS[part][way]
            scratch.append(pltpu.VMEM((len(keys) * depth, ranges[part][1], 4, LANES), F32))
    largest = max(length for _, length in ranges)
    dma = pltpu.SemaphoreType.DMA
    scratch += [
        pltpu.VMEM((STAGES, largest, 4, LANES), F32),
        pltpu.VMEM((units, 4, LANES), F32),
        pltpu.VMEM((32, 8, LANES), F32),
        dma((3, 16)),
        dma((3, 16, 4)),
        dma((STAGES,)),
        dma,
        dma((32,)),
        dma((32,)),
    ]
    anywhere = pl.BlockSpec(memory_space=pl.ANY)
    vmem = pl.BlockSpec(memory_space=pltpu.VMEM)
    return pl.pallas_call(
        scatter_kernel,
        out_shape=(
            jax.ShapeDtypeStruct((units, 4, LANES), F32),
            jax.ShapeDtypeStruct((8, LANES), F32),
        ),
        in_specs=[anywhere, vmem],
        out_specs=(anywhere, vmem),
        scratch_shapes=scratch,
        compiler_params=pltpu.CompilerParams(
            collective_id=1, has_side_effects=True, vmem_limit_bytes=63 * 2**20
        ),
        name="scatter_sums",
    )(grads, loss)


def update_values(owned, squares, params, first_moment, second_moment, average):
    clipped = owned * jnp.minimum(1.0, CLIP / jnp.sqrt(squares))
    new_first = BETA_ONE * first_moment + (1.0 - BETA_ONE) * clipped
    new_second = BETA_TWO * second_moment + (1.0 - BETA_TWO) * clipped * clipped
    direction = (
        new_first
        / (1.0 - BETA_ONE**STEP)
        / (jnp.sqrt(new_second / (1.0 - BETA_TWO**STEP)) + ADAM_EPS)
    )
    new_params = params - RATE * (direction + DECAY_WEIGHT * params)
    new_average = AVERAGE_KEEP * average + (1.0 - AVERAGE_KEEP) * new_params
    return new_params, new_first, new_second, new_average


def update_kernel(squares_ref, owned, params, first, second, average, *outs):
    squares = squares_ref[0]

    def step(index, carry):
        block = pl.ds(index * 5, 5)
        values = update_values(
            owned[block], squares, params[block], first[block], second[block], average[block]
        )
        for out, value in zip(outs, values):
            out[block] = value
        return carry

    lax.fori_loop(0, owned.shape[0] // 5, step, 0)


def update(squares, arrays):
    units = arrays[0].shape[0]
    depth = 155
    spec = pl.BlockSpec((depth, 4, LANES), lambda i: (i, 0, 0))
    return pl.pallas_call(
        update_kernel,
        grid=(units // depth,),
        out_shape=[jax.ShapeDtypeStruct((units, 4, LANES), F32)] * 4,
        in_specs=[pl.BlockSpec(memory_space=pltpu.SMEM)] + [spec] * 5,
        out_specs=[spec] * 4,
        name="update",
    )(squares.reshape(1), *arrays)


def sections(layout, base):
    matrices, vectors = [], []
    offset = base
    for shape in layout:
        (matrices if len(shape) == 2 else vectors).append((offset, shape))
        offset += math.prod(shape)
    return matrices, vectors


def matrix_plan(rows):
    enc_matrices, enc_vectors = sections(ENC_LAYOUT, 0)
    dec_matrices, dec_vectors = sections(DEC_LAYOUT, rows * LANES)
    lent = rows * LANES + NDEC
    matrices = enc_matrices + sections(LENT, lent)[0] + dec_matrices
    return matrices, enc_vectors, dec_vectors


def padded(columns):
    return -(-columns // LANES) * LANES


def block_depth(shape):
    if shape[1] % LANES:
        return shape[0]
    depth = shape[0]
    while depth * shape[1] > PIECE * LANES:
        depth //= 2
    return depth


def matrix_kernel(rows, flat_ref, *refs):
    matrices, enc_vectors, dec_vectors = matrix_plan(rows)
    count = len(matrices)
    out_refs = refs[:count]
    vector_refs = refs[count : count + 2]
    blocks = refs[count + 2 : 2 * count + 2]
    flat_in, wide, pairs, vector_in, in_sem, out_sem, vector_sem = refs[2 * count + 2 :]
    lane = lax.broadcasted_iota(jnp.int32, (1, LANES), 1)

    chunks = []
    for number, (offset, shape) in enumerate(matrices):
        depth = block_depth(shape)
        for start in range(0, shape[0], depth):
            place = offset + start * shape[1]
            chunks.append((number, start, depth, place // LANES, place % LANES))

    def load(index):
        number, _, depth, first, shift = chunks[index]
        length = depth * matrices[number][1][1] // LANES
        begin = first // 16 * 16
        end = -(-(first + length + (1 if shift else 0)) // 16) * 16
        copy = pltpu.make_async_copy(
            flat_ref.at[pl.ds(begin, end - begin)],
            flat_in.at[index % 2, pl.ds(0, end - begin)],
            in_sem.at[index % 2],
        )
        return copy, first - begin, end - begin

    def store(index):
        number, start, depth, _, _ = chunks[index]
        slot = start // depth % 2
        return pltpu.make_async_copy(
            blocks[number].at[slot], out_refs[number].at[pl.ds(start, depth)], out_sem.at[number, slot]
        )

    def widen(index, length):
        step = 256

        def one(start, size):
            wide[pl.ds(start, size)] = flat_in[index % 2, pl.ds(start, size)].astype(F32)

        def loop(i, carry):
            one(pl.multiple_of(i * step, step), step)
            return carry

        lax.fori_loop(0, length // step, loop, 0)
        if length % step:
            one(length - length % step, length % step)

    def turned(first, second):
        return pltpu.roll(jnp.where(lane < LANES // 2, second, first), LANES // 2, 1)

    def arrange(index, phase):
        number, start, depth, _, shift = chunks[index]
        columns = matrices[number][1][1]
        block = blocks[number].at[start // depth % 2]
        tiles = columns // LANES

        def plain(i, carry):
            row = pl.multiple_of(i * SUB, SUB)
            for tile in range(tiles):
                value = wide[pl.ds(phase + row * tiles + tile, SUB, stride=tiles)]
                if shift:
                    after = wide[pl.ds(phase + row * tiles + tile + 1, SUB, stride=tiles)]
                    value = turned(value, after)
                block[pl.ds(row, SUB), pl.ds(tile * LANES, LANES)] = value.astype(BF16)
            return carry

        def paired(i, carry):
            stride = 2 * columns // LANES
            half = SUB // 2
            row = pl.multiple_of(i * half, half)
            for tile in range(tiles + 1):
                even = wide[pl.ds(phase + row * stride + tile, half, stride=stride)]
                odd = wide[pl.ds(phase + row * stride + tiles + tile, half, stride=stride)]
                if tile < tiles:
                    after = wide[pl.ds(phase + row * stride + tiles + tile + 1, half, stride=stride)]
                    odd = turned(odd, after)
                else:
                    even = jnp.where(lane < LANES // 2, even, 0.0)
                    odd = jnp.where(lane < LANES // 2, pltpu.roll(odd, LANES // 2, 1), 0.0)
                lanes = pl.ds(tile * LANES, LANES)
                pairs[tile, pl.ds(0, half, stride=2)] = even
                pairs[tile, pl.ds(1, half, stride=2)] = odd
                block[pl.ds(pl.multiple_of(i * SUB, SUB), SUB), lanes] = pairs[tile].astype(BF16)
            return carry

        lax.fori_loop(0, depth // SUB, paired if columns % LANES else plain, 0)

    windows = []
    wanted = [(0, n, v) for n, v in enumerate(enc_vectors)]
    wanted += [(1, n, v) for n, v in enumerate(dec_vectors)]
    for _, _, (offset, shape) in wanted:
        first = offset // LANES // 16 * 16
        end = -(-(offset // LANES + -(-shape[0] // LANES)) // 16) * 16
        if windows and first <= windows[-1][1]:
            windows[-1][1] = max(windows[-1][1], end)
        else:
            windows.append([first, end])
    bases = [sum(e - f for f, e in windows[:n]) for n in range(len(windows))]

    def vector_copy(n):
        first, end = windows[n]
        return pltpu.make_async_copy(
            flat_ref.at[pl.ds(first, end - first)],
            vector_in.at[pl.ds(bases[n], end - first)],
            vector_sem.at[n],
        )

    load(0)[0].start()
    for n in range(len(windows)):
        vector_copy(n).start()
    for index, (number, start, depth, _, _) in enumerate(chunks):
        copy, phase, length = load(index)
        copy.wait()
        if index + 1 < len(chunks):
            load(index + 1)[0].start()
        widen(index, length)
        if start // depth >= 2:
            store(index - 2).wait()
        arrange(index, phase)
        store(index).start()
    for n in range(len(windows)):
        vector_copy(n).wait()
    total = bases[-1] + windows[-1][1] - windows[-1][0]
    wide[pl.ds(0, total)] = vector_in[...].astype(F32)
    for group, n, (offset, shape) in wanted:
        first = offset // LANES
        window = [k for k, (f, e) in enumerate(windows) if f <= first < e][0]
        base = bases[window] + first - windows[window][0]
        for tile in range(-(-shape[0] // LANES)):
            value = wide[pl.ds(base + tile, 1)]
            if shape[0] - tile * LANES < LANES:
                value = jnp.where(lane < shape[0] - tile * LANES, value, 0.0)
            vector_refs[group][pl.ds(n, 1), pl.ds(tile * LANES, LANES)] = value
    for index, (number, start, depth, _, _) in enumerate(chunks):
        if start + 2 * depth >= matrices[number][1][0]:
            store(index).wait()


def weight_matrices(flat):
    rows = flat.shape[0] // 2
    matrices, enc_vectors, dec_vectors = matrix_plan(rows)
    shapes = [(shape[0], padded(shape[1])) for _, shape in matrices]
    buffers = []
    for (_, shape), (_, columns) in zip(matrices, shapes):
        depth = block_depth(shape)
        buffers.append(pltpu.VMEM((min(2, shape[0] // depth), depth, columns), BF16))
    dma = pltpu.SemaphoreType.DMA
    windows = 0
    last = -1
    total = 0
    for offset, shape in enc_vectors + dec_vectors:
        first = offset // LANES // 16 * 16
        end = -(-(offset // LANES + -(-shape[0] // LANES)) // 16) * 16
        if first <= last:
            total += max(0, end - last)
            last = max(last, end)
        else:
            windows += 1
            total += end - first
            last = end
    anywhere = pl.BlockSpec(memory_space=pl.ANY)
    vmem = pl.BlockSpec(memory_space=pltpu.VMEM)
    return pl.pallas_call(
        functools.partial(matrix_kernel, rows),
        out_shape=[jax.ShapeDtypeStruct(shape, BF16) for shape in shapes]
        + [jax.ShapeDtypeStruct((VEC_ROWS, columns), F32) for columns in VEC_COLS],
        in_specs=[anywhere],
        out_specs=[anywhere] * len(shapes) + [vmem, vmem],
        scratch_shapes=buffers
        + [
            pltpu.VMEM((2, PIECE + 32, LANES), BF16),
            pltpu.VMEM((PIECE + 32, LANES), F32),
            pltpu.VMEM((padded(HEAD) // LANES, SUB, LANES), F32),
            pltpu.VMEM((total, LANES), BF16),
            dma((2,)),
            dma((len(shapes), 2)),
            dma((windows,)),
        ],
        compiler_params=pltpu.CompilerParams(vmem_limit_bytes=56 * 2**20),
        name="weight_matrices",
    )(flat)


def stream_items(layout, lent):
    items = []
    offset = 0
    numbers = [0, 0]
    for shape in layout + lent:
        matrix = len(shape) == 2
        number = numbers[matrix]
        numbers[matrix] += 1
        depth = block_depth(shape) if matrix else 0
        for start in range(0, shape[0] if matrix else 1, max(depth, 1)):
            items.append((matrix, number, shape, start, depth, offset))
            offset += depth * shape[1] if matrix else shape[0]
    return items, offset


def product_kernel(rows, layout, lent, count, *refs):
    factors = [refs[4 * n : 4 * n + 4] for n in range(count)]
    mine_ref, other_ref, out_ref = refs[4 * count : 4 * count + 3]
    refs = refs[4 * count + 3 :]
    lefts, rights = refs[:count], refs[count : 2 * count]
    turned_left, tall, rows_out, in_sem, out_sem = refs[2 * count :]
    lane = lax.broadcasted_iota(jnp.int32, (1, LANES), 1)
    half = LANES // 2

    def load(n):
        copies = []
        for side, buffer in ((0, lefts[n]), (1, rights[n])):
            length = factors[n][2 * side].shape[0]
            for part in range(2):
                copies.append(
                    pltpu.make_async_copy(
                        factors[n][2 * side + part],
                        buffer.at[pl.ds(part * length, length)],
                        in_sem.at[n, 2 * side + part],
                    )
                )
        return copies

    for n in range(count):
        for copy in load(n):
            copy.start()

    items, used = stream_items(layout, lent)
    groups = []
    current = []
    for item in items:
        current.append(item)
        if item[0]:
            groups.append(current)
            current = []
    groups.append(current)

    def vector(item, buffer, base):
        _, number, shape, _, _, _ = item
        for tile in range(-(-shape[0] // LANES)):
            lanes = pl.ds(tile * LANES, LANES)
            buffer[pl.ds(base + tile, 1)] = (
                mine_ref[pl.ds(number, 1), lanes] + other_ref[pl.ds(number, 1), lanes]
            )

    def matrix(item, buffer, base):
        _, number, shape, start, depth, offset = item
        columns = shape[1]
        shifted = offset % LANES
        tiles = -(-columns // LANES)
        width = min(WIDTH, columns)
        if start == 0:
            for copy in load(number):
                copy.wait()
            if shifted:
                length = rights[number].shape[0]

                def turn(i, carry):
                    block = pl.ds(pl.multiple_of(i * 64, 64), 64)
                    value = rights[number][block].astype(F32)
                    rights[number][block] = pltpu.roll(value, half, 1).astype(BF16)
                    return carry

                lax.fori_loop(0, length // 64, turn, 0)
        length = lefts[number].shape[0]
        sub = min(256, depth)

        def loop(step, carry):
            k = pl.multiple_of(start + step * sub, sub)
            turned_left[pl.ds(0, sub), pl.ds(0, length)] = lefts[number][:, pl.ds(k, sub)].T

            def across(c, carry):
                column = pl.multiple_of(c * width, width)
                value = jnp.dot(
                    turned_left[pl.ds(0, sub), pl.ds(0, length)],
                    rights[number][:, pl.ds(column, width)],
                    preferred_element_type=F32,
                )
                row = base + step * sub * tiles
                for piece in range(width // LANES):
                    part = value[:, piece * LANES : (piece + 1) * LANES]
                    tile = c * (width // LANES) + piece
                    if columns % LANES:
                        tall[tile, pl.ds(step * sub, sub)] = part
                    elif shifted and piece == 0:
                        first = row + tile

                        @pl.when(c == 0)
                        def _():
                            before = pltpu.roll(part, 1, 0)
                            index = lax.broadcasted_iota(jnp.int32, (sub, LANES), 0)
                            held = buffer[pl.ds(row, 1)]
                            before = jnp.where(index == 0, held, before)
                            merged = jnp.where(lane < half, before, part)
                            buffer[pl.ds(row, sub, stride=tiles)] = merged
                            buffer[pl.ds(row + sub * tiles, 1)] = part[sub - 1 :]

                        @pl.when(c > 0)
                        def _():
                            buffer[pl.ds(first, sub, stride=tiles)] = part
                    else:
                        buffer[pl.ds(row + tile, sub, stride=tiles)] = part
                return carry

            lax.fori_loop(0, tiles * LANES // width, across, 0)
            return carry

        lax.fori_loop(0, depth // sub, loop, 0)
        if columns % LANES:
            stride = 2 * columns // LANES
            pair = 64

            def weave(i, carry):
                k = pl.multiple_of(i * 2 * pair, 2 * pair)
                row = base + i * pair * stride
                evens = [tall[t, pl.ds(k, pair, stride=2)] for t in range(tiles)]
                odds = [tall[t, pl.ds(k + 1, pair, stride=2)] for t in range(tiles)]
                for t in range(tiles - 1):
                    buffer[pl.ds(row + t, pair, stride=stride)] = evens[t]
                middle = jnp.where(lane < half, evens[-1], pltpu.roll(odds[0], half, 1))
                buffer[pl.ds(row + tiles - 1, pair, stride=stride)] = middle
                for t in range(1, tiles):
                    both_halves = jnp.where(lane < half, odds[t], odds[t - 1])
                    buffer[pl.ds(row + tiles - 1 + t, pair, stride=stride)] = pltpu.roll(
                        both_halves, half, 1
                    )
                return carry

            lax.fori_loop(0, depth // 2 // pair, weave, 0)

    flights = []
    tail = None
    for number, group in enumerate(groups):
        slot = number % 2
        buffer = rows_out.at[slot]
        if number >= 2:
            flights[number - 2].wait()
        first = group[0][5] // LANES if group else used // LANES
        begin = first // 8 * 8
        if tail is not None:
            buffer[pl.ds(0, 8)] = rows_out[1 - slot, pl.ds(tail, 8)]
        for item in group:
            (matrix if item[0] else vector)(item, buffer, item[5] // LANES - begin)
        last = number == len(groups) - 1
        if last:
            at = used // LANES - begin
            if used % LANES:
                buffer[pl.ds(at, 1)] = jnp.where(lane < used % LANES, buffer[pl.ds(at, 1)], 0.0)
                at += 1
            length = rows - begin
            if length > at:
                buffer[pl.ds(at, length - at)] = jnp.zeros((length - at, LANES), F32)
        else:
            end = groups[number + 1][0][5] if groups[number + 1] else used
            tail = (end // LANES - begin) // 8 * 8
            length = tail
        flight = pltpu.make_async_copy(
            buffer.at[pl.ds(0, length)], out_ref.at[pl.ds(begin, length)], out_sem.at[slot]
        )
        flight.start()
        flights.append(flight)
    for flight in flights[-2:]:
        flight.wait()


def flat_gradient(rows, layout, lent, factors, mine, other):
    shapes = [shape for shape in layout if len(shape) == 2] + lent
    lefts = [pltpu.VMEM((2 * f[0].shape[0], f[0].shape[1]), BF16) for f in factors]
    rights = [pltpu.VMEM((2 * f[2].shape[0], f[2].shape[1]), BF16) for f in factors]
    longest = max(2 * f[0].shape[0] for f in factors)
    dma = pltpu.SemaphoreType.DMA
    anywhere = pl.BlockSpec(memory_space=pl.ANY)
    vmem = pl.BlockSpec(memory_space=pltpu.VMEM)
    return pl.pallas_call(
        functools.partial(product_kernel, rows, layout, lent, len(shapes)),
        out_shape=jax.ShapeDtypeStruct((rows, LANES), F32),
        in_specs=[anywhere] * (4 * len(shapes)) + [vmem, vmem],
        out_specs=anywhere,
        scratch_shapes=lefts
        + rights
        + [
            pltpu.VMEM((256, longest), BF16),
            pltpu.VMEM((padded(HEAD) // LANES, DD, LANES), F32),
            pltpu.VMEM((2, PIECE + 128, LANES), F32),
            dma((len(shapes), 4)),
            dma((2,)),
        ],
        compiler_params=pltpu.CompilerParams(vmem_limit_bytes=62 * 2**20),
        name="flat_gradient",
    )(*[a for f in factors for a in f], mine, other)


Bag = types.SimpleNamespace


def position_code(position, scales, width):
    quarter = width // 4
    frequency = jnp.exp(jnp.arange(quarter, dtype=F32) * (-math.log(10000.0) / quarter))
    row_angle = ((position // GSIDE).astype(F32) * scales)[..., None] * frequency
    col_angle = ((position % GSIDE).astype(F32) * scales)[..., None] * frequency
    return jnp.concatenate(
        [jnp.sin(row_angle), jnp.cos(row_angle), jnp.sin(col_angle), jnp.cos(col_angle)], axis=-1
    )


def bands(pixel_rows):
    pixel_ids = jnp.arange(PIX, dtype=jnp.int32)
    coarse = (
        pixel_ids // (3 * PSIDE) // 2 * (PSIDE // 2) + pixel_ids // 3 % PSIDE // 2
    ) * 3 + pixel_ids % 3
    pool_table = (coarse[:, None] == jnp.arange(LOWPIX, dtype=jnp.int32)[None, :]).astype(F32)
    low_band = jnp.dot(pixel_rows, pool_table, precision=HIGHEST) * 0.25
    high_band = pixel_rows - jnp.dot(low_band, pool_table.T, precision=HIGHEST)
    return (low_band, high_band)


def linear(left, right):
    return jnp.einsum("...k,kn->...n", left, right, preferred_element_type=F32)


def input_grad(grad_rows, right):
    return jnp.einsum("...n,kn->...k", grad_rows, right, preferred_element_type=F32)


def norm_forward(state, gain, shift):
    centered = state - jnp.mean(state, axis=-1, keepdims=True)
    inverse = lax.rsqrt(jnp.mean(centered * centered, axis=-1, keepdims=True) + NORM_EPS)
    unit_rows = centered * inverse
    return (unit_rows * gain.astype(F32) + shift.astype(F32), unit_rows, inverse)


def norm_backward(grad_out, unit_rows, inverse, gain):
    grad_unit = grad_out * gain.astype(F32)
    grad_in = inverse * (
        grad_unit
        - jnp.mean(grad_unit, axis=-1, keepdims=True)
        - unit_rows * jnp.mean(grad_unit * unit_rows, axis=-1, keepdims=True)
    )
    return (grad_in, jnp.sum(grad_out * unit_rows, axis=(0, 1)), jnp.sum(grad_out, axis=(0, 1)))


def attention_scores(query_part, key_part, bias):
    head_dim = query_part.shape[-1]
    return (
        jnp.einsum("blhd,bmhd->bhlm", query_part, key_part, preferred_element_type=F32)
        * head_dim ** (-0.5)
        + bias
    )


def gelu_exact(values):
    return jax.nn.gelu(values, approximate=False)


def block_forward(state, weights, heads, bias):
    batch, length, width = state.shape
    normed_one, unit_one, inverse_one = norm_forward(state, weights.ln1_g, weights.ln1_b)
    normed_one = normed_one.astype(BF16)
    qkv = (
        linear(normed_one, weights.qkv_w)
        .astype(BF16)
        .reshape(batch, length, 3, heads, width // heads)
    )
    scores = attention_scores(qkv[:, :, 0], qkv[:, :, 1], bias)
    row_max = jnp.max(scores, axis=-1, keepdims=True)
    shifted = jnp.exp(scores - row_max)
    totals = jnp.sum(shifted, axis=-1, keepdims=True)
    attend = (shifted / totals).astype(BF16)
    logsum = row_max + jnp.log(totals)
    mixed = jnp.einsum("bhlm,bmhd->blhd", attend, qkv[:, :, 2], preferred_element_type=F32)
    mixed = mixed.astype(BF16).reshape(batch, length, width)
    middle = state + linear(mixed, weights.out_w)
    normed_two, unit_two, inverse_two = norm_forward(middle, weights.ln2_g, weights.ln2_b)
    normed_two = normed_two.astype(BF16)
    pre_act = linear(normed_two, weights.fc1_w) + weights.fc1_b.astype(F32)
    active = gelu_exact(pre_act).astype(BF16)
    output = middle + linear(active, weights.fc2_w) + weights.fc2_b.astype(F32)
    kept = Bag(
        normed_one=normed_one,
        unit_one=unit_one,
        inverse_one=inverse_one,
        qkv=qkv,
        logsum=logsum,
        mixed=mixed,
        unit_two=unit_two,
        inverse_two=inverse_two,
        normed_two=normed_two,
        active=active,
        pre_act=pre_act,
    )
    return (output, kept)


def block_backward(grad_out, kept, weights, heads, bias):
    batch, length, width = grad_out.shape
    grads = Bag()
    pairs = Bag()
    grad_low = grad_out.astype(BF16)
    pairs.fc2_w = (kept.active, grad_low)
    grads.fc2_b = jnp.sum(grad_out, axis=(0, 1))
    _, gelu_back = jax.vjp(gelu_exact, kept.pre_act)
    grad_pre = gelu_back(input_grad(grad_low, weights.fc2_w))[0]
    grads.fc1_b = jnp.sum(grad_pre, axis=(0, 1))
    grad_pre_low = grad_pre.astype(BF16)
    pairs.fc1_w = (kept.normed_two, grad_pre_low)
    grad_norm_in, grads.ln2_g, grads.ln2_b = norm_backward(
        input_grad(grad_pre_low, weights.fc1_w),
        kept.unit_two,
        kept.inverse_two,
        weights.ln2_g,
    )
    grad_mid = grad_out + grad_norm_in
    grad_mid_low = grad_mid.astype(BF16)
    pairs.out_w = (kept.mixed, grad_mid_low)
    grad_mixed = (
        input_grad(grad_mid_low, weights.out_w)
        .astype(BF16)
        .reshape(batch, length, heads, width // heads)
    )
    qkv = kept.qkv
    query_part, key_part, value_part = (qkv[:, :, 0], qkv[:, :, 1], qkv[:, :, 2])
    attend = jnp.exp(attention_scores(query_part, key_part, bias) - kept.logsum)
    grad_value = jnp.einsum(
        "bhlm,blhd->bmhd", attend.astype(BF16), grad_mixed, preferred_element_type=F32
    )
    grad_attend = jnp.einsum("blhd,bmhd->bhlm", grad_mixed, value_part, preferred_element_type=F32)
    grad_scores = (
        attend * (grad_attend - jnp.sum(grad_attend * attend, axis=-1, keepdims=True))
    ).astype(BF16)
    score_scale = (width // heads) ** (-0.5)
    grad_query = (
        jnp.einsum("bhlm,bmhd->blhd", grad_scores, key_part, preferred_element_type=F32)
        * score_scale
    )
    grad_key = (
        jnp.einsum("bhlm,blhd->bmhd", grad_scores, query_part, preferred_element_type=F32)
        * score_scale
    )
    grad_qkv = (
        jnp.stack([grad_query, grad_key, grad_value], axis=2)
        .reshape(batch, length, 3 * width)
        .astype(BF16)
    )
    pairs.qkv_w = (kept.normed_one, grad_qkv)
    grad_norm_in, grads.ln1_g, grads.ln1_b = norm_backward(
        input_grad(grad_qkv, weights.qkv_w),
        kept.unit_one,
        kept.inverse_one,
        weights.ln1_g,
    )
    return (grad_mid + grad_norm_in, grads, pairs)


def forward_backward(enc, dec, pixels, index_rows, counts, scales, masked_total):
    images = counts.shape[0]
    slots = jnp.arange(VMAX, dtype=jnp.int32)
    valid = slots[None, :] < counts[:, None]
    position = jnp.where(valid, index_rows, 0)
    pixel_images = jnp.pad(pixels.reshape(images, GRID, PIX), ((0, 0), (0, GPAD - GRID), (0, 0)))
    grid = jnp.arange(GPAD, dtype=jnp.int32)
    chosen = ((position[:, :, None] == grid[None, None, :]) & valid[:, :, None]).astype(BF16)
    patches = jnp.einsum("ivg,igp->ivp", chosen, pixel_images, preferred_element_type=F32)
    patches = patches.astype(BF16)
    enc_bias = jnp.where(valid, 0.0, MASK_FILL)[:, None, None, :]
    state = (
        linear(patches, enc.pe_w)
        + enc.pe_b.astype(F32)
        + position_code(position, scales[:, None], DE)
    )
    state, enc_kept = block_forward(state, enc, HE, enc_bias)
    enc_normed, enc_unit, enc_inverse = norm_forward(state, enc.lnf_g, enc.lnf_b)
    enc_normed = enc_normed.astype(BF16)
    sent = (linear(enc_normed, enc.emb_w) + enc.emb_b.astype(F32)).astype(BF16)

    placed = jnp.einsum("ivg,ivd->igd", chosen, sent, preferred_element_type=F32)
    seen = jnp.sum(chosen.astype(F32), axis=1)
    dec_bias = jnp.where(grid < GRID, 0.0, MASK_FILL)[None, None, None, :]
    state = jnp.where(
        seen[:, :, None] > 0.5, placed, dec.mask_tok.astype(F32)
    ) + position_code(jnp.broadcast_to(grid[None], (images, GPAD)), scales[:, None], DD)
    state, dec_kept = block_forward(state, dec, HD, dec_bias)
    normed, unit_rows, inverse = norm_forward(state, dec.lnf_g, dec.lnf_b)
    normed = normed.astype(BF16)
    predicted = linear(normed, dec.head_w[:, :HEAD]) + dec.head_b[:HEAD].astype(F32)
    low_band, high_band = bands(pixel_images.reshape(-1, PIX).astype(F32))
    low_band = low_band.reshape(images, GPAD, -1)
    high_band = high_band.reshape(images, GPAD, -1)
    miss_low = predicted[..., :LOWPIX] - low_band
    miss_high = predicted[..., LOWPIX:] - high_band
    unseen = jnp.where(grid[None] < GRID, 1.0 - seen, 0.0)
    per_patch = jnp.sum(miss_low * miss_low, axis=-1) + jnp.sum(
        jnp.sqrt(miss_high * miss_high + 1.0) - 1.0, axis=-1
    )
    loss_local = jnp.sum(per_patch * unseen)
    row_weight = unseen / masked_total
    grad_pred = (
        jnp.concatenate(
            [2.0 * miss_low, miss_high * lax.rsqrt(miss_high * miss_high + 1.0)], axis=-1
        )
        * row_weight[:, :, None]
    )
    grad_low = jnp.pad(grad_pred, ((0, 0), (0, 0), (0, padded(HEAD) - HEAD))).astype(BF16)
    dec_pairs = Bag(head_w=(normed, grad_low))
    dec_grads = Bag(head_b=jnp.sum(grad_low.astype(F32), axis=(0, 1)))
    grad_state, dec_grads.lnf_g, dec_grads.lnf_b = norm_backward(
        input_grad(grad_low, dec.head_w), unit_rows, inverse, dec.lnf_g
    )
    grad_state, block_grads, block_pairs = block_backward(grad_state, dec_kept, dec, HD, dec_bias)
    vars(dec_grads).update(vars(block_grads))
    vars(dec_pairs).update(vars(block_pairs))
    dec_grads.mask_tok = jnp.sum(grad_state * unseen[:, :, None], axis=(0, 1))
    grad_sent = jnp.einsum(
        "ivg,igd->ivd", chosen, grad_state.astype(BF16), preferred_element_type=F32
    ).astype(BF16)

    enc_pairs = Bag(emb_w=(enc_normed, grad_sent))
    enc_grads = Bag(emb_b=jnp.sum(grad_sent.astype(F32), axis=(0, 1)))
    grad_state, enc_grads.lnf_g, enc_grads.lnf_b = norm_backward(
        input_grad(grad_sent, enc.emb_w), enc_unit, enc_inverse, enc.lnf_g
    )
    grad_state, block_grads, block_pairs = block_backward(grad_state, enc_kept, enc, HE, enc_bias)
    vars(enc_grads).update(vars(block_grads))
    vars(enc_pairs).update(vars(block_pairs))
    enc_pairs.pe_w = (patches, grad_state.astype(BF16))
    enc_grads.pe_b = jnp.sum(grad_state, axis=(0, 1))
    return loss_local, enc_grads, enc_pairs, dec_grads, dec_pairs


def vector_rows(vectors, columns):
    rows = [jnp.pad(vector, (0, columns - vector.shape[0])) for vector in vectors]
    rows += [jnp.zeros((columns,), F32)] * (VEC_ROWS - len(rows))
    return jnp.stack(rows)


def to_core(array, core):
    return lax.ppermute(array, "grp", [(1 - core, core)])


def factor_list(pairs, core):
    factors = []
    for left, right in pairs:
        left = left.reshape(-1, left.shape[-1])
        right = right.reshape(-1, right.shape[-1])
        factors.append((left, to_core(left, core), right, to_core(right, core)))
    return factors


def gradient_row(rows, enc_grads, enc_pairs, dec_grads, dec_pairs):
    e, d = enc_grads, dec_grads
    enc_vectors = vector_rows(
        [e.pe_b, e.ln1_g, e.ln1_b, e.ln2_g, e.ln2_b, e.fc1_b, e.fc2_b, e.lnf_g, e.lnf_b, e.emb_b],
        VEC_COLS[0],
    )
    dec_vectors = vector_rows(
        [d.mask_tok, d.ln1_g, d.ln1_b, d.ln2_g, d.ln2_b]
        + [d.fc1_b, d.fc2_b, d.lnf_g, d.lnf_b, d.head_b],
        VEC_COLS[1],
    )
    e, d = enc_pairs, dec_pairs
    first = factor_list([e.pe_w, e.qkv_w, e.fc1_w, e.emb_w], 0)
    second = factor_list([d.qkv_w, d.out_w, d.fc1_w, d.fc2_w, d.head_w, e.out_w, e.fc2_w], 1)
    enc_other = to_core(enc_vectors, 0)
    dec_other = to_core(dec_vectors, 1)
    return lax.cond(
        lax.axis_index("grp") == 0,
        lambda: flat_gradient(rows, ENC_LAYOUT, [], first, enc_vectors, enc_other),
        lambda: flat_gradient(rows, DEC_LAYOUT, LENT, second, dec_vectors, dec_other),
    )


def bags(parts):
    enc, dec = Bag(), Bag()
    enc.pe_w, enc.qkv_w, enc.fc1_w, enc.emb_w, enc.out_w, enc.fc2_w = parts[:6]
    dec.qkv_w, dec.out_w, dec.fc1_w, dec.fc2_w, dec.head_w = parts[6:11]
    e, d = parts[11:]
    enc.pe_b, enc.ln1_g, enc.ln1_b, enc.ln2_g, enc.ln2_b = [e[n, :DE] for n in range(5)]
    enc.fc1_b = e[5]
    enc.fc2_b, enc.lnf_g, enc.lnf_b = [e[n, :DE] for n in range(6, 9)]
    enc.emb_b = e[9, :DD]
    dec.mask_tok, dec.ln1_g, dec.ln1_b, dec.ln2_g, dec.ln2_b = [d[n, :DD] for n in range(5)]
    dec.fc1_b = d[5]
    dec.fc2_b, dec.lnf_g, dec.lnf_b = [d[n, :DD] for n in range(6, 9)]
    dec.head_b = d[9, : padded(HEAD)]
    return enc, dec


def body(
    params, first_moment, second_moment, average, pixels, visible_index, visible_count, gsd_id
):
    chips = lax.axis_size("dp")
    rows = params.shape[1] // LANES
    special = chips == math.prod(DP_GRID) and rows % 4 == 0
    masked = jnp.sum(GRID - visible_count).astype(F32)
    if special:
        shards = [a.reshape(-1, 4, LANES) for a in (params, first_moment, second_moment, average)]
        copies, masked_tile = gather_rows(shards[0], jnp.full((8, LANES), masked))
        masked_total = masked_tile[0, 0]
    else:
        copies = lax.all_gather(params.astype(BF16).reshape(-1, LANES), "dp", axis=0, tiled=True)
        copies = lax.all_gather(copies, "grp", axis=0, tiled=True)
        masked_total = lax.psum(masked, "dp")
    enc, dec = bags(weight_matrices(copies.reshape(-1, LANES)))

    half = visible_count.shape[0] // 2
    core = lax.axis_index("grp")

    def mine(array, count):
        return lax.dynamic_slice_in_dim(array, core * count, count, 0)

    scales = 0.5 + 0.25 * mine(gsd_id, half).astype(F32)
    loss_local, enc_grads, enc_pairs, dec_grads, dec_pairs = forward_backward(
        enc,
        dec,
        mine(pixels, half * GRID),
        mine(visible_index, half),
        mine(visible_count, half),
        scales,
        masked_total,
    )
    gradient = gradient_row(chips * rows, enc_grads, enc_pairs, dec_grads, dec_pairs)
    if special:
        owned, sums = scatter_sums(
            gradient.reshape(chips, rows // 4, 4, LANES), jnp.full((8, LANES), loss_local)
        )
        squares = jnp.sum(sums[:4])
        loss_sum = sums[4, 0]
        outs = update(squares, [owned] + shards)
        outs = [out.reshape(params.shape) for out in outs]
    else:
        owned = lax.psum_scatter(gradient, "dp", scatter_dimension=0, tiled=True)
        owned = owned.reshape(params.shape)
        squares, loss_sum = lax.psum((jnp.sum(owned * owned), loss_local), ("grp", "dp"))
        outs = update_values(owned, squares, params, first_moment, second_moment, average)
    return (*outs, loss_sum, masked_total, jnp.sqrt(squares))


def solution(mesh):
    return jax.shard_map(
        body,
        mesh=mesh,
        in_specs=(P("grp", "dp"),) * 4 + (P("dp", None), P("dp", None), P("dp"), P("dp")),
        out_specs=(P("grp", "dp"),) * 4 + (P(), P(), P()),
        check_vma=False,
    )
```

```python
import functools
import math
import types

import jax
import jax.numpy as jnp
from jax import lax
from jax.experimental import pallas as pl
from jax.experimental.pallas import tpu as pltpu
from jax.sharding import PartitionSpec as P

DE = 1024
HE = 16
FE = 4096
DD = 512
HD = 16
FD = 2048
PSIDE = 16
GSIDE = 14
VMAX = 64
STEP = 10
PIX = 768
LOWPIX = 192
GRID = 196
GPAD = 208
NENC = 8662528
NDEC = 3644352
LANES = 128
UNIT = 4 * LANES

HIGHEST = lax.Precision.HIGHEST
CLIP = 0.05
RATE = 0.01
BETA_ONE = 0.5
BETA_TWO = 0.5
ADAM_EPS = 1e-08
DECAY_WEIGHT = 0.05
AVERAGE_KEEP = 0.9
NORM_EPS = 1e-06
MASK_FILL = -1000000000.0
F32 = jnp.float32
BF16 = jnp.bfloat16
MESH = pl.DeviceIdType.MESH

WIDTH = 256
SUB = 64
PIECE = 8192
VEC_ROWS = 16
VEC_COLS = (FE, FD)
HEAD = LOWPIX + PIX

ENC_LAYOUT = [
    (PIX, DE),
    (DE,),
    (DE,),
    (DE,),
    (DE, 3 * DE),
    (DE,),
    (DE,),
    (DE, FE),
    (FE,),
    (DE,),
    (DE,),
    (DE,),
    (DE, DD),
    (DD,),
]
DEC_LAYOUT = [
    (DD,),
    (DD,),
    (DD,),
    (DD, 3 * DD),
    (DD, DD),
    (DD,),
    (DD,),
    (DD, FD),
    (FD,),
    (FD, DD),
    (DD,),
    (DD,),
    (DD,),
    (DD, HEAD),
    (HEAD,),
]
LENT = [(DE, DE), (FE, DE)]


DP_GRID = (4, 2, 2)
YZX, XZY, ZXY = ("y", "z", "x"), ("x", "z", "y"), ("z", "x", "y")
SPLIT = 2
ORDERS = (YZX,) * SPLIT + (XZY,) * SPLIT + (ZXY,) * SPLIT
PARTS = len(ORDERS)
OWN_FIRST = tuple(range(2 * SPLIT, 3 * SPLIT)) + tuple(range(2 * SPLIT))
SHARES = (0.41, 0.26, 0.33)
WAYS = ("x", "y", "up", "down")
CHUNK = 16
OPPOSITE = {"x": "x", "y": "y", "up": "down", "down": "up"}


def part_ranges(units):
    ends = [0]
    for share in SHARES:
        for _ in range(SPLIT):
            ends.append(ends[-1] + share / SPLIT)
    ends = [round(end * units) for end in ends[:-1]] + [units]
    return [(start, end - start) for start, end in zip(ends, ends[1:])]


def relatives():
    places = [(dz, dy, dx) for dz in range(-3, 4) for dy in (0, 1) for dx in (0, 1)]
    places.remove((0, 0, 0))
    return sorted(places, key=lambda r: abs(r[0]) + r[1] + r[2])


def last_axis(order, place):
    differs = {"z": place[0] != 0, "y": place[1] != 0, "x": place[2] != 0}
    return [axis for axis in order if differs[axis]][-1]


def onward(order, place):
    if place == (0, 0, 0):
        return ["up", "down", "x", "y"]
    axis = last_axis(order, place)
    ways = []
    if axis == "z":
        ways.append("up" if place[0] < 0 else "down")
    for later in order[order.index(axis) + 1 :]:
        ways += ["up", "down"] if later == "z" else [later]
    return ways


def when(condition, action):
    if condition is None:
        action()
    else:
        pl.when(condition)(action)


def both(left, right):
    if left is None:
        return right
    return left if right is None else left & right


class Spot:
    def __init__(self):
        self.grp = lax.axis_index("grp")
        self.dp = lax.axis_index("dp")
        self.x = self.dp % 2
        self.y = (self.dp // 2) % 2
        self.z = self.dp // 4
        self.neighbour = {
            "x": (self.grp, self.index(self.z, self.y, 1 - self.x)),
            "y": (self.grp, self.index(self.z, 1 - self.y, self.x)),
            "up": (self.grp, self.index(jnp.minimum(self.z + 1, 3), self.y, self.x)),
            "down": (self.grp, self.index(jnp.maximum(self.z - 1, 0), self.y, self.x)),
            "core": (1 - self.grp, self.dp),
        }
        self.exists = {"x": None, "y": None, "up": self.z < 3, "down": self.z > 0, "core": None}

    def index(self, z, y, x):
        return z * 4 + y * 2 + x

    def at(self, place):
        z = self.z + place[0]
        y = 1 - self.y if place[1] else self.y
        x = 1 - self.x if place[2] else self.x
        inside = None if place[0] == 0 else (z >= 0) & (z <= 3)
        return z, self.index(z, y, x), inside

    def greet(self):
        barrier = pltpu.get_barrier_semaphore()
        me = self.grp * 16 + self.dp

        def signal(step, carry):
            other = (me + step) % 32
            pl.semaphore_signal(
                barrier, inc=1, device_id=(other // 16, other % 16), device_id_type=MESH
            )
            return carry

        lax.fori_loop(1, 32, signal, 0)
        pl.semaphore_wait(barrier, 31)


def tell_all(spot, tiles, send_sem, recv_sem):
    me = spot.grp * 16 + spot.dp

    def copy(number, other):
        return pltpu.make_async_remote_copy(
            src_ref=tiles.at[number],
            dst_ref=tiles.at[number],
            send_sem=send_sem.at[other],
            recv_sem=recv_sem.at[number],
            device_id=(other // 16, other % 16),
            device_id_type=MESH,
        )

    def start(step, carry):
        copy(me, (me + step) % 32).start()
        return carry

    def finish(step, carry):
        other = (me + step) % 32
        copy(other, other).wait_recv()
        copy(me, other).wait_send()
        return carry

    return (
        lambda: lax.fori_loop(1, 32, start, 0),
        lambda: lax.fori_loop(1, 32, finish, 0),
    )


def gather_kernel(
    master_ref,
    masked_ref,
    out_ref,
    masked_out,
    master,
    own_ref,
    tiles,
    local_sem,
    send_sem,
    recv_sem,
    core_send,
    core_recv,
    tile_send,
    tile_recv,
):
    spot = Spot()
    read = pltpu.make_async_copy(master_ref, master, local_sem)
    read.start()
    tiles[spot.grp * 16 + spot.dp] = masked_ref[...]
    spot.greet()
    tell, told = tell_all(spot, tiles, tile_send, tile_recv)
    ranges = part_ranges(own_ref.shape[0])
    read.wait()

    def round_off(start, length):
        block = pl.ds(start, length)
        own_ref[block] = master[block].astype(BF16)

    def step(index, carry):
        round_off(index * CHUNK, CHUNK)
        return carry

    units = own_ref.shape[0]
    lax.fori_loop(0, units // CHUNK, step, 0)
    if units % CHUNK:
        round_off(units - units % CHUNK, units % CHUNK)

    def copy(part, source, way, from_own):
        target = out_ref.at[spot.grp, source, pl.ds(*ranges[part])]
        origin = own_ref.at[pl.ds(*ranges[part])] if from_own else target
        if way == "core":
            sems = (core_send.at[part, source], core_recv.at[part, source])
        else:
            sems = (send_sem.at[part, source, WAYS.index(way)], recv_sem.at[part, source])
        return pltpu.make_async_remote_copy(
            src_ref=origin,
            dst_ref=target,
            send_sem=sems[0],
            recv_sem=sems[1],
            device_id=spot.neighbour[way],
            device_id_type=MESH,
        )

    sent = []
    for part in OWN_FIRST:
        for way in onward(ORDERS[part], (0, 0, 0)):
            when(
                spot.exists[way],
                lambda part=part, way=way: copy(part, spot.dp, way, True).start(),
            )
            sent.append((part, spot.dp, way, spot.exists[way], True))
    local = pltpu.make_async_copy(own_ref, out_ref.at[spot.grp, spot.dp], local_sem)
    local.start()
    tell()
    for part in range(PARTS):
        copy(part, spot.dp, "core", True).start()
        sent.append((part, spot.dp, "core", None, True))
    for place in relatives():
        _, source, inside = spot.at(place)
        for part in range(PARTS):
            ways = onward(ORDERS[part], place)

            def pass_on(part=part, source=source, ways=ways):
                copy(part, source, "x", False).wait_recv()
                for way in ways:
                    when(
                        spot.exists[way],
                        lambda way=way: copy(part, source, way, False).start(),
                    )
                copy(part, source, "core", False).start()

            when(inside, pass_on)
            for way in ways + ["core"]:
                sent.append((part, source, way, both(inside, spot.exists[way]), False))
    for part, source, way, condition, from_own in sent:
        when(condition, lambda: copy(part, source, way, from_own).wait_send())

    def await_core(source, carry):
        for part in range(PARTS):
            landed = out_ref.at[1 - spot.grp, source, pl.ds(*ranges[part])]
            pltpu.make_async_remote_copy(
                src_ref=landed,
                dst_ref=landed,
                send_sem=core_send.at[part, source],
                recv_sem=core_recv.at[part, source],
                device_id=spot.neighbour["core"],
                device_id_type=MESH,
            ).wait_recv()
        return carry

    lax.fori_loop(0, 16, await_core, 0)
    told()
    masked_out[...] = jnp.sum(tiles[pl.ds(0, 16)], axis=0)
    local.wait()


def gather_rows(master, masked):
    units = master.shape[0]
    dma = pltpu.SemaphoreType.DMA
    anywhere = pl.BlockSpec(memory_space=pl.ANY)
    vmem = pl.BlockSpec(memory_space=pltpu.VMEM)
    return pl.pallas_call(
        gather_kernel,
        out_shape=(
            jax.ShapeDtypeStruct((2, 16, units, 4, LANES), BF16),
            jax.ShapeDtypeStruct((8, LANES), F32),
        ),
        in_specs=[anywhere, vmem],
        out_specs=(anywhere, vmem),
        scratch_shapes=[
            pltpu.VMEM((units, 4, LANES), F32),
            pltpu.VMEM((units, 4, LANES), BF16),
            pltpu.VMEM((32, 8, LANES), F32),
            dma,
            dma((PARTS, 16, 4)),
            dma((PARTS, 16)),
            dma((PARTS, 16)),
            dma((PARTS, 16)),
            dma((32,)),
            dma((32,)),
        ],
        compiler_params=pltpu.CompilerParams(collective_id=0, has_side_effects=True),
        name="gather_rows",
    )(master, masked)


def slot_tables():
    tables = []
    for order in ORDERS:
        table = {}
        for way in WAYS:
            keys = []
            along = False
            for place in [(0, 0, 0)] + relatives():
                if way in onward(order, place):
                    if place[1:] not in keys:
                        keys.append(place[1:])
                    along = along or place[0] != 0
            table[way] = (keys, 3 if way in ("up", "down") else (4 if along else 1))
        tables.append(table)
    return tables


SLOTS = slot_tables()
STAGES = 4


def scatter_kernel(grad_ref, loss_ref, out_ref, sums_ref, *refs):
    ranges = part_ranges(grad_ref.shape[1])
    landing = {}
    for part in range(PARTS):
        for number, way in enumerate(WAYS):
            landing[part, way] = refs[part * 4 + number]
    stage, total, tiles, send_sem, recv_sem, stage_sem, out_sem, tile_send, tile_recv = refs[4 * PARTS :]
    spot = Spot()
    spot.greet()

    def slot(part, way, place, z):
        keys, depth = SLOTS[part][way]
        base = keys.index(place[1:]) * depth
        if way == "up":
            return base + z
        if way == "down":
            return base + z - 1
        return base + (z if depth == 4 else 0)

    def parent(part, place):
        axis = last_axis(ORDERS[part], place)
        if axis == "z":
            return "up" if place[0] > 0 else "down"
        return axis

    def seen_from_parent(part, place):
        way = parent(part, place)
        dz, dy, dx = place
        if way == "x":
            return (dz, dy, 0)
        if way == "y":
            return (dz, 0, dx)
        return (dz - 1 if way == "up" else dz + 1, dy, dx)

    def send(part, place, origin):
        z, owner, _ = spot.at(place)
        way = parent(part, place)
        back = OPPOSITE[way]
        return pltpu.make_async_remote_copy(
            src_ref=origin,
            dst_ref=landing[part, back].at[slot(part, back, seen_from_parent(part, place), z)],
            send_sem=send_sem.at[part, owner],
            recv_sem=recv_sem.at[part, owner, WAYS.index(back)],
            device_id=spot.neighbour[way],
            device_id_type=MESH,
        )

    def own(part, owner):
        return grad_ref.at[owner, pl.ds(*ranges[part])]

    nodes = [(place, part) for place in relatives()[::-1] for part in range(PARTS)]
    nodes += [((0, 0, 0), part) for part in range(PARTS)]
    sent = []
    inner = []
    for place, part in nodes:
        z, owner, inside = spot.at(place)
        ways = onward(ORDERS[part], place)
        if place != (0, 0, 0):
            sent.append((part, place, owner, inside))
        inner.append((part, place, ways, z, owner, inside))
    staged_nodes = [node for node in inner if node[2]]

    def staged(number):
        part, _, _, _, owner, _ = staged_nodes[number]
        return pltpu.make_async_copy(
            own(part, owner),
            stage.at[number % STAGES, pl.ds(0, ranges[part][1])],
            stage_sem.at[number % STAGES],
        )

    for number in range(STAGES - 1):
        when(staged_nodes[number][5], lambda: staged(number).start())
    number = -1
    for part, place, ways, z, owner, inside in inner:
        if not ways:
            when(inside, lambda: send(part, place, own(part, owner)).start())
            continue
        number += 1
        ahead = number + STAGES - 1
        if ahead < len(staged_nodes):
            when(staged_nodes[ahead][5], lambda: staged(ahead).start())
        length = ranges[part][1]
        root = place == (0, 0, 0)

        def combine(arriving, number=number, part=part, place=place, z=z, owner=owner):
            slots = []
            for way in arriving:
                spot_of = landing[part, way].at[slot(part, way, place, z)]
                pltpu.make_async_remote_copy(
                    src_ref=spot_of,
                    dst_ref=spot_of,
                    send_sem=send_sem.at[part, owner],
                    recv_sem=recv_sem.at[part, owner, WAYS.index(way)],
                    device_id=spot.neighbour[way],
                    device_id_type=MESH,
                ).wait_recv()
                slots.append(spot_of)
            staged(number).wait()
            if slots:
                target = total.at[pl.ds(*ranges[part])] if root else slots[0]

                def add(start, count):
                    value = stage[number % STAGES, pl.ds(start, count)]
                    for item in slots:
                        value = value + item[pl.ds(start, count)]
                    target[pl.ds(start, count)] = value

                def step(index, carry):
                    add(index * CHUNK, CHUNK)
                    return carry

                lax.fori_loop(0, length // CHUNK, step, 0)
                if length % CHUNK:
                    add(length - length % CHUNK, length % CHUNK)
            if not root:
                send(part, place, slots[0] if slots else own(part, owner)).start()

        def choose(ways=ways, combine=combine):
            flat = [way for way in ways if way in ("x", "y")]
            along = [way for way in ways if way in ("up", "down")]
            if not along:
                combine(flat)
            elif len(along) == 1:
                there = spot.exists[along[0]]
                pl.when(there)(lambda: combine(flat + along))
                pl.when(jnp.logical_not(there))(lambda: combine(flat))
            else:
                up, down = spot.exists["up"], spot.exists["down"]
                pl.when(up & down)(lambda: combine(flat + ["up", "down"]))
                pl.when(jnp.logical_not(down))(lambda: combine(flat + ["up"]))
                pl.when(jnp.logical_not(up))(lambda: combine(flat + ["down"]))

        when(inside, choose)
    out = pltpu.make_async_copy(total, out_ref, out_sem)
    out.start()
    units = total.shape[0]

    def square(start, count, running):
        value = total[pl.ds(start, count)]
        return running + jnp.sum(value * value, axis=0)

    squares = lax.fori_loop(
        0,
        units // CHUNK,
        lambda index, running: square(index * CHUNK, CHUNK, running),
        jnp.zeros((4, LANES), F32),
    )
    if units % CHUNK:
        squares = square(units - units % CHUNK, units % CHUNK, squares)
    me = spot.grp * 16 + spot.dp
    tiles[me, pl.ds(0, 4)] = squares
    tiles[me, pl.ds(4, 4)] = loss_ref[pl.ds(4, 4)]
    tell, told = tell_all(spot, tiles, tile_send, tile_recv)
    tell()
    for part, place, owner, inside in sent:
        when(inside, lambda: send(part, place, own(part, owner)).wait_send())
    told()
    sums_ref[...] = jnp.sum(tiles[...], axis=0)
    out.wait()


def scatter_sums(grads, loss):
    units = grads.shape[1]
    ranges = part_ranges(units)
    scratch = []
    for part in range(PARTS):
        for way in WAYS:
            keys, depth = SLOTS[part][way]
            scratch.append(pltpu.VMEM((len(keys) * depth, ranges[part][1], 4, LANES), F32))
    largest = max(length for _, length in ranges)
    dma = pltpu.SemaphoreType.DMA
    scratch += [
        pltpu.VMEM((STAGES, largest, 4, LANES), F32),
        pltpu.VMEM((units, 4, LANES), F32),
        pltpu.VMEM((32, 8, LANES), F32),
        dma((PARTS, 16)),
        dma((PARTS, 16, 4)),
        dma((STAGES,)),
        dma,
        dma((32,)),
        dma((32,)),
    ]
    anywhere = pl.BlockSpec(memory_space=pl.ANY)
    vmem = pl.BlockSpec(memory_space=pltpu.VMEM)
    return pl.pallas_call(
        scatter_kernel,
        out_shape=(
            jax.ShapeDtypeStruct((units, 4, LANES), F32),
            jax.ShapeDtypeStruct((8, LANES), F32),
        ),
        in_specs=[anywhere, vmem],
        out_specs=(anywhere, vmem),
        scratch_shapes=scratch,
        compiler_params=pltpu.CompilerParams(
            collective_id=1, has_side_effects=True, vmem_limit_bytes=63 * 2**20
        ),
        name="scatter_sums",
    )(grads, loss)


def update_values(owned, scale, params, first_moment, second_moment, average):
    clipped = owned * scale
    new_first = BETA_ONE * first_moment + (1.0 - BETA_ONE) * clipped
    new_second = BETA_TWO * second_moment + (1.0 - BETA_TWO) * clipped * clipped
    root = jnp.sqrt(new_second * (1.0 / (1.0 - BETA_TWO**STEP)))
    direction = new_first * (1.0 / (1.0 - BETA_ONE**STEP)) / (root + ADAM_EPS)
    new_params = params - RATE * (direction + DECAY_WEIGHT * params)
    new_average = AVERAGE_KEEP * average + (1.0 - AVERAGE_KEEP) * new_params
    return new_params, new_first, new_second, new_average


def update_kernel(scale_ref, *refs):
    scale = scale_ref[0]
    step = 31

    def one(index, carry):
        block = pl.ds(index * step, step)
        owned, params, first, second, average = [ref[block] for ref in refs[:5]]
        values = update_values(owned, scale, params, first, second, average)
        for out, value in zip(refs[5:], values):
            out[block] = value
        return carry

    lax.fori_loop(0, refs[0].shape[0] // step, one, 0)


def update(scale, arrays):
    units = arrays[0].shape[0]
    depth = 155
    spec = pl.BlockSpec((depth, 4, LANES), lambda i: (i, 0, 0))
    return pl.pallas_call(
        update_kernel,
        grid=(units // depth,),
        out_shape=[jax.ShapeDtypeStruct((units, 4, LANES), F32)] * 4,
        in_specs=[pl.BlockSpec(memory_space=pltpu.SMEM)] + [spec] * 5,
        out_specs=[spec] * 4,
        name="update",
    )(scale.reshape(1), *arrays)


def sections(layout, base):
    matrices, vectors = [], []
    offset = base
    for shape in layout:
        (matrices if len(shape) == 2 else vectors).append((offset, shape))
        offset += math.prod(shape)
    return matrices, vectors


def matrix_plan(rows):
    enc_matrices, enc_vectors = sections(ENC_LAYOUT, 0)
    dec_matrices, dec_vectors = sections(DEC_LAYOUT, rows * LANES)
    lent = rows * LANES + NDEC
    matrices = enc_matrices + sections(LENT, lent)[0] + dec_matrices
    return matrices, enc_vectors, dec_vectors


def padded(columns):
    return -(-columns // LANES) * LANES


def block_depth(shape):
    if shape[1] % LANES:
        return shape[0]
    depth = shape[0]
    while depth * shape[1] > PIECE * LANES:
        depth //= 2
    return depth


def matrix_kernel(rows, flat_ref, *refs):
    matrices, enc_vectors, dec_vectors = matrix_plan(rows)
    count = len(matrices)
    out_refs = refs[:count]
    vector_refs = refs[count : count + 2]
    blocks = refs[count + 2 : 2 * count + 2]
    flat_in, wide, pairs, vector_in, in_sem, out_sem, vector_sem = refs[2 * count + 2 :]
    lane = lax.broadcasted_iota(jnp.int32, (1, LANES), 1)

    chunks = []
    for number, (offset, shape) in enumerate(matrices):
        depth = block_depth(shape)
        for start in range(0, shape[0], depth):
            place = offset + start * shape[1]
            chunks.append((number, start, depth, place // LANES, place % LANES))

    def load(index):
        number, _, depth, first, shift = chunks[index]
        length = depth * matrices[number][1][1] // LANES
        begin = first // 16 * 16
        end = -(-(first + length + (1 if shift else 0)) // 16) * 16
        copy = pltpu.make_async_copy(
            flat_ref.at[pl.ds(begin, end - begin)],
            flat_in.at[index % 2, pl.ds(0, end - begin)],
            in_sem.at[index % 2],
        )
        return copy, first - begin, end - begin

    def store(index):
        number, start, depth, _, _ = chunks[index]
        slot = start // depth % 2
        return pltpu.make_async_copy(
            blocks[number].at[slot], out_refs[number].at[pl.ds(start, depth)], out_sem.at[number, slot]
        )

    def widen(index, length):
        step = 256

        def one(start, size):
            wide[pl.ds(start, size)] = flat_in[index % 2, pl.ds(start, size)].astype(F32)

        def loop(i, carry):
            one(pl.multiple_of(i * step, step), step)
            return carry

        lax.fori_loop(0, length // step, loop, 0)
        if length % step:
            one(length - length % step, length % step)

    def turned(first, second):
        return pltpu.roll(jnp.where(lane < LANES // 2, second, first), LANES // 2, 1)

    def arrange(index, phase):
        number, start, depth, _, shift = chunks[index]
        columns = matrices[number][1][1]
        block = blocks[number].at[start // depth % 2]
        tiles = columns // LANES

        def plain(i, carry):
            row = pl.multiple_of(i * SUB, SUB)
            for tile in range(tiles):
                value = wide[pl.ds(phase + row * tiles + tile, SUB, stride=tiles)]
                if shift:
                    after = wide[pl.ds(phase + row * tiles + tile + 1, SUB, stride=tiles)]
                    value = turned(value, after)
                block[pl.ds(row, SUB), pl.ds(tile * LANES, LANES)] = value.astype(BF16)
            return carry

        def paired(i, carry):
            stride = 2 * columns // LANES
            half = SUB // 2
            row = pl.multiple_of(i * half, half)
            for tile in range(tiles + 1):
                even = wide[pl.ds(phase + row * stride + tile, half, stride=stride)]
                odd = wide[pl.ds(phase + row * stride + tiles + tile, half, stride=stride)]
                if tile < tiles:
                    after = wide[pl.ds(phase + row * stride + tiles + tile + 1, half, stride=stride)]
                    odd = turned(odd, after)
                else:
                    even = jnp.where(lane < LANES // 2, even, 0.0)
                    odd = jnp.where(lane < LANES // 2, pltpu.roll(odd, LANES // 2, 1), 0.0)
                lanes = pl.ds(tile * LANES, LANES)
                pairs[tile, pl.ds(0, half, stride=2)] = even
                pairs[tile, pl.ds(1, half, stride=2)] = odd
                block[pl.ds(pl.multiple_of(i * SUB, SUB), SUB), lanes] = pairs[tile].astype(BF16)
            return carry

        lax.fori_loop(0, depth // SUB, paired if columns % LANES else plain, 0)

    windows = []
    wanted = [(0, n, v) for n, v in enumerate(enc_vectors)]
    wanted += [(1, n, v) for n, v in enumerate(dec_vectors)]
    for _, _, (offset, shape) in wanted:
        first = offset // LANES // 16 * 16
        end = -(-(offset // LANES + -(-shape[0] // LANES)) // 16) * 16
        if windows and first <= windows[-1][1]:
            windows[-1][1] = max(windows[-1][1], end)
        else:
            windows.append([first, end])
    bases = [sum(e - f for f, e in windows[:n]) for n in range(len(windows))]

    def vector_copy(n):
        first, end = windows[n]
        return pltpu.make_async_copy(
            flat_ref.at[pl.ds(first, end - first)],
            vector_in.at[pl.ds(bases[n], end - first)],
            vector_sem.at[n],
        )

    load(0)[0].start()
    for n in range(len(windows)):
        vector_copy(n).start()
    for index, (number, start, depth, _, _) in enumerate(chunks):
        copy, phase, length = load(index)
        copy.wait()
        if index + 1 < len(chunks):
            load(index + 1)[0].start()
        widen(index, length)
        if start // depth >= 2:
            store(index - 2).wait()
        arrange(index, phase)
        store(index).start()
    for n in range(len(windows)):
        vector_copy(n).wait()
    total = bases[-1] + windows[-1][1] - windows[-1][0]
    wide[pl.ds(0, total)] = vector_in[...].astype(F32)
    for group, n, (offset, shape) in wanted:
        first = offset // LANES
        window = [k for k, (f, e) in enumerate(windows) if f <= first < e][0]
        base = bases[window] + first - windows[window][0]
        for tile in range(-(-shape[0] // LANES)):
            value = wide[pl.ds(base + tile, 1)]
            if shape[0] - tile * LANES < LANES:
                value = jnp.where(lane < shape[0] - tile * LANES, value, 0.0)
            vector_refs[group][pl.ds(n, 1), pl.ds(tile * LANES, LANES)] = value
    for index, (number, start, depth, _, _) in enumerate(chunks):
        if start + 2 * depth >= matrices[number][1][0]:
            store(index).wait()


def weight_matrices(flat):
    rows = flat.shape[0] // 2
    matrices, enc_vectors, dec_vectors = matrix_plan(rows)
    shapes = [(shape[0], padded(shape[1])) for _, shape in matrices]
    buffers = []
    for (_, shape), (_, columns) in zip(matrices, shapes):
        depth = block_depth(shape)
        buffers.append(pltpu.VMEM((min(2, shape[0] // depth), depth, columns), BF16))
    dma = pltpu.SemaphoreType.DMA
    windows = 0
    last = -1
    total = 0
    for offset, shape in enc_vectors + dec_vectors:
        first = offset // LANES // 16 * 16
        end = -(-(offset // LANES + -(-shape[0] // LANES)) // 16) * 16
        if first <= last:
            total += max(0, end - last)
            last = max(last, end)
        else:
            windows += 1
            total += end - first
            last = end
    anywhere = pl.BlockSpec(memory_space=pl.ANY)
    vmem = pl.BlockSpec(memory_space=pltpu.VMEM)
    return pl.pallas_call(
        functools.partial(matrix_kernel, rows),
        out_shape=[jax.ShapeDtypeStruct(shape, BF16) for shape in shapes]
        + [jax.ShapeDtypeStruct((VEC_ROWS, columns), F32) for columns in VEC_COLS],
        in_specs=[anywhere],
        out_specs=[anywhere] * len(shapes) + [vmem, vmem],
        scratch_shapes=buffers
        + [
            pltpu.VMEM((2, PIECE + 32, LANES), BF16),
            pltpu.VMEM((PIECE + 32, LANES), F32),
            pltpu.VMEM((padded(HEAD) // LANES, SUB, LANES), F32),
            pltpu.VMEM((total, LANES), BF16),
            dma((2,)),
            dma((len(shapes), 2)),
            dma((windows,)),
        ],
        compiler_params=pltpu.CompilerParams(vmem_limit_bytes=56 * 2**20),
        name="weight_matrices",
    )(flat)


def stream_items(layout, lent):
    items = []
    offset = 0
    numbers = [0, 0]
    for shape in layout + lent:
        matrix = len(shape) == 2
        number = numbers[matrix]
        numbers[matrix] += 1
        depth = block_depth(shape) if matrix else 0
        for start in range(0, shape[0] if matrix else 1, max(depth, 1)):
            items.append((matrix, number, shape, start, depth, offset))
            offset += depth * shape[1] if matrix else shape[0]
    return items, offset


ROLES = (
    (ENC_LAYOUT, [], (0, 1, 2, 3)),
    (DEC_LAYOUT, LENT, (6, 7, 8, 9, 10, 4, 5)),
)
PAIRS = 11


def factor_buffers(shapes):
    sizes = []
    places = {}
    for role in (1, 0):
        taken = set()
        for number in ROLES[role][2]:
            for side in range(2):
                length, columns = shapes[2 * number + side]
                fits = [
                    n
                    for n, size in enumerate(sizes)
                    if n not in taken and size[0] == 2 * length and size[1] >= columns
                ]
                if fits:
                    place = min(fits, key=lambda n: sizes[n][1])
                else:
                    place = len(sizes)
                    sizes.append((2 * length, columns))
                taken.add(place)
                places[role, number, side] = place
    return sizes, places


def product_kernel(rows, shapes, *refs):
    factors, vectors, out_ref = refs[: 2 * PAIRS], refs[2 * PAIRS : 2 * PAIRS + 2], refs[24]
    sizes, places = factor_buffers(shapes)
    buffers = refs[25 : 25 + len(sizes)]
    refs = refs[25 + len(sizes) :]
    others = refs[:2]
    turned_left, tall, rows_out, own_sem, send_sem, recv_sem, out_sem = refs[2:]
    core = lax.axis_index("grp")
    sibling = (1 - core, lax.axis_index("dp"))
    barrier = pltpu.get_barrier_semaphore()
    pl.semaphore_signal(barrier, inc=1, device_id=sibling, device_id_type=MESH)
    pl.semaphore_wait(barrier, 1)

    def half_of(role, number, side, part):
        length, columns = shapes[2 * number + side]
        buffer = buffers[places[role, number, side]]
        return buffer.at[pl.ds(part * length, length), pl.ds(0, columns)]

    def local(role, number, side):
        return pltpu.make_async_copy(
            factors[2 * number + side], half_of(role, number, side, 0), own_sem.at[number, side]
        )

    def remote(role, number, side):
        return pltpu.make_async_remote_copy(
            src_ref=factors[2 * number + side],
            dst_ref=half_of(role, number, side, 1),
            send_sem=send_sem.at[number, side],
            recv_sem=recv_sem.at[number, side],
            device_id=sibling,
            device_id_type=MESH,
        )

    def remote_vectors(role):
        return pltpu.make_async_remote_copy(
            src_ref=vectors[role],
            dst_ref=others[role],
            send_sem=send_sem.at[PAIRS, role],
            recv_sem=recv_sem.at[PAIRS, role],
            device_id=sibling,
            device_id_type=MESH,
        )

    def act(role):
        remote_vectors(1 - role).start()
        pending = [(number, side) for number in ROLES[role][2] for side in range(2)]
        for number, side in pending:
            local(role, number, side).start()
        given = [(number, side) for number in ROLES[1 - role][2] for side in range(2)]
        for number, side in given:
            remote(1 - role, number, side).start()
        remote_vectors(role).wait_recv()

        def ready(number):
            for side in range(2):
                local(role, number, side).wait()
                remote(role, number, side).wait_recv()

        lefts, rights = [], []
        for number in ROLES[role][2]:
            for side, views in ((0, lefts), (1, rights)):
                length, columns = shapes[2 * number + side]
                buffer = buffers[places[role, number, side]]
                views.append(buffer.at[pl.ds(0, 2 * length), pl.ds(0, columns)])
        fill_row(
            rows,
            ROLES[role],
            ready,
            lefts,
            rights,
            vectors[role],
            others[role],
            turned_left,
            tall,
            rows_out,
            out_ref,
            out_sem,
        )
        for number, side in given:
            remote(1 - role, number, side).wait_send()
        remote_vectors(1 - role).wait_send()

    for role in range(2):
        pl.when(core == role)(functools.partial(act, role))


def fill_row(
    rows,
    role,
    ready,
    lefts,
    rights,
    mine_ref,
    other_ref,
    turned_left,
    tall,
    rows_out,
    out_ref,
    out_sem,
):
    layout, lent, numbers = role
    lane = lax.broadcasted_iota(jnp.int32, (1, LANES), 1)
    half = LANES // 2
    items, used = stream_items(layout, lent)
    groups = []
    current = []
    for item in items:
        current.append(item)
        if item[0]:
            groups.append(current)
            current = []
    groups.append(current)

    def vector(item, buffer, base):
        _, number, shape, _, _, _ = item
        for tile in range(-(-shape[0] // LANES)):
            lanes = pl.ds(tile * LANES, LANES)
            buffer[pl.ds(base + tile, 1)] = (
                mine_ref[pl.ds(number, 1), lanes] + other_ref[pl.ds(number, 1), lanes]
            )

    def matrix(item, buffer, base):
        _, number, shape, start, depth, offset = item
        columns = shape[1]
        shifted = offset % LANES
        tiles = -(-columns // LANES)
        width = min(WIDTH, columns)
        if start == 0:
            ready(numbers[number])
            if shifted:
                length = rights[number].shape[0]

                def turn(i, carry):
                    block = pl.ds(pl.multiple_of(i * 64, 64), 64)
                    value = rights[number][block].astype(F32)
                    rights[number][block] = pltpu.roll(value, half, 1).astype(BF16)
                    return carry

                lax.fori_loop(0, length // 64, turn, 0)
        length = lefts[number].shape[0]
        sub = min(256, depth)

        def loop(step, carry):
            k = pl.multiple_of(start + step * sub, sub)
            turned_left[pl.ds(0, sub), pl.ds(0, length)] = lefts[number][:, pl.ds(k, sub)].T

            def across(c, carry):
                column = pl.multiple_of(c * width, width)
                value = jnp.dot(
                    turned_left[pl.ds(0, sub), pl.ds(0, length)],
                    rights[number][:, pl.ds(column, width)],
                    preferred_element_type=F32,
                )
                row = base + step * sub * tiles
                for piece in range(width // LANES):
                    part = value[:, piece * LANES : (piece + 1) * LANES]
                    tile = c * (width // LANES) + piece
                    if columns % LANES:
                        tall[tile, pl.ds(step * sub, sub)] = part
                    elif shifted and piece == 0:
                        first = row + tile

                        @pl.when(c == 0)
                        def _():
                            before = pltpu.roll(part, 1, 0)
                            index = lax.broadcasted_iota(jnp.int32, (sub, LANES), 0)
                            held = buffer[pl.ds(row, 1)]
                            before = jnp.where(index == 0, held, before)
                            merged = jnp.where(lane < half, before, part)
                            buffer[pl.ds(row, sub, stride=tiles)] = merged
                            buffer[pl.ds(row + sub * tiles, 1)] = part[sub - 1 :]

                        @pl.when(c > 0)
                        def _():
                            buffer[pl.ds(first, sub, stride=tiles)] = part
                    else:
                        buffer[pl.ds(row + tile, sub, stride=tiles)] = part
                return carry

            lax.fori_loop(0, tiles * LANES // width, across, 0)
            return carry

        lax.fori_loop(0, depth // sub, loop, 0)
        if columns % LANES:
            stride = 2 * columns // LANES
            pair = 64

            def weave(i, carry):
                k = pl.multiple_of(i * 2 * pair, 2 * pair)
                row = base + i * pair * stride
                evens = [tall[t, pl.ds(k, pair, stride=2)] for t in range(tiles)]
                odds = [tall[t, pl.ds(k + 1, pair, stride=2)] for t in range(tiles)]
                for t in range(tiles - 1):
                    buffer[pl.ds(row + t, pair, stride=stride)] = evens[t]
                middle = jnp.where(lane < half, evens[-1], pltpu.roll(odds[0], half, 1))
                buffer[pl.ds(row + tiles - 1, pair, stride=stride)] = middle
                for t in range(1, tiles):
                    both_halves = jnp.where(lane < half, odds[t], odds[t - 1])
                    buffer[pl.ds(row + tiles - 1 + t, pair, stride=stride)] = pltpu.roll(
                        both_halves, half, 1
                    )
                return carry

            lax.fori_loop(0, depth // 2 // pair, weave, 0)

    flights = []
    tail = None
    for number, group in enumerate(groups):
        slot = number % 2
        buffer = rows_out.at[slot]
        if number >= 2:
            flights[number - 2].wait()
        first = group[0][5] // LANES if group else used // LANES
        begin = first // 8 * 8
        if tail is not None:
            buffer[pl.ds(0, 8)] = rows_out[1 - slot, pl.ds(tail, 8)]
        for item in group:
            (matrix if item[0] else vector)(item, buffer, item[5] // LANES - begin)
        last = number == len(groups) - 1
        if last:
            at = used // LANES - begin
            if used % LANES:
                buffer[pl.ds(at, 1)] = jnp.where(lane < used % LANES, buffer[pl.ds(at, 1)], 0.0)
                at += 1
            length = rows - begin
            if length > at:
                buffer[pl.ds(at, length - at)] = jnp.zeros((length - at, LANES), F32)
        else:
            end = groups[number + 1][0][5] if groups[number + 1] else used
            tail = (end // LANES - begin) // 8 * 8
            length = tail
        flight = pltpu.make_async_copy(
            buffer.at[pl.ds(0, length)], out_ref.at[pl.ds(begin, length)], out_sem.at[slot]
        )
        flight.start()
        flights.append(flight)
    for flight in flights[-2:]:
        flight.wait()


def flat_gradient(rows, factors, enc_vectors, dec_vectors):
    shapes = [factor.shape for factor in factors]
    sizes, _ = factor_buffers(shapes)
    longest = max(length for length, _ in sizes)
    dma = pltpu.SemaphoreType.DMA
    anywhere = pl.BlockSpec(memory_space=pl.ANY)
    vmem = pl.BlockSpec(memory_space=pltpu.VMEM)
    return pl.pallas_call(
        functools.partial(product_kernel, rows, shapes),
        out_shape=jax.ShapeDtypeStruct((rows, LANES), F32),
        in_specs=[anywhere] * (2 * PAIRS) + [vmem, vmem],
        out_specs=anywhere,
        scratch_shapes=[pltpu.VMEM(size, BF16) for size in sizes]
        + [
            pltpu.VMEM(enc_vectors.shape, F32),
            pltpu.VMEM(dec_vectors.shape, F32),
            pltpu.VMEM((256, longest), BF16),
            pltpu.VMEM((padded(HEAD) // LANES, DD, LANES), F32),
            pltpu.VMEM((2, PIECE + 128, LANES), F32),
            dma((PAIRS, 2)),
            dma((PAIRS + 1, 2)),
            dma((PAIRS + 1, 2)),
            dma((2,)),
        ],
        compiler_params=pltpu.CompilerParams(
            collective_id=2, has_side_effects=True, vmem_limit_bytes=63 * 2**20
        ),
        name="flat_gradient",
    )(*factors, enc_vectors, dec_vectors)


Bag = types.SimpleNamespace


def position_code(position, scales, width):
    quarter = width // 4
    frequency = jnp.exp(jnp.arange(quarter, dtype=F32) * (-math.log(10000.0) / quarter))
    row_angle = ((position // GSIDE).astype(F32) * scales)[..., None] * frequency
    col_angle = ((position % GSIDE).astype(F32) * scales)[..., None] * frequency
    return jnp.concatenate(
        [jnp.sin(row_angle), jnp.cos(row_angle), jnp.sin(col_angle), jnp.cos(col_angle)], axis=-1
    )


def bands(pixel_rows):
    pixel_ids = jnp.arange(PIX, dtype=jnp.int32)
    coarse = (
        pixel_ids // (3 * PSIDE) // 2 * (PSIDE // 2) + pixel_ids // 3 % PSIDE // 2
    ) * 3 + pixel_ids % 3
    pool_table = (coarse[:, None] == jnp.arange(LOWPIX, dtype=jnp.int32)[None, :]).astype(F32)
    low_band = jnp.dot(pixel_rows, pool_table, precision=HIGHEST) * 0.25
    high_band = pixel_rows - jnp.dot(low_band, pool_table.T, precision=HIGHEST)
    return (low_band, high_band)


def linear(left, right):
    return jnp.einsum("...k,kn->...n", left, right, preferred_element_type=F32)


def input_grad(grad_rows, right):
    return jnp.einsum("...n,kn->...k", grad_rows, right, preferred_element_type=F32)


def norm_forward(state, gain, shift):
    centered = state - jnp.mean(state, axis=-1, keepdims=True)
    inverse = lax.rsqrt(jnp.mean(centered * centered, axis=-1, keepdims=True) + NORM_EPS)
    unit_rows = centered * inverse
    return (unit_rows * gain.astype(F32) + shift.astype(F32), unit_rows, inverse)


def norm_backward(grad_out, unit_rows, inverse, gain):
    grad_unit = grad_out * gain.astype(F32)
    grad_in = inverse * (
        grad_unit
        - jnp.mean(grad_unit, axis=-1, keepdims=True)
        - unit_rows * jnp.mean(grad_unit * unit_rows, axis=-1, keepdims=True)
    )
    return (grad_in, jnp.sum(grad_out * unit_rows, axis=(0, 1)), jnp.sum(grad_out, axis=(0, 1)))


def attention_scores(query_part, key_part, bias):
    head_dim = query_part.shape[-1]
    return (
        jnp.einsum("blhd,bmhd->bhlm", query_part, key_part, preferred_element_type=F32)
        * head_dim ** (-0.5)
        + bias
    )


def gelu_exact(values):
    return jax.nn.gelu(values, approximate=False)


def block_forward(state, weights, heads, bias):
    batch, length, width = state.shape
    normed_one, unit_one, inverse_one = norm_forward(state, weights.ln1_g, weights.ln1_b)
    normed_one = normed_one.astype(BF16)
    qkv = (
        linear(normed_one, weights.qkv_w)
        .astype(BF16)
        .reshape(batch, length, 3, heads, width // heads)
    )
    scores = attention_scores(qkv[:, :, 0], qkv[:, :, 1], bias)
    row_max = jnp.max(scores, axis=-1, keepdims=True)
    shifted = jnp.exp(scores - row_max)
    totals = jnp.sum(shifted, axis=-1, keepdims=True)
    attend = (shifted / totals).astype(BF16)
    logsum = row_max + jnp.log(totals)
    mixed = jnp.einsum("bhlm,bmhd->blhd", attend, qkv[:, :, 2], preferred_element_type=F32)
    mixed = mixed.astype(BF16).reshape(batch, length, width)
    middle = state + linear(mixed, weights.out_w)
    normed_two, unit_two, inverse_two = norm_forward(middle, weights.ln2_g, weights.ln2_b)
    normed_two = normed_two.astype(BF16)
    pre_act = linear(normed_two, weights.fc1_w) + weights.fc1_b.astype(F32)
    active = gelu_exact(pre_act).astype(BF16)
    output = middle + linear(active, weights.fc2_w) + weights.fc2_b.astype(F32)
    kept = Bag(
        normed_one=normed_one,
        unit_one=unit_one,
        inverse_one=inverse_one,
        qkv=qkv,
        logsum=logsum,
        mixed=mixed,
        unit_two=unit_two,
        inverse_two=inverse_two,
        normed_two=normed_two,
        active=active,
        pre_act=pre_act,
    )
    return (output, kept)


def block_backward(grad_out, kept, weights, heads, bias):
    batch, length, width = grad_out.shape
    grads = Bag()
    pairs = Bag()
    grad_low = grad_out.astype(BF16)
    pairs.fc2_w = (kept.active, grad_low)
    grads.fc2_b = jnp.sum(grad_out, axis=(0, 1))
    _, gelu_back = jax.vjp(gelu_exact, kept.pre_act)
    grad_pre = gelu_back(input_grad(grad_low, weights.fc2_w))[0]
    grads.fc1_b = jnp.sum(grad_pre, axis=(0, 1))
    grad_pre_low = grad_pre.astype(BF16)
    pairs.fc1_w = (kept.normed_two, grad_pre_low)
    grad_norm_in, grads.ln2_g, grads.ln2_b = norm_backward(
        input_grad(grad_pre_low, weights.fc1_w),
        kept.unit_two,
        kept.inverse_two,
        weights.ln2_g,
    )
    grad_mid = grad_out + grad_norm_in
    grad_mid_low = grad_mid.astype(BF16)
    pairs.out_w = (kept.mixed, grad_mid_low)
    grad_mixed = (
        input_grad(grad_mid_low, weights.out_w)
        .astype(BF16)
        .reshape(batch, length, heads, width // heads)
    )
    qkv = kept.qkv
    query_part, key_part, value_part = (qkv[:, :, 0], qkv[:, :, 1], qkv[:, :, 2])
    attend = jnp.exp(attention_scores(query_part, key_part, bias) - kept.logsum)
    grad_value = jnp.einsum(
        "bhlm,blhd->bmhd", attend.astype(BF16), grad_mixed, preferred_element_type=F32
    )
    grad_attend = jnp.einsum("blhd,bmhd->bhlm", grad_mixed, value_part, preferred_element_type=F32)
    grad_scores = (
        attend * (grad_attend - jnp.sum(grad_attend * attend, axis=-1, keepdims=True))
    ).astype(BF16)
    score_scale = (width // heads) ** (-0.5)
    grad_query = (
        jnp.einsum("bhlm,bmhd->blhd", grad_scores, key_part, preferred_element_type=F32)
        * score_scale
    )
    grad_key = (
        jnp.einsum("bhlm,blhd->bmhd", grad_scores, query_part, preferred_element_type=F32)
        * score_scale
    )
    grad_qkv = (
        jnp.stack([grad_query, grad_key, grad_value], axis=2)
        .reshape(batch, length, 3 * width)
        .astype(BF16)
    )
    pairs.qkv_w = (kept.normed_one, grad_qkv)
    grad_norm_in, grads.ln1_g, grads.ln1_b = norm_backward(
        input_grad(grad_qkv, weights.qkv_w),
        kept.unit_one,
        kept.inverse_one,
        weights.ln1_g,
    )
    return (grad_mid + grad_norm_in, grads, pairs)


def forward_backward(enc, dec, pixels, index_rows, counts, scales, masked_total):
    images = counts.shape[0]
    slots = jnp.arange(VMAX, dtype=jnp.int32)
    valid = slots[None, :] < counts[:, None]
    position = jnp.where(valid, index_rows, 0)
    pixel_images = jnp.pad(pixels.reshape(images, GRID, PIX), ((0, 0), (0, GPAD - GRID), (0, 0)))
    grid = jnp.arange(GPAD, dtype=jnp.int32)
    chosen = ((position[:, :, None] == grid[None, None, :]) & valid[:, :, None]).astype(BF16)
    patches = jnp.einsum("ivg,igp->ivp", chosen, pixel_images, preferred_element_type=F32)
    patches = patches.astype(BF16)
    enc_bias = jnp.where(valid, 0.0, MASK_FILL)[:, None, None, :]
    state = (
        linear(patches, enc.pe_w)
        + enc.pe_b.astype(F32)
        + position_code(position, scales[:, None], DE)
    )
    state, enc_kept = block_forward(state, enc, HE, enc_bias)
    enc_normed, enc_unit, enc_inverse = norm_forward(state, enc.lnf_g, enc.lnf_b)
    enc_normed = enc_normed.astype(BF16)
    sent = (linear(enc_normed, enc.emb_w) + enc.emb_b.astype(F32)).astype(BF16)

    placed = jnp.einsum("ivg,ivd->igd", chosen, sent, preferred_element_type=F32)
    seen = jnp.sum(chosen.astype(F32), axis=1)
    dec_bias = jnp.where(grid < GRID, 0.0, MASK_FILL)[None, None, None, :]
    state = jnp.where(
        seen[:, :, None] > 0.5, placed, dec.mask_tok.astype(F32)
    ) + position_code(jnp.broadcast_to(grid[None], (images, GPAD)), scales[:, None], DD)
    state, dec_kept = block_forward(state, dec, HD, dec_bias)
    normed, unit_rows, inverse = norm_forward(state, dec.lnf_g, dec.lnf_b)
    normed = normed.astype(BF16)
    predicted = linear(normed, dec.head_w[:, :HEAD]) + dec.head_b[:HEAD].astype(F32)
    low_band, high_band = bands(pixel_images.reshape(-1, PIX).astype(F32))
    low_band = low_band.reshape(images, GPAD, -1)
    high_band = high_band.reshape(images, GPAD, -1)
    miss_low = predicted[..., :LOWPIX] - low_band
    miss_high = predicted[..., LOWPIX:] - high_band
    unseen = jnp.where(grid[None] < GRID, 1.0 - seen, 0.0)
    per_patch = jnp.sum(miss_low * miss_low, axis=-1) + jnp.sum(
        jnp.sqrt(miss_high * miss_high + 1.0) - 1.0, axis=-1
    )
    loss_local = jnp.sum(per_patch * unseen)
    row_weight = unseen / masked_total
    grad_pred = (
        jnp.concatenate(
            [2.0 * miss_low, miss_high * lax.rsqrt(miss_high * miss_high + 1.0)], axis=-1
        )
        * row_weight[:, :, None]
    )
    grad_low = jnp.pad(grad_pred, ((0, 0), (0, 0), (0, padded(HEAD) - HEAD))).astype(BF16)
    dec_pairs = Bag(head_w=(normed, grad_low))
    dec_grads = Bag(head_b=jnp.sum(grad_low.astype(F32), axis=(0, 1)))
    grad_state, dec_grads.lnf_g, dec_grads.lnf_b = norm_backward(
        input_grad(grad_low, dec.head_w), unit_rows, inverse, dec.lnf_g
    )
    grad_state, block_grads, block_pairs = block_backward(grad_state, dec_kept, dec, HD, dec_bias)
    vars(dec_grads).update(vars(block_grads))
    vars(dec_pairs).update(vars(block_pairs))
    dec_grads.mask_tok = jnp.sum(grad_state * unseen[:, :, None], axis=(0, 1))
    grad_sent = jnp.einsum(
        "ivg,igd->ivd", chosen, grad_state.astype(BF16), preferred_element_type=F32
    ).astype(BF16)

    enc_pairs = Bag(emb_w=(enc_normed, grad_sent))
    enc_grads = Bag(emb_b=jnp.sum(grad_sent.astype(F32), axis=(0, 1)))
    grad_state, enc_grads.lnf_g, enc_grads.lnf_b = norm_backward(
        input_grad(grad_sent, enc.emb_w), enc_unit, enc_inverse, enc.lnf_g
    )
    grad_state, block_grads, block_pairs = block_backward(grad_state, enc_kept, enc, HE, enc_bias)
    vars(enc_grads).update(vars(block_grads))
    vars(enc_pairs).update(vars(block_pairs))
    enc_pairs.pe_w = (patches, grad_state.astype(BF16))
    enc_grads.pe_b = jnp.sum(grad_state, axis=(0, 1))
    return loss_local, enc_grads, enc_pairs, dec_grads, dec_pairs


def vector_rows(vectors, columns):
    rows = [jnp.pad(vector, (0, columns - vector.shape[0])) for vector in vectors]
    rows += [jnp.zeros((columns,), F32)] * (VEC_ROWS - len(rows))
    return jnp.stack(rows)


def gradient_row(rows, enc_grads, enc_pairs, dec_grads, dec_pairs):
    e, d = enc_grads, dec_grads
    enc_vectors = vector_rows(
        [e.pe_b, e.ln1_g, e.ln1_b, e.ln2_g, e.ln2_b, e.fc1_b, e.fc2_b, e.lnf_g, e.lnf_b, e.emb_b],
        VEC_COLS[0],
    )
    dec_vectors = vector_rows(
        [d.mask_tok, d.ln1_g, d.ln1_b, d.ln2_g, d.ln2_b]
        + [d.fc1_b, d.fc2_b, d.lnf_g, d.lnf_b, d.head_b],
        VEC_COLS[1],
    )
    e, d = enc_pairs, dec_pairs
    pairs = [e.pe_w, e.qkv_w, e.fc1_w, e.emb_w, e.out_w, e.fc2_w]
    pairs += [d.qkv_w, d.out_w, d.fc1_w, d.fc2_w, d.head_w]
    factors = [factor.reshape(-1, factor.shape[-1]) for pair in pairs for factor in pair]
    return flat_gradient(rows, factors, enc_vectors, dec_vectors)


def bags(parts):
    enc, dec = Bag(), Bag()
    enc.pe_w, enc.qkv_w, enc.fc1_w, enc.emb_w, enc.out_w, enc.fc2_w = parts[:6]
    dec.qkv_w, dec.out_w, dec.fc1_w, dec.fc2_w, dec.head_w = parts[6:11]
    e, d = parts[11:]
    enc.pe_b, enc.ln1_g, enc.ln1_b, enc.ln2_g, enc.ln2_b = [e[n, :DE] for n in range(5)]
    enc.fc1_b = e[5]
    enc.fc2_b, enc.lnf_g, enc.lnf_b = [e[n, :DE] for n in range(6, 9)]
    enc.emb_b = e[9, :DD]
    dec.mask_tok, dec.ln1_g, dec.ln1_b, dec.ln2_g, dec.ln2_b = [d[n, :DD] for n in range(5)]
    dec.fc1_b = d[5]
    dec.fc2_b, dec.lnf_g, dec.lnf_b = [d[n, :DD] for n in range(6, 9)]
    dec.head_b = d[9, : padded(HEAD)]
    return enc, dec


def clip_scale(squares):
    return jnp.minimum(1.0, CLIP / jnp.sqrt(squares))


def body(
    params, first_moment, second_moment, average, pixels, visible_index, visible_count, gsd_id
):
    chips = lax.axis_size("dp")
    rows = params.shape[1] // LANES
    special = chips == math.prod(DP_GRID) and rows % 4 == 0
    masked = jnp.sum(GRID - visible_count).astype(F32)
    if special:
        shards = [a.reshape(-1, 4, LANES) for a in (params, first_moment, second_moment, average)]
        copies, masked_tile = gather_rows(shards[0], jnp.full((8, LANES), masked))
        masked_total = masked_tile[0, 0]
    else:
        copies = lax.all_gather(params.astype(BF16).reshape(-1, LANES), "dp", axis=0, tiled=True)
        copies = lax.all_gather(copies, "grp", axis=0, tiled=True)
        masked_total = lax.psum(masked, "dp")
    enc, dec = bags(weight_matrices(copies.reshape(-1, LANES)))

    half = visible_count.shape[0] // 2
    core = lax.axis_index("grp")

    def mine(array, count):
        return lax.dynamic_slice_in_dim(array, core * count, count, 0)

    scales = 0.5 + 0.25 * mine(gsd_id, half).astype(F32)
    loss_local, enc_grads, enc_pairs, dec_grads, dec_pairs = forward_backward(
        enc,
        dec,
        mine(pixels, half * GRID),
        mine(visible_index, half),
        mine(visible_count, half),
        scales,
        masked_total,
    )
    gradient = gradient_row(chips * rows, enc_grads, enc_pairs, dec_grads, dec_pairs)
    if special:
        owned, sums = scatter_sums(
            gradient.reshape(chips, rows // 4, 4, LANES), jnp.full((8, LANES), loss_local)
        )
        squares = jnp.sum(sums[:4])
        loss_sum = sums[4, 0]
        outs = update(clip_scale(squares), [owned] + shards)
        outs = [out.reshape(params.shape) for out in outs]
    else:
        owned = lax.psum_scatter(gradient, "dp", scatter_dimension=0, tiled=True)
        owned = owned.reshape(params.shape)
        squares, loss_sum = lax.psum((jnp.sum(owned * owned), loss_local), ("grp", "dp"))
        outs = update_values(owned, clip_scale(squares), params, first_moment, second_moment, average)
    return (*outs, loss_sum, masked_total, jnp.sqrt(squares))


def solution(mesh):
    return jax.shard_map(
        body,
        mesh=mesh,
        in_specs=(P("grp", "dp"),) * 4 + (P("dp", None), P("dp", None), P("dp"), P("dp")),
        out_specs=(P("grp", "dp"),) * 4 + (P(), P(), P()),
        check_vma=False,
    )
```

```python
import functools
import math

import jax
import jax.numpy as jnp
from jax import lax
from jax.experimental import pallas as pl
from jax.experimental.pallas import tpu as pltpu
from jax.sharding import PartitionSpec as P

DE = 1024
HE = 16
FE = 4096
DD = 512
HD = 16
FD = 2048
PSIDE = 16
GSIDE = 14
VMAX = 64
STEP = 10
PIX = 768
LOWPIX = 192
GRID = 196
GPAD = 208
NENC = 8662528
NDEC = 3644352
LANES = 128
UNIT = 4 * LANES

HIGHEST = lax.Precision.HIGHEST
CLIP = 0.05
RATE = 0.01
BETA_ONE = 0.5
BETA_TWO = 0.5
ADAM_EPS = 1e-08
DECAY_WEIGHT = 0.05
AVERAGE_KEEP = 0.9
NORM_EPS = 1e-06
MASK_FILL = -1000000000.0
F32 = jnp.float32
BF16 = jnp.bfloat16
MESH = pl.DeviceIdType.MESH

WIDTH = 256
SUB = 64
PIECE = 8192
VEC_ROWS = 16
VEC_COLS = (FE, FD)
HEAD = LOWPIX + PIX

ENC_LAYOUT = [
    (PIX, DE),
    (DE,),
    (DE,),
    (DE,),
    (DE, 3 * DE),
    (DE,),
    (DE,),
    (DE, FE),
    (FE,),
    (DE,),
    (DE,),
    (DE,),
    (DE, DD),
    (DD,),
]
DEC_LAYOUT = [
    (DD,),
    (DD,),
    (DD,),
    (DD, 3 * DD),
    (DD, DD),
    (DD,),
    (DD,),
    (DD, FD),
    (FD,),
    (FD, DD),
    (DD,),
    (DD,),
    (DD,),
    (DD, HEAD),
    (HEAD,),
]
LENT = [(DE, DE), (FE, DE)]


DP_GRID = (4, 2, 2)
YZX, XZY, ZXY = ("y", "z", "x"), ("x", "z", "y"), ("z", "x", "y")
SPLIT = 2
ORDERS = (YZX,) * SPLIT + (XZY,) * SPLIT + (ZXY,) * SPLIT
PARTS = len(ORDERS)
OWN_FIRST = tuple(range(2 * SPLIT, 3 * SPLIT)) + tuple(range(2 * SPLIT))
SHARES = (0.41, 0.26, 0.33)
WAYS = ("x", "y", "up", "down")
CHUNK = 16
OPPOSITE = {"x": "x", "y": "y", "up": "down", "down": "up"}


def part_ranges(units):
    ends = [0]
    for share in SHARES:
        for _ in range(SPLIT):
            ends.append(ends[-1] + share / SPLIT)
    ends = [round(end * units) for end in ends[:-1]] + [units]
    return [(start, end - start) for start, end in zip(ends, ends[1:])]


def relatives():
    places = [(dz, dy, dx) for dz in range(-3, 4) for dy in (0, 1) for dx in (0, 1)]
    places.remove((0, 0, 0))
    return sorted(places, key=lambda r: abs(r[0]) + r[1] + r[2])


def last_axis(order, place):
    differs = {"z": place[0] != 0, "y": place[1] != 0, "x": place[2] != 0}
    return [axis for axis in order if differs[axis]][-1]


def onward(order, place):
    if place == (0, 0, 0):
        return ["up", "down", "x", "y"]
    axis = last_axis(order, place)
    ways = []
    if axis == "z":
        ways.append("up" if place[0] < 0 else "down")
    for later in order[order.index(axis) + 1 :]:
        ways += ["up", "down"] if later == "z" else [later]
    return ways


def when(condition, action):
    if condition is None:
        action()
    else:
        pl.when(condition)(action)


def both(left, right):
    if left is None:
        return right
    return left if right is None else left & right


class Spot:
    def __init__(self):
        self.grp = lax.axis_index("grp")
        self.dp = lax.axis_index("dp")
        self.x = self.dp % 2
        self.y = (self.dp // 2) % 2
        self.z = self.dp // 4
        self.neighbour = {
            "x": (self.grp, self.index(self.z, self.y, 1 - self.x)),
            "y": (self.grp, self.index(self.z, 1 - self.y, self.x)),
            "up": (self.grp, self.index(jnp.minimum(self.z + 1, 3), self.y, self.x)),
            "down": (self.grp, self.index(jnp.maximum(self.z - 1, 0), self.y, self.x)),
            "core": (1 - self.grp, self.dp),
        }
        self.exists = {"x": None, "y": None, "up": self.z < 3, "down": self.z > 0, "core": None}

    def index(self, z, y, x):
        return z * 4 + y * 2 + x

    def at(self, place):
        z = self.z + place[0]
        y = 1 - self.y if place[1] else self.y
        x = 1 - self.x if place[2] else self.x
        inside = None if place[0] == 0 else (z >= 0) & (z <= 3)
        return z, self.index(z, y, x), inside

    def greet(self):
        barrier = pltpu.get_barrier_semaphore()
        me = self.grp * 16 + self.dp

        def signal(step, carry):
            other = (me + step) % 32
            pl.semaphore_signal(
                barrier, inc=1, device_id=(other // 16, other % 16), device_id_type=MESH
            )
            return carry

        lax.fori_loop(1, 32, signal, 0)
        pl.semaphore_wait(barrier, 31)


def tell_all(spot, tiles, send_sem, recv_sem):
    me = spot.grp * 16 + spot.dp

    def copy(number, other):
        return pltpu.make_async_remote_copy(
            src_ref=tiles.at[number],
            dst_ref=tiles.at[number],
            send_sem=send_sem.at[other],
            recv_sem=recv_sem.at[number],
            device_id=(other // 16, other % 16),
            device_id_type=MESH,
        )

    def start(step, carry):
        copy(me, (me + step) % 32).start()
        return carry

    def finish(step, carry):
        other = (me + step) % 32
        copy(other, other).wait_recv()
        copy(me, other).wait_send()
        return carry

    return (
        lambda: lax.fori_loop(1, 32, start, 0),
        lambda: lax.fori_loop(1, 32, finish, 0),
    )


def gather_kernel(
    master_ref,
    masked_ref,
    out_ref,
    masked_out,
    master,
    own_ref,
    tiles,
    local_sem,
    send_sem,
    recv_sem,
    core_send,
    core_recv,
    tile_send,
    tile_recv,
):
    spot = Spot()
    read = pltpu.make_async_copy(master_ref, master, local_sem)
    read.start()
    tiles[spot.grp * 16 + spot.dp] = masked_ref[...]
    spot.greet()
    tell, told = tell_all(spot, tiles, tile_send, tile_recv)
    ranges = part_ranges(own_ref.shape[0])
    read.wait()

    def round_off(start, length):
        block = pl.ds(start, length)
        own_ref[block] = master[block].astype(BF16)

    def step(index, carry):
        round_off(index * CHUNK, CHUNK)
        return carry

    units = own_ref.shape[0]
    lax.fori_loop(0, units // CHUNK, step, 0)
    if units % CHUNK:
        round_off(units - units % CHUNK, units % CHUNK)

    def copy(part, source, way, from_own):
        target = out_ref.at[spot.grp, source, pl.ds(*ranges[part])]
        origin = own_ref.at[pl.ds(*ranges[part])] if from_own else target
        if way == "core":
            sems = (core_send.at[part, source], core_recv.at[part, source])
        else:
            sems = (send_sem.at[part, source, WAYS.index(way)], recv_sem.at[part, source])
        return pltpu.make_async_remote_copy(
            src_ref=origin,
            dst_ref=target,
            send_sem=sems[0],
            recv_sem=sems[1],
            device_id=spot.neighbour[way],
            device_id_type=MESH,
        )

    sent = []
    for part in OWN_FIRST:
        for way in onward(ORDERS[part], (0, 0, 0)):
            when(
                spot.exists[way],
                lambda part=part, way=way: copy(part, spot.dp, way, True).start(),
            )
            sent.append((part, spot.dp, way, spot.exists[way], True))
    local = pltpu.make_async_copy(own_ref, out_ref.at[spot.grp, spot.dp], local_sem)
    local.start()
    tell()
    for part in range(PARTS):
        copy(part, spot.dp, "core", True).start()
        sent.append((part, spot.dp, "core", None, True))
    for place in relatives():
        _, source, inside = spot.at(place)
        for part in range(PARTS):
            ways = onward(ORDERS[part], place)

            def pass_on(part=part, source=source, ways=ways):
                copy(part, source, "x", False).wait_recv()
                for way in ways:
                    when(
                        spot.exists[way],
                        lambda way=way: copy(part, source, way, False).start(),
                    )
                copy(part, source, "core", False).start()

            when(inside, pass_on)
            for way in ways + ["core"]:
                sent.append((part, source, way, both(inside, spot.exists[way]), False))
    for part, source, way, condition, from_own in sent:
        when(condition, lambda: copy(part, source, way, from_own).wait_send())

    def await_core(source, carry):
        for part in range(PARTS):
            landed = out_ref.at[1 - spot.grp, source, pl.ds(*ranges[part])]
            pltpu.make_async_remote_copy(
                src_ref=landed,
                dst_ref=landed,
                send_sem=core_send.at[part, source],
                recv_sem=core_recv.at[part, source],
                device_id=spot.neighbour["core"],
                device_id_type=MESH,
            ).wait_recv()
        return carry

    lax.fori_loop(0, 16, await_core, 0)
    told()
    masked_out[...] = jnp.sum(tiles[pl.ds(0, 16)], axis=0)
    local.wait()


def gather_rows(master, masked):
    units = master.shape[0]
    dma = pltpu.SemaphoreType.DMA
    anywhere = pl.BlockSpec(memory_space=pl.ANY)
    vmem = pl.BlockSpec(memory_space=pltpu.VMEM)
    return pl.pallas_call(
        gather_kernel,
        out_shape=(
            jax.ShapeDtypeStruct((2, 16, units, 4, LANES), BF16),
            jax.ShapeDtypeStruct((8, LANES), F32),
        ),
        in_specs=[anywhere, vmem],
        out_specs=(anywhere, vmem),
        scratch_shapes=[
            pltpu.VMEM((units, 4, LANES), F32),
            pltpu.VMEM((units, 4, LANES), BF16),
            pltpu.VMEM((32, 8, LANES), F32),
            dma,
            dma((PARTS, 16, 4)),
            dma((PARTS, 16)),
            dma((PARTS, 16)),
            dma((PARTS, 16)),
            dma((32,)),
            dma((32,)),
        ],
        compiler_params=pltpu.CompilerParams(collective_id=0, has_side_effects=True),
        name="gather_rows",
    )(master, masked)


def slot_tables():
    tables = []
    for order in ORDERS:
        table = {}
        for way in WAYS:
            keys = []
            along = False
            for place in [(0, 0, 0)] + relatives():
                if way in onward(order, place):
                    if place[1:] not in keys:
                        keys.append(place[1:])
                    along = along or place[0] != 0
            table[way] = (keys, 3 if way in ("up", "down") else (4 if along else 1))
        tables.append(table)
    return tables


SLOTS = slot_tables()
STAGES = 4


def scatter_kernel(grad_ref, loss_ref, out_ref, sums_ref, *refs):
    ranges = part_ranges(grad_ref.shape[1])
    landing = {}
    for part in range(PARTS):
        for number, way in enumerate(WAYS):
            landing[part, way] = refs[part * 4 + number]
    stage, total, tiles, send_sem, recv_sem, stage_sem, out_sem, tile_send, tile_recv = refs[4 * PARTS :]
    spot = Spot()
    spot.greet()

    def slot(part, way, place, z):
        keys, depth = SLOTS[part][way]
        base = keys.index(place[1:]) * depth
        if way == "up":
            return base + z
        if way == "down":
            return base + z - 1
        return base + (z if depth == 4 else 0)

    def parent(part, place):
        axis = last_axis(ORDERS[part], place)
        if axis == "z":
            return "up" if place[0] > 0 else "down"
        return axis

    def seen_from_parent(part, place):
        way = parent(part, place)
        dz, dy, dx = place
        if way == "x":
            return (dz, dy, 0)
        if way == "y":
            return (dz, 0, dx)
        return (dz - 1 if way == "up" else dz + 1, dy, dx)

    def send(part, place, origin):
        z, owner, _ = spot.at(place)
        way = parent(part, place)
        back = OPPOSITE[way]
        return pltpu.make_async_remote_copy(
            src_ref=origin,
            dst_ref=landing[part, back].at[slot(part, back, seen_from_parent(part, place), z)],
            send_sem=send_sem.at[part, owner],
            recv_sem=recv_sem.at[part, owner, WAYS.index(back)],
            device_id=spot.neighbour[way],
            device_id_type=MESH,
        )

    def own(part, owner):
        return grad_ref.at[owner, pl.ds(*ranges[part])]

    nodes = [(place, part) for place in relatives()[::-1] for part in range(PARTS)]
    nodes += [((0, 0, 0), part) for part in range(PARTS)]
    sent = []
    inner = []
    for place, part in nodes:
        z, owner, inside = spot.at(place)
        ways = onward(ORDERS[part], place)
        if place != (0, 0, 0):
            sent.append((part, place, owner, inside))
        inner.append((part, place, ways, z, owner, inside))
    staged_nodes = [node for node in inner if node[2]]

    def staged(number):
        part, _, _, _, owner, _ = staged_nodes[number]
        return pltpu.make_async_copy(
            own(part, owner),
            stage.at[number % STAGES, pl.ds(0, ranges[part][1])],
            stage_sem.at[number % STAGES],
        )

    for number in range(STAGES - 1):
        when(staged_nodes[number][5], lambda: staged(number).start())
    number = -1
    for part, place, ways, z, owner, inside in inner:
        if not ways:
            when(inside, lambda: send(part, place, own(part, owner)).start())
            continue
        number += 1
        ahead = number + STAGES - 1
        if ahead < len(staged_nodes):
            when(staged_nodes[ahead][5], lambda: staged(ahead).start())
        length = ranges[part][1]
        root = place == (0, 0, 0)

        def combine(arriving, number=number, part=part, place=place, z=z, owner=owner):
            slots = []
            for way in arriving:
                spot_of = landing[part, way].at[slot(part, way, place, z)]
                pltpu.make_async_remote_copy(
                    src_ref=spot_of,
                    dst_ref=spot_of,
                    send_sem=send_sem.at[part, owner],
                    recv_sem=recv_sem.at[part, owner, WAYS.index(way)],
                    device_id=spot.neighbour[way],
                    device_id_type=MESH,
                ).wait_recv()
                slots.append(spot_of)
            staged(number).wait()
            if slots:
                target = total.at[pl.ds(*ranges[part])] if root else slots[0]

                def add(start, count):
                    value = stage[number % STAGES, pl.ds(start, count)]
                    for item in slots:
                        value = value + item[pl.ds(start, count)]
                    target[pl.ds(start, count)] = value

                def step(index, carry):
                    add(index * CHUNK, CHUNK)
                    return carry

                lax.fori_loop(0, length // CHUNK, step, 0)
                if length % CHUNK:
                    add(length - length % CHUNK, length % CHUNK)
            if not root:
                send(part, place, slots[0] if slots else own(part, owner)).start()

        def choose(ways=ways, combine=combine):
            flat = [way for way in ways if way in ("x", "y")]
            along = [way for way in ways if way in ("up", "down")]
            if not along:
                combine(flat)
            elif len(along) == 1:
                there = spot.exists[along[0]]
                pl.when(there)(lambda: combine(flat + along))
                pl.when(jnp.logical_not(there))(lambda: combine(flat))
            else:
                up, down = spot.exists["up"], spot.exists["down"]
                pl.when(up & down)(lambda: combine(flat + ["up", "down"]))
                pl.when(jnp.logical_not(down))(lambda: combine(flat + ["up"]))
                pl.when(jnp.logical_not(up))(lambda: combine(flat + ["down"]))

        when(inside, choose)
    out = pltpu.make_async_copy(total, out_ref, out_sem)
    out.start()
    units = total.shape[0]

    def square(start, count, running):
        value = total[pl.ds(start, count)]
        return running + jnp.sum(value * value, axis=0)

    squares = lax.fori_loop(
        0,
        units // CHUNK,
        lambda index, running: square(index * CHUNK, CHUNK, running),
        jnp.zeros((4, LANES), F32),
    )
    if units % CHUNK:
        squares = square(units - units % CHUNK, units % CHUNK, squares)
    me = spot.grp * 16 + spot.dp
    tiles[me, pl.ds(0, 4)] = squares
    tiles[me, pl.ds(4, 4)] = loss_ref[pl.ds(4, 4)]
    tell, told = tell_all(spot, tiles, tile_send, tile_recv)
    tell()
    for part, place, owner, inside in sent:
        when(inside, lambda: send(part, place, own(part, owner)).wait_send())
    told()
    sums_ref[...] = jnp.sum(tiles[...], axis=0)
    out.wait()


def scatter_sums(grads, loss):
    units = grads.shape[1]
    ranges = part_ranges(units)
    scratch = []
    for part in range(PARTS):
        for way in WAYS:
            keys, depth = SLOTS[part][way]
            scratch.append(pltpu.VMEM((len(keys) * depth, ranges[part][1], 4, LANES), F32))
    largest = max(length for _, length in ranges)
    dma = pltpu.SemaphoreType.DMA
    scratch += [
        pltpu.VMEM((STAGES, largest, 4, LANES), F32),
        pltpu.VMEM((units, 4, LANES), F32),
        pltpu.VMEM((32, 8, LANES), F32),
        dma((PARTS, 16)),
        dma((PARTS, 16, 4)),
        dma((STAGES,)),
        dma,
        dma((32,)),
        dma((32,)),
    ]
    anywhere = pl.BlockSpec(memory_space=pl.ANY)
    vmem = pl.BlockSpec(memory_space=pltpu.VMEM)
    return pl.pallas_call(
        scatter_kernel,
        out_shape=(
            jax.ShapeDtypeStruct((units, 4, LANES), F32),
            jax.ShapeDtypeStruct((8, LANES), F32),
        ),
        in_specs=[anywhere, vmem],
        out_specs=(anywhere, vmem),
        scratch_shapes=scratch,
        compiler_params=pltpu.CompilerParams(
            collective_id=1, has_side_effects=True, vmem_limit_bytes=63 * 2**20
        ),
        name="scatter_sums",
    )(grads, loss)


def update_values(owned, scale, params, first_moment, second_moment, average):
    clipped = owned * scale
    new_first = BETA_ONE * first_moment + (1.0 - BETA_ONE) * clipped
    new_second = BETA_TWO * second_moment + (1.0 - BETA_TWO) * clipped * clipped
    root = jnp.sqrt(new_second * (1.0 / (1.0 - BETA_TWO**STEP)))
    direction = new_first * (1.0 / (1.0 - BETA_ONE**STEP)) / (root + ADAM_EPS)
    new_params = params - RATE * (direction + DECAY_WEIGHT * params)
    new_average = AVERAGE_KEEP * average + (1.0 - AVERAGE_KEEP) * new_params
    return new_params, new_first, new_second, new_average


def update_kernel(scale_ref, *refs):
    scale = scale_ref[0]
    step = 31

    def one(index, carry):
        block = pl.ds(index * step, step)
        owned, params, first, second, average = [ref[block] for ref in refs[:5]]
        values = update_values(owned, scale, params, first, second, average)
        for out, value in zip(refs[5:], values):
            out[block] = value
        return carry

    lax.fori_loop(0, refs[0].shape[0] // step, one, 0)


def update(scale, arrays):
    units = arrays[0].shape[0]
    depth = 155
    spec = pl.BlockSpec((depth, 4, LANES), lambda i: (i, 0, 0))
    return pl.pallas_call(
        update_kernel,
        grid=(units // depth,),
        out_shape=[jax.ShapeDtypeStruct((units, 4, LANES), F32)] * 4,
        in_specs=[pl.BlockSpec(memory_space=pltpu.SMEM)] + [spec] * 5,
        out_specs=[spec] * 4,
        name="update",
    )(scale.reshape(1), *arrays)


def sections(layout, base):
    matrices, vectors = [], []
    offset = base
    for shape in layout:
        (matrices if len(shape) == 2 else vectors).append((offset, shape))
        offset += math.prod(shape)
    return matrices, vectors


def matrix_plan(rows):
    enc_matrices, enc_vectors = sections(ENC_LAYOUT, 0)
    dec_matrices, dec_vectors = sections(DEC_LAYOUT, rows * LANES)
    lent = rows * LANES + NDEC
    matrices = enc_matrices + sections(LENT, lent)[0] + dec_matrices
    return matrices, enc_vectors, dec_vectors


def padded(columns):
    return -(-columns // LANES) * LANES


def block_depth(shape):
    if shape[1] % LANES:
        return shape[0]
    depth = shape[0]
    while depth * shape[1] > PIECE * LANES:
        depth //= 2
    return depth


def matrix_kernel(rows, flat_ref, *refs):
    matrices, enc_vectors, dec_vectors = matrix_plan(rows)
    count = len(matrices)
    out_refs = refs[:count]
    vector_refs = refs[count : count + 2]
    blocks = refs[count + 2 : 2 * count + 2]
    flat_in, wide, pairs, vector_in, in_sem, out_sem, vector_sem = refs[2 * count + 2 :]
    lane = lax.broadcasted_iota(jnp.int32, (1, LANES), 1)

    chunks = []
    for number, (offset, shape) in enumerate(matrices):
        depth = block_depth(shape)
        for start in range(0, shape[0], depth):
            place = offset + start * shape[1]
            chunks.append((number, start, depth, place // LANES, place % LANES))

    def load(index):
        number, _, depth, first, shift = chunks[index]
        length = depth * matrices[number][1][1] // LANES
        begin = first // 16 * 16
        end = -(-(first + length + (1 if shift else 0)) // 16) * 16
        copy = pltpu.make_async_copy(
            flat_ref.at[pl.ds(begin, end - begin)],
            flat_in.at[index % 2, pl.ds(0, end - begin)],
            in_sem.at[index % 2],
        )
        return copy, first - begin, end - begin

    def store(index):
        number, start, depth, _, _ = chunks[index]
        slot = start // depth % 2
        return pltpu.make_async_copy(
            blocks[number].at[slot], out_refs[number].at[pl.ds(start, depth)], out_sem.at[number, slot]
        )

    def widen(index, length):
        step = 256

        def one(start, size):
            wide[pl.ds(start, size)] = flat_in[index % 2, pl.ds(start, size)].astype(F32)

        def loop(i, carry):
            one(pl.multiple_of(i * step, step), step)
            return carry

        lax.fori_loop(0, length // step, loop, 0)
        if length % step:
            one(length - length % step, length % step)

    def turned(first, second):
        return pltpu.roll(jnp.where(lane < LANES // 2, second, first), LANES // 2, 1)

    def arrange(index, phase):
        number, start, depth, _, shift = chunks[index]
        columns = matrices[number][1][1]
        block = blocks[number].at[start // depth % 2]
        tiles = columns // LANES

        def plain(i, carry):
            row = pl.multiple_of(i * SUB, SUB)
            for tile in range(tiles):
                value = wide[pl.ds(phase + row * tiles + tile, SUB, stride=tiles)]
                if shift:
                    after = wide[pl.ds(phase + row * tiles + tile + 1, SUB, stride=tiles)]
                    value = turned(value, after)
                block[pl.ds(row, SUB), pl.ds(tile * LANES, LANES)] = value.astype(BF16)
            return carry

        def paired(i, carry):
            stride = 2 * columns // LANES
            half = SUB // 2
            row = pl.multiple_of(i * half, half)
            for tile in range(tiles + 1):
                even = wide[pl.ds(phase + row * stride + tile, half, stride=stride)]
                odd = wide[pl.ds(phase + row * stride + tiles + tile, half, stride=stride)]
                if tile < tiles:
                    after = wide[pl.ds(phase + row * stride + tiles + tile + 1, half, stride=stride)]
                    odd = turned(odd, after)
                else:
                    even = jnp.where(lane < LANES // 2, even, 0.0)
                    odd = jnp.where(lane < LANES // 2, pltpu.roll(odd, LANES // 2, 1), 0.0)
                lanes = pl.ds(tile * LANES, LANES)
                pairs[tile, pl.ds(0, half, stride=2)] = even
                pairs[tile, pl.ds(1, half, stride=2)] = odd
                block[pl.ds(pl.multiple_of(i * SUB, SUB), SUB), lanes] = pairs[tile].astype(BF16)
            return carry

        lax.fori_loop(0, depth // SUB, paired if columns % LANES else plain, 0)

    windows = []
    wanted = [(0, n, v) for n, v in enumerate(enc_vectors)]
    wanted += [(1, n, v) for n, v in enumerate(dec_vectors)]
    for _, _, (offset, shape) in wanted:
        first = offset // LANES // 16 * 16
        end = -(-(offset // LANES + -(-shape[0] // LANES)) // 16) * 16
        if windows and first <= windows[-1][1]:
            windows[-1][1] = max(windows[-1][1], end)
        else:
            windows.append([first, end])
    bases = [sum(e - f for f, e in windows[:n]) for n in range(len(windows))]

    def vector_copy(n):
        first, end = windows[n]
        return pltpu.make_async_copy(
            flat_ref.at[pl.ds(first, end - first)],
            vector_in.at[pl.ds(bases[n], end - first)],
            vector_sem.at[n],
        )

    load(0)[0].start()
    for n in range(len(windows)):
        vector_copy(n).start()
    for index, (number, start, depth, _, _) in enumerate(chunks):
        copy, phase, length = load(index)
        copy.wait()
        if index + 1 < len(chunks):
            load(index + 1)[0].start()
        widen(index, length)
        if start // depth >= 2:
            store(index - 2).wait()
        arrange(index, phase)
        store(index).start()
    for n in range(len(windows)):
        vector_copy(n).wait()
    total = bases[-1] + windows[-1][1] - windows[-1][0]
    wide[pl.ds(0, total)] = vector_in[...].astype(F32)
    for group, n, (offset, shape) in wanted:
        first = offset // LANES
        window = [k for k, (f, e) in enumerate(windows) if f <= first < e][0]
        base = bases[window] + first - windows[window][0]
        for tile in range(-(-shape[0] // LANES)):
            value = wide[pl.ds(base + tile, 1)]
            if shape[0] - tile * LANES < LANES:
                value = jnp.where(lane < shape[0] - tile * LANES, value, 0.0)
            vector_refs[group][pl.ds(n, 1), pl.ds(tile * LANES, LANES)] = value
    for index, (number, start, depth, _, _) in enumerate(chunks):
        if start + 2 * depth >= matrices[number][1][0]:
            store(index).wait()


def weight_matrices(flat):
    rows = flat.shape[0] // 2
    matrices, enc_vectors, dec_vectors = matrix_plan(rows)
    shapes = [(shape[0], padded(shape[1])) for _, shape in matrices]
    buffers = []
    for (_, shape), (_, columns) in zip(matrices, shapes):
        depth = block_depth(shape)
        buffers.append(pltpu.VMEM((min(2, shape[0] // depth), depth, columns), BF16))
    dma = pltpu.SemaphoreType.DMA
    windows = 0
    last = -1
    total = 0
    for offset, shape in enc_vectors + dec_vectors:
        first = offset // LANES // 16 * 16
        end = -(-(offset // LANES + -(-shape[0] // LANES)) // 16) * 16
        if first <= last:
            total += max(0, end - last)
            last = max(last, end)
        else:
            windows += 1
            total += end - first
            last = end
    anywhere = pl.BlockSpec(memory_space=pl.ANY)
    vmem = pl.BlockSpec(memory_space=pltpu.VMEM)
    return pl.pallas_call(
        functools.partial(matrix_kernel, rows),
        out_shape=[jax.ShapeDtypeStruct(shape, BF16) for shape in shapes]
        + [jax.ShapeDtypeStruct((VEC_ROWS, columns), F32) for columns in VEC_COLS],
        in_specs=[anywhere],
        out_specs=[anywhere] * len(shapes) + [vmem, vmem],
        scratch_shapes=buffers
        + [
            pltpu.VMEM((2, PIECE + 32, LANES), BF16),
            pltpu.VMEM((PIECE + 32, LANES), F32),
            pltpu.VMEM((padded(HEAD) // LANES, SUB, LANES), F32),
            pltpu.VMEM((total, LANES), BF16),
            dma((2,)),
            dma((len(shapes), 2)),
            dma((windows,)),
        ],
        compiler_params=pltpu.CompilerParams(vmem_limit_bytes=56 * 2**20),
        name="weight_matrices",
    )(flat)


def stream_items(layout, lent):
    items = []
    offset = 0
    numbers = [0, 0]
    for shape in layout + lent:
        matrix = len(shape) == 2
        number = numbers[matrix]
        numbers[matrix] += 1
        depth = block_depth(shape) if matrix else 0
        for start in range(0, shape[0] if matrix else 1, max(depth, 1)):
            items.append((matrix, number, shape, start, depth, offset))
            offset += depth * shape[1] if matrix else shape[0]
    return items, offset


ROLES = (
    (ENC_LAYOUT, [], (0, 1, 2, 3)),
    (DEC_LAYOUT, LENT, (6, 7, 8, 9, 10, 4, 5)),
)
PAIRS = 11


def factor_buffers(shapes):
    sizes = []
    places = {}
    for role in (1, 0):
        taken = set()
        for number in ROLES[role][2]:
            for side in range(2):
                length, columns = shapes[2 * number + side]
                fits = [
                    n
                    for n, size in enumerate(sizes)
                    if n not in taken and size[0] == 2 * length and size[1] >= columns
                ]
                if fits:
                    place = min(fits, key=lambda n: sizes[n][1])
                else:
                    place = len(sizes)
                    sizes.append((2 * length, columns))
                taken.add(place)
                places[role, number, side] = place
    return sizes, places


def product_kernel(rows, shapes, *refs):
    factors, vectors, out_ref = refs[: 2 * PAIRS], refs[2 * PAIRS : 2 * PAIRS + 2], refs[24]
    sizes, places = factor_buffers(shapes)
    buffers = refs[25 : 25 + len(sizes)]
    refs = refs[25 + len(sizes) :]
    others = refs[:2]
    turned_left, tall, rows_out, own_sem, send_sem, recv_sem, out_sem = refs[2:]
    core = lax.axis_index("grp")
    sibling = (1 - core, lax.axis_index("dp"))
    barrier = pltpu.get_barrier_semaphore()
    pl.semaphore_signal(barrier, inc=1, device_id=sibling, device_id_type=MESH)
    pl.semaphore_wait(barrier, 1)

    def half_of(role, number, side, part):
        length, columns = shapes[2 * number + side]
        buffer = buffers[places[role, number, side]]
        return buffer.at[pl.ds(part * length, length), pl.ds(0, columns)]

    def local(role, number, side):
        return pltpu.make_async_copy(
            factors[2 * number + side], half_of(role, number, side, 0), own_sem.at[number, side]
        )

    def remote(role, number, side):
        return pltpu.make_async_remote_copy(
            src_ref=factors[2 * number + side],
            dst_ref=half_of(role, number, side, 1),
            send_sem=send_sem.at[number, side],
            recv_sem=recv_sem.at[number, side],
            device_id=sibling,
            device_id_type=MESH,
        )

    def remote_vectors(role):
        return pltpu.make_async_remote_copy(
            src_ref=vectors[role],
            dst_ref=others[role],
            send_sem=send_sem.at[PAIRS, role],
            recv_sem=recv_sem.at[PAIRS, role],
            device_id=sibling,
            device_id_type=MESH,
        )

    def act(role):
        remote_vectors(1 - role).start()
        pending = [(number, side) for number in ROLES[role][2] for side in range(2)]
        for number, side in pending:
            local(role, number, side).start()
        given = [(number, side) for number in ROLES[1 - role][2] for side in range(2)]
        for number, side in given:
            remote(1 - role, number, side).start()
        remote_vectors(role).wait_recv()

        def ready(number):
            for side in range(2):
                local(role, number, side).wait()
                remote(role, number, side).wait_recv()

        lefts, rights = [], []
        for number in ROLES[role][2]:
            for side, views in ((0, lefts), (1, rights)):
                length, columns = shapes[2 * number + side]
                buffer = buffers[places[role, number, side]]
                views.append(buffer.at[pl.ds(0, 2 * length), pl.ds(0, columns)])
        fill_row(
            rows,
            ROLES[role],
            ready,
            lefts,
            rights,
            vectors[role],
            others[role],
            turned_left,
            tall,
            rows_out,
            out_ref,
            out_sem,
        )
        for number, side in given:
            remote(1 - role, number, side).wait_send()
        remote_vectors(1 - role).wait_send()

    for role in range(2):
        pl.when(core == role)(functools.partial(act, role))


def fill_row(
    rows,
    role,
    ready,
    lefts,
    rights,
    mine_ref,
    other_ref,
    turned_left,
    tall,
    rows_out,
    out_ref,
    out_sem,
):
    layout, lent, numbers = role
    lane = lax.broadcasted_iota(jnp.int32, (1, LANES), 1)
    half = LANES // 2
    items, used = stream_items(layout, lent)
    groups = []
    current = []
    for item in items:
        current.append(item)
        if item[0]:
            groups.append(current)
            current = []
    groups.append(current)

    def vector(item, buffer, base):
        _, number, shape, _, _, _ = item
        for tile in range(-(-shape[0] // LANES)):
            lanes = pl.ds(tile * LANES, LANES)
            buffer[pl.ds(base + tile, 1)] = (
                mine_ref[pl.ds(number, 1), lanes] + other_ref[pl.ds(number, 1), lanes]
            )

    def matrix(item, buffer, base):
        _, number, shape, start, depth, offset = item
        columns = shape[1]
        shifted = offset % LANES
        tiles = -(-columns // LANES)
        width = min(WIDTH, columns)
        if start == 0:
            ready(numbers[number])
            if shifted:
                length = rights[number].shape[0]

                def turn(i, carry):
                    block = pl.ds(pl.multiple_of(i * 64, 64), 64)
                    value = rights[number][block].astype(F32)
                    rights[number][block] = pltpu.roll(value, half, 1).astype(BF16)
                    return carry

                lax.fori_loop(0, length // 64, turn, 0)
        length = lefts[number].shape[0]
        sub = min(256, depth)

        def loop(step, carry):
            k = pl.multiple_of(start + step * sub, sub)
            turned_left[pl.ds(0, sub), pl.ds(0, length)] = lefts[number][:, pl.ds(k, sub)].T

            def across(c, carry):
                column = pl.multiple_of(c * width, width)
                value = jnp.dot(
                    turned_left[pl.ds(0, sub), pl.ds(0, length)],
                    rights[number][:, pl.ds(column, width)],
                    preferred_element_type=F32,
                )
                row = base + step * sub * tiles
                for piece in range(width // LANES):
                    part = value[:, piece * LANES : (piece + 1) * LANES]
                    tile = c * (width // LANES) + piece
                    if columns % LANES:
                        tall[tile, pl.ds(step * sub, sub)] = part
                    elif shifted and piece == 0:
                        first = row + tile

                        @pl.when(c == 0)
                        def _():
                            before = pltpu.roll(part, 1, 0)
                            index = lax.broadcasted_iota(jnp.int32, (sub, LANES), 0)
                            held = buffer[pl.ds(row, 1)]
                            before = jnp.where(index == 0, held, before)
                            merged = jnp.where(lane < half, before, part)
                            buffer[pl.ds(row, sub, stride=tiles)] = merged
                            buffer[pl.ds(row + sub * tiles, 1)] = part[sub - 1 :]

                        @pl.when(c > 0)
                        def _():
                            buffer[pl.ds(first, sub, stride=tiles)] = part
                    else:
                        buffer[pl.ds(row + tile, sub, stride=tiles)] = part
                return carry

            lax.fori_loop(0, tiles * LANES // width, across, 0)
            return carry

        lax.fori_loop(0, depth // sub, loop, 0)
        if columns % LANES:
            stride = 2 * columns // LANES
            pair = 64

            def weave(i, carry):
                k = pl.multiple_of(i * 2 * pair, 2 * pair)
                row = base + i * pair * stride
                evens = [tall[t, pl.ds(k, pair, stride=2)] for t in range(tiles)]
                odds = [tall[t, pl.ds(k + 1, pair, stride=2)] for t in range(tiles)]
                for t in range(tiles - 1):
                    buffer[pl.ds(row + t, pair, stride=stride)] = evens[t]
                middle = jnp.where(lane < half, evens[-1], pltpu.roll(odds[0], half, 1))
                buffer[pl.ds(row + tiles - 1, pair, stride=stride)] = middle
                for t in range(1, tiles):
                    both_halves = jnp.where(lane < half, odds[t], odds[t - 1])
                    buffer[pl.ds(row + tiles - 1 + t, pair, stride=stride)] = pltpu.roll(
                        both_halves, half, 1
                    )
                return carry

            lax.fori_loop(0, depth // 2 // pair, weave, 0)

    flights = []
    tail = None
    for number, group in enumerate(groups):
        slot = number % 2
        buffer = rows_out.at[slot]
        if number >= 2:
            flights[number - 2].wait()
        first = group[0][5] // LANES if group else used // LANES
        begin = first // 8 * 8
        if tail is not None:
            buffer[pl.ds(0, 8)] = rows_out[1 - slot, pl.ds(tail, 8)]
        for item in group:
            (matrix if item[0] else vector)(item, buffer, item[5] // LANES - begin)
        last = number == len(groups) - 1
        if last:
            at = used // LANES - begin
            if used % LANES:
                buffer[pl.ds(at, 1)] = jnp.where(lane < used % LANES, buffer[pl.ds(at, 1)], 0.0)
                at += 1
            length = rows - begin
            if length > at:
                buffer[pl.ds(at, length - at)] = jnp.zeros((length - at, LANES), F32)
        else:
            end = groups[number + 1][0][5] if groups[number + 1] else used
            tail = (end // LANES - begin) // 8 * 8
            length = tail
        flight = pltpu.make_async_copy(
            buffer.at[pl.ds(0, length)], out_ref.at[pl.ds(begin, length)], out_sem.at[slot]
        )
        flight.start()
        flights.append(flight)
    for flight in flights[-2:]:
        flight.wait()


def flat_gradient(rows, factors, enc_vectors, dec_vectors):
    shapes = [factor.shape for factor in factors]
    sizes, _ = factor_buffers(shapes)
    longest = max(length for length, _ in sizes)
    dma = pltpu.SemaphoreType.DMA
    anywhere = pl.BlockSpec(memory_space=pl.ANY)
    vmem = pl.BlockSpec(memory_space=pltpu.VMEM)
    return pl.pallas_call(
        functools.partial(product_kernel, rows, shapes),
        out_shape=jax.ShapeDtypeStruct((rows, LANES), F32),
        in_specs=[anywhere] * (2 * PAIRS) + [vmem, vmem],
        out_specs=anywhere,
        scratch_shapes=[pltpu.VMEM(size, BF16) for size in sizes]
        + [
            pltpu.VMEM(enc_vectors.shape, F32),
            pltpu.VMEM(dec_vectors.shape, F32),
            pltpu.VMEM((256, longest), BF16),
            pltpu.VMEM((padded(HEAD) // LANES, DD, LANES), F32),
            pltpu.VMEM((2, PIECE + 128, LANES), F32),
            dma((PAIRS, 2)),
            dma((PAIRS + 1, 2)),
            dma((PAIRS + 1, 2)),
            dma((2,)),
        ],
        compiler_params=pltpu.CompilerParams(
            collective_id=2, has_side_effects=True, vmem_limit_bytes=63 * 2**20
        ),
        name="flat_gradient",
    )(*factors, enc_vectors, dec_vectors)


LN1_G, LN1_B, LN2_G, LN2_B, FC1_B, FC2_B, LNF_G, LNF_B, LAST_B = range(1, 10)
GROUP = 256
TURNS = 16
BATCH = 2


def dot(left, right):
    return jnp.dot(left, right, preferred_element_type=F32)


def dot_nt(left, right):
    return lax.dot_general(left, right, (((1,), (1,)), ((), ())), preferred_element_type=F32)


def dot_tn(left, right):
    return lax.dot_general(left, right, (((0,), (0,)), ((), ())), preferred_element_type=F32)


def blocks(length, size, action):
    def step(index, carry):
        action(pl.ds(pl.multiple_of(index * size, size), size))
        return carry

    lax.fori_loop(0, length // size, step, 0)


def row_step(length):
    return 208 if length % 208 == 0 else 128


def score_step(length):
    return 832 if length % 208 == 0 else 256


def normed(state):
    centered = state - jnp.mean(state, axis=-1, keepdims=True)
    inverse = lax.rsqrt(jnp.mean(centered * centered, axis=-1, keepdims=True) + NORM_EPS)
    return centered * inverse, inverse


def norm_rows(source, target, vectors, gain):
    width = source.shape[1]

    def one(rows):
        unit, _ = normed(source[rows])
        value = unit * vectors[pl.ds(gain, 1), pl.ds(0, width)]
        target[rows] = (value + vectors[pl.ds(gain + 1, 1), pl.ds(0, width)]).astype(BF16)

    blocks(source.shape[0], row_step(source.shape[0]), one)


def norm_rows_back(source, grad, vectors, sums, gain, finish):
    width = source.shape[1]
    lanes = pl.ds(0, width)

    def one(rows):
        unit, inverse = normed(source[rows])
        out = grad[rows]
        sums[pl.ds(gain, 1), lanes] += jnp.sum(out * unit, axis=0, keepdims=True)
        sums[pl.ds(gain + 1, 1), lanes] += jnp.sum(out, axis=0, keepdims=True)
        scaled = out * vectors[pl.ds(gain, 1), lanes]
        mean = jnp.mean(scaled, axis=-1, keepdims=True)
        along = jnp.mean(scaled * unit, axis=-1, keepdims=True)
        finish(rows, inverse * (scaled - mean - unit * along))

    blocks(source.shape[0], row_step(source.shape[0]), one)


def gelu_parts(value):
    below = 0.5 * (1.0 + lax.erf(value * math.sqrt(0.5)))
    return below, value * below


def head_masks(depth):
    lane = lax.broadcasted_iota(jnp.int32, (1, GROUP), 1)
    return [
        ((lane >= head * depth) & (lane < (head + 1) * depth)).astype(F32).astype(BF16)
        for head in range(GROUP // depth)
    ]


def stack_heads(target, value, masks):
    length = value.shape[0]
    for head, mask in enumerate(masks):
        target[pl.ds(head * length, length)] = value * mask


def attention_forward(images, length, heads, qkv, bias, attend, attend_low, stacked, mixed):
    width = mixed.shape[1]
    depth = width // heads
    masks = head_masks(depth)
    groups = width // GROUP
    scale = depth**-0.5

    def one(index, carry):
        image, group = index // groups, index % groups
        rows = pl.ds(pl.multiple_of(image * length, length), length)

        def lanes(part):
            return pl.ds(pl.multiple_of(part * width + group * GROUP, GROUP), GROUP)

        stack_heads(stacked, qkv[rows, lanes(0)], masks)
        attend[index] = dot_nt(stacked[...], qkv[rows, lanes(1)])
        shift = bias[pl.ds(image, 1)]

        def softmax(block):
            scores = attend[index, block] * scale + shift
            raised = jnp.exp(scores - jnp.max(scores, axis=-1, keepdims=True))
            value = raised / jnp.sum(raised, axis=-1, keepdims=True)
            attend[index, block] = value
            attend_low[block] = value.astype(BF16)

        blocks(len(masks) * length, score_step(length), softmax)
        value = qkv[rows, lanes(2)]
        total = jnp.zeros((length, GROUP), F32)
        for head, mask in enumerate(masks):
            total += dot(attend_low[pl.ds(head * length, length)], value * mask)
        mixed[rows, lanes(0)] = total.astype(BF16)
        return carry

    lax.fori_loop(0, images * groups, one, 0)


def attention_backward(
    images, length, heads, qkv, grad_mixed, attend, attend_low, grad_low, grads, stacked, other, out
):
    width = grad_mixed.shape[1]
    depth = width // heads
    masks = head_masks(depth)
    groups = width // GROUP
    scale = depth**-0.5

    def one(index, carry):
        image, group = index // groups, index % groups
        rows = pl.ds(pl.multiple_of(image * length, length), length)

        def lanes(part):
            return pl.ds(pl.multiple_of(part * width + group * GROUP, GROUP), GROUP)

        stack_heads(stacked, qkv[rows, lanes(0)], masks)
        stack_heads(other, grad_mixed[rows, lanes(0)], masks)
        grads[...] = dot_nt(other[...], qkv[rows, lanes(2)])

        def scores(block):
            value = attend[index, block]
            grad = grads[block]
            total = jnp.sum(grad * value, axis=-1, keepdims=True)
            grad_low[block] = (value * (grad - total)).astype(BF16)
            attend_low[block] = value.astype(BF16)

        blocks(len(masks) * length, score_step(length), scores)
        out[rows, lanes(2)] = dot_tn(attend_low[...], other[...]).astype(BF16)
        out[rows, lanes(1)] = (dot_tn(grad_low[...], stacked[...]) * scale).astype(BF16)
        key = qkv[rows, lanes(1)]
        total = jnp.zeros((length, GROUP), F32)
        for head, mask in enumerate(masks):
            total += dot(grad_low[pl.ds(head * length, length)], key * mask)
        out[rows, lanes(0)] = (total * scale).astype(BF16)
        return carry

    lax.fori_loop(0, images * groups, one, 0)


def columns_loop(columns, size, action):
    blocks(columns, min(size, columns), action)


def feed_forward(normed_two, fc1_w, fc2_w, vectors, middle, pre, active, state):
    bias = pl.ds(FC1_B, 1)

    def up(lanes):
        value = dot(normed_two[...], fc1_w[:, lanes]) + vectors[bias, lanes]
        pre[:, lanes] = value
        active[:, lanes] = gelu_parts(value)[1].astype(BF16)

    columns_loop(pre.shape[1], 256, up)

    def down(lanes):
        value = dot(active[...], fc2_w[:, lanes])
        state[:, lanes] = middle[:, lanes] + value + vectors[pl.ds(FC2_B, 1), lanes]

    columns_loop(state.shape[1], 256, down)


def feed_backward(grad_low, fc1_w, fc2_w, pre, sums, grad_pre, out):
    def up(lanes):
        value = pre[:, lanes]
        below, _ = gelu_parts(value)
        slope = below + value * (jnp.exp(-0.5 * value * value) * (1.0 / math.sqrt(2.0 * math.pi)))
        grad = dot_nt(grad_low[...], fc2_w[lanes]) * slope
        sums[pl.ds(FC1_B, 1), lanes] += jnp.sum(grad, axis=0, keepdims=True)
        grad_pre[:, lanes] = grad.astype(BF16)

    columns_loop(pre.shape[1], 256, up)

    def down(lanes):
        out[:, lanes] = dot_nt(grad_pre[...], fc1_w[lanes])

    columns_loop(out.shape[1], 256, down)


def turn_code(places, table):
    lane = lax.broadcasted_iota(jnp.int32, (places.shape[0], TURNS), 1)
    passed = (lane > 0) & (lane < TURNS - 1) & (places >= lane * GSIDE)
    row = jnp.sum(passed.astype(F32), axis=1, keepdims=True).astype(jnp.int32)
    parts = []
    for pick in (row, places - row * GSIDE):
        chosen = (lane == pick).astype(F32)
        parts.append(jnp.dot(chosen, table, precision=HIGHEST, preferred_element_type=F32))
    return jnp.concatenate(parts, axis=1)


def decoder_kernel(
    sent,
    pixels,
    spot_rows,
    spot_columns,
    table,
    masked_ref,
    bands_w,
    vectors,
    qkv_w,
    out_w,
    fc1_w,
    fc2_w,
    head_w,
    normed_one,
    grad_qkv,
    mixed,
    grad_middle_low,
    normed_two,
    grad_pre,
    active,
    grad_out_low,
    normed_last,
    grad_predicted,
    grad_sent,
    sums,
    loss,
    seen,
    bias,
    state,
    middle,
    last,
    grad,
    spare,
    qkv,
    pre,
    attend,
    attend_low,
    scores_low,
    scores_grad,
    stacked,
    other,
    grad_mixed,
):
    width = state.shape[1]
    lanes = pl.ds(0, width)

    @pl.when(pl.program_id(0) == 0)
    def _():
        sums[...] = jnp.zeros_like(sums)
        loss[...] = jnp.zeros_like(loss)

    grid = lax.broadcasted_iota(jnp.int32, (GPAD, 1), 0)
    key = lax.broadcasted_iota(jnp.int32, (1, GPAD), 1)
    token = vectors[pl.ds(0, 1), lanes]
    for image in range(BATCH):
        rows = pl.ds(image * GPAD, GPAD)
        chosen = (grid == spot_rows[image]).astype(F32)
        shown = jnp.sum(chosen, axis=1, keepdims=True)
        placed = dot(chosen.astype(BF16), sent[pl.ds(image * VMAX, VMAX)])
        seen[rows] = jnp.where(grid < GRID, shown, 1.0)
        code = turn_code(grid, table[image])
        state[rows] = jnp.where(shown > 0.5, placed, token) + code
        bias[pl.ds(image, 1)] = jnp.where(key < GRID, 0.0, MASK_FILL)

    norm_rows(state, normed_one, vectors, LN1_G)

    def project(part):
        qkv[:, part] = dot(normed_one[...], qkv_w[:, part]).astype(BF16)

    columns_loop(qkv.shape[1], 256, project)
    attention_forward(
        BATCH, GPAD, HD, qkv, bias, attend, attend_low, stacked, mixed
    )

    def output(part):
        middle[:, part] = state[:, part] + dot(mixed[...], out_w[:, part])

    columns_loop(width, 256, output)
    norm_rows(middle, normed_two, vectors, LN2_G)
    feed_forward(normed_two, fc1_w, fc2_w, vectors, middle, pre, active, last)
    norm_rows(last, normed_last, vectors, LNF_G)

    weight = 1.0 / masked_ref[pl.ds(0, 1), pl.ds(0, 1)]

    def predict(part):
        value = dot(normed_last[...], head_w[:, part]) + vectors[pl.ds(LAST_B, 1), part]
        miss = value - dot(pixels[...], bands_w[:, part])
        index = lax.broadcasted_iota(jnp.int32, (1, GROUP), 1) + part.start
        low = index < LOWPIX
        square = miss * miss
        root = jnp.sqrt(square + 1.0)
        unseen = 1.0 - seen[...]
        loss[...] += jnp.sum(jnp.where(low, square, root - 1.0) * unseen).reshape(1, 1)
        slope = jnp.where(low, 2.0 * miss, miss / root) * (unseen * weight)
        rounded = slope.astype(BF16)
        grad_predicted[:, part] = rounded
        sums[pl.ds(LAST_B, 1), part] += jnp.sum(rounded.astype(F32), axis=0, keepdims=True)

    columns_loop(head_w.shape[1], GROUP, predict)

    def head_back(part):
        spare[:, part] = dot_nt(grad_predicted[...], head_w[part])

    columns_loop(width, 256, head_back)

    def last_back(rows, value):
        grad[rows] = value
        grad_out_low[rows] = value.astype(BF16)
        sums[pl.ds(FC2_B, 1), lanes] += jnp.sum(value, axis=0, keepdims=True)

    norm_rows_back(last, spare, vectors, sums, LNF_G, last_back)
    block_backward(
        BATCH,
        GPAD,
        HD,
        (qkv_w, out_w, fc1_w, fc2_w),
        vectors,
        sums,
        (state, middle, grad, spare, pre, qkv),
        (grad_out_low, grad_pre, grad_middle_low, grad_mixed, grad_qkv),
        (attend, attend_low, scores_low, scores_grad, stacked, other),
    )
    unseen = 1.0 - seen[...]
    sums[pl.ds(0, 1), lanes] += jnp.sum(grad[...] * unseen, axis=0, keepdims=True)
    for image in range(BATCH):
        chosen = (spot_columns[pl.ds(image * VMAX, VMAX)] == key).astype(F32).astype(BF16)
        value = dot(chosen, grad[pl.ds(image * GPAD, GPAD)].astype(BF16))
        grad_sent[pl.ds(image * VMAX, VMAX)] = value.astype(BF16)


def block_backward(images, length, heads, weights, vectors, sums, states, lows, scratch):
    qkv_w, out_w, fc1_w, fc2_w = weights
    state, middle, grad, spare, pre, qkv = states
    grad_out_low, grad_pre, grad_middle_low, grad_mixed, grad_qkv = lows
    attend, attend_low, scores_low, scores_grad, stacked, other = scratch
    width = state.shape[1]
    feed_backward(grad_out_low, fc1_w, fc2_w, pre, sums, grad_pre, spare)

    def middle_back(rows, value):
        total = grad[rows] + value
        grad[rows] = total
        grad_middle_low[rows] = total.astype(BF16)

    norm_rows_back(middle, spare, vectors, sums, LN2_G, middle_back)

    def mixed_back(part):
        grad_mixed[:, part] = dot_nt(grad_middle_low[...], out_w[part]).astype(BF16)

    columns_loop(width, 256, mixed_back)
    attention_backward(
        images,
        length,
        heads,
        qkv,
        grad_mixed,
        attend,
        attend_low,
        scores_low,
        scores_grad,
        stacked,
        other,
        grad_qkv,
    )

    def first_back(part):
        spare[:, part] = dot_nt(grad_qkv[...], qkv_w[part])

    columns_loop(width, 256, first_back)

    def state_back(rows, value):
        grad[rows] = grad[rows] + value

    norm_rows_back(state, spare, vectors, sums, LN1_G, state_back)


def decoder(sent, pixels, spots, tables, masked_tile, vectors, weights):
    images = spots.shape[0]
    rows = BATCH * GPAD
    shown = BATCH * VMAX
    stack = GROUP // (DD // HD) * GPAD
    widths = [DD, 3 * DD, DD, DD, DD, FD, FD, DD, DD, padded(HEAD)]
    whole = lambda array: pl.BlockSpec(array.shape, lambda i: (0,) * array.ndim)
    by_rows = lambda length, columns: pl.BlockSpec((length, columns), lambda i: (i, 0))
    bands_w = band_matrix()
    out_shape = [jax.ShapeDtypeStruct((images * GPAD, columns), BF16) for columns in widths]
    out_shape.append(jax.ShapeDtypeStruct((images * VMAX, DD), BF16))
    out_shape.append(jax.ShapeDtypeStruct((VEC_ROWS, VEC_COLS[1]), F32))
    out_shape.append(jax.ShapeDtypeStruct((1, 1), F32))
    operands = [masked_tile, bands_w, vectors, *weights]
    f32 = lambda *shape: pltpu.VMEM(shape, F32)
    b16 = lambda *shape: pltpu.VMEM(shape, BF16)
    return pl.pallas_call(
        decoder_kernel,
        grid=(images // BATCH,),
        out_shape=out_shape,
        in_specs=[
            by_rows(shown, DD),
            by_rows(rows, PIX),
            pl.BlockSpec((BATCH, 1, VMAX), lambda i: (i, 0, 0)),
            by_rows(shown, 1),
            pl.BlockSpec((BATCH, TURNS, DD // 2), lambda i: (i, 0, 0)),
        ]
        + [whole(operand) for operand in operands],
        out_specs=[by_rows(rows, columns) for columns in widths]
        + [by_rows(shown, DD)]
        + [pl.BlockSpec(shape.shape, lambda i: (0, 0)) for shape in out_shape[-2:]],
        scratch_shapes=[
            f32(rows, 1),
            f32(BATCH, GPAD),
            f32(rows, DD),
            f32(rows, DD),
            f32(rows, DD),
            f32(rows, DD),
            f32(rows, DD),
            b16(rows, 3 * DD),
            f32(rows, FD),
            f32(BATCH * DD // GROUP, stack, GPAD),
            b16(stack, GPAD),
            b16(stack, GPAD),
            f32(stack, GPAD),
            b16(stack, GROUP),
            b16(stack, GROUP),
            b16(rows, DD),
        ],
        compiler_params=pltpu.CompilerParams(vmem_limit_bytes=62 * 2**20),
        name="decoder",
    )(sent, pixels, spots.reshape(images, 1, VMAX), spots.reshape(-1, 1), tables, *operands)


def encoder_forward_kernel(
    pixels,
    spot_rows,
    spot_columns,
    table,
    vectors,
    pe_hbm,
    qkv_hbm,
    out_hbm,
    fc1_hbm,
    fc2_hbm,
    emb_hbm,
    sent,
    patches,
    state,
    normed_one,
    qkv,
    mixed,
    middle,
    normed_two,
    pre,
    active,
    last,
    normed_last,
    attend,
    pe_w,
    qkv_w,
    out_w,
    fc1_w,
    fc2_w,
    emb_w,
    bias,
    attend_low,
    stacked,
    sems,
):
    pairs = [
        (pe_hbm, pe_w),
        (qkv_hbm, qkv_w),
        (out_hbm, out_w),
        (fc1_hbm, fc1_w),
        (fc2_hbm, fc2_w),
        (emb_hbm, emb_w),
    ]
    copies = [pltpu.make_async_copy(*pair, sems.at[n]) for n, pair in enumerate(pairs)]
    for copy in copies:
        copy.start()
    images = spot_rows.shape[0]
    key = lax.broadcasted_iota(jnp.int32, (1, GPAD), 1)
    for image in range(images):
        rows = pl.ds(image * VMAX, VMAX)
        place = spot_columns[rows]
        chosen = (place == key).astype(F32).astype(BF16)
        patches[rows] = dot(chosen, pixels[pl.ds(image * GPAD, GPAD)]).astype(BF16)
        code = turn_code(jnp.maximum(place, 0), table[image])
        state[rows] = code + vectors[pl.ds(0, 1), pl.ds(0, DE)]
        bias[pl.ds(image, 1)] = jnp.where(spot_rows[image] < 0, MASK_FILL, 0.0)
    copies[0].wait()

    def embed(part):
        state[:, part] += dot(patches[...], pe_w[:, part])

    columns_loop(DE, 256, embed)
    norm_rows(state, normed_one, vectors, LN1_G)
    copies[1].wait()

    def project(part):
        qkv[:, part] = dot(normed_one[...], qkv_w[:, part]).astype(BF16)

    columns_loop(3 * DE, 256, project)
    attention_forward(images, VMAX, HE, qkv, bias, attend, attend_low, stacked, mixed)
    copies[2].wait()

    def output(part):
        middle[:, part] = state[:, part] + dot(mixed[...], out_w[:, part])

    columns_loop(DE, 256, output)
    norm_rows(middle, normed_two, vectors, LN2_G)
    copies[3].wait()
    copies[4].wait()
    feed_forward(normed_two, fc1_w, fc2_w, vectors, middle, pre, active, last)
    norm_rows(last, normed_last, vectors, LNF_G)
    copies[5].wait()
    value = dot(normed_last[...], emb_w[...]) + vectors[pl.ds(LAST_B, 1), pl.ds(0, DD)]
    sent[...] = value.astype(BF16)


def encoder_forward(pixels, spots, tables, vectors, weights):
    images = spots.shape[0]
    rows = images * VMAX
    stack = GROUP // (DE // HE) * VMAX
    anywhere = pl.BlockSpec(memory_space=pl.ANY)
    vmem = pl.BlockSpec(memory_space=pltpu.VMEM)
    kept = [
        (DD, BF16),
        (PIX, BF16),
        (DE, F32),
        (DE, BF16),
        (3 * DE, BF16),
        (DE, BF16),
        (DE, F32),
        (DE, BF16),
        (FE, F32),
        (FE, BF16),
        (DE, F32),
        (DE, BF16),
    ]
    out_shape = [jax.ShapeDtypeStruct((rows, columns), kind) for columns, kind in kept]
    out_shape.append(jax.ShapeDtypeStruct((images * DE // GROUP, stack, VMAX), F32))
    return pl.pallas_call(
        encoder_forward_kernel,
        out_shape=out_shape,
        in_specs=[vmem] * 5 + [anywhere] * 6,
        out_specs=[vmem] * len(out_shape),
        scratch_shapes=[pltpu.VMEM(weight.shape, BF16) for weight in weights]
        + [
            pltpu.VMEM((images, VMAX), F32),
            pltpu.VMEM((stack, VMAX), BF16),
            pltpu.VMEM((stack, GROUP), BF16),
            pltpu.SemaphoreType.DMA((6,)),
        ],
        compiler_params=pltpu.CompilerParams(vmem_limit_bytes=60 * 2**20),
        name="encoder_forward",
    )(pixels, spots.reshape(images, 1, VMAX), spots.reshape(-1, 1), tables, vectors, *weights)


def encoder_backward_kernel(
    grad_sent,
    vectors,
    state,
    qkv,
    middle,
    pre,
    last,
    attend,
    qkv_hbm,
    out_hbm,
    fc1_hbm,
    fc2_hbm,
    emb_hbm,
    grad_state_low,
    grad_qkv,
    grad_middle_low,
    grad_pre,
    grad_out_low,
    sums,
    qkv_w,
    out_w,
    fc1_w,
    fc2_w,
    emb_w,
    grad,
    spare,
    grad_mixed,
    attend_low,
    scores_low,
    scores_grad,
    stacked,
    other,
    sems,
):
    pairs = [
        (emb_hbm, emb_w),
        (fc2_hbm, fc2_w),
        (fc1_hbm, fc1_w),
        (out_hbm, out_w),
        (qkv_hbm, qkv_w),
    ]
    copies = [pltpu.make_async_copy(*pair, sems.at[n]) for n, pair in enumerate(pairs)]
    for copy in copies:
        copy.start()
    lanes = pl.ds(0, DE)
    sums[...] = jnp.zeros_like(sums)
    summed = jnp.sum(grad_sent[...].astype(F32), axis=0, keepdims=True)
    sums[pl.ds(LAST_B, 1), pl.ds(0, DD)] = summed
    copies[0].wait()

    def sent_back(part):
        spare[:, part] = dot_nt(grad_sent[...], emb_w[part])

    columns_loop(DE, 256, sent_back)

    def last_back(rows, value):
        grad[rows] = value
        grad_out_low[rows] = value.astype(BF16)
        sums[pl.ds(FC2_B, 1), lanes] += jnp.sum(value, axis=0, keepdims=True)

    norm_rows_back(last, spare, vectors, sums, LNF_G, last_back)
    for copy in copies[1:]:
        copy.wait()
    block_backward(
        state.shape[0] // VMAX,
        VMAX,
        HE,
        (qkv_w, out_w, fc1_w, fc2_w),
        vectors,
        sums,
        (state, middle, grad, spare, pre, qkv),
        (grad_out_low, grad_pre, grad_middle_low, grad_mixed, grad_qkv),
        (attend, attend_low, scores_low, scores_grad, stacked, other),
    )

    def first(rows):
        value = grad[rows]
        sums[pl.ds(0, 1), lanes] += jnp.sum(value, axis=0, keepdims=True)
        grad_state_low[rows] = value.astype(BF16)

    blocks(grad.shape[0], row_step(grad.shape[0]), first)


def encoder_backward(grad_sent, vectors, kept, weights):
    state, qkv, middle, pre, last, attend = kept
    rows = state.shape[0]
    stack = attend.shape[1]
    anywhere = pl.BlockSpec(memory_space=pl.ANY)
    vmem = pl.BlockSpec(memory_space=pltpu.VMEM)
    out_shape = [
        jax.ShapeDtypeStruct((rows, columns), BF16) for columns in (DE, 3 * DE, DE, FE, DE)
    ]
    out_shape.append(jax.ShapeDtypeStruct((VEC_ROWS, VEC_COLS[0]), F32))
    f32 = lambda *shape: pltpu.VMEM(shape, F32)
    b16 = lambda *shape: pltpu.VMEM(shape, BF16)
    return pl.pallas_call(
        encoder_backward_kernel,
        out_shape=out_shape,
        in_specs=[vmem] * 8 + [anywhere] * 5,
        out_specs=[vmem] * len(out_shape),
        scratch_shapes=[pltpu.VMEM(weight.shape, BF16) for weight in weights]
        + [
            f32(rows, DE),
            f32(rows, DE),
            b16(rows, DE),
            b16(stack, VMAX),
            b16(stack, VMAX),
            f32(stack, VMAX),
            b16(stack, GROUP),
            b16(stack, GROUP),
            pltpu.SemaphoreType.DMA((5,)),
        ],
        compiler_params=pltpu.CompilerParams(vmem_limit_bytes=60 * 2**20),
        name="encoder_backward",
    )(grad_sent, vectors, state, qkv, middle, pre, last, attend, *weights)


def band_matrix():
    ids = jnp.arange(PIX, dtype=jnp.int32)
    coarse = (ids // (3 * PSIDE) // 2 * (PSIDE // 2) + ids // 3 % PSIDE // 2) * 3 + ids % 3
    low = jnp.where(coarse[:, None] == jnp.arange(LOWPIX, dtype=jnp.int32)[None], 0.25, 0.0)
    same = jnp.where(coarse[:, None] == coarse[None], 0.25, 0.0)
    high = jnp.where(ids[:, None] == ids[None], 1.0, 0.0) - same
    rest = jnp.zeros((PIX, padded(HEAD) - HEAD), F32)
    return jnp.concatenate([low, high, rest], axis=1).astype(BF16)


def turn_table(scales, width):
    quarter = width // 4
    frequency = jnp.exp(jnp.arange(quarter, dtype=F32) * (-math.log(10000.0) / quarter))
    angle = (jnp.arange(TURNS, dtype=F32)[None] * scales[:, None])[..., None] * frequency
    return jnp.concatenate([jnp.sin(angle), jnp.cos(angle)], axis=-1)


def forward_backward(parts, pixels, index_rows, counts, scales, masked_tile):
    pe_w, qkv_w, fc1_w, emb_w, out_w, fc2_w = parts[:6]
    dec_weights = parts[6:11]
    enc_vectors, dec_vectors = parts[11:]
    images = counts.shape[0]
    valid = jnp.arange(VMAX, dtype=jnp.int32)[None, :] < counts[:, None]
    spots = jnp.where(valid, index_rows, -1)
    pixels = jnp.pad(pixels.reshape(images, GRID, PIX), ((0, 0), (0, GPAD - GRID), (0, 0)))
    pixels = pixels.reshape(images * GPAD, PIX)
    (
        sent,
        patches,
        state,
        normed_one,
        qkv,
        mixed,
        middle,
        normed_two,
        pre,
        active,
        last,
        normed_last,
        attend,
    ) = encoder_forward(
        pixels,
        spots,
        turn_table(scales, DE),
        enc_vectors,
        [pe_w, qkv_w, out_w, fc1_w, fc2_w, emb_w],
    )
    *dec_factors, grad_sent, dec_sums, loss = decoder(
        sent, pixels, spots, turn_table(scales, DD), masked_tile, dec_vectors, dec_weights
    )
    grad_state, grad_qkv, grad_middle, grad_pre, grad_out, enc_sums = encoder_backward(
        grad_sent,
        enc_vectors,
        [state, qkv, middle, pre, last, attend],
        [qkv_w, out_w, fc1_w, fc2_w, emb_w],
    )
    factors = [patches, grad_state, normed_one, grad_qkv, normed_two, grad_pre]
    factors += [normed_last, grad_sent, mixed, grad_middle, active, grad_out]
    return factors + dec_factors, enc_sums, dec_sums, loss[0, 0]


def clip_scale(squares):
    return jnp.minimum(1.0, CLIP / jnp.sqrt(squares))


def body(
    params, first_moment, second_moment, average, pixels, visible_index, visible_count, gsd_id
):
    chips = lax.axis_size("dp")
    rows = params.shape[1] // LANES
    special = chips == math.prod(DP_GRID) and rows % 4 == 0
    masked = jnp.sum(GRID - visible_count).astype(F32)
    if special:
        shards = [a.reshape(-1, 4, LANES) for a in (params, first_moment, second_moment, average)]
        copies, masked_tile = gather_rows(shards[0], jnp.full((8, LANES), masked))
    else:
        copies = lax.all_gather(params.astype(BF16).reshape(-1, LANES), "dp", axis=0, tiled=True)
        copies = lax.all_gather(copies, "grp", axis=0, tiled=True)
        masked_tile = jnp.full((8, LANES), lax.psum(masked, "dp"))
    parts = weight_matrices(copies.reshape(-1, LANES))

    half = visible_count.shape[0] // 2
    core = lax.axis_index("grp")

    def mine(array, count):
        return lax.dynamic_slice_in_dim(array, core * count, count, 0)

    scales = 0.5 + 0.25 * mine(gsd_id, half).astype(F32)
    factors, enc_sums, dec_sums, loss_local = forward_backward(
        parts,
        mine(pixels, half * GRID),
        mine(visible_index, half),
        mine(visible_count, half),
        scales,
        masked_tile,
    )
    gradient = flat_gradient(chips * rows, factors, enc_sums, dec_sums)
    if special:
        owned, sums = scatter_sums(
            gradient.reshape(chips, rows // 4, 4, LANES), jnp.full((8, LANES), loss_local)
        )
        squares = jnp.sum(sums[:4])
        loss_sum = sums[4, 0]
        outs = update(clip_scale(squares), [owned] + shards)
        outs = [out.reshape(params.shape) for out in outs]
    else:
        owned = lax.psum_scatter(gradient, "dp", scatter_dimension=0, tiled=True)
        owned = owned.reshape(params.shape)
        squares, loss_sum = lax.psum((jnp.sum(owned * owned), loss_local), ("grp", "dp"))
        outs = update_values(owned, clip_scale(squares), params, first_moment, second_moment, average)
    return (*outs, loss_sum, masked_tile[0, 0], jnp.sqrt(squares))


def solution(mesh):
    return jax.shard_map(
        body,
        mesh=mesh,
        in_specs=(P("grp", "dp"),) * 4 + (P("dp", None), P("dp", None), P("dp"), P("dp")),
        out_specs=(P("grp", "dp"),) * 4 + (P(), P(), P()),
        check_vma=False,
    )
```

```python
import functools
import math

import jax
import jax.numpy as jnp
from jax import lax
from jax.experimental import pallas as pl
from jax.experimental.pallas import tpu as pltpu
from jax.sharding import PartitionSpec as P

DE = 1024
HE = 16
FE = 4096
DD = 512
HD = 16
FD = 2048
PSIDE = 16
GSIDE = 14
VMAX = 64
STEP = 10
PIX = 768
LOWPIX = 192
GRID = 196
GPAD = 208
NENC = 8662528
NDEC = 3644352
LANES = 128
UNIT = 4 * LANES

HIGHEST = lax.Precision.HIGHEST
CLIP = 0.05
RATE = 0.01
BETA_ONE = 0.5
BETA_TWO = 0.5
ADAM_EPS = 1e-08
DECAY_WEIGHT = 0.05
AVERAGE_KEEP = 0.9
NORM_EPS = 1e-06
MASK_FILL = -1000000000.0
F32 = jnp.float32
BF16 = jnp.bfloat16
MESH = pl.DeviceIdType.MESH

WIDTH = 512
SUB = 64
PIECE = 8192
VEC_ROWS = 16
VEC_COLS = (FE, FD)
HEAD = LOWPIX + PIX

ENC_LAYOUT = [
    (PIX, DE),
    (DE,),
    (DE,),
    (DE,),
    (DE, 3 * DE),
    (DE,),
    (DE,),
    (DE, FE),
    (FE,),
    (DE,),
    (DE,),
    (DE,),
    (DE, DD),
    (DD,),
]
DEC_LAYOUT = [
    (DD,),
    (DD,),
    (DD,),
    (DD, 3 * DD),
    (DD, DD),
    (DD,),
    (DD,),
    (DD, FD),
    (FD,),
    (FD, DD),
    (DD,),
    (DD,),
    (DD,),
    (DD, HEAD),
    (HEAD,),
]
LENT = [(DE, DE), (FE, DE)]


DP_GRID = (4, 2, 2)
YZX, XZY, ZXY = ("y", "z", "x"), ("x", "z", "y"), ("z", "x", "y")
SPLIT = 2
ORDERS = (YZX,) * SPLIT + (XZY,) * SPLIT + (ZXY,) * SPLIT
PARTS = len(ORDERS)
OWN_FIRST = tuple(range(2 * SPLIT, 3 * SPLIT)) + tuple(range(2 * SPLIT))
SHARES = (0.41, 0.26, 0.33)
WAYS = ("x", "y", "up", "down")
CHUNK = 16
OPPOSITE = {"x": "x", "y": "y", "up": "down", "down": "up"}


def part_ranges(units):
    ends = [0]
    for share in SHARES:
        for _ in range(SPLIT):
            ends.append(ends[-1] + share / SPLIT)
    ends = [round(end * units) for end in ends[:-1]] + [units]
    return [(start, end - start) for start, end in zip(ends, ends[1:])]


def relatives():
    places = [(dz, dy, dx) for dz in range(-3, 4) for dy in (0, 1) for dx in (0, 1)]
    places.remove((0, 0, 0))
    return sorted(places, key=lambda r: abs(r[0]) + r[1] + r[2])


def last_axis(order, place):
    differs = {"z": place[0] != 0, "y": place[1] != 0, "x": place[2] != 0}
    return [axis for axis in order if differs[axis]][-1]


def onward(order, place):
    if place == (0, 0, 0):
        return ["up", "down", "x", "y"]
    axis = last_axis(order, place)
    ways = []
    if axis == "z":
        ways.append("up" if place[0] < 0 else "down")
    for later in order[order.index(axis) + 1 :]:
        ways += ["up", "down"] if later == "z" else [later]
    return ways


def when(condition, action):
    if condition is None:
        action()
    else:
        pl.when(condition)(action)


def both(left, right):
    if left is None:
        return right
    return left if right is None else left & right


class Spot:
    def __init__(self):
        self.grp = lax.axis_index("grp")
        self.dp = lax.axis_index("dp")
        self.x = self.dp % 2
        self.y = (self.dp // 2) % 2
        self.z = self.dp // 4
        self.neighbour = {
            "x": (self.grp, self.index(self.z, self.y, 1 - self.x)),
            "y": (self.grp, self.index(self.z, 1 - self.y, self.x)),
            "up": (self.grp, self.index(jnp.minimum(self.z + 1, 3), self.y, self.x)),
            "down": (self.grp, self.index(jnp.maximum(self.z - 1, 0), self.y, self.x)),
            "core": (1 - self.grp, self.dp),
        }
        self.exists = {"x": None, "y": None, "up": self.z < 3, "down": self.z > 0, "core": None}

    def index(self, z, y, x):
        return z * 4 + y * 2 + x

    def at(self, place):
        z = self.z + place[0]
        y = 1 - self.y if place[1] else self.y
        x = 1 - self.x if place[2] else self.x
        inside = None if place[0] == 0 else (z >= 0) & (z <= 3)
        return z, self.index(z, y, x), inside

    def greet(self):
        barrier = pltpu.get_barrier_semaphore()
        me = self.grp * 16 + self.dp

        def signal(step, carry):
            other = (me + step) % 32
            pl.semaphore_signal(
                barrier, inc=1, device_id=(other // 16, other % 16), device_id_type=MESH
            )
            return carry

        lax.fori_loop(1, 32, signal, 0)

    def await_all(self):
        pl.semaphore_wait(pltpu.get_barrier_semaphore(), 31)


def tell_all(spot, tiles, send_sem, recv_sem):
    me = spot.grp * 16 + spot.dp

    def copy(number, other):
        return pltpu.make_async_remote_copy(
            src_ref=tiles.at[number],
            dst_ref=tiles.at[number],
            send_sem=send_sem.at[other],
            recv_sem=recv_sem.at[number],
            device_id=(other // 16, other % 16),
            device_id_type=MESH,
        )

    def start(step, carry):
        copy(me, (me + step) % 32).start()
        return carry

    def finish(step, carry):
        other = (me + step) % 32
        copy(other, other).wait_recv()
        copy(me, other).wait_send()
        return carry

    return (
        lambda: lax.fori_loop(1, 32, start, 0),
        lambda: lax.fori_loop(1, 32, finish, 0),
    )


def gather_kernel(
    master_ref,
    masked_ref,
    out_ref,
    masked_out,
    master,
    own_ref,
    tiles,
    local_sem,
    send_sem,
    recv_sem,
    core_send,
    core_recv,
    tile_send,
    tile_recv,
):
    spot = Spot()
    read = pltpu.make_async_copy(master_ref, master, local_sem)
    read.start()
    tiles[spot.grp * 16 + spot.dp] = masked_ref[...]
    spot.greet()
    tell, told = tell_all(spot, tiles, tile_send, tile_recv)
    ranges = part_ranges(own_ref.shape[0])
    read.wait()

    def round_off(start, length):
        block = pl.ds(start, length)
        own_ref[block] = master[block].astype(BF16)

    def step(index, carry):
        round_off(index * CHUNK, CHUNK)
        return carry

    units = own_ref.shape[0]
    lax.fori_loop(0, units // CHUNK, step, 0)
    if units % CHUNK:
        round_off(units - units % CHUNK, units % CHUNK)
    spot.await_all()

    def copy(part, source, way, from_own):
        target = out_ref.at[spot.grp, source, pl.ds(*ranges[part])]
        origin = own_ref.at[pl.ds(*ranges[part])] if from_own else target
        if way == "core":
            sems = (core_send.at[part, source], core_recv.at[part, source])
        else:
            sems = (send_sem.at[part, source, WAYS.index(way)], recv_sem.at[part, source])
        return pltpu.make_async_remote_copy(
            src_ref=origin,
            dst_ref=target,
            send_sem=sems[0],
            recv_sem=sems[1],
            device_id=spot.neighbour[way],
            device_id_type=MESH,
        )

    sent = []
    for part in OWN_FIRST:
        for way in onward(ORDERS[part], (0, 0, 0)):
            when(
                spot.exists[way],
                lambda part=part, way=way: copy(part, spot.dp, way, True).start(),
            )
            sent.append((part, spot.dp, way, spot.exists[way], True))
    local = pltpu.make_async_copy(own_ref, out_ref.at[spot.grp, spot.dp], local_sem)
    local.start()
    tell()
    for part in range(PARTS):
        copy(part, spot.dp, "core", True).start()
        sent.append((part, spot.dp, "core", None, True))
    for place in relatives():
        _, source, inside = spot.at(place)
        for part in range(PARTS):
            ways = onward(ORDERS[part], place)

            def pass_on(part=part, source=source, ways=ways):
                copy(part, source, "x", False).wait_recv()
                for way in ways:
                    when(
                        spot.exists[way],
                        lambda way=way: copy(part, source, way, False).start(),
                    )
                copy(part, source, "core", False).start()

            when(inside, pass_on)
            for way in ways + ["core"]:
                sent.append((part, source, way, both(inside, spot.exists[way]), False))
    for part, source, way, condition, from_own in sent:
        when(condition, lambda: copy(part, source, way, from_own).wait_send())

    def await_core(source, carry):
        for part in range(PARTS):
            landed = out_ref.at[1 - spot.grp, source, pl.ds(*ranges[part])]
            pltpu.make_async_remote_copy(
                src_ref=landed,
                dst_ref=landed,
                send_sem=core_send.at[part, source],
                recv_sem=core_recv.at[part, source],
                device_id=spot.neighbour["core"],
                device_id_type=MESH,
            ).wait_recv()
        return carry

    lax.fori_loop(0, 16, await_core, 0)
    told()
    masked_out[...] = jnp.sum(tiles[pl.ds(0, 16)], axis=0)
    local.wait()


def gather_rows(master, masked):
    units = master.shape[0]
    dma = pltpu.SemaphoreType.DMA
    anywhere = pl.BlockSpec(memory_space=pl.ANY)
    vmem = pl.BlockSpec(memory_space=pltpu.VMEM)
    return pl.pallas_call(
        gather_kernel,
        out_shape=(
            jax.ShapeDtypeStruct((2, 16, units, 4, LANES), BF16),
            jax.ShapeDtypeStruct((8, LANES), F32),
        ),
        in_specs=[anywhere, vmem],
        out_specs=(anywhere, vmem),
        scratch_shapes=[
            pltpu.VMEM((units, 4, LANES), F32),
            pltpu.VMEM((units, 4, LANES), BF16),
            pltpu.VMEM((32, 8, LANES), F32),
            dma,
            dma((PARTS, 16, 4)),
            dma((PARTS, 16)),
            dma((PARTS, 16)),
            dma((PARTS, 16)),
            dma((32,)),
            dma((32,)),
        ],
        compiler_params=pltpu.CompilerParams(collective_id=0, has_side_effects=True),
        name="gather_rows",
    )(master, masked)


def slot_tables():
    tables = []
    for order in ORDERS:
        table = {}
        for way in WAYS:
            keys = []
            along = False
            for place in [(0, 0, 0)] + relatives():
                if way in onward(order, place):
                    if place[1:] not in keys:
                        keys.append(place[1:])
                    along = along or place[0] != 0
            table[way] = (keys, 3 if way in ("up", "down") else (4 if along else 1))
        tables.append(table)
    return tables


SLOTS = slot_tables()
STAGES = 4


def scatter_kernel(grad_ref, loss_ref, out_ref, sums_ref, *refs):
    ranges = part_ranges(grad_ref.shape[1])
    landing = {}
    for part in range(PARTS):
        for number, way in enumerate(WAYS):
            landing[part, way] = refs[part * 4 + number]
    stage, total, tiles, send_sem, recv_sem, stage_sem, out_sem, tile_send, tile_recv = refs[4 * PARTS :]
    spot = Spot()
    spot.greet()
    spot.await_all()

    def slot(part, way, place, z):
        keys, depth = SLOTS[part][way]
        base = keys.index(place[1:]) * depth
        if way == "up":
            return base + z
        if way == "down":
            return base + z - 1
        return base + (z if depth == 4 else 0)

    def parent(part, place):
        axis = last_axis(ORDERS[part], place)
        if axis == "z":
            return "up" if place[0] > 0 else "down"
        return axis

    def seen_from_parent(part, place):
        way = parent(part, place)
        dz, dy, dx = place
        if way == "x":
            return (dz, dy, 0)
        if way == "y":
            return (dz, 0, dx)
        return (dz - 1 if way == "up" else dz + 1, dy, dx)

    def send(part, place, origin):
        z, owner, _ = spot.at(place)
        way = parent(part, place)
        back = OPPOSITE[way]
        return pltpu.make_async_remote_copy(
            src_ref=origin,
            dst_ref=landing[part, back].at[slot(part, back, seen_from_parent(part, place), z)],
            send_sem=send_sem.at[part, owner],
            recv_sem=recv_sem.at[part, owner, WAYS.index(back)],
            device_id=spot.neighbour[way],
            device_id_type=MESH,
        )

    def own(part, owner):
        return grad_ref.at[owner, pl.ds(*ranges[part])]

    nodes = [(place, part) for place in relatives()[::-1] for part in range(PARTS)]
    nodes += [((0, 0, 0), part) for part in range(PARTS)]
    sent = []
    inner = []
    for place, part in nodes:
        z, owner, inside = spot.at(place)
        ways = onward(ORDERS[part], place)
        if place != (0, 0, 0):
            sent.append((part, place, owner, inside))
        inner.append((part, place, ways, z, owner, inside))
    staged_nodes = [node for node in inner if node[2]]

    def staged(number):
        part, _, _, _, owner, _ = staged_nodes[number]
        return pltpu.make_async_copy(
            own(part, owner),
            stage.at[number % STAGES, pl.ds(0, ranges[part][1])],
            stage_sem.at[number % STAGES],
        )

    for number in range(STAGES - 1):
        when(staged_nodes[number][5], lambda: staged(number).start())
    number = -1
    for part, place, ways, z, owner, inside in inner:
        if not ways:
            when(inside, lambda: send(part, place, own(part, owner)).start())
            continue
        number += 1
        ahead = number + STAGES - 1
        if ahead < len(staged_nodes):
            when(staged_nodes[ahead][5], lambda: staged(ahead).start())
        length = ranges[part][1]
        root = place == (0, 0, 0)

        def combine(arriving, number=number, part=part, place=place, z=z, owner=owner):
            slots = []
            for way in arriving:
                spot_of = landing[part, way].at[slot(part, way, place, z)]
                pltpu.make_async_remote_copy(
                    src_ref=spot_of,
                    dst_ref=spot_of,
                    send_sem=send_sem.at[part, owner],
                    recv_sem=recv_sem.at[part, owner, WAYS.index(way)],
                    device_id=spot.neighbour[way],
                    device_id_type=MESH,
                ).wait_recv()
                slots.append(spot_of)
            staged(number).wait()
            if slots:
                target = total.at[pl.ds(*ranges[part])] if root else slots[0]

                def add(start, count):
                    value = stage[number % STAGES, pl.ds(start, count)]
                    for item in slots:
                        value = value + item[pl.ds(start, count)]
                    target[pl.ds(start, count)] = value

                def step(index, carry):
                    add(index * CHUNK, CHUNK)
                    return carry

                lax.fori_loop(0, length // CHUNK, step, 0)
                if length % CHUNK:
                    add(length - length % CHUNK, length % CHUNK)
            if not root:
                send(part, place, slots[0] if slots else own(part, owner)).start()

        def choose(ways=ways, combine=combine):
            flat = [way for way in ways if way in ("x", "y")]
            along = [way for way in ways if way in ("up", "down")]
            if not along:
                combine(flat)
            elif len(along) == 1:
                there = spot.exists[along[0]]
                pl.when(there)(lambda: combine(flat + along))
                pl.when(jnp.logical_not(there))(lambda: combine(flat))
            else:
                up, down = spot.exists["up"], spot.exists["down"]
                pl.when(up & down)(lambda: combine(flat + ["up", "down"]))
                pl.when(jnp.logical_not(down))(lambda: combine(flat + ["up"]))
                pl.when(jnp.logical_not(up))(lambda: combine(flat + ["down"]))

        when(inside, choose)
    out = pltpu.make_async_copy(total, out_ref, out_sem)
    out.start()
    units = total.shape[0]

    def square(start, count, running):
        value = total[pl.ds(start, count)]
        return running + jnp.sum(value * value, axis=0)

    squares = lax.fori_loop(
        0,
        units // CHUNK,
        lambda index, running: square(index * CHUNK, CHUNK, running),
        jnp.zeros((4, LANES), F32),
    )
    if units % CHUNK:
        squares = square(units - units % CHUNK, units % CHUNK, squares)
    me = spot.grp * 16 + spot.dp
    tiles[me, pl.ds(0, 4)] = squares
    tiles[me, pl.ds(4, 4)] = loss_ref[pl.ds(4, 4)]
    tell, told = tell_all(spot, tiles, tile_send, tile_recv)
    tell()
    for part, place, owner, inside in sent:
        when(inside, lambda: send(part, place, own(part, owner)).wait_send())
    told()
    sums_ref[...] = jnp.sum(tiles[...], axis=0)
    out.wait()


def scatter_sums(grads, loss):
    units = grads.shape[1]
    ranges = part_ranges(units)
    scratch = []
    for part in range(PARTS):
        for way in WAYS:
            keys, depth = SLOTS[part][way]
            scratch.append(pltpu.VMEM((len(keys) * depth, ranges[part][1], 4, LANES), F32))
    largest = max(length for _, length in ranges)
    dma = pltpu.SemaphoreType.DMA
    scratch += [
        pltpu.VMEM((STAGES, largest, 4, LANES), F32),
        pltpu.VMEM((units, 4, LANES), F32),
        pltpu.VMEM((32, 8, LANES), F32),
        dma((PARTS, 16)),
        dma((PARTS, 16, 4)),
        dma((STAGES,)),
        dma,
        dma((32,)),
        dma((32,)),
    ]
    anywhere = pl.BlockSpec(memory_space=pl.ANY)
    vmem = pl.BlockSpec(memory_space=pltpu.VMEM)
    return pl.pallas_call(
        scatter_kernel,
        out_shape=(
            jax.ShapeDtypeStruct((units, 4, LANES), F32),
            jax.ShapeDtypeStruct((8, LANES), F32),
        ),
        in_specs=[anywhere, vmem],
        out_specs=(anywhere, vmem),
        scratch_shapes=scratch,
        compiler_params=pltpu.CompilerParams(
            collective_id=1, has_side_effects=True, vmem_limit_bytes=63 * 2**20
        ),
        name="scatter_sums",
    )(grads, loss)


def update_values(owned, scale, params, first_moment, second_moment, average):
    clipped = owned * scale
    new_first = BETA_ONE * first_moment + (1.0 - BETA_ONE) * clipped
    new_second = BETA_TWO * second_moment + (1.0 - BETA_TWO) * clipped * clipped
    root = jnp.sqrt(new_second * (1.0 / (1.0 - BETA_TWO**STEP)))
    direction = new_first * (1.0 / (1.0 - BETA_ONE**STEP)) / (root + ADAM_EPS)
    new_params = params - RATE * (direction + DECAY_WEIGHT * params)
    new_average = AVERAGE_KEEP * average + (1.0 - AVERAGE_KEEP) * new_params
    return new_params, new_first, new_second, new_average


def update_kernel(scale_ref, *refs):
    scale = scale_ref[0]
    step = 31

    def one(index, carry):
        block = pl.ds(index * step, step)
        owned, params, first, second, average = [ref[block] for ref in refs[:5]]
        values = update_values(owned, scale, params, first, second, average)
        for out, value in zip(refs[5:], values):
            out[block] = value
        return carry

    lax.fori_loop(0, refs[0].shape[0] // step, one, 0)


def update(scale, arrays):
    units = arrays[0].shape[0]
    depth = 155
    spec = pl.BlockSpec((depth, 4, LANES), lambda i: (i, 0, 0))
    return pl.pallas_call(
        update_kernel,
        grid=(units // depth,),
        out_shape=[jax.ShapeDtypeStruct((units, 4, LANES), F32)] * 4,
        in_specs=[pl.BlockSpec(memory_space=pltpu.SMEM)] + [spec] * 5,
        out_specs=[spec] * 4,
        name="update",
    )(scale.reshape(1), *arrays)


SLOTS_IN = 5


def sections(layout, base):
    matrices, vectors = [], []
    offset = base
    for shape in layout:
        (matrices if len(shape) == 2 else vectors).append((offset, shape))
        offset += math.prod(shape)
    return matrices, vectors


def matrix_plan(rows):
    enc_matrices, enc_vectors = sections(ENC_LAYOUT, 0)
    dec_matrices, dec_vectors = sections(DEC_LAYOUT, rows * LANES)
    lent = rows * LANES + NDEC
    matrices = enc_matrices + sections(LENT, lent)[0] + dec_matrices
    return matrices, enc_vectors, dec_vectors


def padded(columns):
    return -(-columns // LANES) * LANES


def block_depth(shape):
    if shape[1] % LANES:
        return shape[0]
    depth = shape[0]
    while depth * shape[1] > PIECE * LANES:
        depth //= 2
    return depth


def matrix_kernel(rows, flat_ref, *refs):
    matrices, enc_vectors, dec_vectors = matrix_plan(rows)
    count = len(matrices)
    out_refs = refs[:count]
    vector_refs = refs[count : count + 2]
    blocks = refs[count + 2 : 2 * count + 2]
    flat_in, wide, pairs, vector_in, in_sem, out_sem, vector_sem = refs[2 * count + 2 :]
    lane = lax.broadcasted_iota(jnp.int32, (1, LANES), 1)

    chunks = []
    for number, (offset, shape) in enumerate(matrices):
        depth = block_depth(shape)
        for start in range(0, shape[0], depth):
            place = offset + start * shape[1]
            chunks.append((number, start, depth, place // LANES, place % LANES))

    def load(index):
        number, _, depth, first, shift = chunks[index]
        length = depth * matrices[number][1][1] // LANES
        begin = first // 16 * 16
        end = -(-(first + length + (1 if shift else 0)) // 16) * 16
        copy = pltpu.make_async_copy(
            flat_ref.at[pl.ds(begin, end - begin)],
            flat_in.at[index % SLOTS_IN, pl.ds(0, end - begin)],
            in_sem.at[index % SLOTS_IN],
        )
        return copy, first - begin, end - begin

    def store(index):
        number, start, depth, _, _ = chunks[index]
        slot = start // depth % 2
        return pltpu.make_async_copy(
            blocks[number].at[slot], out_refs[number].at[pl.ds(start, depth)], out_sem.at[number, slot]
        )

    def widen(index, length):
        step = 256

        def one(start, size):
            wide[pl.ds(start, size)] = flat_in[index % SLOTS_IN, pl.ds(start, size)].astype(F32)

        def loop(i, carry):
            one(pl.multiple_of(i * step, step), step)
            return carry

        lax.fori_loop(0, length // step, loop, 0)
        if length % step:
            one(length - length % step, length % step)

    def turned(first, second):
        return pltpu.roll(jnp.where(lane < LANES // 2, second, first), LANES // 2, 1)

    def arrange(index, phase):
        number, start, depth, _, shift = chunks[index]
        columns = matrices[number][1][1]
        block = blocks[number].at[start // depth % 2]
        tiles = columns // LANES

        def plain(i, carry):
            row = pl.multiple_of(i * SUB, SUB)
            packed = wide[pl.ds(phase + row * tiles, SUB * tiles)].reshape(SUB, tiles, LANES)
            swapped = jnp.swapaxes(packed, 0, 1)
            for tile in range(tiles):
                value = swapped[tile]
                if shift:
                    after = wide[pl.ds(phase + row * tiles + tile + 1, SUB, stride=tiles)]
                    value = turned(value, after)
                block[pl.ds(row, SUB), pl.ds(tile * LANES, LANES)] = value.astype(BF16)
            return carry

        def paired(i, carry):
            stride = 2 * columns // LANES
            half = SUB // 2
            row = pl.multiple_of(i * half, half)
            for tile in range(tiles + 1):
                even = wide[pl.ds(phase + row * stride + tile, half, stride=stride)]
                odd = wide[pl.ds(phase + row * stride + tiles + tile, half, stride=stride)]
                if tile < tiles:
                    after = wide[pl.ds(phase + row * stride + tiles + tile + 1, half, stride=stride)]
                    odd = turned(odd, after)
                else:
                    even = jnp.where(lane < LANES // 2, even, 0.0)
                    odd = jnp.where(lane < LANES // 2, pltpu.roll(odd, LANES // 2, 1), 0.0)
                lanes = pl.ds(tile * LANES, LANES)
                pairs[tile, pl.ds(0, half, stride=2)] = even
                pairs[tile, pl.ds(1, half, stride=2)] = odd
                block[pl.ds(pl.multiple_of(i * SUB, SUB), SUB), lanes] = pairs[tile].astype(BF16)
            return carry

        lax.fori_loop(0, depth // SUB, paired if columns % LANES else plain, 0)

    windows = []
    wanted = [(0, n, v) for n, v in enumerate(enc_vectors)]
    wanted += [(1, n, v) for n, v in enumerate(dec_vectors)]
    for _, _, (offset, shape) in wanted:
        first = offset // LANES // 16 * 16
        end = -(-(offset // LANES + -(-shape[0] // LANES)) // 16) * 16
        if windows and first <= windows[-1][1]:
            windows[-1][1] = max(windows[-1][1], end)
        else:
            windows.append([first, end])
    bases = [sum(e - f for f, e in windows[:n]) for n in range(len(windows))]

    def vector_copy(n):
        first, end = windows[n]
        return pltpu.make_async_copy(
            flat_ref.at[pl.ds(first, end - first)],
            vector_in.at[pl.ds(bases[n], end - first)],
            vector_sem.at[n],
        )

    for index in range(SLOTS_IN - 1):
        load(index)[0].start()
    for n in range(len(windows)):
        vector_copy(n).start()
    for index, (number, start, depth, _, _) in enumerate(chunks):
        copy, phase, length = load(index)
        copy.wait()
        if index + SLOTS_IN - 1 < len(chunks):
            load(index + SLOTS_IN - 1)[0].start()
        widen(index, length)
        if start // depth >= 2:
            store(index - 2).wait()
        arrange(index, phase)
        store(index).start()
    for n in range(len(windows)):
        vector_copy(n).wait()
    total = bases[-1] + windows[-1][1] - windows[-1][0]
    wide[pl.ds(0, total)] = vector_in[...].astype(F32)
    for group, n, (offset, shape) in wanted:
        first = offset // LANES
        window = [k for k, (f, e) in enumerate(windows) if f <= first < e][0]
        base = bases[window] + first - windows[window][0]
        for tile in range(-(-shape[0] // LANES)):
            value = wide[pl.ds(base + tile, 1)]
            if shape[0] - tile * LANES < LANES:
                value = jnp.where(lane < shape[0] - tile * LANES, value, 0.0)
            vector_refs[group][pl.ds(n, 1), pl.ds(tile * LANES, LANES)] = value
    for index, (number, start, depth, _, _) in enumerate(chunks):
        if start + 2 * depth >= matrices[number][1][0]:
            store(index).wait()


def weight_matrices(flat):
    rows = flat.shape[0] // 2
    matrices, enc_vectors, dec_vectors = matrix_plan(rows)
    shapes = [(shape[0], padded(shape[1])) for _, shape in matrices]
    buffers = []
    for (_, shape), (_, columns) in zip(matrices, shapes):
        depth = block_depth(shape)
        buffers.append(pltpu.VMEM((min(2, shape[0] // depth), depth, columns), BF16))
    dma = pltpu.SemaphoreType.DMA
    windows = 0
    last = -1
    total = 0
    for offset, shape in enc_vectors + dec_vectors:
        first = offset // LANES // 16 * 16
        end = -(-(offset // LANES + -(-shape[0] // LANES)) // 16) * 16
        if first <= last:
            total += max(0, end - last)
            last = max(last, end)
        else:
            windows += 1
            total += end - first
            last = end
    anywhere = pl.BlockSpec(memory_space=pl.ANY)
    vmem = pl.BlockSpec(memory_space=pltpu.VMEM)
    return pl.pallas_call(
        functools.partial(matrix_kernel, rows),
        out_shape=[jax.ShapeDtypeStruct(shape, BF16) for shape in shapes]
        + [jax.ShapeDtypeStruct((VEC_ROWS, columns), F32) for columns in VEC_COLS],
        in_specs=[anywhere],
        out_specs=[anywhere] * len(shapes) + [vmem, vmem],
        scratch_shapes=buffers
        + [
            pltpu.VMEM((SLOTS_IN, PIECE + 32, LANES), BF16),
            pltpu.VMEM((PIECE + 32, LANES), F32),
            pltpu.VMEM((padded(HEAD) // LANES, SUB, LANES), F32),
            pltpu.VMEM((total, LANES), BF16),
            dma((SLOTS_IN,)),
            dma((len(shapes), 2)),
            dma((windows,)),
        ],
        compiler_params=pltpu.CompilerParams(vmem_limit_bytes=56 * 2**20),
        name="weight_matrices",
    )(flat)


def stream_items(layout, lent):
    items = []
    offset = 0
    numbers = [0, 0]
    for shape in layout + lent:
        matrix = len(shape) == 2
        number = numbers[matrix]
        numbers[matrix] += 1
        depth = block_depth(shape) if matrix else 0
        for start in range(0, shape[0] if matrix else 1, max(depth, 1)):
            items.append((matrix, number, shape, start, depth, offset))
            offset += depth * shape[1] if matrix else shape[0]
    return items, offset


ROLES = (
    (ENC_LAYOUT, [], (0, 1, 2, 3)),
    (DEC_LAYOUT, LENT, (6, 7, 8, 9, 10, 4, 5)),
)
PAIRS = 11
FLIGHTS = 4
DEPTH = 1024


def factor_buffers(shapes):
    sizes = []
    places = {}
    for role in (1, 0):
        taken = set()
        for number in ROLES[role][2]:
            for side in range(2):
                length, columns = shapes[2 * number + side]
                fits = [
                    n
                    for n, size in enumerate(sizes)
                    if n not in taken and size[0] == 2 * length and size[1] >= columns
                ]
                if fits:
                    place = min(fits, key=lambda n: sizes[n][1])
                else:
                    place = len(sizes)
                    sizes.append((2 * length, columns))
                taken.add(place)
                places[role, number, side] = place
    return sizes, places


def product_kernel(rows, shapes, *refs):
    factors, vectors, out_ref = refs[: 2 * PAIRS], refs[2 * PAIRS : 2 * PAIRS + 2], refs[24]
    sizes, places = factor_buffers(shapes)
    buffers = refs[25 : 25 + len(sizes)]
    refs = refs[25 + len(sizes) :]
    others = refs[:2]
    turned_left, tall, rows_out, own_sem, send_sem, recv_sem, out_sem = refs[2:]
    core = lax.axis_index("grp")
    sibling = (1 - core, lax.axis_index("dp"))
    barrier = pltpu.get_barrier_semaphore()
    pl.semaphore_signal(barrier, inc=1, device_id=sibling, device_id_type=MESH)
    pl.semaphore_wait(barrier, 1)

    def half_of(role, number, side, part):
        length, columns = shapes[2 * number + side]
        buffer = buffers[places[role, number, side]]
        return buffer.at[pl.ds(part * length, length), pl.ds(0, columns)]

    def local(role, number, side):
        return pltpu.make_async_copy(
            factors[2 * number + side], half_of(role, number, side, 0), own_sem.at[number, side]
        )

    def remote(role, number, side):
        return pltpu.make_async_remote_copy(
            src_ref=factors[2 * number + side],
            dst_ref=half_of(role, number, side, 1),
            send_sem=send_sem.at[number, side],
            recv_sem=recv_sem.at[number, side],
            device_id=sibling,
            device_id_type=MESH,
        )

    def remote_vectors(role):
        return pltpu.make_async_remote_copy(
            src_ref=vectors[role],
            dst_ref=others[role],
            send_sem=send_sem.at[PAIRS, role],
            recv_sem=recv_sem.at[PAIRS, role],
            device_id=sibling,
            device_id_type=MESH,
        )

    def act(role):
        remote_vectors(1 - role).start()
        pending = [(number, side) for number in ROLES[role][2] for side in range(2)]
        for number, side in pending:
            local(role, number, side).start()
        given = [(number, side) for number in ROLES[1 - role][2] for side in range(2)]
        for number, side in given:
            remote(1 - role, number, side).start()
        remote_vectors(role).wait_recv()

        def ready(number):
            for side in range(2):
                local(role, number, side).wait()
                remote(role, number, side).wait_recv()

        lefts, rights = [], []
        for number in ROLES[role][2]:
            for side, views in ((0, lefts), (1, rights)):
                length, columns = shapes[2 * number + side]
                buffer = buffers[places[role, number, side]]
                views.append(buffer.at[pl.ds(0, 2 * length), pl.ds(0, columns)])
        fill_row(
            rows,
            ROLES[role],
            ready,
            lefts,
            rights,
            vectors[role],
            others[role],
            turned_left,
            tall,
            rows_out,
            out_ref,
            out_sem,
        )
        for number, side in given:
            remote(1 - role, number, side).wait_send()
        remote_vectors(1 - role).wait_send()

    for role in range(2):
        pl.when(core == role)(functools.partial(act, role))


def fill_row(
    rows,
    role,
    ready,
    lefts,
    rights,
    mine_ref,
    other_ref,
    turned_left,
    tall,
    rows_out,
    out_ref,
    out_sem,
):
    layout, lent, numbers = role
    lane = lax.broadcasted_iota(jnp.int32, (1, LANES), 1)
    half = LANES // 2
    items, used = stream_items(layout, lent)
    groups = []
    current = []
    for item in items:
        current.append(item)
        if item[0]:
            groups.append(current)
            current = []
    groups.append(current)

    def vector(item, buffer, base):
        _, number, shape, _, _, _ = item
        for tile in range(-(-shape[0] // LANES)):
            lanes = pl.ds(tile * LANES, LANES)
            buffer[pl.ds(base + tile, 1)] = (
                mine_ref[pl.ds(number, 1), lanes] + other_ref[pl.ds(number, 1), lanes]
            )

    def matrix(item, buffer, base):
        _, number, shape, start, depth, offset = item
        columns = shape[1]
        shifted = offset % LANES
        tiles = -(-columns // LANES)
        width = min(WIDTH, columns)
        if start == 0:
            ready(numbers[number])
            if shifted:
                length = rights[number].shape[0]

                def turn(i, carry):
                    block = pl.ds(pl.multiple_of(i * 64, 64), 64)
                    value = rights[number][block].astype(F32)
                    rights[number][block] = pltpu.roll(value, half, 1).astype(BF16)
                    return carry

                lax.fori_loop(0, length // 64, turn, 0)
        length = lefts[number].shape[0]
        sub = min(DEPTH, depth)

        def loop(step, carry):
            k = pl.multiple_of(start + step * sub, sub)
            turned_left[pl.ds(0, sub), pl.ds(0, length)] = lefts[number][:, pl.ds(k, sub)].T

            def across(c, carry):
                column = pl.multiple_of(c * width, width)
                value = jnp.dot(
                    turned_left[pl.ds(0, sub), pl.ds(0, length)],
                    rights[number][:, pl.ds(column, width)],
                    preferred_element_type=F32,
                )
                row = base + step * sub * tiles
                for piece in range(width // LANES):
                    part = value[:, piece * LANES : (piece + 1) * LANES]
                    tile = c * (width // LANES) + piece
                    if columns % LANES:
                        tall[tile, pl.ds(step * sub, sub)] = part
                    elif shifted and piece == 0:
                        first = row + tile

                        @pl.when(c == 0)
                        def _():
                            before = pltpu.roll(part, 1, 0)
                            index = lax.broadcasted_iota(jnp.int32, (sub, LANES), 0)
                            held = buffer[pl.ds(row, 1)]
                            before = jnp.where(index == 0, held, before)
                            merged = jnp.where(lane < half, before, part)
                            buffer[pl.ds(row, sub, stride=tiles)] = merged
                            buffer[pl.ds(row + sub * tiles, 1)] = part[sub - 1 :]

                        @pl.when(c > 0)
                        def _():
                            buffer[pl.ds(first, sub, stride=tiles)] = part
                    else:
                        buffer[pl.ds(row + tile, sub, stride=tiles)] = part
                return carry

            lax.fori_loop(0, tiles * LANES // width, across, 0)
            return carry

        lax.fori_loop(0, depth // sub, loop, 0)
        if columns % LANES:
            stride = 2 * columns // LANES
            pair = 64

            def weave(i, carry):
                k = pl.multiple_of(i * 2 * pair, 2 * pair)
                row = base + i * pair * stride
                evens = [tall[t, pl.ds(k, pair, stride=2)] for t in range(tiles)]
                odds = [tall[t, pl.ds(k + 1, pair, stride=2)] for t in range(tiles)]
                for t in range(tiles - 1):
                    buffer[pl.ds(row + t, pair, stride=stride)] = evens[t]
                middle = jnp.where(lane < half, evens[-1], pltpu.roll(odds[0], half, 1))
                buffer[pl.ds(row + tiles - 1, pair, stride=stride)] = middle
                for t in range(1, tiles):
                    both_halves = jnp.where(lane < half, odds[t], odds[t - 1])
                    buffer[pl.ds(row + tiles - 1 + t, pair, stride=stride)] = pltpu.roll(
                        both_halves, half, 1
                    )
                return carry

            lax.fori_loop(0, depth // 2 // pair, weave, 0)

    flights = []
    tail = None
    for number, group in enumerate(groups):
        slot = number % 2
        buffer = rows_out.at[slot]
        if number >= 2:
            for copy in flights[number - 2]:
                copy.wait()
        first = group[0][5] // LANES if group else used // LANES
        begin = first // 8 * 8
        if tail is not None:
            buffer[pl.ds(0, 8)] = rows_out[1 - slot, pl.ds(tail, 8)]
        for item in group:
            (matrix if item[0] else vector)(item, buffer, item[5] // LANES - begin)
        last = number == len(groups) - 1
        if last:
            at = used // LANES - begin
            if used % LANES:
                buffer[pl.ds(at, 1)] = jnp.where(lane < used % LANES, buffer[pl.ds(at, 1)], 0.0)
                at += 1
            length = rows - begin
            if length > at:
                buffer[pl.ds(at, length - at)] = jnp.zeros((length - at, LANES), F32)
        else:
            end = groups[number + 1][0][5] if groups[number + 1] else used
            tail = (end // LANES - begin) // 8 * 8
            length = tail
        cuts = [length * n // FLIGHTS // 8 * 8 for n in range(FLIGHTS)] + [length]
        flight = [
            pltpu.make_async_copy(
                buffer.at[pl.ds(lower, upper - lower)],
                out_ref.at[pl.ds(begin + lower, upper - lower)],
                out_sem.at[slot, n],
            )
            for n, (lower, upper) in enumerate(zip(cuts, cuts[1:]))
            if upper > lower
        ]
        for copy in flight:
            copy.start()
        flights.append(flight)
    for flight in flights[-2:]:
        for copy in flight:
            copy.wait()


def flat_gradient(rows, factors, enc_vectors, dec_vectors):
    shapes = [factor.shape for factor in factors]
    sizes, _ = factor_buffers(shapes)
    longest = max(length for length, _ in sizes)
    dma = pltpu.SemaphoreType.DMA
    anywhere = pl.BlockSpec(memory_space=pl.ANY)
    vmem = pl.BlockSpec(memory_space=pltpu.VMEM)
    return pl.pallas_call(
        functools.partial(product_kernel, rows, shapes),
        out_shape=jax.ShapeDtypeStruct((rows, LANES), F32),
        in_specs=[anywhere] * (2 * PAIRS) + [vmem, vmem],
        out_specs=anywhere,
        scratch_shapes=[pltpu.VMEM(size, BF16) for size in sizes]
        + [
            pltpu.VMEM(enc_vectors.shape, F32),
            pltpu.VMEM(dec_vectors.shape, F32),
            pltpu.VMEM((DEPTH, longest), BF16),
            pltpu.VMEM((padded(HEAD) // LANES, DD, LANES), F32),
            pltpu.VMEM((2, PIECE + 128, LANES), F32),
            dma((PAIRS, 2)),
            dma((PAIRS + 1, 2)),
            dma((PAIRS + 1, 2)),
            dma((2, FLIGHTS)),
        ],
        compiler_params=pltpu.CompilerParams(
            collective_id=2, has_side_effects=True, vmem_limit_bytes=63 * 2**20
        ),
        name="flat_gradient",
    )(*factors, enc_vectors, dec_vectors)


LN1_G, LN1_B, LN2_G, LN2_B, FC1_B, FC2_B, LNF_G, LNF_B, LAST_B = range(1, 10)
GROUP = 256
TURNS = 16
BATCH = 2


def dot(left, right):
    return jnp.dot(left, right, preferred_element_type=F32)


def dot_nt(left, right):
    return lax.dot_general(left, right, (((1,), (1,)), ((), ())), preferred_element_type=F32)


def dot_tn(left, right):
    return lax.dot_general(left, right, (((0,), (0,)), ((), ())), preferred_element_type=F32)


def blocks(length, size, action):
    def step(index, carry):
        action(pl.ds(pl.multiple_of(index * size, size), size))
        return carry

    lax.fori_loop(0, length // size, step, 0)


def row_step(length):
    return 208 if length % 208 == 0 else 128


def score_step(length):
    return 832 if length % 208 == 0 else 256


def normed(state):
    centered = state - jnp.mean(state, axis=-1, keepdims=True)
    inverse = lax.rsqrt(jnp.mean(centered * centered, axis=-1, keepdims=True) + NORM_EPS)
    return centered * inverse, inverse


def norm_rows(source, target, vectors, gain):
    width = source.shape[1]

    def one(rows):
        unit, _ = normed(source[rows])
        value = unit * vectors[pl.ds(gain, 1), pl.ds(0, width)]
        target[rows] = (value + vectors[pl.ds(gain + 1, 1), pl.ds(0, width)]).astype(BF16)

    blocks(source.shape[0], row_step(source.shape[0]), one)


def norm_rows_back(source, grad, vectors, sums, gain, finish):
    width = source.shape[1]
    lanes = pl.ds(0, width)

    def one(rows):
        unit, inverse = normed(source[rows])
        out = grad[rows]
        sums[pl.ds(gain, 1), lanes] += jnp.sum(out * unit, axis=0, keepdims=True)
        sums[pl.ds(gain + 1, 1), lanes] += jnp.sum(out, axis=0, keepdims=True)
        scaled = out * vectors[pl.ds(gain, 1), lanes]
        mean = jnp.mean(scaled, axis=-1, keepdims=True)
        along = jnp.mean(scaled * unit, axis=-1, keepdims=True)
        finish(rows, inverse * (scaled - mean - unit * along))

    blocks(source.shape[0], row_step(source.shape[0]), one)


def gelu_parts(value):
    below = 0.5 * (1.0 + lax.erf(value * math.sqrt(0.5)))
    return below, value * below


def head_masks(depth):
    lane = lax.broadcasted_iota(jnp.int32, (1, GROUP), 1)
    return [
        ((lane >= head * depth) & (lane < (head + 1) * depth)).astype(F32).astype(BF16)
        for head in range(GROUP // depth)
    ]


def stack_heads(target, value, masks):
    length = value.shape[0]
    for head, mask in enumerate(masks):
        target[pl.ds(head * length, length)] = value * mask


def attention_forward(images, length, heads, qkv, bias, attend, attend_low, stacked, mixed):
    width = mixed.shape[1]
    depth = width // heads
    masks = head_masks(depth)
    groups = width // GROUP
    scale = depth**-0.5

    def one(index, carry):
        image, group = index // groups, index % groups
        rows = pl.ds(pl.multiple_of(image * length, length), length)

        def lanes(part):
            return pl.ds(pl.multiple_of(part * width + group * GROUP, GROUP), GROUP)

        stack_heads(stacked, qkv[rows, lanes(0)], masks)
        attend[index] = dot_nt(stacked[...], qkv[rows, lanes(1)])
        shift = bias[pl.ds(image, 1)]

        def softmax(block):
            scores = attend[index, block] * scale + shift
            raised = jnp.exp(scores - jnp.max(scores, axis=-1, keepdims=True))
            value = raised / jnp.sum(raised, axis=-1, keepdims=True)
            attend[index, block] = value
            attend_low[block] = value.astype(BF16)

        blocks(len(masks) * length, score_step(length), softmax)
        value = qkv[rows, lanes(2)]
        total = jnp.zeros((length, GROUP), F32)
        for head, mask in enumerate(masks):
            total += dot(attend_low[pl.ds(head * length, length)], value * mask)
        mixed[rows, lanes(0)] = total.astype(BF16)
        return carry

    lax.fori_loop(0, images * groups, one, 0)


def attention_backward(
    images, length, heads, qkv, grad_mixed, attend, attend_low, grad_low, grads, stacked, other, out
):
    width = grad_mixed.shape[1]
    depth = width // heads
    masks = head_masks(depth)
    groups = width // GROUP
    scale = depth**-0.5

    def one(index, carry):
        image, group = index // groups, index % groups
        rows = pl.ds(pl.multiple_of(image * length, length), length)

        def lanes(part):
            return pl.ds(pl.multiple_of(part * width + group * GROUP, GROUP), GROUP)

        stack_heads(stacked, qkv[rows, lanes(0)], masks)
        stack_heads(other, grad_mixed[rows, lanes(0)], masks)
        grads[...] = dot_nt(other[...], qkv[rows, lanes(2)])

        def scores(block):
            value = attend[index, block]
            grad = grads[block]
            total = jnp.sum(grad * value, axis=-1, keepdims=True)
            grad_low[block] = (value * (grad - total)).astype(BF16)
            attend_low[block] = value.astype(BF16)

        blocks(len(masks) * length, score_step(length), scores)
        out[rows, lanes(2)] = dot_tn(attend_low[...], other[...]).astype(BF16)
        out[rows, lanes(1)] = (dot_tn(grad_low[...], stacked[...]) * scale).astype(BF16)
        key = qkv[rows, lanes(1)]
        total = jnp.zeros((length, GROUP), F32)
        for head, mask in enumerate(masks):
            total += dot(grad_low[pl.ds(head * length, length)], key * mask)
        out[rows, lanes(0)] = (total * scale).astype(BF16)
        return carry

    lax.fori_loop(0, images * groups, one, 0)


def columns_loop(columns, size, action):
    blocks(columns, min(size, columns), action)


def feed_forward(normed_two, fc1_w, fc2_w, vectors, middle, pre, active, state):
    bias = pl.ds(FC1_B, 1)

    def up(lanes):
        value = dot(normed_two[...], fc1_w[:, lanes]) + vectors[bias, lanes]
        pre[:, lanes] = value
        active[:, lanes] = gelu_parts(value)[1].astype(BF16)

    columns_loop(pre.shape[1], 256, up)

    def down(lanes):
        value = dot(active[...], fc2_w[:, lanes])
        state[:, lanes] = middle[:, lanes] + value + vectors[pl.ds(FC2_B, 1), lanes]

    columns_loop(state.shape[1], 256, down)


def feed_backward(grad_low, fc1_w, fc2_w, pre, sums, grad_pre, out):
    def up(lanes):
        value = pre[:, lanes]
        below, _ = gelu_parts(value)
        slope = below + value * (jnp.exp(-0.5 * value * value) * (1.0 / math.sqrt(2.0 * math.pi)))
        grad = dot_nt(grad_low[...], fc2_w[lanes]) * slope
        sums[pl.ds(FC1_B, 1), lanes] += jnp.sum(grad, axis=0, keepdims=True)
        grad_pre[:, lanes] = grad.astype(BF16)

    columns_loop(pre.shape[1], 256, up)

    def down(lanes):
        out[:, lanes] = dot_nt(grad_pre[...], fc1_w[lanes])

    columns_loop(out.shape[1], 256, down)


def turn_code(places, table):
    lane = lax.broadcasted_iota(jnp.int32, (places.shape[0], TURNS), 1)
    passed = (lane > 0) & (lane < TURNS - 1) & (places >= lane * GSIDE)
    row = jnp.sum(passed.astype(F32), axis=1, keepdims=True).astype(jnp.int32)
    parts = []
    for pick in (row, places - row * GSIDE):
        chosen = (lane == pick).astype(F32)
        parts.append(jnp.dot(chosen, table, precision=HIGHEST, preferred_element_type=F32))
    return jnp.concatenate(parts, axis=1)


def decoder_kernel(
    sent,
    pixels,
    spot_rows,
    spot_columns,
    table,
    masked_ref,
    bands_w,
    vectors,
    qkv_w,
    out_w,
    fc1_w,
    fc2_w,
    head_w,
    normed_one,
    grad_qkv,
    mixed,
    grad_middle_low,
    normed_two,
    grad_pre,
    active,
    grad_out_low,
    normed_last,
    grad_predicted,
    grad_sent,
    sums,
    loss,
    seen,
    bias,
    state,
    middle,
    last,
    grad,
    spare,
    qkv,
    pre,
    attend,
    attend_low,
    scores_low,
    scores_grad,
    stacked,
    other,
    grad_mixed,
):
    width = state.shape[1]
    lanes = pl.ds(0, width)

    @pl.when(pl.program_id(0) == 0)
    def _():
        sums[...] = jnp.zeros_like(sums)
        loss[...] = jnp.zeros_like(loss)

    grid = lax.broadcasted_iota(jnp.int32, (GPAD, 1), 0)
    key = lax.broadcasted_iota(jnp.int32, (1, GPAD), 1)
    token = vectors[pl.ds(0, 1), lanes]
    for image in range(BATCH):
        rows = pl.ds(image * GPAD, GPAD)
        chosen = (grid == spot_rows[image]).astype(F32)
        shown = jnp.sum(chosen, axis=1, keepdims=True)
        placed = dot(chosen.astype(BF16), sent[pl.ds(image * VMAX, VMAX)])
        seen[rows] = jnp.where(grid < GRID, shown, 1.0)
        code = turn_code(grid, table[image])
        state[rows] = jnp.where(shown > 0.5, placed, token) + code
        bias[pl.ds(image, 1)] = jnp.where(key < GRID, 0.0, MASK_FILL)

    norm_rows(state, normed_one, vectors, LN1_G)

    def project(part):
        qkv[:, part] = dot(normed_one[...], qkv_w[:, part]).astype(BF16)

    columns_loop(qkv.shape[1], 256, project)
    attention_forward(
        BATCH, GPAD, HD, qkv, bias, attend, attend_low, stacked, mixed
    )

    def output(part):
        middle[:, part] = state[:, part] + dot(mixed[...], out_w[:, part])

    columns_loop(width, 256, output)
    norm_rows(middle, normed_two, vectors, LN2_G)
    feed_forward(normed_two, fc1_w, fc2_w, vectors, middle, pre, active, last)
    norm_rows(last, normed_last, vectors, LNF_G)

    weight = 1.0 / masked_ref[pl.ds(0, 1), pl.ds(0, 1)]

    def predict(part):
        value = dot(normed_last[...], head_w[:, part]) + vectors[pl.ds(LAST_B, 1), part]
        miss = value - dot(pixels[...], bands_w[:, part])
        index = lax.broadcasted_iota(jnp.int32, (1, GROUP), 1) + part.start
        low = index < LOWPIX
        square = miss * miss
        root = jnp.sqrt(square + 1.0)
        unseen = 1.0 - seen[...]
        loss[...] += jnp.sum(jnp.where(low, square, root - 1.0) * unseen).reshape(1, 1)
        slope = jnp.where(low, 2.0 * miss, miss / root) * (unseen * weight)
        rounded = slope.astype(BF16)
        grad_predicted[:, part] = rounded
        sums[pl.ds(LAST_B, 1), part] += jnp.sum(rounded.astype(F32), axis=0, keepdims=True)

    columns_loop(head_w.shape[1], GROUP, predict)

    def head_back(part):
        spare[:, part] = dot_nt(grad_predicted[...], head_w[part])

    columns_loop(width, 256, head_back)

    def last_back(rows, value):
        grad[rows] = value
        grad_out_low[rows] = value.astype(BF16)
        sums[pl.ds(FC2_B, 1), lanes] += jnp.sum(value, axis=0, keepdims=True)

    norm_rows_back(last, spare, vectors, sums, LNF_G, last_back)
    block_backward(
        BATCH,
        GPAD,
        HD,
        (qkv_w, out_w, fc1_w, fc2_w),
        vectors,
        sums,
        (state, middle, grad, spare, pre, qkv),
        (grad_out_low, grad_pre, grad_middle_low, grad_mixed, grad_qkv),
        (attend, attend_low, scores_low, scores_grad, stacked, other),
    )
    unseen = 1.0 - seen[...]
    sums[pl.ds(0, 1), lanes] += jnp.sum(grad[...] * unseen, axis=0, keepdims=True)
    for image in range(BATCH):
        chosen = (spot_columns[pl.ds(image * VMAX, VMAX)] == key).astype(F32).astype(BF16)
        value = dot(chosen, grad[pl.ds(image * GPAD, GPAD)].astype(BF16))
        grad_sent[pl.ds(image * VMAX, VMAX)] = value.astype(BF16)


def block_backward(images, length, heads, weights, vectors, sums, states, lows, scratch):
    qkv_w, out_w, fc1_w, fc2_w = weights
    state, middle, grad, spare, pre, qkv = states
    grad_out_low, grad_pre, grad_middle_low, grad_mixed, grad_qkv = lows
    attend, attend_low, scores_low, scores_grad, stacked, other = scratch
    width = state.shape[1]
    feed_backward(grad_out_low, fc1_w, fc2_w, pre, sums, grad_pre, spare)

    def middle_back(rows, value):
        total = grad[rows] + value
        grad[rows] = total
        grad_middle_low[rows] = total.astype(BF16)

    norm_rows_back(middle, spare, vectors, sums, LN2_G, middle_back)

    def mixed_back(part):
        grad_mixed[:, part] = dot_nt(grad_middle_low[...], out_w[part]).astype(BF16)

    columns_loop(width, 256, mixed_back)
    attention_backward(
        images,
        length,
        heads,
        qkv,
        grad_mixed,
        attend,
        attend_low,
        scores_low,
        scores_grad,
        stacked,
        other,
        grad_qkv,
    )

    def first_back(part):
        spare[:, part] = dot_nt(grad_qkv[...], qkv_w[part])

    columns_loop(width, 256, first_back)

    def state_back(rows, value):
        grad[rows] = grad[rows] + value

    norm_rows_back(state, spare, vectors, sums, LN1_G, state_back)


def decoder(sent, pixels, spots, tables, masked_tile, vectors, weights):
    images = spots.shape[0]
    rows = BATCH * GPAD
    shown = BATCH * VMAX
    stack = GROUP // (DD // HD) * GPAD
    widths = [DD, 3 * DD, DD, DD, DD, FD, FD, DD, DD, padded(HEAD)]
    whole = lambda array: pl.BlockSpec(array.shape, lambda i: (0,) * array.ndim)
    by_rows = lambda length, columns: pl.BlockSpec((length, columns), lambda i: (i, 0))
    bands_w = band_matrix()
    out_shape = [jax.ShapeDtypeStruct((images * GPAD, columns), BF16) for columns in widths]
    out_shape.append(jax.ShapeDtypeStruct((images * VMAX, DD), BF16))
    out_shape.append(jax.ShapeDtypeStruct((VEC_ROWS, VEC_COLS[1]), F32))
    out_shape.append(jax.ShapeDtypeStruct((1, 1), F32))
    operands = [masked_tile, bands_w, vectors, *weights]
    f32 = lambda *shape: pltpu.VMEM(shape, F32)
    b16 = lambda *shape: pltpu.VMEM(shape, BF16)
    return pl.pallas_call(
        decoder_kernel,
        grid=(images // BATCH,),
        out_shape=out_shape,
        in_specs=[
            by_rows(shown, DD),
            by_rows(rows, PIX),
            pl.BlockSpec((BATCH, 1, VMAX), lambda i: (i, 0, 0)),
            by_rows(shown, 1),
            pl.BlockSpec((BATCH, TURNS, DD // 2), lambda i: (i, 0, 0)),
        ]
        + [whole(operand) for operand in operands],
        out_specs=[by_rows(rows, columns) for columns in widths]
        + [by_rows(shown, DD)]
        + [pl.BlockSpec(shape.shape, lambda i: (0, 0)) for shape in out_shape[-2:]],
        scratch_shapes=[
            f32(rows, 1),
            f32(BATCH, GPAD),
            f32(rows, DD),
            f32(rows, DD),
            f32(rows, DD),
            f32(rows, DD),
            f32(rows, DD),
            b16(rows, 3 * DD),
            f32(rows, FD),
            f32(BATCH * DD // GROUP, stack, GPAD),
            b16(stack, GPAD),
            b16(stack, GPAD),
            f32(stack, GPAD),
            b16(stack, GROUP),
            b16(stack, GROUP),
            b16(rows, DD),
        ],
        compiler_params=pltpu.CompilerParams(vmem_limit_bytes=62 * 2**20),
        name="decoder",
    )(sent, pixels, spots.reshape(images, 1, VMAX), spots.reshape(-1, 1), tables, *operands)


def encoder_forward_kernel(
    pixels,
    spot_rows,
    spot_columns,
    table,
    vectors,
    pe_hbm,
    qkv_hbm,
    out_hbm,
    fc1_hbm,
    fc2_hbm,
    emb_hbm,
    sent,
    patches,
    state,
    normed_one,
    qkv,
    mixed,
    middle,
    normed_two,
    pre,
    active,
    last,
    normed_last,
    attend,
    pe_w,
    qkv_w,
    out_w,
    fc1_w,
    fc2_w,
    emb_w,
    bias,
    attend_low,
    stacked,
    sems,
):
    pairs = [
        (pe_hbm, pe_w),
        (qkv_hbm, qkv_w),
        (out_hbm, out_w),
        (fc1_hbm, fc1_w),
        (fc2_hbm, fc2_w),
        (emb_hbm, emb_w),
    ]
    copies = [pltpu.make_async_copy(*pair, sems.at[n]) for n, pair in enumerate(pairs)]
    for copy in copies:
        copy.start()
    images = spot_rows.shape[0]
    key = lax.broadcasted_iota(jnp.int32, (1, GPAD), 1)
    for image in range(images):
        rows = pl.ds(image * VMAX, VMAX)
        place = spot_columns[rows]
        chosen = (place == key).astype(F32).astype(BF16)
        patches[rows] = dot(chosen, pixels[pl.ds(image * GPAD, GPAD)]).astype(BF16)
        code = turn_code(jnp.maximum(place, 0), table[image])
        state[rows] = code + vectors[pl.ds(0, 1), pl.ds(0, DE)]
        bias[pl.ds(image, 1)] = jnp.where(spot_rows[image] < 0, MASK_FILL, 0.0)
    copies[0].wait()

    def embed(part):
        state[:, part] += dot(patches[...], pe_w[:, part])

    columns_loop(DE, 256, embed)
    norm_rows(state, normed_one, vectors, LN1_G)
    copies[1].wait()

    def project(part):
        qkv[:, part] = dot(normed_one[...], qkv_w[:, part]).astype(BF16)

    columns_loop(3 * DE, 256, project)
    attention_forward(images, VMAX, HE, qkv, bias, attend, attend_low, stacked, mixed)
    copies[2].wait()

    def output(part):
        middle[:, part] = state[:, part] + dot(mixed[...], out_w[:, part])

    columns_loop(DE, 256, output)
    norm_rows(middle, normed_two, vectors, LN2_G)
    copies[3].wait()
    copies[4].wait()
    feed_forward(normed_two, fc1_w, fc2_w, vectors, middle, pre, active, last)
    norm_rows(last, normed_last, vectors, LNF_G)
    copies[5].wait()
    value = dot(normed_last[...], emb_w[...]) + vectors[pl.ds(LAST_B, 1), pl.ds(0, DD)]
    sent[...] = value.astype(BF16)


def encoder_forward(pixels, spots, tables, vectors, weights):
    images = spots.shape[0]
    rows = images * VMAX
    stack = GROUP // (DE // HE) * VMAX
    anywhere = pl.BlockSpec(memory_space=pl.ANY)
    vmem = pl.BlockSpec(memory_space=pltpu.VMEM)
    kept = [
        (DD, BF16),
        (PIX, BF16),
        (DE, F32),
        (DE, BF16),
        (3 * DE, BF16),
        (DE, BF16),
        (DE, F32),
        (DE, BF16),
        (FE, F32),
        (FE, BF16),
        (DE, F32),
        (DE, BF16),
    ]
    out_shape = [jax.ShapeDtypeStruct((rows, columns), kind) for columns, kind in kept]
    out_shape.append(jax.ShapeDtypeStruct((images * DE // GROUP, stack, VMAX), F32))
    return pl.pallas_call(
        encoder_forward_kernel,
        out_shape=out_shape,
        in_specs=[vmem] * 5 + [anywhere] * 6,
        out_specs=[vmem] * len(out_shape),
        scratch_shapes=[pltpu.VMEM(weight.shape, BF16) for weight in weights]
        + [
            pltpu.VMEM((images, VMAX), F32),
            pltpu.VMEM((stack, VMAX), BF16),
            pltpu.VMEM((stack, GROUP), BF16),
            pltpu.SemaphoreType.DMA((6,)),
        ],
        compiler_params=pltpu.CompilerParams(vmem_limit_bytes=60 * 2**20),
        name="encoder_forward",
    )(pixels, spots.reshape(images, 1, VMAX), spots.reshape(-1, 1), tables, vectors, *weights)


def encoder_backward_kernel(
    grad_sent,
    vectors,
    state,
    qkv,
    middle,
    pre,
    last,
    attend,
    qkv_hbm,
    out_hbm,
    fc1_hbm,
    fc2_hbm,
    emb_hbm,
    grad_state_low,
    grad_qkv,
    grad_middle_low,
    grad_pre,
    grad_out_low,
    sums,
    qkv_w,
    out_w,
    fc1_w,
    fc2_w,
    emb_w,
    grad,
    spare,
    grad_mixed,
    attend_low,
    scores_low,
    scores_grad,
    stacked,
    other,
    sems,
):
    pairs = [
        (emb_hbm, emb_w),
        (fc2_hbm, fc2_w),
        (fc1_hbm, fc1_w),
        (out_hbm, out_w),
        (qkv_hbm, qkv_w),
    ]
    copies = [pltpu.make_async_copy(*pair, sems.at[n]) for n, pair in enumerate(pairs)]
    for copy in copies:
        copy.start()
    lanes = pl.ds(0, DE)
    sums[...] = jnp.zeros_like(sums)
    summed = jnp.sum(grad_sent[...].astype(F32), axis=0, keepdims=True)
    sums[pl.ds(LAST_B, 1), pl.ds(0, DD)] = summed
    copies[0].wait()

    def sent_back(part):
        spare[:, part] = dot_nt(grad_sent[...], emb_w[part])

    columns_loop(DE, 256, sent_back)

    def last_back(rows, value):
        grad[rows] = value
        grad_out_low[rows] = value.astype(BF16)
        sums[pl.ds(FC2_B, 1), lanes] += jnp.sum(value, axis=0, keepdims=True)

    norm_rows_back(last, spare, vectors, sums, LNF_G, last_back)
    for copy in copies[1:]:
        copy.wait()
    block_backward(
        state.shape[0] // VMAX,
        VMAX,
        HE,
        (qkv_w, out_w, fc1_w, fc2_w),
        vectors,
        sums,
        (state, middle, grad, spare, pre, qkv),
        (grad_out_low, grad_pre, grad_middle_low, grad_mixed, grad_qkv),
        (attend, attend_low, scores_low, scores_grad, stacked, other),
    )

    def first(rows):
        value = grad[rows]
        sums[pl.ds(0, 1), lanes] += jnp.sum(value, axis=0, keepdims=True)
        grad_state_low[rows] = value.astype(BF16)

    blocks(grad.shape[0], row_step(grad.shape[0]), first)


def encoder_backward(grad_sent, vectors, kept, weights):
    state, qkv, middle, pre, last, attend = kept
    rows = state.shape[0]
    stack = attend.shape[1]
    anywhere = pl.BlockSpec(memory_space=pl.ANY)
    vmem = pl.BlockSpec(memory_space=pltpu.VMEM)
    out_shape = [
        jax.ShapeDtypeStruct((rows, columns), BF16) for columns in (DE, 3 * DE, DE, FE, DE)
    ]
    out_shape.append(jax.ShapeDtypeStruct((VEC_ROWS, VEC_COLS[0]), F32))
    f32 = lambda *shape: pltpu.VMEM(shape, F32)
    b16 = lambda *shape: pltpu.VMEM(shape, BF16)
    return pl.pallas_call(
        encoder_backward_kernel,
        out_shape=out_shape,
        in_specs=[vmem] * 8 + [anywhere] * 5,
        out_specs=[vmem] * len(out_shape),
        scratch_shapes=[pltpu.VMEM(weight.shape, BF16) for weight in weights]
        + [
            f32(rows, DE),
            f32(rows, DE),
            b16(rows, DE),
            b16(stack, VMAX),
            b16(stack, VMAX),
            f32(stack, VMAX),
            b16(stack, GROUP),
            b16(stack, GROUP),
            pltpu.SemaphoreType.DMA((5,)),
        ],
        compiler_params=pltpu.CompilerParams(vmem_limit_bytes=60 * 2**20),
        name="encoder_backward",
    )(grad_sent, vectors, state, qkv, middle, pre, last, attend, *weights)


def band_matrix():
    ids = jnp.arange(PIX, dtype=jnp.int32)
    coarse = (ids // (3 * PSIDE) // 2 * (PSIDE // 2) + ids // 3 % PSIDE // 2) * 3 + ids % 3
    low = jnp.where(coarse[:, None] == jnp.arange(LOWPIX, dtype=jnp.int32)[None], 0.25, 0.0)
    same = jnp.where(coarse[:, None] == coarse[None], 0.25, 0.0)
    high = jnp.where(ids[:, None] == ids[None], 1.0, 0.0) - same
    rest = jnp.zeros((PIX, padded(HEAD) - HEAD), F32)
    return jnp.concatenate([low, high, rest], axis=1).astype(BF16)


def turn_table(scales, width):
    quarter = width // 4
    frequency = jnp.exp(jnp.arange(quarter, dtype=F32) * (-math.log(10000.0) / quarter))
    angle = (jnp.arange(TURNS, dtype=F32)[None] * scales[:, None])[..., None] * frequency
    return jnp.concatenate([jnp.sin(angle), jnp.cos(angle)], axis=-1)


def forward_backward(parts, pixels, index_rows, counts, scales, masked_tile):
    pe_w, qkv_w, fc1_w, emb_w, out_w, fc2_w = parts[:6]
    dec_weights = parts[6:11]
    enc_vectors, dec_vectors = parts[11:]
    images = counts.shape[0]
    valid = jnp.arange(VMAX, dtype=jnp.int32)[None, :] < counts[:, None]
    spots = jnp.where(valid, index_rows, -1)
    pixels = jnp.pad(pixels.reshape(images, GRID, PIX), ((0, 0), (0, GPAD - GRID), (0, 0)))
    pixels = pixels.reshape(images * GPAD, PIX)
    (
        sent,
        patches,
        state,
        normed_one,
        qkv,
        mixed,
        middle,
        normed_two,
        pre,
        active,
        last,
        normed_last,
        attend,
    ) = encoder_forward(
        pixels,
        spots,
        turn_table(scales, DE),
        enc_vectors,
        [pe_w, qkv_w, out_w, fc1_w, fc2_w, emb_w],
    )
    *dec_factors, grad_sent, dec_sums, loss = decoder(
        sent, pixels, spots, turn_table(scales, DD), masked_tile, dec_vectors, dec_weights
    )
    grad_state, grad_qkv, grad_middle, grad_pre, grad_out, enc_sums = encoder_backward(
        grad_sent,
        enc_vectors,
        [state, qkv, middle, pre, last, attend],
        [qkv_w, out_w, fc1_w, fc2_w, emb_w],
    )
    factors = [patches, grad_state, normed_one, grad_qkv, normed_two, grad_pre]
    factors += [normed_last, grad_sent, mixed, grad_middle, active, grad_out]
    return factors + dec_factors, enc_sums, dec_sums, loss[0, 0]


def clip_scale(squares):
    return jnp.minimum(1.0, CLIP / jnp.sqrt(squares))


def body(
    params, first_moment, second_moment, average, pixels, visible_index, visible_count, gsd_id
):
    chips = lax.axis_size("dp")
    rows = params.shape[1] // LANES
    special = chips == math.prod(DP_GRID) and rows % 4 == 0
    masked = jnp.sum(GRID - visible_count).astype(F32)
    if special:
        shards = [a.reshape(-1, 4, LANES) for a in (params, first_moment, second_moment, average)]
        copies, masked_tile = gather_rows(shards[0], jnp.full((8, LANES), masked))
    else:
        copies = lax.all_gather(params.astype(BF16).reshape(-1, LANES), "dp", axis=0, tiled=True)
        copies = lax.all_gather(copies, "grp", axis=0, tiled=True)
        masked_tile = jnp.full((8, LANES), lax.psum(masked, "dp"))
    parts = weight_matrices(copies.reshape(-1, LANES))

    half = visible_count.shape[0] // 2
    core = lax.axis_index("grp")

    def mine(array, count):
        return lax.dynamic_slice_in_dim(array, core * count, count, 0)

    scales = 0.5 + 0.25 * mine(gsd_id, half).astype(F32)
    factors, enc_sums, dec_sums, loss_local = forward_backward(
        parts,
        mine(pixels, half * GRID),
        mine(visible_index, half),
        mine(visible_count, half),
        scales,
        masked_tile,
    )
    gradient = flat_gradient(chips * rows, factors, enc_sums, dec_sums)
    if special:
        owned, sums = scatter_sums(
            gradient.reshape(chips, rows // 4, 4, LANES), jnp.full((8, LANES), loss_local)
        )
        squares = jnp.sum(sums[:4])
        loss_sum = sums[4, 0]
        outs = update(clip_scale(squares), [owned] + shards)
        outs = [out.reshape(params.shape) for out in outs]
    else:
        owned = lax.psum_scatter(gradient, "dp", scatter_dimension=0, tiled=True)
        owned = owned.reshape(params.shape)
        squares, loss_sum = lax.psum((jnp.sum(owned * owned), loss_local), ("grp", "dp"))
        outs = update_values(owned, clip_scale(squares), params, first_moment, second_moment, average)
    return (*outs, loss_sum, masked_tile[0, 0], jnp.sqrt(squares))


def solution(mesh):
    return jax.shard_map(
        body,
        mesh=mesh,
        in_specs=(P("grp", "dp"),) * 4 + (P("dp", None), P("dp", None), P("dp"), P("dp")),
        out_specs=(P("grp", "dp"),) * 4 + (P(), P(), P()),
        check_vma=False,
    )
```

```python
import functools
import math

import jax
import jax.numpy as jnp
from jax import lax
from jax.experimental import pallas as pl
from jax.experimental.pallas import tpu as pltpu
from jax.sharding import PartitionSpec as P

DE = 1024
HE = 16
FE = 4096
DD = 512
HD = 16
FD = 2048
PSIDE = 16
GSIDE = 14
VMAX = 64
STEP = 10
PIX = 768
LOWPIX = 192
GRID = 196
GPAD = 208
NENC = 8662528
NDEC = 3644352
LANES = 128
UNIT = 4 * LANES

HIGHEST = lax.Precision.HIGHEST
CLIP = 0.05
RATE = 0.01
BETA_ONE = 0.5
BETA_TWO = 0.5
ADAM_EPS = 1e-08
DECAY_WEIGHT = 0.05
AVERAGE_KEEP = 0.9
NORM_EPS = 1e-06
MASK_FILL = -1000000000.0
F32 = jnp.float32
BF16 = jnp.bfloat16
MESH = pl.DeviceIdType.MESH

WIDTH = 512
SUB = 64
PIECE = 8192
VEC_ROWS = 16
VEC_COLS = (FE, FD)
HEAD = LOWPIX + PIX

ENC_LAYOUT = [
    (PIX, DE),
    (DE,),
    (DE,),
    (DE,),
    (DE, 3 * DE),
    (DE,),
    (DE,),
    (DE, FE),
    (FE,),
    (DE,),
    (DE,),
    (DE,),
    (DE, DD),
    (DD,),
]
DEC_LAYOUT = [
    (DD,),
    (DD,),
    (DD,),
    (DD, 3 * DD),
    (DD, DD),
    (DD,),
    (DD,),
    (DD, FD),
    (FD,),
    (FD, DD),
    (DD,),
    (DD,),
    (DD,),
    (DD, HEAD),
    (HEAD,),
]
LENT = [(DE, DE), (FE, DE)]


DP_GRID = (4, 2, 2)
YZX, XZY, ZXY = ("y", "z", "x"), ("x", "z", "y"), ("z", "x", "y")
SPLIT = 2
ORDERS = (YZX,) * SPLIT + (XZY,) * SPLIT + (ZXY,) * SPLIT
PARTS = len(ORDERS)
OWN_FIRST = tuple(range(2 * SPLIT, 3 * SPLIT)) + tuple(range(2 * SPLIT))
SHARES = (0.41, 0.26, 0.33)
WAYS = ("x", "y", "up", "down")
CHUNK = 64
AXIS_SIZE = {"z": 4, "y": 2, "x": 2}
OPPOSITE = {"x": "x", "y": "y", "up": "down", "down": "up"}


def part_ranges(units):
    ends = [0]
    for share in SHARES:
        for _ in range(SPLIT):
            ends.append(ends[-1] + share / SPLIT)
    ends = [round(end * units) for end in ends[:-1]] + [units]
    return [(start, end - start) for start, end in zip(ends, ends[1:])]


def relatives():
    places = [(dz, dy, dx) for dz in range(-3, 4) for dy in (0, 1) for dx in (0, 1)]
    places.remove((0, 0, 0))
    return sorted(places, key=lambda r: abs(r[0]) + r[1] + r[2])


def last_axis(order, place):
    differs = {"z": place[0] != 0, "y": place[1] != 0, "x": place[2] != 0}
    return [axis for axis in order if differs[axis]][-1]


def onward(order, place):
    if place == (0, 0, 0):
        return ["up", "down", "x", "y"]
    axis = last_axis(order, place)
    ways = []
    if axis == "z":
        ways.append("up" if place[0] < 0 else "down")
    for later in order[order.index(axis) + 1 :]:
        ways += ["up", "down"] if later == "z" else [later]
    return ways


def when(condition, action):
    if condition is None:
        action()
    else:
        pl.when(condition)(action)


def both(left, right):
    if left is None:
        return right
    return left if right is None else left & right


class Spot:
    def __init__(self):
        self.grp = lax.axis_index("grp")
        self.dp = lax.axis_index("dp")
        self.x = self.dp % 2
        self.y = (self.dp // 2) % 2
        self.z = self.dp // 4
        self.neighbour = {
            "x": (self.grp, self.index(self.z, self.y, 1 - self.x)),
            "y": (self.grp, self.index(self.z, 1 - self.y, self.x)),
            "up": (self.grp, self.index(jnp.minimum(self.z + 1, 3), self.y, self.x)),
            "down": (self.grp, self.index(jnp.maximum(self.z - 1, 0), self.y, self.x)),
            "core": (1 - self.grp, self.dp),
        }
        self.exists = {"x": None, "y": None, "up": self.z < 3, "down": self.z > 0, "core": None}

    def index(self, z, y, x):
        return z * 4 + y * 2 + x

    def at(self, place):
        z = self.z + place[0]
        y = 1 - self.y if place[1] else self.y
        x = 1 - self.x if place[2] else self.x
        inside = None if place[0] == 0 else (z >= 0) & (z <= 3)
        return z, self.index(z, y, x), inside

    def greet(self):
        barrier = pltpu.get_barrier_semaphore()
        me = self.grp * 16 + self.dp

        def signal(step, carry):
            other = (me + step) % 32
            pl.semaphore_signal(
                barrier, inc=1, device_id=(other // 16, other % 16), device_id_type=MESH
            )
            return carry

        lax.fori_loop(1, 32, signal, 0)

    def await_all(self):
        pl.semaphore_wait(pltpu.get_barrier_semaphore(), 31)


def tell_all(spot, tiles, send_sem, recv_sem):
    me = spot.grp * 16 + spot.dp

    def copy(number, other):
        return pltpu.make_async_remote_copy(
            src_ref=tiles.at[number],
            dst_ref=tiles.at[number],
            send_sem=send_sem.at[other],
            recv_sem=recv_sem.at[number],
            device_id=(other // 16, other % 16),
            device_id_type=MESH,
        )

    def start(step, carry):
        copy(me, (me + step) % 32).start()
        return carry

    def finish(step, carry):
        other = (me + step) % 32
        copy(other, other).wait_recv()
        copy(me, other).wait_send()
        return carry

    return (
        lambda: lax.fori_loop(1, 32, start, 0),
        lambda: lax.fori_loop(1, 32, finish, 0),
    )


def gather_kernel(
    master_ref,
    masked_ref,
    out_ref,
    masked_out,
    master,
    own_ref,
    tiles,
    local_sem,
    send_sem,
    recv_sem,
    core_send,
    core_recv,
    tile_send,
    tile_recv,
):
    spot = Spot()
    read = pltpu.make_async_copy(master_ref, master, local_sem)
    read.start()
    tiles[spot.grp * 16 + spot.dp] = masked_ref[...]
    spot.greet()
    tell, told = tell_all(spot, tiles, tile_send, tile_recv)
    ranges = part_ranges(own_ref.shape[0])
    read.wait()

    def round_off(start, length):
        block = pl.ds(start, length)
        own_ref[block] = master[block].astype(BF16)

    def step(index, carry):
        round_off(index * CHUNK, CHUNK)
        return carry

    units = own_ref.shape[0]
    lax.fori_loop(0, units // CHUNK, step, 0)
    if units % CHUNK:
        round_off(units - units % CHUNK, units % CHUNK)
    spot.await_all()

    def copy(part, source, way, from_own):
        target = out_ref.at[spot.grp, source, pl.ds(*ranges[part])]
        origin = own_ref.at[pl.ds(*ranges[part])] if from_own else target
        if way == "core":
            sems = (core_send.at[part, source], core_recv.at[part, source])
        else:
            sems = (send_sem.at[part, source, WAYS.index(way)], recv_sem.at[part, source])
        return pltpu.make_async_remote_copy(
            src_ref=origin,
            dst_ref=target,
            send_sem=sems[0],
            recv_sem=sems[1],
            device_id=spot.neighbour[way],
            device_id_type=MESH,
        )

    sent = []
    for part in OWN_FIRST:
        for way in onward(ORDERS[part], (0, 0, 0)):
            when(
                spot.exists[way],
                lambda part=part, way=way: copy(part, spot.dp, way, True).start(),
            )
            sent.append((part, spot.dp, way, spot.exists[way], True))
    local = pltpu.make_async_copy(own_ref, out_ref.at[spot.grp, spot.dp], local_sem)
    local.start()
    tell()
    for part in range(PARTS):
        copy(part, spot.dp, "core", True).start()
        sent.append((part, spot.dp, "core", None, True))
    for place in relatives():
        _, source, inside = spot.at(place)
        for part in range(PARTS):
            ways = onward(ORDERS[part], place)

            def pass_on(part=part, source=source, ways=ways):
                copy(part, source, "x", False).wait_recv()
                for way in ways:
                    when(
                        spot.exists[way],
                        lambda way=way: copy(part, source, way, False).start(),
                    )
                copy(part, source, "core", False).start()

            when(inside, pass_on)
            for way in ways + ["core"]:
                sent.append((part, source, way, both(inside, spot.exists[way]), False))
    for part, source, way, condition, from_own in sent:
        when(condition, lambda: copy(part, source, way, from_own).wait_send())

    def await_core(source, carry):
        for part in range(PARTS):
            landed = out_ref.at[1 - spot.grp, source, pl.ds(*ranges[part])]
            pltpu.make_async_remote_copy(
                src_ref=landed,
                dst_ref=landed,
                send_sem=core_send.at[part, source],
                recv_sem=core_recv.at[part, source],
                device_id=spot.neighbour["core"],
                device_id_type=MESH,
            ).wait_recv()
        return carry

    lax.fori_loop(0, 16, await_core, 0)
    told()
    masked_out[...] = jnp.sum(tiles[pl.ds(0, 16)], axis=0)
    local.wait()


def gather_rows(master, masked):
    units = master.shape[0]
    dma = pltpu.SemaphoreType.DMA
    anywhere = pl.BlockSpec(memory_space=pl.ANY)
    vmem = pl.BlockSpec(memory_space=pltpu.VMEM)
    return pl.pallas_call(
        gather_kernel,
        out_shape=(
            jax.ShapeDtypeStruct((2, 16, units, 4, LANES), BF16),
            jax.ShapeDtypeStruct((8, LANES), F32),
        ),
        in_specs=[anywhere, vmem],
        out_specs=(anywhere, vmem),
        scratch_shapes=[
            pltpu.VMEM((units, 4, LANES), F32),
            pltpu.VMEM((units, 4, LANES), BF16),
            pltpu.VMEM((32, 8, LANES), F32),
            dma,
            dma((PARTS, 16, 4)),
            dma((PARTS, 16)),
            dma((PARTS, 16)),
            dma((PARTS, 16)),
            dma((32,)),
            dma((32,)),
        ],
        compiler_params=pltpu.CompilerParams(collective_id=0, has_side_effects=True),
        name="gather_rows",
    )(master, masked)


def slot_tables():
    tables = []
    for order in ORDERS:
        table = {}
        for way in WAYS:
            keys = []
            along = False
            for place in [(0, 0, 0)] + relatives():
                if way in onward(order, place):
                    if place[1:] not in keys:
                        keys.append(place[1:])
                    along = along or place[0] != 0
            table[way] = (keys, 3 if way in ("up", "down") else (4 if along else 1))
        tables.append(table)
    return tables


SLOTS = slot_tables()
STAGES = 4
RING = 20
MANY = 6


def wide_shards(units):
    shard = units * UNIT
    last_matrix = sum(math.prod(shape) for shape in ENC_LAYOUT[:-2])
    return ((last_matrix // shard, 16), (0, -(-NDEC // shard)))


def scatter_kernel(grad_ref, loss_ref, out_ref, sums_ref, *refs):
    ranges = part_ranges(grad_ref.shape[1])
    landing = {}
    for part in range(PARTS):
        for number, way in enumerate(WAYS):
            landing[part, way] = refs[part * 4 + number]
    stage, ring, total, tiles, send_sem, recv_sem, stage_sem, out_sem, tile_send, tile_recv = refs[
        4 * PARTS :
    ]
    spot = Spot()
    spot.greet()
    spot.await_all()
    bounds = wide_shards(grad_ref.shape[1])
    z_here = spot.z

    def is_wide(owner):
        low = jnp.where(spot.grp == 0, bounds[0][0], bounds[1][0])
        high = jnp.where(spot.grp == 0, bounds[0][1], bounds[1][1])
        return (owner >= low) & (owner < high)

    def is_split(part, way, z, owner):
        axis = way if way in ("x", "y") else "z"
        order = ORDERS[part]
        chips = math.prod(AXIS_SIZE[later] for later in order[order.index(axis) + 1 :])
        if axis != "z":
            return True if chips >= MANY else is_wide(owner)
        chips = chips * (z + 1 if way == "up" else DP_GRID[0] - z)
        return is_wide(owner) | (chips >= MANY)

    def slot(part, way, place, z):
        keys, depth = SLOTS[part][way]
        base = keys.index(place[1:]) * depth
        if way == "up":
            return base + z
        if way == "down":
            return base + z - 1
        return base + (z if depth == 4 else 0)

    def parent(part, place):
        axis = last_axis(ORDERS[part], place)
        if axis == "z":
            return "up" if place[0] > 0 else "down"
        return axis

    def seen_from_parent(part, place):
        way = parent(part, place)
        dz, dy, dx = place
        if way == "x":
            return (dz, dy, 0)
        if way == "y":
            return (dz, 0, dx)
        return (dz - 1 if way == "up" else dz + 1, dy, dx)

    def send(part, place, origin, half):
        z, owner, _ = spot.at(place)
        way = parent(part, place)
        back = OPPOSITE[way]
        place_there = slot(part, back, seen_from_parent(part, place), z)
        return pltpu.make_async_remote_copy(
            src_ref=origin.at[half],
            dst_ref=landing[part, back].at[place_there, half],
            send_sem=send_sem.at[part, owner, half],
            recv_sem=recv_sem.at[part, owner, WAYS.index(back), half],
            device_id=spot.neighbour[way],
            device_id_type=MESH,
        )

    nodes = []
    for place in relatives()[::-1] + [(0, 0, 0)]:
        for part in range(PARTS):
            z, owner, inside = spot.at(place)
            nodes.append((part, place, onward(ORDERS[part], place), z, owner, inside))

    def staged(number):
        part, _, _, _, owner, _ = nodes[number]
        return pltpu.make_async_copy(
            grad_ref.at[owner, pl.ds(*ranges[part])],
            stage.at[number % STAGES, pl.ds(0, ranges[part][1])],
            stage_sem.at[number % STAGES],
        )

    def ring_part(index, part):
        return ring.at[index % RING, :, pl.ds(0, ranges[part][1])]

    def finish_send(number):
        part, place, _, _, owner, inside = nodes[number]
        split = is_split(part, parent(part, place), spot.z, owner)

        def finish():
            source = ring_part(0, part)
            send(part, place, source, 0).wait_send()
            when(
                None if split is True else split,
                lambda: send(part, place, source, 1).wait_send(),
            )

        when(inside, finish)

    for number in range(STAGES - 1):
        when(nodes[number][5], lambda: staged(number).start())
    ringed = []
    for number, (part, place, ways, z, owner, inside) in enumerate(nodes):
        ahead = number + STAGES - 1
        if ahead < len(nodes):
            when(nodes[ahead][5], lambda: staged(ahead).start())
        length = ranges[part][1]
        root = place == (0, 0, 0)
        flat = [way for way in ways if way in ("x", "y")]
        along = [way for way in ways if way in ("up", "down")]
        if not flat:
            if len(ringed) >= RING:
                finish_send(ringed[-RING])
            ringed.append(number)
        ring_index = len(ringed) - 1

        def combine(arriving, number=number, part=part, place=place, z=z, owner=owner):
            slots = [landing[part, way].at[slot(part, way, place, z)] for way in arriving]
            target = slots[0] if slots else ring_part(ring_index, part)

            def arrived(way, item, half):
                pltpu.make_async_remote_copy(
                    src_ref=item.at[half],
                    dst_ref=item.at[half],
                    send_sem=send_sem.at[part, owner, half],
                    recv_sem=recv_sem.at[part, owner, WAYS.index(way), half],
                    device_id=spot.neighbour[way],
                    device_id_type=MESH,
                ).wait_recv()

            def lines(ref):
                return ref.reshape(ref.shape[0] * 4, LANES)

            mine = lines(stage.at[number % STAGES, pl.ds(0, length)])

            def every(action):
                count = 4 * length
                some = 4 * CHUNK

                def step(index, carry):
                    action(pl.ds(pl.multiple_of(index * some, some), some))
                    return carry

                lax.fori_loop(0, count // some, step, 0)
                if count % some:
                    action(pl.ds(count - count % some, count % some))

            def put(rows, value, split):
                if root:
                    lines(total.at[pl.ds(*ranges[part])])[rows] = value
                    return
                high = value.astype(BF16)
                lines(target.at[0])[rows] = high
                if split:
                    lines(target.at[1])[rows] = (value - high.astype(F32)).astype(BF16)

            def summed(rows):
                value = mine[rows]
                for item in slots:
                    value = value + lines(item.at[0])[rows].astype(F32)
                return value

            for way, item in zip(arriving, slots):
                arrived(way, item, 0)
            staged(number).wait()
            theirs = []
            for way in arriving:
                there = {"up": z_here + 1, "down": z_here - 1}.get(way, z_here)
                theirs.append(is_split(part, OPPOSITE[way], there, owner))
            ours = False if root else is_split(part, parent(part, place), z_here, owner)
            some_split = functools.reduce(lambda a, b: a | b, theirs + [ours])

            def short():
                every(lambda rows: put(rows, summed(rows), False))

            def long():
                def first(rows):
                    mine[rows] = summed(rows)

                if slots:
                    every(first)
                for way, item, split in zip(arriving, slots, theirs):

                    def rest(way=way, item=item):
                        arrived(way, item, 1)

                        def one(rows):
                            mine[rows] = mine[rows] + lines(item.at[1])[rows].astype(F32)

                        every(one)

                    when(None if split is True else split, rest)
                every(lambda rows: put(rows, mine[rows], True))

            if some_split is True:
                long()
            else:
                pl.when(some_split)(long)
                pl.when(jnp.logical_not(some_split))(short)
            if not root:
                send(part, place, target, 0).start()
                when(
                    None if ours is True else ours,
                    lambda: send(part, place, target, 1).start(),
                )

        def choose(flat=flat, along=along, combine=combine):
            if not along:
                combine(flat)
            elif len(along) == 1:
                there = spot.exists[along[0]]
                pl.when(there)(lambda: combine(flat + along))
                pl.when(jnp.logical_not(there))(lambda: combine(flat))
            else:
                up, down = spot.exists["up"], spot.exists["down"]
                pl.when(up & down)(lambda: combine(flat + ["up", "down"]))
                pl.when(jnp.logical_not(down))(lambda: combine(flat + ["up"]))
                pl.when(jnp.logical_not(up))(lambda: combine(flat + ["down"]))

        when(inside, choose)
    out = pltpu.make_async_copy(total, out_ref, out_sem)
    out.start()
    units = total.shape[0]

    def square(start, count, running):
        value = total[pl.ds(start, count)]
        return running + jnp.sum(value * value, axis=0)

    squares = lax.fori_loop(
        0,
        units // CHUNK,
        lambda index, running: square(index * CHUNK, CHUNK, running),
        jnp.zeros((4, LANES), F32),
    )
    if units % CHUNK:
        squares = square(units - units % CHUNK, units % CHUNK, squares)
    me = spot.grp * 16 + spot.dp
    tiles[me, pl.ds(0, 4)] = squares
    tiles[me, pl.ds(4, 4)] = loss_ref[pl.ds(4, 4)]
    tell, told = tell_all(spot, tiles, tile_send, tile_recv)
    tell()
    done = set(ringed[:-RING])
    for number, node in enumerate(nodes):
        if number not in done and node[1] != (0, 0, 0):
            finish_send(number)
    told()
    sums_ref[...] = jnp.sum(tiles[...], axis=0)
    out.wait()


def scatter_sums(grads, loss):
    units = grads.shape[1]
    ranges = part_ranges(units)
    scratch = []
    for part in range(PARTS):
        for way in WAYS:
            keys, depth = SLOTS[part][way]
            shape = (len(keys) * depth, 2, ranges[part][1], 4, LANES)
            scratch.append(pltpu.VMEM(shape, BF16))
    largest = max(length for _, length in ranges)
    dma = pltpu.SemaphoreType.DMA
    scratch += [
        pltpu.VMEM((STAGES, largest, 4, LANES), F32),
        pltpu.VMEM((RING, 2, largest, 4, LANES), BF16),
        pltpu.VMEM((units, 4, LANES), F32),
        pltpu.VMEM((32, 8, LANES), F32),
        dma((PARTS, 16, 2)),
        dma((PARTS, 16, 4, 2)),
        dma((STAGES,)),
        dma,
        dma((32,)),
        dma((32,)),
    ]
    anywhere = pl.BlockSpec(memory_space=pl.ANY)
    vmem = pl.BlockSpec(memory_space=pltpu.VMEM)
    return pl.pallas_call(
        scatter_kernel,
        out_shape=(
            jax.ShapeDtypeStruct((units, 4, LANES), F32),
            jax.ShapeDtypeStruct((8, LANES), F32),
        ),
        in_specs=[anywhere, vmem],
        out_specs=(anywhere, vmem),
        scratch_shapes=scratch,
        compiler_params=pltpu.CompilerParams(
            collective_id=1, has_side_effects=True, vmem_limit_bytes=63 * 2**20
        ),
        name="scatter_sums",
    )(grads, loss)


def update_values(owned, scale, params, first_moment, second_moment, average):
    clipped = owned * scale
    new_first = BETA_ONE * first_moment + (1.0 - BETA_ONE) * clipped
    new_second = BETA_TWO * second_moment + (1.0 - BETA_TWO) * clipped * clipped
    root = jnp.sqrt(new_second * (1.0 / (1.0 - BETA_TWO**STEP)))
    direction = new_first * (1.0 / (1.0 - BETA_ONE**STEP)) / (root + ADAM_EPS)
    new_params = params - RATE * (direction + DECAY_WEIGHT * params)
    new_average = AVERAGE_KEEP * average + (1.0 - AVERAGE_KEEP) * new_params
    return new_params, new_first, new_second, new_average


def update_kernel(scale_ref, *refs):
    scale = scale_ref[0]
    step = 31

    def one(index, carry):
        block = pl.ds(index * step, step)
        owned, params, first, second, average = [ref[block] for ref in refs[:5]]
        values = update_values(owned, scale, params, first, second, average)
        for out, value in zip(refs[5:], values):
            out[block] = value
        return carry

    lax.fori_loop(0, refs[0].shape[0] // step, one, 0)


def update(scale, arrays):
    units = arrays[0].shape[0]
    depth = 155
    spec = pl.BlockSpec((depth, 4, LANES), lambda i: (i, 0, 0))
    return pl.pallas_call(
        update_kernel,
        grid=(units // depth,),
        out_shape=[jax.ShapeDtypeStruct((units, 4, LANES), F32)] * 4,
        in_specs=[pl.BlockSpec(memory_space=pltpu.SMEM)] + [spec] * 5,
        out_specs=[spec] * 4,
        name="update",
    )(scale.reshape(1), *arrays)


SLOTS_IN = 5


def sections(layout, base):
    matrices, vectors = [], []
    offset = base
    for shape in layout:
        (matrices if len(shape) == 2 else vectors).append((offset, shape))
        offset += math.prod(shape)
    return matrices, vectors


def matrix_plan(rows):
    enc_matrices, enc_vectors = sections(ENC_LAYOUT, 0)
    dec_matrices, dec_vectors = sections(DEC_LAYOUT, rows * LANES)
    lent = rows * LANES + NDEC
    matrices = enc_matrices + sections(LENT, lent)[0] + dec_matrices
    return matrices, enc_vectors, dec_vectors


def padded(columns):
    return -(-columns // LANES) * LANES


def block_depth(shape):
    if shape[1] % LANES:
        return shape[0]
    depth = shape[0]
    while depth * shape[1] > PIECE * LANES:
        depth //= 2
    return depth


def matrix_kernel(rows, flat_ref, *refs):
    matrices, enc_vectors, dec_vectors = matrix_plan(rows)
    count = len(matrices)
    out_refs = refs[:count]
    vector_refs = refs[count : count + 2]
    blocks = refs[count + 2 : 2 * count + 2]
    flat_in, wide, pairs, vector_in, in_sem, out_sem, vector_sem = refs[2 * count + 2 :]
    lane = lax.broadcasted_iota(jnp.int32, (1, LANES), 1)

    chunks = []
    for number, (offset, shape) in enumerate(matrices):
        depth = block_depth(shape)
        for start in range(0, shape[0], depth):
            place = offset + start * shape[1]
            chunks.append((number, start, depth, place // LANES, place % LANES))

    def load(index):
        number, _, depth, first, shift = chunks[index]
        length = depth * matrices[number][1][1] // LANES
        begin = first // 16 * 16
        end = -(-(first + length + (1 if shift else 0)) // 16) * 16
        copy = pltpu.make_async_copy(
            flat_ref.at[pl.ds(begin, end - begin)],
            flat_in.at[index % SLOTS_IN, pl.ds(0, end - begin)],
            in_sem.at[index % SLOTS_IN],
        )
        return copy, first - begin, end - begin

    def store(index):
        number, start, depth, _, _ = chunks[index]
        slot = start // depth % 2
        return pltpu.make_async_copy(
            blocks[number].at[slot], out_refs[number].at[pl.ds(start, depth)], out_sem.at[number, slot]
        )

    def widen(index, length):
        step = 256

        def one(start, size):
            wide[pl.ds(start, size)] = flat_in[index % SLOTS_IN, pl.ds(start, size)].astype(F32)

        def loop(i, carry):
            one(pl.multiple_of(i * step, step), step)
            return carry

        lax.fori_loop(0, length // step, loop, 0)
        if length % step:
            one(length - length % step, length % step)

    def turned(first, second):
        return pltpu.roll(jnp.where(lane < LANES // 2, second, first), LANES // 2, 1)

    def arrange(index, phase):
        number, start, depth, _, shift = chunks[index]
        columns = matrices[number][1][1]
        block = blocks[number].at[start // depth % 2]
        tiles = columns // LANES

        def plain(i, carry):
            row = pl.multiple_of(i * SUB, SUB)
            packed = wide[pl.ds(phase + row * tiles, SUB * tiles)].reshape(SUB, tiles, LANES)
            swapped = jnp.swapaxes(packed, 0, 1)
            for tile in range(tiles):
                value = swapped[tile]
                if shift:
                    after = wide[pl.ds(phase + row * tiles + tile + 1, SUB, stride=tiles)]
                    value = turned(value, after)
                block[pl.ds(row, SUB), pl.ds(tile * LANES, LANES)] = value.astype(BF16)
            return carry

        def paired(i, carry):
            stride = 2 * columns // LANES
            half = SUB // 2
            row = pl.multiple_of(i * half, half)
            for tile in range(tiles + 1):
                even = wide[pl.ds(phase + row * stride + tile, half, stride=stride)]
                odd = wide[pl.ds(phase + row * stride + tiles + tile, half, stride=stride)]
                if tile < tiles:
                    after = wide[pl.ds(phase + row * stride + tiles + tile + 1, half, stride=stride)]
                    odd = turned(odd, after)
                else:
                    even = jnp.where(lane < LANES // 2, even, 0.0)
                    odd = jnp.where(lane < LANES // 2, pltpu.roll(odd, LANES // 2, 1), 0.0)
                lanes = pl.ds(tile * LANES, LANES)
                pairs[tile, pl.ds(0, half, stride=2)] = even
                pairs[tile, pl.ds(1, half, stride=2)] = odd
                block[pl.ds(pl.multiple_of(i * SUB, SUB), SUB), lanes] = pairs[tile].astype(BF16)
            return carry

        lax.fori_loop(0, depth // SUB, paired if columns % LANES else plain, 0)

    windows = []
    wanted = [(0, n, v) for n, v in enumerate(enc_vectors)]
    wanted += [(1, n, v) for n, v in enumerate(dec_vectors)]
    for _, _, (offset, shape) in wanted:
        first = offset // LANES // 16 * 16
        end = -(-(offset // LANES + -(-shape[0] // LANES)) // 16) * 16
        if windows and first <= windows[-1][1]:
            windows[-1][1] = max(windows[-1][1], end)
        else:
            windows.append([first, end])
    bases = [sum(e - f for f, e in windows[:n]) for n in range(len(windows))]

    def vector_copy(n):
        first, end = windows[n]
        return pltpu.make_async_copy(
            flat_ref.at[pl.ds(first, end - first)],
            vector_in.at[pl.ds(bases[n], end - first)],
            vector_sem.at[n],
        )

    for index in range(SLOTS_IN - 1):
        load(index)[0].start()
    for n in range(len(windows)):
        vector_copy(n).start()
    for index, (number, start, depth, _, _) in enumerate(chunks):
        copy, phase, length = load(index)
        copy.wait()
        if index + SLOTS_IN - 1 < len(chunks):
            load(index + SLOTS_IN - 1)[0].start()
        widen(index, length)
        if start // depth >= 2:
            store(index - 2).wait()
        arrange(index, phase)
        store(index).start()
    for n in range(len(windows)):
        vector_copy(n).wait()
    total = bases[-1] + windows[-1][1] - windows[-1][0]
    wide[pl.ds(0, total)] = vector_in[...].astype(F32)
    for group, n, (offset, shape) in wanted:
        first = offset // LANES
        window = [k for k, (f, e) in enumerate(windows) if f <= first < e][0]
        base = bases[window] + first - windows[window][0]
        for tile in range(-(-shape[0] // LANES)):
            value = wide[pl.ds(base + tile, 1)]
            if shape[0] - tile * LANES < LANES:
                value = jnp.where(lane < shape[0] - tile * LANES, value, 0.0)
            vector_refs[group][pl.ds(n, 1), pl.ds(tile * LANES, LANES)] = value
    for index, (number, start, depth, _, _) in enumerate(chunks):
        if start + 2 * depth >= matrices[number][1][0]:
            store(index).wait()


def weight_matrices(flat):
    rows = flat.shape[0] // 2
    matrices, enc_vectors, dec_vectors = matrix_plan(rows)
    shapes = [(shape[0], padded(shape[1])) for _, shape in matrices]
    buffers = []
    for (_, shape), (_, columns) in zip(matrices, shapes):
        depth = block_depth(shape)
        buffers.append(pltpu.VMEM((min(2, shape[0] // depth), depth, columns), BF16))
    dma = pltpu.SemaphoreType.DMA
    windows = 0
    last = -1
    total = 0
    for offset, shape in enc_vectors + dec_vectors:
        first = offset // LANES // 16 * 16
        end = -(-(offset // LANES + -(-shape[0] // LANES)) // 16) * 16
        if first <= last:
            total += max(0, end - last)
            last = max(last, end)
        else:
            windows += 1
            total += end - first
            last = end
    anywhere = pl.BlockSpec(memory_space=pl.ANY)
    vmem = pl.BlockSpec(memory_space=pltpu.VMEM)
    return pl.pallas_call(
        functools.partial(matrix_kernel, rows),
        out_shape=[jax.ShapeDtypeStruct(shape, BF16) for shape in shapes]
        + [jax.ShapeDtypeStruct((VEC_ROWS, columns), F32) for columns in VEC_COLS],
        in_specs=[anywhere],
        out_specs=[anywhere] * len(shapes) + [vmem, vmem],
        scratch_shapes=buffers
        + [
            pltpu.VMEM((SLOTS_IN, PIECE + 32, LANES), BF16),
            pltpu.VMEM((PIECE + 32, LANES), F32),
            pltpu.VMEM((padded(HEAD) // LANES, SUB, LANES), F32),
            pltpu.VMEM((total, LANES), BF16),
            dma((SLOTS_IN,)),
            dma((len(shapes), 2)),
            dma((windows,)),
        ],
        compiler_params=pltpu.CompilerParams(vmem_limit_bytes=56 * 2**20),
        name="weight_matrices",
    )(flat)


def stream_items(layout, lent):
    items = []
    offset = 0
    numbers = [0, 0]
    for shape in layout + lent:
        matrix = len(shape) == 2
        number = numbers[matrix]
        numbers[matrix] += 1
        depth = block_depth(shape) if matrix else 0
        for start in range(0, shape[0] if matrix else 1, max(depth, 1)):
            items.append((matrix, number, shape, start, depth, offset))
            offset += depth * shape[1] if matrix else shape[0]
    return items, offset


ROLES = (
    (ENC_LAYOUT, [], (0, 1, 2, 3)),
    (DEC_LAYOUT, LENT, (6, 7, 8, 9, 10, 4, 5)),
)
PAIRS = 11
FLIGHTS = 4
DEPTH = 1024


def factor_buffers(shapes):
    sizes = []
    places = {}
    for role in (1, 0):
        taken = set()
        for number in ROLES[role][2]:
            for side in range(2):
                length, columns = shapes[2 * number + side]
                fits = [
                    n
                    for n, size in enumerate(sizes)
                    if n not in taken and size[0] == 2 * length and size[1] >= columns
                ]
                if fits:
                    place = min(fits, key=lambda n: sizes[n][1])
                else:
                    place = len(sizes)
                    sizes.append((2 * length, columns))
                taken.add(place)
                places[role, number, side] = place
    return sizes, places


def product_kernel(rows, shapes, *refs):
    factors, vectors, out_ref = refs[: 2 * PAIRS], refs[2 * PAIRS : 2 * PAIRS + 2], refs[24]
    sizes, places = factor_buffers(shapes)
    buffers = refs[25 : 25 + len(sizes)]
    refs = refs[25 + len(sizes) :]
    others = refs[:2]
    turned_left, tall, rows_out, own_sem, send_sem, recv_sem, out_sem = refs[2:]
    core = lax.axis_index("grp")
    sibling = (1 - core, lax.axis_index("dp"))
    barrier = pltpu.get_barrier_semaphore()
    pl.semaphore_signal(barrier, inc=1, device_id=sibling, device_id_type=MESH)
    pl.semaphore_wait(barrier, 1)

    def half_of(role, number, side, part):
        length, columns = shapes[2 * number + side]
        buffer = buffers[places[role, number, side]]
        return buffer.at[pl.ds(part * length, length), pl.ds(0, columns)]

    def local(role, number, side):
        return pltpu.make_async_copy(
            factors[2 * number + side], half_of(role, number, side, 0), own_sem.at[number, side]
        )

    def remote(role, number, side):
        return pltpu.make_async_remote_copy(
            src_ref=factors[2 * number + side],
            dst_ref=half_of(role, number, side, 1),
            send_sem=send_sem.at[number, side],
            recv_sem=recv_sem.at[number, side],
            device_id=sibling,
            device_id_type=MESH,
        )

    def remote_vectors(role):
        return pltpu.make_async_remote_copy(
            src_ref=vectors[role],
            dst_ref=others[role],
            send_sem=send_sem.at[PAIRS, role],
            recv_sem=recv_sem.at[PAIRS, role],
            device_id=sibling,
            device_id_type=MESH,
        )

    def act(role):
        remote_vectors(1 - role).start()
        pending = [(number, side) for number in ROLES[role][2] for side in range(2)]
        for number, side in pending:
            local(role, number, side).start()
        given = [(number, side) for number in ROLES[1 - role][2] for side in range(2)]
        for number, side in given:
            remote(1 - role, number, side).start()
        remote_vectors(role).wait_recv()

        def ready(number):
            for side in range(2):
                local(role, number, side).wait()
                remote(role, number, side).wait_recv()

        lefts, rights = [], []
        for number in ROLES[role][2]:
            for side, views in ((0, lefts), (1, rights)):
                length, columns = shapes[2 * number + side]
                buffer = buffers[places[role, number, side]]
                views.append(buffer.at[pl.ds(0, 2 * length), pl.ds(0, columns)])
        fill_row(
            rows,
            ROLES[role],
            ready,
            lefts,
            rights,
            vectors[role],
            others[role],
            turned_left,
            tall,
            rows_out,
            out_ref,
            out_sem,
        )
        for number, side in given:
            remote(1 - role, number, side).wait_send()
        remote_vectors(1 - role).wait_send()

    for role in range(2):
        pl.when(core == role)(functools.partial(act, role))


def fill_row(
    rows,
    role,
    ready,
    lefts,
    rights,
    mine_ref,
    other_ref,
    turned_left,
    tall,
    rows_out,
    out_ref,
    out_sem,
):
    layout, lent, numbers = role
    lane = lax.broadcasted_iota(jnp.int32, (1, LANES), 1)
    half = LANES // 2
    items, used = stream_items(layout, lent)
    groups = []
    current = []
    for item in items:
        current.append(item)
        if item[0]:
            groups.append(current)
            current = []
    groups.append(current)

    def vector(item, buffer, base):
        _, number, shape, _, _, _ = item
        for tile in range(-(-shape[0] // LANES)):
            lanes = pl.ds(tile * LANES, LANES)
            buffer[pl.ds(base + tile, 1)] = (
                mine_ref[pl.ds(number, 1), lanes] + other_ref[pl.ds(number, 1), lanes]
            )

    def matrix(item, buffer, base):
        _, number, shape, start, depth, offset = item
        columns = shape[1]
        shifted = offset % LANES
        tiles = -(-columns // LANES)
        width = min(WIDTH, columns)
        if start == 0:
            ready(numbers[number])
            if shifted:
                length = rights[number].shape[0]

                def turn(i, carry):
                    block = pl.ds(pl.multiple_of(i * 64, 64), 64)
                    value = rights[number][block].astype(F32)
                    rights[number][block] = pltpu.roll(value, half, 1).astype(BF16)
                    return carry

                lax.fori_loop(0, length // 64, turn, 0)
        length = lefts[number].shape[0]
        sub = min(DEPTH, depth)

        def loop(step, carry):
            k = pl.multiple_of(start + step * sub, sub)
            turned_left[pl.ds(0, sub), pl.ds(0, length)] = lefts[number][:, pl.ds(k, sub)].T

            def across(c, carry):
                column = pl.multiple_of(c * width, width)
                value = jnp.dot(
                    turned_left[pl.ds(0, sub), pl.ds(0, length)],
                    rights[number][:, pl.ds(column, width)],
                    preferred_element_type=F32,
                )
                row = base + step * sub * tiles
                for piece in range(width // LANES):
                    part = value[:, piece * LANES : (piece + 1) * LANES]
                    tile = c * (width // LANES) + piece
                    if columns % LANES:
                        tall[tile, pl.ds(step * sub, sub)] = part
                    elif shifted and piece == 0:
                        first = row + tile

                        @pl.when(c == 0)
                        def _():
                            before = pltpu.roll(part, 1, 0)
                            index = lax.broadcasted_iota(jnp.int32, (sub, LANES), 0)
                            held = buffer[pl.ds(row, 1)]
                            before = jnp.where(index == 0, held, before)
                            merged = jnp.where(lane < half, before, part)
                            buffer[pl.ds(row, sub, stride=tiles)] = merged
                            buffer[pl.ds(row + sub * tiles, 1)] = part[sub - 1 :]

                        @pl.when(c > 0)
                        def _():
                            buffer[pl.ds(first, sub, stride=tiles)] = part
                    else:
                        buffer[pl.ds(row + tile, sub, stride=tiles)] = part
                return carry

            lax.fori_loop(0, tiles * LANES // width, across, 0)
            return carry

        lax.fori_loop(0, depth // sub, loop, 0)
        if columns % LANES:
            stride = 2 * columns // LANES
            pair = 64

            def weave(i, carry):
                k = pl.multiple_of(i * 2 * pair, 2 * pair)
                row = base + i * pair * stride
                evens = [tall[t, pl.ds(k, pair, stride=2)] for t in range(tiles)]
                odds = [tall[t, pl.ds(k + 1, pair, stride=2)] for t in range(tiles)]
                for t in range(tiles - 1):
                    buffer[pl.ds(row + t, pair, stride=stride)] = evens[t]
                middle = jnp.where(lane < half, evens[-1], pltpu.roll(odds[0], half, 1))
                buffer[pl.ds(row + tiles - 1, pair, stride=stride)] = middle
                for t in range(1, tiles):
                    both_halves = jnp.where(lane < half, odds[t], odds[t - 1])
                    buffer[pl.ds(row + tiles - 1 + t, pair, stride=stride)] = pltpu.roll(
                        both_halves, half, 1
                    )
                return carry

            lax.fori_loop(0, depth // 2 // pair, weave, 0)

    flights = []
    tail = None
    for number, group in enumerate(groups):
        slot = number % 2
        buffer = rows_out.at[slot]
        if number >= 2:
            for copy in flights[number - 2]:
                copy.wait()
        first = group[0][5] // LANES if group else used // LANES
        begin = first // 8 * 8
        if tail is not None:
            buffer[pl.ds(0, 8)] = rows_out[1 - slot, pl.ds(tail, 8)]
        for item in group:
            (matrix if item[0] else vector)(item, buffer, item[5] // LANES - begin)
        last = number == len(groups) - 1
        if last:
            at = used // LANES - begin
            if used % LANES:
                buffer[pl.ds(at, 1)] = jnp.where(lane < used % LANES, buffer[pl.ds(at, 1)], 0.0)
                at += 1
            length = rows - begin
            if length > at:
                buffer[pl.ds(at, length - at)] = jnp.zeros((length - at, LANES), F32)
        else:
            end = groups[number + 1][0][5] if groups[number + 1] else used
            tail = (end // LANES - begin) // 8 * 8
            length = tail
        cuts = [length * n // FLIGHTS // 8 * 8 for n in range(FLIGHTS)] + [length]
        flight = [
            pltpu.make_async_copy(
                buffer.at[pl.ds(lower, upper - lower)],
                out_ref.at[pl.ds(begin + lower, upper - lower)],
                out_sem.at[slot, n],
            )
            for n, (lower, upper) in enumerate(zip(cuts, cuts[1:]))
            if upper > lower
        ]
        for copy in flight:
            copy.start()
        flights.append(flight)
    for flight in flights[-2:]:
        for copy in flight:
            copy.wait()


def flat_gradient(rows, factors, enc_vectors, dec_vectors):
    shapes = [factor.shape for factor in factors]
    sizes, _ = factor_buffers(shapes)
    longest = max(length for length, _ in sizes)
    dma = pltpu.SemaphoreType.DMA
    anywhere = pl.BlockSpec(memory_space=pl.ANY)
    vmem = pl.BlockSpec(memory_space=pltpu.VMEM)
    return pl.pallas_call(
        functools.partial(product_kernel, rows, shapes),
        out_shape=jax.ShapeDtypeStruct((rows, LANES), F32),
        in_specs=[anywhere] * (2 * PAIRS) + [vmem, vmem],
        out_specs=anywhere,
        scratch_shapes=[pltpu.VMEM(size, BF16) for size in sizes]
        + [
            pltpu.VMEM(enc_vectors.shape, F32),
            pltpu.VMEM(dec_vectors.shape, F32),
            pltpu.VMEM((DEPTH, longest), BF16),
            pltpu.VMEM((padded(HEAD) // LANES, DD, LANES), F32),
            pltpu.VMEM((2, PIECE + 128, LANES), F32),
            dma((PAIRS, 2)),
            dma((PAIRS + 1, 2)),
            dma((PAIRS + 1, 2)),
            dma((2, FLIGHTS)),
        ],
        compiler_params=pltpu.CompilerParams(
            collective_id=2, has_side_effects=True, vmem_limit_bytes=63 * 2**20
        ),
        name="flat_gradient",
    )(*factors, enc_vectors, dec_vectors)


LN1_G, LN1_B, LN2_G, LN2_B, FC1_B, FC2_B, LNF_G, LNF_B, LAST_B = range(1, 10)
GROUP = 256
TURNS = 16
BATCH = 2


def dot(left, right):
    return jnp.dot(left, right, preferred_element_type=F32)


def dot_nt(left, right):
    return lax.dot_general(left, right, (((1,), (1,)), ((), ())), preferred_element_type=F32)


def dot_tn(left, right):
    return lax.dot_general(left, right, (((0,), (0,)), ((), ())), preferred_element_type=F32)


def blocks(length, size, action):
    def step(index, carry):
        action(pl.ds(pl.multiple_of(index * size, size), size))
        return carry

    lax.fori_loop(0, length // size, step, 0)


def row_step(length):
    return 208 if length % 208 == 0 else 128


def score_step(length):
    return 832 if length % 208 == 0 else 256


def normed(state):
    centered = state - jnp.mean(state, axis=-1, keepdims=True)
    inverse = lax.rsqrt(jnp.mean(centered * centered, axis=-1, keepdims=True) + NORM_EPS)
    return centered * inverse, inverse


def norm_rows(source, target, vectors, gain):
    width = source.shape[1]

    def one(rows):
        unit, _ = normed(source[rows])
        value = unit * vectors[pl.ds(gain, 1), pl.ds(0, width)]
        target[rows] = (value + vectors[pl.ds(gain + 1, 1), pl.ds(0, width)]).astype(BF16)

    blocks(source.shape[0], row_step(source.shape[0]), one)


def norm_rows_back(source, grad, vectors, sums, gain, finish):
    width = source.shape[1]
    lanes = pl.ds(0, width)

    def one(rows):
        unit, inverse = normed(source[rows])
        out = grad[rows]
        sums[pl.ds(gain, 1), lanes] += jnp.sum(out * unit, axis=0, keepdims=True)
        sums[pl.ds(gain + 1, 1), lanes] += jnp.sum(out, axis=0, keepdims=True)
        scaled = out * vectors[pl.ds(gain, 1), lanes]
        mean = jnp.mean(scaled, axis=-1, keepdims=True)
        along = jnp.mean(scaled * unit, axis=-1, keepdims=True)
        finish(rows, inverse * (scaled - mean - unit * along))

    blocks(source.shape[0], row_step(source.shape[0]), one)


def gelu_parts(value):
    below = 0.5 * (1.0 + lax.erf(value * math.sqrt(0.5)))
    return below, value * below


def head_masks(depth):
    lane = lax.broadcasted_iota(jnp.int32, (1, GROUP), 1)
    return [
        ((lane >= head * depth) & (lane < (head + 1) * depth)).astype(F32).astype(BF16)
        for head in range(GROUP // depth)
    ]


def stack_heads(target, value, masks):
    length = value.shape[0]
    for head, mask in enumerate(masks):
        target[pl.ds(head * length, length)] = value * mask


def attention_forward(images, length, heads, qkv, bias, attend, attend_low, stacked, mixed):
    width = mixed.shape[1]
    depth = width // heads
    masks = head_masks(depth)
    groups = width // GROUP
    scale = depth**-0.5

    def one(index, carry):
        image, group = index // groups, index % groups
        rows = pl.ds(pl.multiple_of(image * length, length), length)

        def lanes(part):
            return pl.ds(pl.multiple_of(part * width + group * GROUP, GROUP), GROUP)

        stack_heads(stacked, qkv[rows, lanes(0)], masks)
        attend[index] = dot_nt(stacked[...], qkv[rows, lanes(1)])
        shift = bias[pl.ds(image, 1)]

        def softmax(block):
            scores = attend[index, block] * scale + shift
            raised = jnp.exp(scores - jnp.max(scores, axis=-1, keepdims=True))
            value = raised / jnp.sum(raised, axis=-1, keepdims=True)
            attend[index, block] = value
            attend_low[block] = value.astype(BF16)

        blocks(len(masks) * length, score_step(length), softmax)
        value = qkv[rows, lanes(2)]
        total = jnp.zeros((length, GROUP), F32)
        for head, mask in enumerate(masks):
            total += dot(attend_low[pl.ds(head * length, length)], value * mask)
        mixed[rows, lanes(0)] = total.astype(BF16)
        return carry

    lax.fori_loop(0, images * groups, one, 0)


def attention_backward(
    images, length, heads, qkv, grad_mixed, attend, attend_low, grad_low, grads, stacked, other, out
):
    width = grad_mixed.shape[1]
    depth = width // heads
    masks = head_masks(depth)
    groups = width // GROUP
    scale = depth**-0.5

    def one(index, carry):
        image, group = index // groups, index % groups
        rows = pl.ds(pl.multiple_of(image * length, length), length)

        def lanes(part):
            return pl.ds(pl.multiple_of(part * width + group * GROUP, GROUP), GROUP)

        stack_heads(stacked, qkv[rows, lanes(0)], masks)
        stack_heads(other, grad_mixed[rows, lanes(0)], masks)
        grads[...] = dot_nt(other[...], qkv[rows, lanes(2)])

        def scores(block):
            value = attend[index, block]
            grad = grads[block]
            total = jnp.sum(grad * value, axis=-1, keepdims=True)
            grad_low[block] = (value * (grad - total)).astype(BF16)
            attend_low[block] = value.astype(BF16)

        blocks(len(masks) * length, score_step(length), scores)
        out[rows, lanes(2)] = dot_tn(attend_low[...], other[...]).astype(BF16)
        out[rows, lanes(1)] = (dot_tn(grad_low[...], stacked[...]) * scale).astype(BF16)
        key = qkv[rows, lanes(1)]
        total = jnp.zeros((length, GROUP), F32)
        for head, mask in enumerate(masks):
            total += dot(grad_low[pl.ds(head * length, length)], key * mask)
        out[rows, lanes(0)] = (total * scale).astype(BF16)
        return carry

    lax.fori_loop(0, images * groups, one, 0)


def columns_loop(columns, size, action):
    blocks(columns, min(size, columns), action)


def feed_forward(normed_two, fc1_w, fc2_w, vectors, middle, pre, active, state):
    bias = pl.ds(FC1_B, 1)

    def up(lanes):
        value = dot(normed_two[...], fc1_w[:, lanes]) + vectors[bias, lanes]
        pre[:, lanes] = value
        active[:, lanes] = gelu_parts(value)[1].astype(BF16)

    columns_loop(pre.shape[1], 256, up)

    def down(lanes):
        value = dot(active[...], fc2_w[:, lanes])
        state[:, lanes] = middle[:, lanes] + value + vectors[pl.ds(FC2_B, 1), lanes]

    columns_loop(state.shape[1], 256, down)


def feed_backward(grad_low, fc1_w, fc2_w, pre, sums, grad_pre, out):
    def up(lanes):
        value = pre[:, lanes]
        below, _ = gelu_parts(value)
        slope = below + value * (jnp.exp(-0.5 * value * value) * (1.0 / math.sqrt(2.0 * math.pi)))
        grad = dot_nt(grad_low[...], fc2_w[lanes]) * slope
        sums[pl.ds(FC1_B, 1), lanes] += jnp.sum(grad, axis=0, keepdims=True)
        grad_pre[:, lanes] = grad.astype(BF16)

    columns_loop(pre.shape[1], 256, up)

    def down(lanes):
        out[:, lanes] = dot_nt(grad_pre[...], fc1_w[lanes])

    columns_loop(out.shape[1], 256, down)


def turn_code(places, table):
    lane = lax.broadcasted_iota(jnp.int32, (places.shape[0], TURNS), 1)
    passed = (lane > 0) & (lane < TURNS - 1) & (places >= lane * GSIDE)
    row = jnp.sum(passed.astype(F32), axis=1, keepdims=True).astype(jnp.int32)
    parts = []
    for pick in (row, places - row * GSIDE):
        chosen = (lane == pick).astype(F32)
        parts.append(jnp.dot(chosen, table, precision=HIGHEST, preferred_element_type=F32))
    return jnp.concatenate(parts, axis=1)


def decoder_kernel(
    sent,
    pixels,
    spot_rows,
    spot_columns,
    table,
    masked_ref,
    bands_w,
    vectors,
    qkv_w,
    out_w,
    fc1_w,
    fc2_w,
    head_w,
    normed_one,
    grad_qkv,
    mixed,
    grad_middle_low,
    normed_two,
    grad_pre,
    active,
    grad_out_low,
    normed_last,
    grad_predicted,
    grad_sent,
    sums,
    loss,
    seen,
    bias,
    state,
    middle,
    last,
    grad,
    spare,
    qkv,
    pre,
    attend,
    attend_low,
    scores_low,
    scores_grad,
    stacked,
    other,
    grad_mixed,
):
    width = state.shape[1]
    lanes = pl.ds(0, width)

    @pl.when(pl.program_id(0) == 0)
    def _():
        sums[...] = jnp.zeros_like(sums)
        loss[...] = jnp.zeros_like(loss)

    grid = lax.broadcasted_iota(jnp.int32, (GPAD, 1), 0)
    key = lax.broadcasted_iota(jnp.int32, (1, GPAD), 1)
    token = vectors[pl.ds(0, 1), lanes]
    for image in range(BATCH):
        rows = pl.ds(image * GPAD, GPAD)
        chosen = (grid == spot_rows[image]).astype(F32)
        shown = jnp.sum(chosen, axis=1, keepdims=True)
        placed = dot(chosen.astype(BF16), sent[pl.ds(image * VMAX, VMAX)])
        seen[rows] = jnp.where(grid < GRID, shown, 1.0)
        code = turn_code(grid, table[image])
        state[rows] = jnp.where(shown > 0.5, placed, token) + code
        bias[pl.ds(image, 1)] = jnp.where(key < GRID, 0.0, MASK_FILL)

    norm_rows(state, normed_one, vectors, LN1_G)

    def project(part):
        qkv[:, part] = dot(normed_one[...], qkv_w[:, part]).astype(BF16)

    columns_loop(qkv.shape[1], 256, project)
    attention_forward(
        BATCH, GPAD, HD, qkv, bias, attend, attend_low, stacked, mixed
    )

    def output(part):
        middle[:, part] = state[:, part] + dot(mixed[...], out_w[:, part])

    columns_loop(width, 256, output)
    norm_rows(middle, normed_two, vectors, LN2_G)
    feed_forward(normed_two, fc1_w, fc2_w, vectors, middle, pre, active, last)
    norm_rows(last, normed_last, vectors, LNF_G)

    weight = 1.0 / masked_ref[pl.ds(0, 1), pl.ds(0, 1)]

    def predict(part):
        value = dot(normed_last[...], head_w[:, part]) + vectors[pl.ds(LAST_B, 1), part]
        miss = value - dot(pixels[...], bands_w[:, part])
        index = lax.broadcasted_iota(jnp.int32, (1, GROUP), 1) + part.start
        low = index < LOWPIX
        square = miss * miss
        root = jnp.sqrt(square + 1.0)
        unseen = 1.0 - seen[...]
        loss[...] += jnp.sum(jnp.where(low, square, root - 1.0) * unseen).reshape(1, 1)
        slope = jnp.where(low, 2.0 * miss, miss / root) * (unseen * weight)
        rounded = slope.astype(BF16)
        grad_predicted[:, part] = rounded
        sums[pl.ds(LAST_B, 1), part] += jnp.sum(rounded.astype(F32), axis=0, keepdims=True)

    columns_loop(head_w.shape[1], GROUP, predict)

    def head_back(part):
        spare[:, part] = dot_nt(grad_predicted[...], head_w[part])

    columns_loop(width, 256, head_back)

    def last_back(rows, value):
        grad[rows] = value
        grad_out_low[rows] = value.astype(BF16)
        sums[pl.ds(FC2_B, 1), lanes] += jnp.sum(value, axis=0, keepdims=True)

    norm_rows_back(last, spare, vectors, sums, LNF_G, last_back)
    block_backward(
        BATCH,
        GPAD,
        HD,
        (qkv_w, out_w, fc1_w, fc2_w),
        vectors,
        sums,
        (state, middle, grad, spare, pre, qkv),
        (grad_out_low, grad_pre, grad_middle_low, grad_mixed, grad_qkv),
        (attend, attend_low, scores_low, scores_grad, stacked, other),
    )
    unseen = 1.0 - seen[...]
    sums[pl.ds(0, 1), lanes] += jnp.sum(grad[...] * unseen, axis=0, keepdims=True)
    for image in range(BATCH):
        chosen = (spot_columns[pl.ds(image * VMAX, VMAX)] == key).astype(F32).astype(BF16)
        value = dot(chosen, grad[pl.ds(image * GPAD, GPAD)].astype(BF16))
        grad_sent[pl.ds(image * VMAX, VMAX)] = value.astype(BF16)


def block_backward(images, length, heads, weights, vectors, sums, states, lows, scratch):
    qkv_w, out_w, fc1_w, fc2_w = weights
    state, middle, grad, spare, pre, qkv = states
    grad_out_low, grad_pre, grad_middle_low, grad_mixed, grad_qkv = lows
    attend, attend_low, scores_low, scores_grad, stacked, other = scratch
    width = state.shape[1]
    feed_backward(grad_out_low, fc1_w, fc2_w, pre, sums, grad_pre, spare)

    def middle_back(rows, value):
        total = grad[rows] + value
        grad[rows] = total
        grad_middle_low[rows] = total.astype(BF16)

    norm_rows_back(middle, spare, vectors, sums, LN2_G, middle_back)

    def mixed_back(part):
        grad_mixed[:, part] = dot_nt(grad_middle_low[...], out_w[part]).astype(BF16)

    columns_loop(width, 256, mixed_back)
    attention_backward(
        images,
        length,
        heads,
        qkv,
        grad_mixed,
        attend,
        attend_low,
        scores_low,
        scores_grad,
        stacked,
        other,
        grad_qkv,
    )

    def first_back(part):
        spare[:, part] = dot_nt(grad_qkv[...], qkv_w[part])

    columns_loop(width, 256, first_back)

    def state_back(rows, value):
        grad[rows] = grad[rows] + value

    norm_rows_back(state, spare, vectors, sums, LN1_G, state_back)


def decoder(sent, pixels, spots, tables, masked_tile, vectors, weights):
    images = spots.shape[0]
    rows = BATCH * GPAD
    shown = BATCH * VMAX
    stack = GROUP // (DD // HD) * GPAD
    widths = [DD, 3 * DD, DD, DD, DD, FD, FD, DD, DD, padded(HEAD)]
    whole = lambda array: pl.BlockSpec(array.shape, lambda i: (0,) * array.ndim)
    by_rows = lambda length, columns: pl.BlockSpec((length, columns), lambda i: (i, 0))
    bands_w = band_matrix()
    out_shape = [jax.ShapeDtypeStruct((images * GPAD, columns), BF16) for columns in widths]
    out_shape.append(jax.ShapeDtypeStruct((images * VMAX, DD), BF16))
    out_shape.append(jax.ShapeDtypeStruct((VEC_ROWS, VEC_COLS[1]), F32))
    out_shape.append(jax.ShapeDtypeStruct((1, 1), F32))
    operands = [masked_tile, bands_w, vectors, *weights]
    f32 = lambda *shape: pltpu.VMEM(shape, F32)
    b16 = lambda *shape: pltpu.VMEM(shape, BF16)
    return pl.pallas_call(
        decoder_kernel,
        grid=(images // BATCH,),
        out_shape=out_shape,
        in_specs=[
            by_rows(shown, DD),
            by_rows(rows, PIX),
            pl.BlockSpec((BATCH, 1, VMAX), lambda i: (i, 0, 0)),
            by_rows(shown, 1),
            pl.BlockSpec((BATCH, TURNS, DD // 2), lambda i: (i, 0, 0)),
        ]
        + [whole(operand) for operand in operands],
        out_specs=[by_rows(rows, columns) for columns in widths]
        + [by_rows(shown, DD)]
        + [pl.BlockSpec(shape.shape, lambda i: (0, 0)) for shape in out_shape[-2:]],
        scratch_shapes=[
            f32(rows, 1),
            f32(BATCH, GPAD),
            f32(rows, DD),
            f32(rows, DD),
            f32(rows, DD),
            f32(rows, DD),
            f32(rows, DD),
            b16(rows, 3 * DD),
            f32(rows, FD),
            f32(BATCH * DD // GROUP, stack, GPAD),
            b16(stack, GPAD),
            b16(stack, GPAD),
            f32(stack, GPAD),
            b16(stack, GROUP),
            b16(stack, GROUP),
            b16(rows, DD),
        ],
        compiler_params=pltpu.CompilerParams(vmem_limit_bytes=62 * 2**20),
        name="decoder",
    )(sent, pixels, spots.reshape(images, 1, VMAX), spots.reshape(-1, 1), tables, *operands)


def encoder_forward_kernel(
    pixels,
    spot_rows,
    spot_columns,
    table,
    vectors,
    pe_hbm,
    qkv_hbm,
    out_hbm,
    fc1_hbm,
    fc2_hbm,
    emb_hbm,
    sent,
    patches,
    state,
    normed_one,
    qkv,
    mixed,
    middle,
    normed_two,
    pre,
    active,
    last,
    normed_last,
    attend,
    pe_w,
    qkv_w,
    out_w,
    fc1_w,
    fc2_w,
    emb_w,
    bias,
    attend_low,
    stacked,
    sems,
):
    pairs = [
        (pe_hbm, pe_w),
        (qkv_hbm, qkv_w),
        (out_hbm, out_w),
        (fc1_hbm, fc1_w),
        (fc2_hbm, fc2_w),
        (emb_hbm, emb_w),
    ]
    copies = [pltpu.make_async_copy(*pair, sems.at[n]) for n, pair in enumerate(pairs)]
    for copy in copies:
        copy.start()
    images = spot_rows.shape[0]
    key = lax.broadcasted_iota(jnp.int32, (1, GPAD), 1)
    for image in range(images):
        rows = pl.ds(image * VMAX, VMAX)
        place = spot_columns[rows]
        chosen = (place == key).astype(F32).astype(BF16)
        patches[rows] = dot(chosen, pixels[pl.ds(image * GPAD, GPAD)]).astype(BF16)
        code = turn_code(jnp.maximum(place, 0), table[image])
        state[rows] = code + vectors[pl.ds(0, 1), pl.ds(0, DE)]
        bias[pl.ds(image, 1)] = jnp.where(spot_rows[image] < 0, MASK_FILL, 0.0)
    copies[0].wait()

    def embed(part):
        state[:, part] += dot(patches[...], pe_w[:, part])

    columns_loop(DE, 256, embed)
    norm_rows(state, normed_one, vectors, LN1_G)
    copies[1].wait()

    def project(part):
        qkv[:, part] = dot(normed_one[...], qkv_w[:, part]).astype(BF16)

    columns_loop(3 * DE, 256, project)
    attention_forward(images, VMAX, HE, qkv, bias, attend, attend_low, stacked, mixed)
    copies[2].wait()

    def output(part):
        middle[:, part] = state[:, part] + dot(mixed[...], out_w[:, part])

    columns_loop(DE, 256, output)
    norm_rows(middle, normed_two, vectors, LN2_G)
    copies[3].wait()
    copies[4].wait()
    feed_forward(normed_two, fc1_w, fc2_w, vectors, middle, pre, active, last)
    norm_rows(last, normed_last, vectors, LNF_G)
    copies[5].wait()
    value = dot(normed_last[...], emb_w[...]) + vectors[pl.ds(LAST_B, 1), pl.ds(0, DD)]
    sent[...] = value.astype(BF16)


def encoder_forward(pixels, spots, tables, vectors, weights):
    images = spots.shape[0]
    rows = images * VMAX
    stack = GROUP // (DE // HE) * VMAX
    anywhere = pl.BlockSpec(memory_space=pl.ANY)
    vmem = pl.BlockSpec(memory_space=pltpu.VMEM)
    kept = [
        (DD, BF16),
        (PIX, BF16),
        (DE, F32),
        (DE, BF16),
        (3 * DE, BF16),
        (DE, BF16),
        (DE, F32),
        (DE, BF16),
        (FE, F32),
        (FE, BF16),
        (DE, F32),
        (DE, BF16),
    ]
    out_shape = [jax.ShapeDtypeStruct((rows, columns), kind) for columns, kind in kept]
    out_shape.append(jax.ShapeDtypeStruct((images * DE // GROUP, stack, VMAX), F32))
    return pl.pallas_call(
        encoder_forward_kernel,
        out_shape=out_shape,
        in_specs=[vmem] * 5 + [anywhere] * 6,
        out_specs=[vmem] * len(out_shape),
        scratch_shapes=[pltpu.VMEM(weight.shape, BF16) for weight in weights]
        + [
            pltpu.VMEM((images, VMAX), F32),
            pltpu.VMEM((stack, VMAX), BF16),
            pltpu.VMEM((stack, GROUP), BF16),
            pltpu.SemaphoreType.DMA((6,)),
        ],
        compiler_params=pltpu.CompilerParams(vmem_limit_bytes=60 * 2**20),
        name="encoder_forward",
    )(pixels, spots.reshape(images, 1, VMAX), spots.reshape(-1, 1), tables, vectors, *weights)


def encoder_backward_kernel(
    grad_sent,
    vectors,
    state,
    qkv,
    middle,
    pre,
    last,
    attend,
    qkv_hbm,
    out_hbm,
    fc1_hbm,
    fc2_hbm,
    emb_hbm,
    grad_state_low,
    grad_qkv,
    grad_middle_low,
    grad_pre,
    grad_out_low,
    sums,
    qkv_w,
    out_w,
    fc1_w,
    fc2_w,
    emb_w,
    grad,
    spare,
    grad_mixed,
    attend_low,
    scores_low,
    scores_grad,
    stacked,
    other,
    sems,
):
    pairs = [
        (emb_hbm, emb_w),
        (fc2_hbm, fc2_w),
        (fc1_hbm, fc1_w),
        (out_hbm, out_w),
        (qkv_hbm, qkv_w),
    ]
    copies = [pltpu.make_async_copy(*pair, sems.at[n]) for n, pair in enumerate(pairs)]
    for copy in copies:
        copy.start()
    lanes = pl.ds(0, DE)
    sums[...] = jnp.zeros_like(sums)
    summed = jnp.sum(grad_sent[...].astype(F32), axis=0, keepdims=True)
    sums[pl.ds(LAST_B, 1), pl.ds(0, DD)] = summed
    copies[0].wait()

    def sent_back(part):
        spare[:, part] = dot_nt(grad_sent[...], emb_w[part])

    columns_loop(DE, 256, sent_back)

    def last_back(rows, value):
        grad[rows] = value
        grad_out_low[rows] = value.astype(BF16)
        sums[pl.ds(FC2_B, 1), lanes] += jnp.sum(value, axis=0, keepdims=True)

    norm_rows_back(last, spare, vectors, sums, LNF_G, last_back)
    for copy in copies[1:]:
        copy.wait()
    block_backward(
        state.shape[0] // VMAX,
        VMAX,
        HE,
        (qkv_w, out_w, fc1_w, fc2_w),
        vectors,
        sums,
        (state, middle, grad, spare, pre, qkv),
        (grad_out_low, grad_pre, grad_middle_low, grad_mixed, grad_qkv),
        (attend, attend_low, scores_low, scores_grad, stacked, other),
    )

    def first(rows):
        value = grad[rows]
        sums[pl.ds(0, 1), lanes] += jnp.sum(value, axis=0, keepdims=True)
        grad_state_low[rows] = value.astype(BF16)

    blocks(grad.shape[0], row_step(grad.shape[0]), first)


def encoder_backward(grad_sent, vectors, kept, weights):
    state, qkv, middle, pre, last, attend = kept
    rows = state.shape[0]
    stack = attend.shape[1]
    anywhere = pl.BlockSpec(memory_space=pl.ANY)
    vmem = pl.BlockSpec(memory_space=pltpu.VMEM)
    out_shape = [
        jax.ShapeDtypeStruct((rows, columns), BF16) for columns in (DE, 3 * DE, DE, FE, DE)
    ]
    out_shape.append(jax.ShapeDtypeStruct((VEC_ROWS, VEC_COLS[0]), F32))
    f32 = lambda *shape: pltpu.VMEM(shape, F32)
    b16 = lambda *shape: pltpu.VMEM(shape, BF16)
    return pl.pallas_call(
        encoder_backward_kernel,
        out_shape=out_shape,
        in_specs=[vmem] * 8 + [anywhere] * 5,
        out_specs=[vmem] * len(out_shape),
        scratch_shapes=[pltpu.VMEM(weight.shape, BF16) for weight in weights]
        + [
            f32(rows, DE),
            f32(rows, DE),
            b16(rows, DE),
            b16(stack, VMAX),
            b16(stack, VMAX),
            f32(stack, VMAX),
            b16(stack, GROUP),
            b16(stack, GROUP),
            pltpu.SemaphoreType.DMA((5,)),
        ],
        compiler_params=pltpu.CompilerParams(vmem_limit_bytes=60 * 2**20),
        name="encoder_backward",
    )(grad_sent, vectors, state, qkv, middle, pre, last, attend, *weights)


def band_matrix():
    ids = jnp.arange(PIX, dtype=jnp.int32)
    coarse = (ids // (3 * PSIDE) // 2 * (PSIDE // 2) + ids // 3 % PSIDE // 2) * 3 + ids % 3
    low = jnp.where(coarse[:, None] == jnp.arange(LOWPIX, dtype=jnp.int32)[None], 0.25, 0.0)
    same = jnp.where(coarse[:, None] == coarse[None], 0.25, 0.0)
    high = jnp.where(ids[:, None] == ids[None], 1.0, 0.0) - same
    rest = jnp.zeros((PIX, padded(HEAD) - HEAD), F32)
    return jnp.concatenate([low, high, rest], axis=1).astype(BF16)


def turn_table(scales, width):
    quarter = width // 4
    frequency = jnp.exp(jnp.arange(quarter, dtype=F32) * (-math.log(10000.0) / quarter))
    angle = (jnp.arange(TURNS, dtype=F32)[None] * scales[:, None])[..., None] * frequency
    return jnp.concatenate([jnp.sin(angle), jnp.cos(angle)], axis=-1)


def forward_backward(parts, pixels, index_rows, counts, scales, masked_tile):
    pe_w, qkv_w, fc1_w, emb_w, out_w, fc2_w = parts[:6]
    dec_weights = parts[6:11]
    enc_vectors, dec_vectors = parts[11:]
    images = counts.shape[0]
    valid = jnp.arange(VMAX, dtype=jnp.int32)[None, :] < counts[:, None]
    spots = jnp.where(valid, index_rows, -1)
    pixels = jnp.pad(pixels.reshape(images, GRID, PIX), ((0, 0), (0, GPAD - GRID), (0, 0)))
    pixels = pixels.reshape(images * GPAD, PIX)
    (
        sent,
        patches,
        state,
        normed_one,
        qkv,
        mixed,
        middle,
        normed_two,
        pre,
        active,
        last,
        normed_last,
        attend,
    ) = encoder_forward(
        pixels,
        spots,
        turn_table(scales, DE),
        enc_vectors,
        [pe_w, qkv_w, out_w, fc1_w, fc2_w, emb_w],
    )
    *dec_factors, grad_sent, dec_sums, loss = decoder(
        sent, pixels, spots, turn_table(scales, DD), masked_tile, dec_vectors, dec_weights
    )
    grad_state, grad_qkv, grad_middle, grad_pre, grad_out, enc_sums = encoder_backward(
        grad_sent,
        enc_vectors,
        [state, qkv, middle, pre, last, attend],
        [qkv_w, out_w, fc1_w, fc2_w, emb_w],
    )
    factors = [patches, grad_state, normed_one, grad_qkv, normed_two, grad_pre]
    factors += [normed_last, grad_sent, mixed, grad_middle, active, grad_out]
    return factors + dec_factors, enc_sums, dec_sums, loss[0, 0]


def clip_scale(squares):
    return jnp.minimum(1.0, CLIP / jnp.sqrt(squares))


def body(
    params, first_moment, second_moment, average, pixels, visible_index, visible_count, gsd_id
):
    chips = lax.axis_size("dp")
    rows = params.shape[1] // LANES
    special = chips == math.prod(DP_GRID) and rows % 4 == 0
    masked = jnp.sum(GRID - visible_count).astype(F32)
    if special:
        shards = [a.reshape(-1, 4, LANES) for a in (params, first_moment, second_moment, average)]
        copies, masked_tile = gather_rows(shards[0], jnp.full((8, LANES), masked))
    else:
        copies = lax.all_gather(params.astype(BF16).reshape(-1, LANES), "dp", axis=0, tiled=True)
        copies = lax.all_gather(copies, "grp", axis=0, tiled=True)
        masked_tile = jnp.full((8, LANES), lax.psum(masked, "dp"))
    parts = weight_matrices(copies.reshape(-1, LANES))

    half = visible_count.shape[0] // 2
    core = lax.axis_index("grp")

    def mine(array, count):
        return lax.dynamic_slice_in_dim(array, core * count, count, 0)

    scales = 0.5 + 0.25 * mine(gsd_id, half).astype(F32)
    factors, enc_sums, dec_sums, loss_local = forward_backward(
        parts,
        mine(pixels, half * GRID),
        mine(visible_index, half),
        mine(visible_count, half),
        scales,
        masked_tile,
    )
    gradient = flat_gradient(chips * rows, factors, enc_sums, dec_sums)
    if special:
        owned, sums = scatter_sums(
            gradient.reshape(chips, rows // 4, 4, LANES), jnp.full((8, LANES), loss_local)
        )
        squares = jnp.sum(sums[:4])
        loss_sum = sums[4, 0]
        outs = update(clip_scale(squares), [owned] + shards)
        outs = [out.reshape(params.shape) for out in outs]
    else:
        owned = lax.psum_scatter(gradient, "dp", scatter_dimension=0, tiled=True)
        owned = owned.reshape(params.shape)
        squares, loss_sum = lax.psum((jnp.sum(owned * owned), loss_local), ("grp", "dp"))
        outs = update_values(owned, clip_scale(squares), params, first_moment, second_moment, average)
    return (*outs, loss_sum, masked_tile[0, 0], jnp.sqrt(squares))


def solution(mesh):
    return jax.shard_map(
        body,
        mesh=mesh,
        in_specs=(P("grp", "dp"),) * 4 + (P("dp", None), P("dp", None), P("dp"), P("dp")),
        out_specs=(P("grp", "dp"),) * 4 + (P(), P(), P()),
        check_vma=False,
    )
```

```python
import functools
import math

import jax
import jax.numpy as jnp
import ml_dtypes
import numpy as np
from jax import lax
from jax.experimental import pallas as pl
from jax.experimental.pallas import tpu as pltpu
from jax.sharding import PartitionSpec as P

DE = 1024
HE = 16
FE = 4096
DD = 512
HD = 16
FD = 2048
PSIDE = 16
GSIDE = 14
VMAX = 64
STEP = 10
PIX = 768
LOWPIX = 192
GRID = 196
GPAD = 208
NENC = 8662528
NDEC = 3644352
LANES = 128
UNIT = 4 * LANES

HIGHEST = lax.Precision.HIGHEST
CLIP = 0.05
RATE = 0.01
BETA_ONE = 0.5
BETA_TWO = 0.5
ADAM_EPS = 1e-08
DECAY_WEIGHT = 0.05
AVERAGE_KEEP = 0.9
NORM_EPS = 1e-06
MASK_FILL = -1000000000.0
F32 = jnp.float32
BF16 = jnp.bfloat16
MESH = pl.DeviceIdType.MESH

WIDTH = 512
SUB = 64
PIECE = 8192
VEC_ROWS = 16
VEC_COLS = (FE, FD)
HEAD = LOWPIX + PIX

ENC_LAYOUT = [
    (PIX, DE),
    (DE,),
    (DE,),
    (DE,),
    (DE, 3 * DE),
    (DE,),
    (DE,),
    (DE, FE),
    (FE,),
    (DE,),
    (DE,),
    (DE,),
    (DE, DD),
    (DD,),
]
DEC_LAYOUT = [
    (DD,),
    (DD,),
    (DD,),
    (DD, 3 * DD),
    (DD, DD),
    (DD,),
    (DD,),
    (DD, FD),
    (FD,),
    (FD, DD),
    (DD,),
    (DD,),
    (DD,),
    (DD, HEAD),
    (HEAD,),
]
LENT = [(DE, DE), (FE, DE)]


DP_GRID = (4, 2, 2)
YZX, XZY, ZXY = ("y", "z", "x"), ("x", "z", "y"), ("z", "x", "y")
SPLIT = 2
ORDERS = (YZX,) * SPLIT + (XZY,) * SPLIT + (ZXY,) * SPLIT
PARTS = len(ORDERS)
OWN_FIRST = tuple(range(2 * SPLIT, 3 * SPLIT)) + tuple(range(2 * SPLIT))
SHARES = (0.41, 0.26, 0.33)
WAYS = ("x", "y", "up", "down")
CHUNK = 64
AXIS_SIZE = {"z": 4, "y": 2, "x": 2}
OPPOSITE = {"x": "x", "y": "y", "up": "down", "down": "up"}


def part_ranges(units):
    ends = [0]
    for share in SHARES:
        for _ in range(SPLIT):
            ends.append(ends[-1] + share / SPLIT)
    ends = [round(end * units) for end in ends[:-1]] + [units]
    return [(start, end - start) for start, end in zip(ends, ends[1:])]


def relatives():
    places = [(dz, dy, dx) for dz in range(-3, 4) for dy in (0, 1) for dx in (0, 1)]
    places.remove((0, 0, 0))
    return sorted(places, key=lambda r: abs(r[0]) + r[1] + r[2])


def last_axis(order, place):
    differs = {"z": place[0] != 0, "y": place[1] != 0, "x": place[2] != 0}
    return [axis for axis in order if differs[axis]][-1]


def onward(order, place):
    if place == (0, 0, 0):
        return ["up", "down", "x", "y"]
    axis = last_axis(order, place)
    ways = []
    if axis == "z":
        ways.append("up" if place[0] < 0 else "down")
    for later in order[order.index(axis) + 1 :]:
        ways += ["up", "down"] if later == "z" else [later]
    return ways


def when(condition, action):
    if condition is None:
        action()
    else:
        pl.when(condition)(action)


def both(left, right):
    if left is None:
        return right
    return left if right is None else left & right


class Spot:
    def __init__(self):
        self.grp = lax.axis_index("grp")
        self.dp = lax.axis_index("dp")
        self.x = self.dp % 2
        self.y = (self.dp // 2) % 2
        self.z = self.dp // 4
        self.neighbour = {
            "x": (self.grp, self.index(self.z, self.y, 1 - self.x)),
            "y": (self.grp, self.index(self.z, 1 - self.y, self.x)),
            "up": (self.grp, self.index(jnp.minimum(self.z + 1, 3), self.y, self.x)),
            "down": (self.grp, self.index(jnp.maximum(self.z - 1, 0), self.y, self.x)),
            "core": (1 - self.grp, self.dp),
        }
        self.exists = {"x": None, "y": None, "up": self.z < 3, "down": self.z > 0, "core": None}

    def index(self, z, y, x):
        return z * 4 + y * 2 + x

    def at(self, place):
        z = self.z + place[0]
        y = 1 - self.y if place[1] else self.y
        x = 1 - self.x if place[2] else self.x
        inside = None if place[0] == 0 else (z >= 0) & (z <= 3)
        return z, self.index(z, y, x), inside

    def greet(self, everyone):
        barrier = pltpu.get_barrier_semaphore()

        def signal(step, carry):
            pl.semaphore_signal(
                barrier, inc=1, device_id=self.partner(step, everyone), device_id_type=MESH
            )
            return carry

        lax.fori_loop(1, 32 if everyone else 16, signal, 0)
        if not everyone:
            sibling = self.neighbour["core"]
            pl.semaphore_signal(barrier, inc=1, device_id=sibling, device_id_type=MESH)

    def await_all(self, everyone):
        pl.semaphore_wait(pltpu.get_barrier_semaphore(), 31 if everyone else 16)

    def number(self, everyone):
        return self.grp * 16 + self.dp if everyone else self.dp

    def partner(self, step, everyone):
        if everyone:
            other = (self.number(True) + step) % 32
            return (other // 16, other % 16)
        return (self.grp, (self.dp + step) % 16)


def tell_all(spot, tiles, send_sem, recv_sem, everyone):
    me = spot.number(everyone)
    count = 32 if everyone else 16

    def copy(number, other, target):
        return pltpu.make_async_remote_copy(
            src_ref=tiles.at[number],
            dst_ref=tiles.at[number],
            send_sem=send_sem.at[other],
            recv_sem=recv_sem.at[number],
            device_id=target,
            device_id_type=MESH,
        )

    def start(step, carry):
        copy(me, (me + step) % count, spot.partner(step, everyone)).start()
        return carry

    def finish(step, carry):
        other = (me + step) % count
        copy(other, other, spot.partner(step, everyone)).wait_recv()
        copy(me, other, spot.partner(step, everyone)).wait_send()
        return carry

    return (
        lambda: lax.fori_loop(1, count, start, 0),
        lambda: lax.fori_loop(1, count, finish, 0),
    )


def gather_kernel(
    master_ref,
    masked_ref,
    out_ref,
    masked_out,
    master,
    own_ref,
    tiles,
    local_sem,
    send_sem,
    recv_sem,
    core_send,
    core_recv,
    tile_send,
    tile_recv,
):
    spot = Spot()
    read = pltpu.make_async_copy(master_ref, master, local_sem)
    read.start()
    tiles[spot.dp] = masked_ref[...]
    spot.greet(False)
    tell, told = tell_all(spot, tiles, tile_send, tile_recv, False)
    ranges = part_ranges(own_ref.shape[0])
    read.wait()

    def round_off(start, length):
        def one(first, count):
            block = pl.ds(first, count)
            own_ref[block] = master[block].astype(BF16)

        def step(index, carry):
            one(start + index * CHUNK, CHUNK)
            return carry

        lax.fori_loop(0, length // CHUNK, step, 0)
        if length % CHUNK:
            one(start + length - length % CHUNK, length % CHUNK)

    def copy(part, source, way, from_own):
        target = out_ref.at[spot.grp, source, pl.ds(*ranges[part])]
        origin = own_ref.at[pl.ds(*ranges[part])] if from_own else target
        if way == "core":
            sems = (core_send.at[part, source], core_recv.at[part, source])
        else:
            sems = (send_sem.at[part, source, WAYS.index(way)], recv_sem.at[part, source])
        return pltpu.make_async_remote_copy(
            src_ref=origin,
            dst_ref=target,
            send_sem=sems[0],
            recv_sem=sems[1],
            device_id=spot.neighbour[way],
            device_id_type=MESH,
        )

    sent = []
    for part in OWN_FIRST:
        round_off(*ranges[part])
        if part == OWN_FIRST[0]:
            spot.await_all(False)
        for way in onward(ORDERS[part], (0, 0, 0)):
            when(
                spot.exists[way],
                lambda part=part, way=way: copy(part, spot.dp, way, True).start(),
            )
            sent.append((part, spot.dp, way, spot.exists[way], True))
    local = pltpu.make_async_copy(own_ref, out_ref.at[spot.grp, spot.dp], local_sem)
    local.start()
    tell()
    for part in range(PARTS):
        copy(part, spot.dp, "core", True).start()
        sent.append((part, spot.dp, "core", None, True))
    for place in relatives():
        _, source, inside = spot.at(place)
        for part in range(PARTS):
            ways = onward(ORDERS[part], place)

            def pass_on(part=part, source=source, ways=ways):
                copy(part, source, "x", False).wait_recv()
                for way in ways:
                    when(
                        spot.exists[way],
                        lambda way=way: copy(part, source, way, False).start(),
                    )
                copy(part, source, "core", False).start()

            when(inside, pass_on)
            for way in ways + ["core"]:
                sent.append((part, source, way, both(inside, spot.exists[way]), False))
    for part, source, way, condition, from_own in sent:
        when(condition, lambda: copy(part, source, way, from_own).wait_send())

    def await_core(source, carry):
        for part in range(PARTS):
            landed = out_ref.at[1 - spot.grp, source, pl.ds(*ranges[part])]
            pltpu.make_async_remote_copy(
                src_ref=landed,
                dst_ref=landed,
                send_sem=core_send.at[part, source],
                recv_sem=core_recv.at[part, source],
                device_id=spot.neighbour["core"],
                device_id_type=MESH,
            ).wait_recv()
        return carry

    lax.fori_loop(0, 16, await_core, 0)
    told()
    masked_out[...] = jnp.sum(tiles[...], axis=0)
    local.wait()


def gather_rows(master, masked):
    units = master.shape[0]
    dma = pltpu.SemaphoreType.DMA
    anywhere = pl.BlockSpec(memory_space=pl.ANY)
    vmem = pl.BlockSpec(memory_space=pltpu.VMEM)
    return pl.pallas_call(
        gather_kernel,
        out_shape=(
            jax.ShapeDtypeStruct((2, 16, units, 4, LANES), BF16),
            jax.ShapeDtypeStruct((8, LANES), F32),
        ),
        in_specs=[anywhere, vmem],
        out_specs=(anywhere, vmem),
        scratch_shapes=[
            pltpu.VMEM((units, 4, LANES), F32),
            pltpu.VMEM((units, 4, LANES), BF16),
            pltpu.VMEM((16, 8, LANES), F32),
            dma,
            dma((PARTS, 16, 4)),
            dma((PARTS, 16)),
            dma((PARTS, 16)),
            dma((PARTS, 16)),
            dma((16,)),
            dma((16,)),
        ],
        compiler_params=pltpu.CompilerParams(collective_id=0, has_side_effects=True),
        name="gather_rows",
    )(master, masked)


def slot_tables():
    tables = []
    for order in ORDERS:
        table = {}
        for way in WAYS:
            keys = []
            along = False
            for place in [(0, 0, 0)] + relatives():
                if way in onward(order, place):
                    if place[1:] not in keys:
                        keys.append(place[1:])
                    along = along or place[0] != 0
            table[way] = (keys, 3 if way in ("up", "down") else (4 if along else 1))
        tables.append(table)
    return tables


SLOTS = slot_tables()
STAGES = 4
RING = 20
MANY = 6


def wide_shards(units):
    shard = units * UNIT
    last_matrix = sum(math.prod(shape) for shape in ENC_LAYOUT[:-2])
    return ((last_matrix // shard, 16), (0, -(-NDEC // shard)))


def scatter_kernel(grad_ref, loss_ref, out_ref, sums_ref, *refs):
    ranges = part_ranges(grad_ref.shape[1])
    landing = {}
    for part in range(PARTS):
        for number, way in enumerate(WAYS):
            landing[part, way] = refs[part * 4 + number]
    stage, ring, total, tiles, send_sem, recv_sem, stage_sem, out_sem, tile_send, tile_recv = refs[
        4 * PARTS :
    ]
    spot = Spot()
    spot.greet(True)
    spot.await_all(True)
    bounds = wide_shards(grad_ref.shape[1])
    z_here = spot.z

    def is_wide(owner):
        low = jnp.where(spot.grp == 0, bounds[0][0], bounds[1][0])
        high = jnp.where(spot.grp == 0, bounds[0][1], bounds[1][1])
        return (owner >= low) & (owner < high)

    def is_split(part, way, z, owner):
        axis = way if way in ("x", "y") else "z"
        order = ORDERS[part]
        chips = math.prod(AXIS_SIZE[later] for later in order[order.index(axis) + 1 :])
        if axis != "z":
            return True if chips >= MANY else is_wide(owner)
        chips = chips * (z + 1 if way == "up" else DP_GRID[0] - z)
        return is_wide(owner) | (chips >= MANY)

    def slot(part, way, place, z):
        keys, depth = SLOTS[part][way]
        base = keys.index(place[1:]) * depth
        if way == "up":
            return base + z
        if way == "down":
            return base + z - 1
        return base + (z if depth == 4 else 0)

    def parent(part, place):
        axis = last_axis(ORDERS[part], place)
        if axis == "z":
            return "up" if place[0] > 0 else "down"
        return axis

    def seen_from_parent(part, place):
        way = parent(part, place)
        dz, dy, dx = place
        if way == "x":
            return (dz, dy, 0)
        if way == "y":
            return (dz, 0, dx)
        return (dz - 1 if way == "up" else dz + 1, dy, dx)

    def send(part, place, origin, half):
        z, owner, _ = spot.at(place)
        way = parent(part, place)
        back = OPPOSITE[way]
        place_there = slot(part, back, seen_from_parent(part, place), z)
        return pltpu.make_async_remote_copy(
            src_ref=origin.at[half],
            dst_ref=landing[part, back].at[place_there, half],
            send_sem=send_sem.at[part, owner, half],
            recv_sem=recv_sem.at[part, owner, WAYS.index(back), half],
            device_id=spot.neighbour[way],
            device_id_type=MESH,
        )

    nodes = []
    for place in relatives()[::-1] + [(0, 0, 0)]:
        for part in range(PARTS):
            z, owner, inside = spot.at(place)
            nodes.append((part, place, onward(ORDERS[part], place), z, owner, inside))

    def staged(number):
        part, _, _, _, owner, _ = nodes[number]
        return pltpu.make_async_copy(
            grad_ref.at[owner, pl.ds(*ranges[part])],
            stage.at[number % STAGES, pl.ds(0, ranges[part][1])],
            stage_sem.at[number % STAGES],
        )

    def ring_part(index, part):
        return ring.at[index % RING, :, pl.ds(0, ranges[part][1])]

    def finish_send(number):
        part, place, _, _, owner, inside = nodes[number]
        split = is_split(part, parent(part, place), spot.z, owner)

        def finish():
            source = ring_part(0, part)
            send(part, place, source, 0).wait_send()
            when(
                None if split is True else split,
                lambda: send(part, place, source, 1).wait_send(),
            )

        when(inside, finish)

    for number in range(STAGES - 1):
        when(nodes[number][5], lambda: staged(number).start())
    ringed = []
    for number, (part, place, ways, z, owner, inside) in enumerate(nodes):
        ahead = number + STAGES - 1
        if ahead < len(nodes):
            when(nodes[ahead][5], lambda: staged(ahead).start())
        length = ranges[part][1]
        root = place == (0, 0, 0)
        flat = [way for way in ways if way in ("x", "y")]
        along = [way for way in ways if way in ("up", "down")]
        if not flat:
            if len(ringed) >= RING:
                finish_send(ringed[-RING])
            ringed.append(number)
        ring_index = len(ringed) - 1

        def combine(arriving, number=number, part=part, place=place, z=z, owner=owner):
            slots = [landing[part, way].at[slot(part, way, place, z)] for way in arriving]
            target = slots[0] if slots else ring_part(ring_index, part)

            def arrived(way, item, half):
                pltpu.make_async_remote_copy(
                    src_ref=item.at[half],
                    dst_ref=item.at[half],
                    send_sem=send_sem.at[part, owner, half],
                    recv_sem=recv_sem.at[part, owner, WAYS.index(way), half],
                    device_id=spot.neighbour[way],
                    device_id_type=MESH,
                ).wait_recv()

            def lines(ref):
                return ref.reshape(ref.shape[0] * 4, LANES)

            mine = lines(stage.at[number % STAGES, pl.ds(0, length)])

            def every(action):
                count = 4 * length
                some = 4 * CHUNK

                def step(index, carry):
                    action(pl.ds(pl.multiple_of(index * some, some), some))
                    return carry

                lax.fori_loop(0, count // some, step, 0)
                if count % some:
                    action(pl.ds(count - count % some, count % some))

            def put(rows, value, split):
                if root:
                    lines(total.at[pl.ds(*ranges[part])])[rows] = value
                    return
                high = value.astype(BF16)
                lines(target.at[0])[rows] = high
                if split:
                    lines(target.at[1])[rows] = (value - high.astype(F32)).astype(BF16)

            def summed(rows):
                value = mine[rows]
                for item in slots:
                    value = value + lines(item.at[0])[rows].astype(F32)
                return value

            for way, item in zip(arriving, slots):
                arrived(way, item, 0)
            staged(number).wait()
            theirs = []
            for way in arriving:
                there = {"up": z_here + 1, "down": z_here - 1}.get(way, z_here)
                theirs.append(is_split(part, OPPOSITE[way], there, owner))
            ours = False if root else is_split(part, parent(part, place), z_here, owner)
            some_split = functools.reduce(lambda a, b: a | b, theirs + [ours])

            def short():
                every(lambda rows: put(rows, summed(rows), False))

            def long():
                def first(rows):
                    mine[rows] = summed(rows)

                if slots:
                    every(first)
                for way, item, split in zip(arriving, slots, theirs):

                    def rest(way=way, item=item):
                        arrived(way, item, 1)

                        def one(rows):
                            mine[rows] = mine[rows] + lines(item.at[1])[rows].astype(F32)

                        every(one)

                    when(None if split is True else split, rest)
                every(lambda rows: put(rows, mine[rows], True))

            if some_split is True:
                long()
            else:
                pl.when(some_split)(long)
                pl.when(jnp.logical_not(some_split))(short)
            if not root:
                send(part, place, target, 0).start()
                when(
                    None if ours is True else ours,
                    lambda: send(part, place, target, 1).start(),
                )

        def choose(flat=flat, along=along, combine=combine):
            if not along:
                combine(flat)
            elif len(along) == 1:
                there = spot.exists[along[0]]
                pl.when(there)(lambda: combine(flat + along))
                pl.when(jnp.logical_not(there))(lambda: combine(flat))
            else:
                up, down = spot.exists["up"], spot.exists["down"]
                pl.when(up & down)(lambda: combine(flat + ["up", "down"]))
                pl.when(jnp.logical_not(down))(lambda: combine(flat + ["up"]))
                pl.when(jnp.logical_not(up))(lambda: combine(flat + ["down"]))

        when(inside, choose)
    out = pltpu.make_async_copy(total, out_ref, out_sem)
    out.start()
    units = total.shape[0]

    def square(start, count, running):
        value = total[pl.ds(start, count)]
        return running + jnp.sum(value * value, axis=0)

    squares = lax.fori_loop(
        0,
        units // CHUNK,
        lambda index, running: square(index * CHUNK, CHUNK, running),
        jnp.zeros((4, LANES), F32),
    )
    if units % CHUNK:
        squares = square(units - units % CHUNK, units % CHUNK, squares)
    me = spot.grp * 16 + spot.dp
    tiles[me, pl.ds(0, 4)] = squares
    tiles[me, pl.ds(4, 4)] = loss_ref[pl.ds(4, 4)]
    tell, told = tell_all(spot, tiles, tile_send, tile_recv, True)
    tell()
    done = set(ringed[:-RING])
    for number, node in enumerate(nodes):
        if number not in done and node[1] != (0, 0, 0):
            finish_send(number)
    told()
    sums_ref[...] = jnp.sum(tiles[...], axis=0)
    out.wait()


def scatter_sums(grads, loss):
    units = grads.shape[1]
    ranges = part_ranges(units)
    scratch = []
    for part in range(PARTS):
        for way in WAYS:
            keys, depth = SLOTS[part][way]
            shape = (len(keys) * depth, 2, ranges[part][1], 4, LANES)
            scratch.append(pltpu.VMEM(shape, BF16))
    largest = max(length for _, length in ranges)
    dma = pltpu.SemaphoreType.DMA
    scratch += [
        pltpu.VMEM((STAGES, largest, 4, LANES), F32),
        pltpu.VMEM((RING, 2, largest, 4, LANES), BF16),
        pltpu.VMEM((units, 4, LANES), F32),
        pltpu.VMEM((32, 8, LANES), F32),
        dma((PARTS, 16, 2)),
        dma((PARTS, 16, 4, 2)),
        dma((STAGES,)),
        dma,
        dma((32,)),
        dma((32,)),
    ]
    anywhere = pl.BlockSpec(memory_space=pl.ANY)
    vmem = pl.BlockSpec(memory_space=pltpu.VMEM)
    return pl.pallas_call(
        scatter_kernel,
        out_shape=(
            jax.ShapeDtypeStruct((units, 4, LANES), F32),
            jax.ShapeDtypeStruct((8, LANES), F32),
        ),
        in_specs=[anywhere, vmem],
        out_specs=(anywhere, vmem),
        scratch_shapes=scratch,
        compiler_params=pltpu.CompilerParams(
            collective_id=1, has_side_effects=True, vmem_limit_bytes=63 * 2**20
        ),
        name="scatter_sums",
    )(grads, loss)


def update_values(owned, scale, params, first_moment, second_moment, average):
    clipped = owned * scale
    new_first = BETA_ONE * first_moment + (1.0 - BETA_ONE) * clipped
    new_second = BETA_TWO * second_moment + (1.0 - BETA_TWO) * clipped * clipped
    root = jnp.sqrt(new_second * (1.0 / (1.0 - BETA_TWO**STEP)))
    direction = new_first * (1.0 / (1.0 - BETA_ONE**STEP)) / (root + ADAM_EPS)
    new_params = params - RATE * (direction + DECAY_WEIGHT * params)
    new_average = AVERAGE_KEEP * average + (1.0 - AVERAGE_KEEP) * new_params
    return new_params, new_first, new_second, new_average


def update_kernel(sums_ref, masked_ref, *refs):
    squares = jnp.sum(sums_ref[pl.ds(0, 4)], axis=0, keepdims=True)
    norm = jnp.sqrt(jnp.sum(squares, axis=1, keepdims=True))
    scale = jnp.minimum(1.0, CLIP / norm)
    step = 31

    def one(index, carry):
        block = pl.ds(index * step, step)
        owned, params, first, second, average = [ref[block] for ref in refs[:5]]
        values = update_values(owned, scale[None], params, first, second, average)
        for out, value in zip(refs[5:9], values):
            out[block] = value
        return carry

    lax.fori_loop(0, refs[0].shape[0] // step, one, 0)
    loss_ref, total_ref, norm_ref = refs[9:]
    loss_ref[...] = sums_ref[pl.ds(4, 1), pl.ds(0, 1)]
    total_ref[...] = masked_ref[pl.ds(0, 1), pl.ds(0, 1)]
    norm_ref[...] = norm


def update(sums, masked, arrays):
    units = arrays[0].shape[0]
    depth = 155
    spec = pl.BlockSpec((depth, 4, LANES), lambda i: (i, 0, 0))
    tile = pl.BlockSpec((8, LANES), lambda i: (0, 0))
    scalar = pl.BlockSpec((1, 1), lambda i: (0, 0))
    return pl.pallas_call(
        update_kernel,
        grid=(units // depth,),
        out_shape=[jax.ShapeDtypeStruct((units, 4, LANES), F32)] * 4
        + [jax.ShapeDtypeStruct((1, 1), F32)] * 3,
        in_specs=[tile, tile] + [spec] * 5,
        out_specs=[spec] * 4 + [scalar] * 3,
        name="update",
    )(sums, masked, *arrays)


SLOTS_IN = 5


def sections(layout, base):
    matrices, vectors = [], []
    offset = base
    for shape in layout:
        (matrices if len(shape) == 2 else vectors).append((offset, shape))
        offset += math.prod(shape)
    return matrices, vectors


def matrix_plan(rows):
    enc_matrices, enc_vectors = sections(ENC_LAYOUT, 0)
    dec_matrices, dec_vectors = sections(DEC_LAYOUT, rows * LANES)
    lent = rows * LANES + NDEC
    matrices = enc_matrices + sections(LENT, lent)[0] + dec_matrices
    return matrices, enc_vectors, dec_vectors


def padded(columns):
    return -(-columns // LANES) * LANES


def block_depth(shape):
    if shape[1] % LANES:
        return shape[0]
    depth = shape[0]
    while depth * shape[1] > PIECE * LANES:
        depth //= 2
    return depth


def matrix_kernel(rows, flat_ref, *refs):
    matrices, enc_vectors, dec_vectors = matrix_plan(rows)
    count = len(matrices)
    out_refs = refs[:count]
    vector_refs = refs[count : count + 2]
    blocks = refs[count + 2 : 2 * count + 2]
    flat_in, wide, pairs, vector_in, in_sem, out_sem, vector_sem = refs[2 * count + 2 :]
    lane = lax.broadcasted_iota(jnp.int32, (1, LANES), 1)

    chunks = []
    for number, (offset, shape) in enumerate(matrices):
        depth = block_depth(shape)
        for start in range(0, shape[0], depth):
            place = offset + start * shape[1]
            chunks.append((number, start, depth, place // LANES, place % LANES))

    def load(index):
        number, _, depth, first, shift = chunks[index]
        length = depth * matrices[number][1][1] // LANES
        begin = first // 16 * 16
        end = -(-(first + length + (1 if shift else 0)) // 16) * 16
        copy = pltpu.make_async_copy(
            flat_ref.at[pl.ds(begin, end - begin)],
            flat_in.at[index % SLOTS_IN, pl.ds(0, end - begin)],
            in_sem.at[index % SLOTS_IN],
        )
        return copy, first - begin, end - begin

    def store(index):
        number, start, depth, _, _ = chunks[index]
        slot = start // depth % 2
        return pltpu.make_async_copy(
            blocks[number].at[slot], out_refs[number].at[pl.ds(start, depth)], out_sem.at[number, slot]
        )

    def widen(index, length):
        step = 256

        def one(start, size):
            wide[pl.ds(start, size)] = flat_in[index % SLOTS_IN, pl.ds(start, size)].astype(F32)

        def loop(i, carry):
            one(pl.multiple_of(i * step, step), step)
            return carry

        lax.fori_loop(0, length // step, loop, 0, unroll=2)
        if length % step:
            one(length - length % step, length % step)

    def turned(first, second):
        return pltpu.roll(jnp.where(lane < LANES // 2, second, first), LANES // 2, 1)

    def arrange(index, phase):
        number, start, depth, _, shift = chunks[index]
        columns = matrices[number][1][1]
        block = blocks[number].at[start // depth % 2]
        tiles = columns // LANES

        def plain(i, carry):
            row = pl.multiple_of(i * SUB, SUB)
            packed = wide[pl.ds(phase + row * tiles, SUB * tiles)].reshape(SUB, tiles, LANES)
            swapped = jnp.swapaxes(packed, 0, 1)
            for tile in range(tiles):
                value = swapped[tile]
                if shift:
                    after = wide[pl.ds(phase + row * tiles + tile + 1, SUB, stride=tiles)]
                    value = turned(value, after)
                block[pl.ds(row, SUB), pl.ds(tile * LANES, LANES)] = value.astype(BF16)
            return carry

        def paired(i, carry):
            stride = 2 * columns // LANES
            half = SUB // 2
            row = pl.multiple_of(i * half, half)
            for tile in range(tiles + 1):
                even = wide[pl.ds(phase + row * stride + tile, half, stride=stride)]
                odd = wide[pl.ds(phase + row * stride + tiles + tile, half, stride=stride)]
                if tile < tiles:
                    after = wide[pl.ds(phase + row * stride + tiles + tile + 1, half, stride=stride)]
                    odd = turned(odd, after)
                else:
                    even = jnp.where(lane < LANES // 2, even, 0.0)
                    odd = jnp.where(lane < LANES // 2, pltpu.roll(odd, LANES // 2, 1), 0.0)
                lanes = pl.ds(tile * LANES, LANES)
                pairs[tile, pl.ds(0, half, stride=2)] = even
                pairs[tile, pl.ds(1, half, stride=2)] = odd
                block[pl.ds(pl.multiple_of(i * SUB, SUB), SUB), lanes] = pairs[tile].astype(BF16)
            return carry

        lax.fori_loop(0, depth // SUB, paired if columns % LANES else plain, 0, unroll=4)

    windows = []
    wanted = [(0, n, v) for n, v in enumerate(enc_vectors)]
    wanted += [(1, n, v) for n, v in enumerate(dec_vectors)]
    for _, _, (offset, shape) in wanted:
        first = offset // LANES // 16 * 16
        end = -(-(offset // LANES + -(-shape[0] // LANES)) // 16) * 16
        if windows and first <= windows[-1][1]:
            windows[-1][1] = max(windows[-1][1], end)
        else:
            windows.append([first, end])
    bases = [sum(e - f for f, e in windows[:n]) for n in range(len(windows))]

    def vector_copy(n):
        first, end = windows[n]
        return pltpu.make_async_copy(
            flat_ref.at[pl.ds(first, end - first)],
            vector_in.at[pl.ds(bases[n], end - first)],
            vector_sem.at[n],
        )

    for index in range(SLOTS_IN - 1):
        load(index)[0].start()
    for n in range(len(windows)):
        vector_copy(n).start()
    for index, (number, start, depth, _, _) in enumerate(chunks):
        copy, phase, length = load(index)
        copy.wait()
        if index + SLOTS_IN - 1 < len(chunks):
            load(index + SLOTS_IN - 1)[0].start()
        widen(index, length)
        if start // depth >= 2:
            store(index - 2).wait()
        arrange(index, phase)
        store(index).start()
    for n in range(len(windows)):
        vector_copy(n).wait()
    total = bases[-1] + windows[-1][1] - windows[-1][0]
    wide[pl.ds(0, total)] = vector_in[...].astype(F32)
    for group, n, (offset, shape) in wanted:
        first = offset // LANES
        window = [k for k, (f, e) in enumerate(windows) if f <= first < e][0]
        base = bases[window] + first - windows[window][0]
        for tile in range(-(-shape[0] // LANES)):
            value = wide[pl.ds(base + tile, 1)]
            if shape[0] - tile * LANES < LANES:
                value = jnp.where(lane < shape[0] - tile * LANES, value, 0.0)
            vector_refs[group][pl.ds(n, 1), pl.ds(tile * LANES, LANES)] = value
    for index, (number, start, depth, _, _) in enumerate(chunks):
        if start + 2 * depth >= matrices[number][1][0]:
            store(index).wait()


def weight_matrices(flat):
    rows = flat.shape[0] // 2
    matrices, enc_vectors, dec_vectors = matrix_plan(rows)
    shapes = [(shape[0], padded(shape[1])) for _, shape in matrices]
    buffers = []
    for (_, shape), (_, columns) in zip(matrices, shapes):
        depth = block_depth(shape)
        buffers.append(pltpu.VMEM((min(2, shape[0] // depth), depth, columns), BF16))
    dma = pltpu.SemaphoreType.DMA
    windows = 0
    last = -1
    total = 0
    for offset, shape in enc_vectors + dec_vectors:
        first = offset // LANES // 16 * 16
        end = -(-(offset // LANES + -(-shape[0] // LANES)) // 16) * 16
        if first <= last:
            total += max(0, end - last)
            last = max(last, end)
        else:
            windows += 1
            total += end - first
            last = end
    anywhere = pl.BlockSpec(memory_space=pl.ANY)
    vmem = pl.BlockSpec(memory_space=pltpu.VMEM)
    return pl.pallas_call(
        functools.partial(matrix_kernel, rows),
        out_shape=[jax.ShapeDtypeStruct(shape, BF16) for shape in shapes]
        + [jax.ShapeDtypeStruct((VEC_ROWS, columns), F32) for columns in VEC_COLS],
        in_specs=[anywhere],
        out_specs=[anywhere] * len(shapes) + [vmem, vmem],
        scratch_shapes=buffers
        + [
            pltpu.VMEM((SLOTS_IN, PIECE + 32, LANES), BF16),
            pltpu.VMEM((PIECE + 32, LANES), F32),
            pltpu.VMEM((padded(HEAD) // LANES, SUB, LANES), F32),
            pltpu.VMEM((total, LANES), BF16),
            dma((SLOTS_IN,)),
            dma((len(shapes), 2)),
            dma((windows,)),
        ],
        compiler_params=pltpu.CompilerParams(vmem_limit_bytes=56 * 2**20),
        name="weight_matrices",
    )(flat)


def stream_items(layout, lent):
    items = []
    offset = 0
    numbers = [0, 0]
    for shape in layout + lent:
        matrix = len(shape) == 2
        number = numbers[matrix]
        numbers[matrix] += 1
        depth = block_depth(shape) if matrix else 0
        for start in range(0, shape[0] if matrix else 1, max(depth, 1)):
            items.append((matrix, number, shape, start, depth, offset))
            offset += depth * shape[1] if matrix else shape[0]
    return items, offset


ROLES = (
    (ENC_LAYOUT, [], (0, 1, 2, 3)),
    (DEC_LAYOUT, LENT, (6, 7, 8, 9, 10, 4, 5)),
)
PAIRS = 11
FLIGHTS = 4
DEPTH = 1024


def factor_buffers(shapes):
    sizes = []
    places = {}
    for role in (1, 0):
        taken = set()
        for number in ROLES[role][2]:
            for side in range(2):
                length, columns = shapes[2 * number + side]
                fits = [
                    n
                    for n, size in enumerate(sizes)
                    if n not in taken and size[0] == 2 * length and size[1] >= columns
                ]
                if fits:
                    place = min(fits, key=lambda n: sizes[n][1])
                else:
                    place = len(sizes)
                    sizes.append((2 * length, columns))
                taken.add(place)
                places[role, number, side] = place
    return sizes, places


def product_kernel(rows, shapes, *refs):
    factors, vectors, out_ref = refs[: 2 * PAIRS], refs[2 * PAIRS : 2 * PAIRS + 2], refs[24]
    sizes, places = factor_buffers(shapes)
    buffers = refs[25 : 25 + len(sizes)]
    refs = refs[25 + len(sizes) :]
    others = refs[:2]
    turned_left, tall, rows_out, own_sem, send_sem, recv_sem, out_sem = refs[2:]
    core = lax.axis_index("grp")
    sibling = (1 - core, lax.axis_index("dp"))
    barrier = pltpu.get_barrier_semaphore()
    pl.semaphore_signal(barrier, inc=1, device_id=sibling, device_id_type=MESH)
    pl.semaphore_wait(barrier, 1)

    def half_of(role, number, side, part):
        length, columns = shapes[2 * number + side]
        buffer = buffers[places[role, number, side]]
        return buffer.at[pl.ds(part * length, length), pl.ds(0, columns)]

    def local(role, number, side):
        return pltpu.make_async_copy(
            factors[2 * number + side], half_of(role, number, side, 0), own_sem.at[number, side]
        )

    def remote(role, number, side):
        return pltpu.make_async_remote_copy(
            src_ref=factors[2 * number + side],
            dst_ref=half_of(role, number, side, 1),
            send_sem=send_sem.at[number, side],
            recv_sem=recv_sem.at[number, side],
            device_id=sibling,
            device_id_type=MESH,
        )

    def remote_vectors(role):
        return pltpu.make_async_remote_copy(
            src_ref=vectors[role],
            dst_ref=others[role],
            send_sem=send_sem.at[PAIRS, role],
            recv_sem=recv_sem.at[PAIRS, role],
            device_id=sibling,
            device_id_type=MESH,
        )

    def act(role):
        remote_vectors(1 - role).start()
        pending = [(number, side) for number in ROLES[role][2] for side in range(2)]
        for number, side in pending:
            local(role, number, side).start()
        given = [(number, side) for number in ROLES[1 - role][2] for side in range(2)]
        for number, side in given:
            remote(1 - role, number, side).start()
        remote_vectors(role).wait_recv()

        def ready(number):
            for side in range(2):
                local(role, number, side).wait()
                remote(role, number, side).wait_recv()

        lefts, rights = [], []
        for number in ROLES[role][2]:
            for side, views in ((0, lefts), (1, rights)):
                length, columns = shapes[2 * number + side]
                buffer = buffers[places[role, number, side]]
                views.append(buffer.at[pl.ds(0, 2 * length), pl.ds(0, columns)])
        fill_row(
            rows,
            ROLES[role],
            ready,
            lefts,
            rights,
            vectors[role],
            others[role],
            turned_left,
            tall,
            rows_out,
            out_ref,
            out_sem,
        )
        for number, side in given:
            remote(1 - role, number, side).wait_send()
        remote_vectors(1 - role).wait_send()

    for role in range(2):
        pl.when(core == role)(functools.partial(act, role))


def fill_row(
    rows,
    role,
    ready,
    lefts,
    rights,
    mine_ref,
    other_ref,
    turned_left,
    tall,
    rows_out,
    out_ref,
    out_sem,
):
    layout, lent, numbers = role
    lane = lax.broadcasted_iota(jnp.int32, (1, LANES), 1)
    half = LANES // 2
    items, used = stream_items(layout, lent)
    groups = []
    current = []
    for item in items:
        current.append(item)
        if item[0]:
            groups.append(current)
            current = []
    groups.append(current)

    def vector(item, buffer, base):
        _, number, shape, _, _, _ = item
        for tile in range(-(-shape[0] // LANES)):
            lanes = pl.ds(tile * LANES, LANES)
            buffer[pl.ds(base + tile, 1)] = (
                mine_ref[pl.ds(number, 1), lanes] + other_ref[pl.ds(number, 1), lanes]
            )

    def matrix(item, buffer, base):
        _, number, shape, start, depth, offset = item
        columns = shape[1]
        shifted = offset % LANES
        tiles = -(-columns // LANES)
        width = min(WIDTH, columns)
        if start == 0:
            ready(numbers[number])
            if shifted:
                length = rights[number].shape[0]

                def turn(i, carry):
                    block = pl.ds(pl.multiple_of(i * 64, 64), 64)
                    value = rights[number][block].astype(F32)
                    rights[number][block] = pltpu.roll(value, half, 1).astype(BF16)
                    return carry

                lax.fori_loop(0, length // 64, turn, 0)
        length = lefts[number].shape[0]
        sub = min(DEPTH, depth)

        def loop(step, carry):
            k = pl.multiple_of(start + step * sub, sub)
            turned_left[pl.ds(0, sub), pl.ds(0, length)] = lefts[number][:, pl.ds(k, sub)].T

            def across(c, carry):
                column = pl.multiple_of(c * width, width)
                value = jnp.dot(
                    turned_left[pl.ds(0, sub), pl.ds(0, length)],
                    rights[number][:, pl.ds(column, width)],
                    preferred_element_type=F32,
                )
                row = base + step * sub * tiles
                for piece in range(width // LANES):
                    part = value[:, piece * LANES : (piece + 1) * LANES]
                    tile = c * (width // LANES) + piece
                    if columns % LANES:
                        tall[tile, pl.ds(step * sub, sub)] = part
                    elif shifted and piece == 0:
                        first = row + tile

                        @pl.when(c == 0)
                        def _():
                            before = pltpu.roll(part, 1, 0)
                            index = lax.broadcasted_iota(jnp.int32, (sub, LANES), 0)
                            held = buffer[pl.ds(row, 1)]
                            before = jnp.where(index == 0, held, before)
                            merged = jnp.where(lane < half, before, part)
                            buffer[pl.ds(row, sub, stride=tiles)] = merged
                            buffer[pl.ds(row + sub * tiles, 1)] = part[sub - 1 :]

                        @pl.when(c > 0)
                        def _():
                            buffer[pl.ds(first, sub, stride=tiles)] = part
                    else:
                        buffer[pl.ds(row + tile, sub, stride=tiles)] = part
                return carry

            count = tiles * LANES // width
            lax.fori_loop(0, count, across, 0, unroll=2 if count % 2 == 0 else 1)
            return carry

        lax.fori_loop(0, depth // sub, loop, 0)
        if columns % LANES:
            stride = 2 * columns // LANES
            pair = 64

            def weave(i, carry):
                k = pl.multiple_of(i * 2 * pair, 2 * pair)
                row = base + i * pair * stride
                evens = [tall[t, pl.ds(k, pair, stride=2)] for t in range(tiles)]
                odds = [tall[t, pl.ds(k + 1, pair, stride=2)] for t in range(tiles)]
                for t in range(tiles - 1):
                    buffer[pl.ds(row + t, pair, stride=stride)] = evens[t]
                middle = jnp.where(lane < half, evens[-1], pltpu.roll(odds[0], half, 1))
                buffer[pl.ds(row + tiles - 1, pair, stride=stride)] = middle
                for t in range(1, tiles):
                    both_halves = jnp.where(lane < half, odds[t], odds[t - 1])
                    buffer[pl.ds(row + tiles - 1 + t, pair, stride=stride)] = pltpu.roll(
                        both_halves, half, 1
                    )
                return carry

            lax.fori_loop(0, depth // 2 // pair, weave, 0)

    flights = []
    tail = None
    for number, group in enumerate(groups):
        slot = number % 2
        buffer = rows_out.at[slot]
        if number >= 2:
            for copy in flights[number - 2]:
                copy.wait()
        first = group[0][5] // LANES if group else used // LANES
        begin = first // 8 * 8
        if tail is not None:
            buffer[pl.ds(0, 8)] = rows_out[1 - slot, pl.ds(tail, 8)]
        for item in group:
            (matrix if item[0] else vector)(item, buffer, item[5] // LANES - begin)
        last = number == len(groups) - 1
        if last:
            at = used // LANES - begin
            if used % LANES:
                buffer[pl.ds(at, 1)] = jnp.where(lane < used % LANES, buffer[pl.ds(at, 1)], 0.0)
                at += 1
            length = rows - begin
            if length > at:
                buffer[pl.ds(at, length - at)] = jnp.zeros((length - at, LANES), F32)
        else:
            end = groups[number + 1][0][5] if groups[number + 1] else used
            tail = (end // LANES - begin) // 8 * 8
            length = tail
        cuts = [length * n // FLIGHTS // 8 * 8 for n in range(FLIGHTS)] + [length]
        flight = [
            pltpu.make_async_copy(
                buffer.at[pl.ds(lower, upper - lower)],
                out_ref.at[pl.ds(begin + lower, upper - lower)],
                out_sem.at[slot, n],
            )
            for n, (lower, upper) in enumerate(zip(cuts, cuts[1:]))
            if upper > lower
        ]
        for copy in flight:
            copy.start()
        flights.append(flight)
    for flight in flights[-2:]:
        for copy in flight:
            copy.wait()


def flat_gradient(rows, factors, enc_vectors, dec_vectors):
    shapes = [factor.shape for factor in factors]
    sizes, _ = factor_buffers(shapes)
    longest = max(length for length, _ in sizes)
    dma = pltpu.SemaphoreType.DMA
    anywhere = pl.BlockSpec(memory_space=pl.ANY)
    vmem = pl.BlockSpec(memory_space=pltpu.VMEM)
    return pl.pallas_call(
        functools.partial(product_kernel, rows, shapes),
        out_shape=jax.ShapeDtypeStruct((rows, LANES), F32),
        in_specs=[anywhere] * (2 * PAIRS) + [vmem, vmem],
        out_specs=anywhere,
        scratch_shapes=[pltpu.VMEM(size, BF16) for size in sizes]
        + [
            pltpu.VMEM(enc_vectors.shape, F32),
            pltpu.VMEM(dec_vectors.shape, F32),
            pltpu.VMEM((DEPTH, longest), BF16),
            pltpu.VMEM((padded(HEAD) // LANES, DD, LANES), F32),
            pltpu.VMEM((2, PIECE + 128, LANES), F32),
            dma((PAIRS, 2)),
            dma((PAIRS + 1, 2)),
            dma((PAIRS + 1, 2)),
            dma((2, FLIGHTS)),
        ],
        compiler_params=pltpu.CompilerParams(
            collective_id=2, has_side_effects=True, vmem_limit_bytes=63 * 2**20
        ),
        name="flat_gradient",
    )(*factors, enc_vectors, dec_vectors)


LN1_G, LN1_B, LN2_G, LN2_B, FC1_B, FC2_B, LNF_G, LNF_B, LAST_B = range(1, 10)
GROUP = 256
TURNS = 16
BATCH = 2


def dot(left, right):
    return jnp.dot(left, right, preferred_element_type=F32)


def dot_nt(left, right):
    return lax.dot_general(left, right, (((1,), (1,)), ((), ())), preferred_element_type=F32)


def dot_tn(left, right):
    return lax.dot_general(left, right, (((0,), (0,)), ((), ())), preferred_element_type=F32)


def blocks(length, size, action):
    def step(index, carry):
        action(pl.ds(pl.multiple_of(index * size, size), size))
        return carry

    count = length // size
    lax.fori_loop(0, count, step, 0, unroll=2 if count % 2 == 0 else 1)


def row_step(length):
    return 208 if length % 208 == 0 else 128


def score_step(length):
    return 832 if length % 208 == 0 else 256


def normed(state):
    centered = state - jnp.mean(state, axis=-1, keepdims=True)
    inverse = lax.rsqrt(jnp.mean(centered * centered, axis=-1, keepdims=True) + NORM_EPS)
    return centered * inverse, inverse


def norm_rows(source, target, vectors, gain):
    width = source.shape[1]

    def one(rows):
        unit, _ = normed(source[rows])
        value = unit * vectors[pl.ds(gain, 1), pl.ds(0, width)]
        target[rows] = (value + vectors[pl.ds(gain + 1, 1), pl.ds(0, width)]).astype(BF16)

    blocks(source.shape[0], row_step(source.shape[0]), one)


def norm_rows_back(source, grad, vectors, sums, gain, finish):
    width = source.shape[1]
    lanes = pl.ds(0, width)

    def one(rows):
        unit, inverse = normed(source[rows])
        out = grad[rows]
        sums[pl.ds(gain, 1), lanes] += jnp.sum(out * unit, axis=0, keepdims=True)
        sums[pl.ds(gain + 1, 1), lanes] += jnp.sum(out, axis=0, keepdims=True)
        scaled = out * vectors[pl.ds(gain, 1), lanes]
        mean = jnp.mean(scaled, axis=-1, keepdims=True)
        along = jnp.mean(scaled * unit, axis=-1, keepdims=True)
        finish(rows, inverse * (scaled - mean - unit * along))

    blocks(source.shape[0], row_step(source.shape[0]), one)


def gelu_parts(value):
    below = 0.5 * (1.0 + lax.erf(value * math.sqrt(0.5)))
    return below, value * below


def head_masks(depth):
    lane = lax.broadcasted_iota(jnp.int32, (1, GROUP), 1)
    return [
        ((lane >= head * depth) & (lane < (head + 1) * depth)).astype(F32).astype(BF16)
        for head in range(GROUP // depth)
    ]


def stack_heads(target, value, masks):
    length = value.shape[0]
    for head, mask in enumerate(masks):
        target[pl.ds(head * length, length)] = value * mask


def attention_forward(images, length, heads, qkv, bias, attend, attend_low, stacked, mixed):
    width = mixed.shape[1]
    depth = width // heads
    masks = head_masks(depth)
    groups = width // GROUP
    scale = depth**-0.5

    def one(index, carry):
        image, group = index // groups, index % groups
        rows = pl.ds(pl.multiple_of(image * length, length), length)

        def lanes(part):
            return pl.ds(pl.multiple_of(part * width + group * GROUP, GROUP), GROUP)

        stack_heads(stacked, qkv[rows, lanes(0)], masks)
        attend[index] = dot_nt(stacked[...], qkv[rows, lanes(1)])
        shift = bias[pl.ds(image, 1)]

        def softmax(block):
            scores = attend[index, block] * scale + shift
            raised = jnp.exp(scores - jnp.max(scores, axis=-1, keepdims=True))
            value = raised / jnp.sum(raised, axis=-1, keepdims=True)
            attend[index, block] = value
            attend_low[block] = value.astype(BF16)

        blocks(len(masks) * length, score_step(length), softmax)
        value = qkv[rows, lanes(2)]
        total = jnp.zeros((length, GROUP), F32)
        for head, mask in enumerate(masks):
            total += dot(attend_low[pl.ds(head * length, length)], value * mask)
        mixed[rows, lanes(0)] = total.astype(BF16)
        return carry

    lax.fori_loop(0, images * groups, one, 0, unroll=4)


def attention_backward(
    images, length, heads, qkv, grad_mixed, attend, attend_low, grad_low, grads, stacked, other, out
):
    width = grad_mixed.shape[1]
    depth = width // heads
    masks = head_masks(depth)
    groups = width // GROUP
    scale = depth**-0.5

    def one(index, carry):
        image, group = index // groups, index % groups
        rows = pl.ds(pl.multiple_of(image * length, length), length)

        def lanes(part):
            return pl.ds(pl.multiple_of(part * width + group * GROUP, GROUP), GROUP)

        stack_heads(stacked, qkv[rows, lanes(0)], masks)
        stack_heads(other, grad_mixed[rows, lanes(0)], masks)
        grads[...] = dot_nt(other[...], qkv[rows, lanes(2)])

        def scores(block):
            value = attend[index, block]
            grad = grads[block]
            total = jnp.sum(grad * value, axis=-1, keepdims=True)
            grad_low[block] = (value * (grad - total)).astype(BF16)
            attend_low[block] = value.astype(BF16)

        blocks(len(masks) * length, score_step(length), scores)
        out[rows, lanes(2)] = dot_tn(attend_low[...], other[...]).astype(BF16)
        out[rows, lanes(1)] = (dot_tn(grad_low[...], stacked[...]) * scale).astype(BF16)
        key = qkv[rows, lanes(1)]
        total = jnp.zeros((length, GROUP), F32)
        for head, mask in enumerate(masks):
            total += dot(grad_low[pl.ds(head * length, length)], key * mask)
        out[rows, lanes(0)] = (total * scale).astype(BF16)
        return carry

    lax.fori_loop(0, images * groups, one, 0, unroll=4)


def columns_loop(columns, size, action):
    blocks(columns, min(2 * size, columns), action)


def feed_forward(normed_two, fc1_w, fc2_w, vectors, middle, pre, active, state):
    bias = pl.ds(FC1_B, 1)

    def up(lanes):
        value = dot(normed_two[...], fc1_w[:, lanes]) + vectors[bias, lanes]
        pre[:, lanes] = value
        active[:, lanes] = gelu_parts(value)[1].astype(BF16)

    columns_loop(pre.shape[1], 256, up)

    def down(lanes):
        value = dot(active[...], fc2_w[:, lanes])
        state[:, lanes] = middle[:, lanes] + value + vectors[pl.ds(FC2_B, 1), lanes]

    columns_loop(state.shape[1], 256, down)


def feed_backward(grad_low, fc1_w, fc2_w, pre, sums, grad_pre, out):
    def up(lanes):
        value = pre[:, lanes]
        below, _ = gelu_parts(value)
        slope = below + value * (jnp.exp(-0.5 * value * value) * (1.0 / math.sqrt(2.0 * math.pi)))
        grad = dot_nt(grad_low[...], fc2_w[lanes]) * slope
        sums[pl.ds(FC1_B, 1), lanes] += jnp.sum(grad, axis=0, keepdims=True)
        grad_pre[:, lanes] = grad.astype(BF16)

    columns_loop(pre.shape[1], 256, up)

    def down(lanes):
        out[:, lanes] = dot_nt(grad_pre[...], fc1_w[lanes])

    columns_loop(out.shape[1], 256, down)


def turn_code(places, table):
    lane = lax.broadcasted_iota(jnp.int32, (places.shape[0], TURNS), 1)
    passed = (lane > 0) & (lane < TURNS - 1) & (places >= lane * GSIDE)
    row = jnp.sum(passed.astype(F32), axis=1, keepdims=True).astype(jnp.int32)
    parts = []
    for pick in (row, places - row * GSIDE):
        chosen = (lane == pick).astype(F32)
        parts.append(jnp.dot(chosen, table, precision=HIGHEST, preferred_element_type=F32))
    return jnp.concatenate(parts, axis=1)


def decoder_kernel(
    sent,
    pixels,
    spot_rows,
    spot_columns,
    table,
    masked_ref,
    bands_w,
    vectors,
    qkv_w,
    out_w,
    fc1_w,
    fc2_w,
    head_w,
    normed_one,
    grad_qkv,
    mixed,
    grad_middle_low,
    normed_two,
    grad_pre,
    active,
    grad_out_low,
    normed_last,
    grad_predicted,
    grad_sent,
    sums,
    loss,
    seen,
    bias,
    state,
    middle,
    last,
    grad,
    spare,
    qkv,
    pre,
    attend,
    attend_low,
    scores_low,
    scores_grad,
    stacked,
    other,
    grad_mixed,
):
    width = state.shape[1]
    lanes = pl.ds(0, width)

    @pl.when(pl.program_id(0) == 0)
    def _():
        sums[...] = jnp.zeros_like(sums)
        loss[...] = jnp.zeros_like(loss)

    grid = lax.broadcasted_iota(jnp.int32, (GPAD, 1), 0)
    key = lax.broadcasted_iota(jnp.int32, (1, GPAD), 1)
    token = vectors[pl.ds(0, 1), lanes]
    for image in range(BATCH):
        rows = pl.ds(image * GPAD, GPAD)
        chosen = (grid == spot_rows[image]).astype(F32)
        shown = jnp.sum(chosen, axis=1, keepdims=True)
        placed = dot(chosen.astype(BF16), sent[pl.ds(image * VMAX, VMAX)])
        seen[rows] = jnp.where(grid < GRID, shown, 1.0)
        code = turn_code(grid, table[image])
        state[rows] = jnp.where(shown > 0.5, placed, token) + code
        bias[pl.ds(image, 1)] = jnp.where(key < GRID, 0.0, MASK_FILL)

    norm_rows(state, normed_one, vectors, LN1_G)

    def project(part):
        qkv[:, part] = dot(normed_one[...], qkv_w[:, part]).astype(BF16)

    columns_loop(qkv.shape[1], 256, project)
    attention_forward(
        BATCH, GPAD, HD, qkv, bias, attend, attend_low, stacked, mixed
    )

    def output(part):
        middle[:, part] = state[:, part] + dot(mixed[...], out_w[:, part])

    columns_loop(width, 256, output)
    norm_rows(middle, normed_two, vectors, LN2_G)
    feed_forward(normed_two, fc1_w, fc2_w, vectors, middle, pre, active, last)
    norm_rows(last, normed_last, vectors, LNF_G)

    weight = 1.0 / masked_ref[pl.ds(0, 1), pl.ds(0, 1)]

    def predict(part):
        value = dot(normed_last[...], head_w[:, part]) + vectors[pl.ds(LAST_B, 1), part]
        miss = value - dot(pixels[...], bands_w[:, part])
        index = lax.broadcasted_iota(jnp.int32, (1, GROUP), 1) + part.start
        low = index < LOWPIX
        square = miss * miss
        root = jnp.sqrt(square + 1.0)
        unseen = 1.0 - seen[...]
        loss[...] += jnp.sum(jnp.where(low, square, root - 1.0) * unseen)
        slope = jnp.where(low, 2.0 * miss, miss / root) * (unseen * weight)
        rounded = slope.astype(BF16)
        grad_predicted[:, part] = rounded
        sums[pl.ds(LAST_B, 1), part] += jnp.sum(rounded.astype(F32), axis=0, keepdims=True)

    blocks(head_w.shape[1], GROUP, predict)

    def head_back(part):
        spare[:, part] = dot_nt(grad_predicted[...], head_w[part])

    columns_loop(width, 256, head_back)

    def last_back(rows, value):
        grad[rows] = value
        grad_out_low[rows] = value.astype(BF16)
        sums[pl.ds(FC2_B, 1), lanes] += jnp.sum(value, axis=0, keepdims=True)

    norm_rows_back(last, spare, vectors, sums, LNF_G, last_back)
    block_backward(
        BATCH,
        GPAD,
        HD,
        (qkv_w, out_w, fc1_w, fc2_w),
        vectors,
        sums,
        (state, middle, grad, spare, pre, qkv),
        (grad_out_low, grad_pre, grad_middle_low, grad_mixed, grad_qkv),
        (attend, attend_low, scores_low, scores_grad, stacked, other),
    )
    unseen = 1.0 - seen[...]
    sums[pl.ds(0, 1), lanes] += jnp.sum(grad[...] * unseen, axis=0, keepdims=True)
    for image in range(BATCH):
        chosen = (spot_columns[pl.ds(image * VMAX, VMAX)] == key).astype(F32).astype(BF16)
        value = dot(chosen, grad[pl.ds(image * GPAD, GPAD)].astype(BF16))
        grad_sent[pl.ds(image * VMAX, VMAX)] = value.astype(BF16)


def block_backward(images, length, heads, weights, vectors, sums, states, lows, scratch):
    qkv_w, out_w, fc1_w, fc2_w = weights
    state, middle, grad, spare, pre, qkv = states
    grad_out_low, grad_pre, grad_middle_low, grad_mixed, grad_qkv = lows
    attend, attend_low, scores_low, scores_grad, stacked, other = scratch
    width = state.shape[1]
    feed_backward(grad_out_low, fc1_w, fc2_w, pre, sums, grad_pre, spare)

    def middle_back(rows, value):
        total = grad[rows] + value
        grad[rows] = total
        grad_middle_low[rows] = total.astype(BF16)

    norm_rows_back(middle, spare, vectors, sums, LN2_G, middle_back)

    def mixed_back(part):
        grad_mixed[:, part] = dot_nt(grad_middle_low[...], out_w[part]).astype(BF16)

    columns_loop(width, 256, mixed_back)
    attention_backward(
        images,
        length,
        heads,
        qkv,
        grad_mixed,
        attend,
        attend_low,
        scores_low,
        scores_grad,
        stacked,
        other,
        grad_qkv,
    )

    def first_back(part):
        spare[:, part] = dot_nt(grad_qkv[...], qkv_w[part])

    columns_loop(width, 256, first_back)

    def state_back(rows, value):
        grad[rows] = grad[rows] + value

    norm_rows_back(state, spare, vectors, sums, LN1_G, state_back)


def decoder(sent, pixels, spots, tables, masked_tile, vectors, weights):
    images = spots.shape[0]
    rows = BATCH * GPAD
    shown = BATCH * VMAX
    stack = GROUP // (DD // HD) * GPAD
    widths = [DD, 3 * DD, DD, DD, DD, FD, FD, DD, DD, padded(HEAD)]
    whole = lambda array: pl.BlockSpec(array.shape, lambda i: (0,) * array.ndim)
    by_rows = lambda length, columns: pl.BlockSpec((length, columns), lambda i: (i, 0))
    bands_w = band_matrix()
    out_shape = [jax.ShapeDtypeStruct((images * GPAD, columns), BF16) for columns in widths]
    out_shape.append(jax.ShapeDtypeStruct((images * VMAX, DD), BF16))
    out_shape.append(jax.ShapeDtypeStruct((VEC_ROWS, VEC_COLS[1]), F32))
    out_shape.append(jax.ShapeDtypeStruct((8, LANES), F32))
    operands = [masked_tile, bands_w, vectors, *weights]
    f32 = lambda *shape: pltpu.VMEM(shape, F32)
    b16 = lambda *shape: pltpu.VMEM(shape, BF16)
    return pl.pallas_call(
        decoder_kernel,
        grid=(images // BATCH,),
        out_shape=out_shape,
        in_specs=[
            by_rows(shown, DD),
            by_rows(rows, PIX),
            pl.BlockSpec((BATCH, 1, VMAX), lambda i: (i, 0, 0)),
            by_rows(shown, 1),
            pl.BlockSpec((BATCH, TURNS, DD // 2), lambda i: (i, 0, 0)),
        ]
        + [whole(operand) for operand in operands],
        out_specs=[by_rows(rows, columns) for columns in widths]
        + [by_rows(shown, DD)]
        + [pl.BlockSpec(shape.shape, lambda i: (0, 0)) for shape in out_shape[-2:]],
        scratch_shapes=[
            f32(rows, 1),
            f32(BATCH, GPAD),
            f32(rows, DD),
            f32(rows, DD),
            f32(rows, DD),
            f32(rows, DD),
            f32(rows, DD),
            b16(rows, 3 * DD),
            f32(rows, FD),
            f32(BATCH * DD // GROUP, stack, GPAD),
            b16(stack, GPAD),
            b16(stack, GPAD),
            f32(stack, GPAD),
            b16(stack, GROUP),
            b16(stack, GROUP),
            b16(rows, DD),
        ],
        compiler_params=pltpu.CompilerParams(vmem_limit_bytes=62 * 2**20),
        name="decoder",
    )(sent, pixels, spots.reshape(images, 1, VMAX), spots.reshape(-1, 1), tables, *operands)


def encoder_forward_kernel(
    pixels,
    spot_rows,
    spot_columns,
    table,
    vectors,
    pe_hbm,
    qkv_hbm,
    out_hbm,
    fc1_hbm,
    fc2_hbm,
    emb_hbm,
    sent,
    patches,
    state,
    normed_one,
    qkv,
    mixed,
    middle,
    normed_two,
    pre,
    active,
    last,
    normed_last,
    attend,
    pe_w,
    qkv_w,
    out_w,
    fc1_w,
    fc2_w,
    emb_w,
    bias,
    attend_low,
    stacked,
    sems,
):
    pairs = [
        (pe_hbm, pe_w),
        (qkv_hbm, qkv_w),
        (out_hbm, out_w),
        (fc1_hbm, fc1_w),
        (fc2_hbm, fc2_w),
        (emb_hbm, emb_w),
    ]
    copies = [pltpu.make_async_copy(*pair, sems.at[n]) for n, pair in enumerate(pairs)]
    for copy in copies:
        copy.start()
    images = spot_rows.shape[0]
    key = lax.broadcasted_iota(jnp.int32, (1, GPAD), 1)
    for image in range(images):
        rows = pl.ds(image * VMAX, VMAX)
        place = spot_columns[rows]
        chosen = (place == key).astype(F32).astype(BF16)
        patches[rows] = dot(chosen, pixels[pl.ds(image * GPAD, GPAD)]).astype(BF16)
        code = turn_code(jnp.maximum(place, 0), table[image])
        state[rows] = code + vectors[pl.ds(0, 1), pl.ds(0, DE)]
        bias[pl.ds(image, 1)] = jnp.where(spot_rows[image] < 0, MASK_FILL, 0.0)
    copies[0].wait()

    def embed(part):
        state[:, part] += dot(patches[...], pe_w[:, part])

    columns_loop(DE, 256, embed)
    norm_rows(state, normed_one, vectors, LN1_G)
    copies[1].wait()

    def project(part):
        qkv[:, part] = dot(normed_one[...], qkv_w[:, part]).astype(BF16)

    columns_loop(3 * DE, 256, project)
    attention_forward(images, VMAX, HE, qkv, bias, attend, attend_low, stacked, mixed)
    copies[2].wait()

    def output(part):
        middle[:, part] = state[:, part] + dot(mixed[...], out_w[:, part])

    columns_loop(DE, 256, output)
    norm_rows(middle, normed_two, vectors, LN2_G)
    copies[3].wait()
    copies[4].wait()
    feed_forward(normed_two, fc1_w, fc2_w, vectors, middle, pre, active, last)
    norm_rows(last, normed_last, vectors, LNF_G)
    copies[5].wait()
    value = dot(normed_last[...], emb_w[...]) + vectors[pl.ds(LAST_B, 1), pl.ds(0, DD)]
    sent[...] = value.astype(BF16)


def encoder_forward(pixels, spots, tables, vectors, weights):
    images = spots.shape[0]
    rows = images * VMAX
    stack = GROUP // (DE // HE) * VMAX
    anywhere = pl.BlockSpec(memory_space=pl.ANY)
    vmem = pl.BlockSpec(memory_space=pltpu.VMEM)
    kept = [
        (DD, BF16),
        (PIX, BF16),
        (DE, F32),
        (DE, BF16),
        (3 * DE, BF16),
        (DE, BF16),
        (DE, F32),
        (DE, BF16),
        (FE, F32),
        (FE, BF16),
        (DE, F32),
        (DE, BF16),
    ]
    out_shape = [jax.ShapeDtypeStruct((rows, columns), kind) for columns, kind in kept]
    out_shape.append(jax.ShapeDtypeStruct((images * DE // GROUP, stack, VMAX), F32))
    return pl.pallas_call(
        encoder_forward_kernel,
        out_shape=out_shape,
        in_specs=[vmem] * 5 + [anywhere] * 6,
        out_specs=[vmem] * len(out_shape),
        scratch_shapes=[pltpu.VMEM(weight.shape, BF16) for weight in weights]
        + [
            pltpu.VMEM((images, VMAX), F32),
            pltpu.VMEM((stack, VMAX), BF16),
            pltpu.VMEM((stack, GROUP), BF16),
            pltpu.SemaphoreType.DMA((6,)),
        ],
        compiler_params=pltpu.CompilerParams(vmem_limit_bytes=60 * 2**20),
        name="encoder_forward",
    )(pixels, spots.reshape(images, 1, VMAX), spots.reshape(-1, 1), tables, vectors, *weights)


def encoder_backward_kernel(
    grad_sent,
    vectors,
    state,
    qkv,
    middle,
    pre,
    last,
    attend,
    qkv_hbm,
    out_hbm,
    fc1_hbm,
    fc2_hbm,
    emb_hbm,
    grad_state_low,
    grad_qkv,
    grad_middle_low,
    grad_pre,
    grad_out_low,
    sums,
    qkv_w,
    out_w,
    fc1_w,
    fc2_w,
    emb_w,
    grad,
    spare,
    grad_mixed,
    attend_low,
    scores_low,
    scores_grad,
    stacked,
    other,
    sems,
):
    pairs = [
        (emb_hbm, emb_w),
        (fc2_hbm, fc2_w),
        (fc1_hbm, fc1_w),
        (out_hbm, out_w),
        (qkv_hbm, qkv_w),
    ]
    copies = [pltpu.make_async_copy(*pair, sems.at[n]) for n, pair in enumerate(pairs)]
    for copy in copies:
        copy.start()
    lanes = pl.ds(0, DE)
    sums[...] = jnp.zeros_like(sums)
    summed = jnp.sum(grad_sent[...].astype(F32), axis=0, keepdims=True)
    sums[pl.ds(LAST_B, 1), pl.ds(0, DD)] = summed
    copies[0].wait()

    def sent_back(part):
        spare[:, part] = dot_nt(grad_sent[...], emb_w[part])

    columns_loop(DE, 256, sent_back)

    def last_back(rows, value):
        grad[rows] = value
        grad_out_low[rows] = value.astype(BF16)
        sums[pl.ds(FC2_B, 1), lanes] += jnp.sum(value, axis=0, keepdims=True)

    norm_rows_back(last, spare, vectors, sums, LNF_G, last_back)
    for copy in copies[1:]:
        copy.wait()
    block_backward(
        state.shape[0] // VMAX,
        VMAX,
        HE,
        (qkv_w, out_w, fc1_w, fc2_w),
        vectors,
        sums,
        (state, middle, grad, spare, pre, qkv),
        (grad_out_low, grad_pre, grad_middle_low, grad_mixed, grad_qkv),
        (attend, attend_low, scores_low, scores_grad, stacked, other),
    )

    def first(rows):
        value = grad[rows]
        sums[pl.ds(0, 1), lanes] += jnp.sum(value, axis=0, keepdims=True)
        grad_state_low[rows] = value.astype(BF16)

    blocks(grad.shape[0], row_step(grad.shape[0]), first)


def encoder_backward(grad_sent, vectors, kept, weights):
    state, qkv, middle, pre, last, attend = kept
    rows = state.shape[0]
    stack = attend.shape[1]
    anywhere = pl.BlockSpec(memory_space=pl.ANY)
    vmem = pl.BlockSpec(memory_space=pltpu.VMEM)
    out_shape = [
        jax.ShapeDtypeStruct((rows, columns), BF16) for columns in (DE, 3 * DE, DE, FE, DE)
    ]
    out_shape.append(jax.ShapeDtypeStruct((VEC_ROWS, VEC_COLS[0]), F32))
    f32 = lambda *shape: pltpu.VMEM(shape, F32)
    b16 = lambda *shape: pltpu.VMEM(shape, BF16)
    return pl.pallas_call(
        encoder_backward_kernel,
        out_shape=out_shape,
        in_specs=[vmem] * 8 + [anywhere] * 5,
        out_specs=[vmem] * len(out_shape),
        scratch_shapes=[pltpu.VMEM(weight.shape, BF16) for weight in weights]
        + [
            f32(rows, DE),
            f32(rows, DE),
            b16(rows, DE),
            b16(stack, VMAX),
            b16(stack, VMAX),
            f32(stack, VMAX),
            b16(stack, GROUP),
            b16(stack, GROUP),
            pltpu.SemaphoreType.DMA((5,)),
        ],
        compiler_params=pltpu.CompilerParams(vmem_limit_bytes=60 * 2**20),
        name="encoder_backward",
    )(grad_sent, vectors, state, qkv, middle, pre, last, attend, *weights)


def band_matrix():
    ids = np.arange(PIX)
    coarse = (ids // (3 * PSIDE) // 2 * (PSIDE // 2) + ids // 3 % PSIDE // 2) * 3 + ids % 3
    low = np.where(coarse[:, None] == np.arange(LOWPIX)[None], 0.25, 0.0)
    high = np.eye(PIX) - np.where(coarse[:, None] == coarse[None], 0.25, 0.0)
    rest = np.zeros((PIX, padded(HEAD) - HEAD))
    return jnp.asarray(np.concatenate([low, high, rest], axis=1).astype(ml_dtypes.bfloat16))


def turn_table(scales, width):
    quarter = width // 4
    frequency = jnp.exp(jnp.arange(quarter, dtype=F32) * (-math.log(10000.0) / quarter))
    angle = (jnp.arange(TURNS, dtype=F32)[None] * scales[:, None])[..., None] * frequency
    return jnp.concatenate([jnp.sin(angle), jnp.cos(angle)], axis=-1)


def forward_backward(parts, pixels, index_rows, counts, scales, masked_tile):
    pe_w, qkv_w, fc1_w, emb_w, out_w, fc2_w = parts[:6]
    dec_weights = parts[6:11]
    enc_vectors, dec_vectors = parts[11:]
    images = counts.shape[0]
    valid = jnp.arange(VMAX, dtype=jnp.int32)[None, :] < counts[:, None]
    spots = jnp.where(valid, index_rows, -1)
    pixels = jnp.pad(pixels.reshape(images, GRID, PIX), ((0, 0), (0, GPAD - GRID), (0, 0)))
    pixels = pixels.reshape(images * GPAD, PIX)
    (
        sent,
        patches,
        state,
        normed_one,
        qkv,
        mixed,
        middle,
        normed_two,
        pre,
        active,
        last,
        normed_last,
        attend,
    ) = encoder_forward(
        pixels,
        spots,
        turn_table(scales, DE),
        enc_vectors,
        [pe_w, qkv_w, out_w, fc1_w, fc2_w, emb_w],
    )
    *dec_factors, grad_sent, dec_sums, loss = decoder(
        sent, pixels, spots, turn_table(scales, DD), masked_tile, dec_vectors, dec_weights
    )
    grad_state, grad_qkv, grad_middle, grad_pre, grad_out, enc_sums = encoder_backward(
        grad_sent,
        enc_vectors,
        [state, qkv, middle, pre, last, attend],
        [qkv_w, out_w, fc1_w, fc2_w, emb_w],
    )
    factors = [patches, grad_state, normed_one, grad_qkv, normed_two, grad_pre]
    factors += [normed_last, grad_sent, mixed, grad_middle, active, grad_out]
    return factors + dec_factors, enc_sums, dec_sums, loss


def body(
    params, first_moment, second_moment, average, pixels, visible_index, visible_count, gsd_id
):
    chips = lax.axis_size("dp")
    rows = params.shape[1] // LANES
    special = chips == math.prod(DP_GRID) and rows % 4 == 0
    masked = jnp.sum(GRID - visible_count).astype(F32)
    if special:
        shards = [a.reshape(-1, 4, LANES) for a in (params, first_moment, second_moment, average)]
        copies, masked_tile = gather_rows(shards[0], jnp.full((8, LANES), masked))
    else:
        copies = lax.all_gather(params.astype(BF16).reshape(-1, LANES), "dp", axis=0, tiled=True)
        copies = lax.all_gather(copies, "grp", axis=0, tiled=True)
        masked_tile = jnp.full((8, LANES), lax.psum(masked, "dp"))
    parts = weight_matrices(copies.reshape(-1, LANES))

    half = visible_count.shape[0] // 2
    core = lax.axis_index("grp")

    def mine(array, count):
        return lax.dynamic_slice_in_dim(array, core * count, count, 0)

    scales = 0.5 + 0.25 * mine(gsd_id, half).astype(F32)
    factors, enc_sums, dec_sums, loss_tile = forward_backward(
        parts,
        mine(pixels, half * GRID),
        mine(visible_index, half),
        mine(visible_count, half),
        scales,
        masked_tile,
    )
    gradient = flat_gradient(chips * rows, factors, enc_sums, dec_sums)
    if special:
        owned, sums = scatter_sums(gradient.reshape(chips, rows // 4, 4, LANES), loss_tile)
        outs = update(sums, masked_tile, [owned] + shards)
        outs = [out.reshape(params.shape) for out in outs[:4]] + [out.reshape(()) for out in outs[4:]]
        return tuple(outs)
    owned = lax.psum_scatter(gradient, "dp", scatter_dimension=0, tiled=True)
    owned = owned.reshape(params.shape)
    squares, loss_sum = lax.psum((jnp.sum(owned * owned), loss_tile[0, 0]), ("grp", "dp"))
    norm = jnp.sqrt(squares)
    scale = jnp.minimum(1.0, CLIP / norm)
    outs = update_values(owned, scale, params, first_moment, second_moment, average)
    return (*outs, loss_sum, masked_tile[0, 0], norm)


def solution(mesh):
    return jax.shard_map(
        body,
        mesh=mesh,
        in_specs=(P("grp", "dp"),) * 4 + (P("dp", None), P("dp", None), P("dp"), P("dp")),
        out_specs=(P("grp", "dp"),) * 4 + (P(), P(), P()),
        check_vma=False,
    )
```

```python
import functools
import math

import jax
import jax.numpy as jnp
import ml_dtypes
import numpy as np
from jax import lax
from jax.experimental import pallas as pl
from jax.experimental.pallas import tpu as pltpu
from jax.sharding import PartitionSpec as P

DE = 1024
HE = 16
FE = 4096
DD = 512
HD = 16
FD = 2048
PSIDE = 16
GSIDE = 14
VMAX = 64
STEP = 10
PIX = 768
LOWPIX = 192
GRID = 196
GPAD = 208
NENC = 8662528
NDEC = 3644352
LANES = 128
UNIT = 4 * LANES

HIGHEST = lax.Precision.HIGHEST
CLIP = 0.05
RATE = 0.01
BETA_ONE = 0.5
BETA_TWO = 0.5
ADAM_EPS = 1e-08
DECAY_WEIGHT = 0.05
AVERAGE_KEEP = 0.9
NORM_EPS = 1e-06
MASK_FILL = -1000000000.0
F32 = jnp.float32
BF16 = jnp.bfloat16
MESH = pl.DeviceIdType.MESH

WIDTH = 512
SUB = 64
PIECE = 8192
VEC_ROWS = 16
VEC_COLS = (FE, FD)
HEAD = LOWPIX + PIX

ENC_LAYOUT = [
    (PIX, DE),
    (DE,),
    (DE,),
    (DE,),
    (DE, 3 * DE),
    (DE,),
    (DE,),
    (DE, FE),
    (FE,),
    (DE,),
    (DE,),
    (DE,),
    (DE, DD),
    (DD,),
]
DEC_LAYOUT = [
    (DD,),
    (DD,),
    (DD,),
    (DD, 3 * DD),
    (DD, DD),
    (DD,),
    (DD,),
    (DD, FD),
    (FD,),
    (FD, DD),
    (DD,),
    (DD,),
    (DD,),
    (DD, HEAD),
    (HEAD,),
]
LENT = [(DE, DE), (FE, DE)]


DP_GRID = (4, 2, 2)
YZX, XZY, ZXY = ("y", "z", "x"), ("x", "z", "y"), ("z", "x", "y")
SPLIT = 2
ORDERS = (YZX,) * SPLIT + (XZY,) * SPLIT + (ZXY,) * SPLIT
PARTS = len(ORDERS)
OWN_FIRST = tuple(range(2 * SPLIT, 3 * SPLIT)) + tuple(range(2 * SPLIT))
SHARES = (0.41, 0.26, 0.33)
WAYS = ("x", "y", "up", "down")
CHUNK = 64
AXIS_SIZE = {"z": 4, "y": 2, "x": 2}
OPPOSITE = {"x": "x", "y": "y", "up": "down", "down": "up"}


def part_ranges(units):
    ends = [0]
    for share in SHARES:
        for _ in range(SPLIT):
            ends.append(ends[-1] + share / SPLIT)
    ends = [round(end * units) for end in ends[:-1]] + [units]
    return [(start, end - start) for start, end in zip(ends, ends[1:])]


def relatives():
    places = [(dz, dy, dx) for dz in range(-3, 4) for dy in (0, 1) for dx in (0, 1)]
    places.remove((0, 0, 0))
    return sorted(places, key=lambda r: abs(r[0]) + r[1] + r[2])


def last_axis(order, place):
    differs = {"z": place[0] != 0, "y": place[1] != 0, "x": place[2] != 0}
    return [axis for axis in order if differs[axis]][-1]


def onward(order, place):
    if place == (0, 0, 0):
        return ["up", "down", "x", "y"]
    axis = last_axis(order, place)
    ways = []
    if axis == "z":
        ways.append("up" if place[0] < 0 else "down")
    for later in order[order.index(axis) + 1 :]:
        ways += ["up", "down"] if later == "z" else [later]
    return ways


def when(condition, action):
    if condition is None:
        action()
    else:
        pl.when(condition)(action)


def both(left, right):
    if left is None:
        return right
    return left if right is None else left & right


class Spot:
    def __init__(self):
        self.grp = lax.axis_index("grp")
        self.dp = lax.axis_index("dp")
        self.x = self.dp % 2
        self.y = (self.dp // 2) % 2
        self.z = self.dp // 4
        self.neighbour = {
            "x": (self.grp, self.index(self.z, self.y, 1 - self.x)),
            "y": (self.grp, self.index(self.z, 1 - self.y, self.x)),
            "up": (self.grp, self.index(jnp.minimum(self.z + 1, 3), self.y, self.x)),
            "down": (self.grp, self.index(jnp.maximum(self.z - 1, 0), self.y, self.x)),
            "core": (1 - self.grp, self.dp),
        }
        self.exists = {"x": None, "y": None, "up": self.z < 3, "down": self.z > 0, "core": None}

    def index(self, z, y, x):
        return z * 4 + y * 2 + x

    def at(self, place):
        z = self.z + place[0]
        y = 1 - self.y if place[1] else self.y
        x = 1 - self.x if place[2] else self.x
        inside = None if place[0] == 0 else (z >= 0) & (z <= 3)
        return z, self.index(z, y, x), inside

    def greet(self, everyone):
        barrier = pltpu.get_barrier_semaphore()

        def signal(step, carry):
            pl.semaphore_signal(
                barrier, inc=1, device_id=self.partner(step, everyone), device_id_type=MESH
            )
            return carry

        lax.fori_loop(1, 32 if everyone else 16, signal, 0)
        if not everyone:
            sibling = self.neighbour["core"]
            pl.semaphore_signal(barrier, inc=1, device_id=sibling, device_id_type=MESH)

    def await_all(self, everyone):
        pl.semaphore_wait(pltpu.get_barrier_semaphore(), 31 if everyone else 16)

    def number(self, everyone):
        return self.grp * 16 + self.dp if everyone else self.dp

    def partner(self, step, everyone):
        if everyone:
            other = (self.number(True) + step) % 32
            return (other // 16, other % 16)
        return (self.grp, (self.dp + step) % 16)


def tell_all(spot, tiles, send_sem, recv_sem, everyone):
    me = spot.number(everyone)
    count = 32 if everyone else 16

    def copy(number, other, target):
        return pltpu.make_async_remote_copy(
            src_ref=tiles.at[number],
            dst_ref=tiles.at[number],
            send_sem=send_sem.at[other],
            recv_sem=recv_sem.at[number],
            device_id=target,
            device_id_type=MESH,
        )

    def start(step, carry):
        copy(me, (me + step) % count, spot.partner(step, everyone)).start()
        return carry

    def finish(step, carry):
        other = (me + step) % count
        copy(other, other, spot.partner(step, everyone)).wait_recv()
        copy(me, other, spot.partner(step, everyone)).wait_send()
        return carry

    return (
        lambda: lax.fori_loop(1, count, start, 0),
        lambda: lax.fori_loop(1, count, finish, 0),
    )


def gather_kernel(
    master_ref,
    masked_ref,
    out_ref,
    masked_out,
    master,
    own_ref,
    tiles,
    local_sem,
    send_sem,
    recv_sem,
    core_send,
    core_recv,
    tile_send,
    tile_recv,
):
    spot = Spot()
    read = pltpu.make_async_copy(master_ref, master, local_sem)
    read.start()
    tiles[spot.dp] = masked_ref[...]
    spot.greet(False)
    tell, told = tell_all(spot, tiles, tile_send, tile_recv, False)
    ranges = part_ranges(own_ref.shape[0])
    read.wait()

    def round_off(start, length):
        def one(first, count):
            block = pl.ds(first, count)
            own_ref[block] = master[block].astype(BF16)

        def step(index, carry):
            one(start + index * CHUNK, CHUNK)
            return carry

        lax.fori_loop(0, length // CHUNK, step, 0)
        if length % CHUNK:
            one(start + length - length % CHUNK, length % CHUNK)

    def copy(part, source, way, from_own):
        target = out_ref.at[spot.grp, source, pl.ds(*ranges[part])]
        origin = own_ref.at[pl.ds(*ranges[part])] if from_own else target
        if way == "core":
            sems = (core_send.at[part, source], core_recv.at[part, source])
        else:
            sems = (send_sem.at[part, source, WAYS.index(way)], recv_sem.at[part, source])
        return pltpu.make_async_remote_copy(
            src_ref=origin,
            dst_ref=target,
            send_sem=sems[0],
            recv_sem=sems[1],
            device_id=spot.neighbour[way],
            device_id_type=MESH,
        )

    sent = []
    for part in OWN_FIRST:
        round_off(*ranges[part])
        if part == OWN_FIRST[0]:
            spot.await_all(False)
        for way in onward(ORDERS[part], (0, 0, 0)):
            when(
                spot.exists[way],
                lambda part=part, way=way: copy(part, spot.dp, way, True).start(),
            )
            sent.append((part, spot.dp, way, spot.exists[way], True))
    local = pltpu.make_async_copy(own_ref, out_ref.at[spot.grp, spot.dp], local_sem)
    local.start()
    tell()
    for part in range(PARTS):
        copy(part, spot.dp, "core", True).start()
        sent.append((part, spot.dp, "core", None, True))
    for place in relatives():
        _, source, inside = spot.at(place)
        for part in range(PARTS):
            ways = onward(ORDERS[part], place)

            def pass_on(part=part, source=source, ways=ways):
                copy(part, source, "x", False).wait_recv()
                for way in ways:
                    when(
                        spot.exists[way],
                        lambda way=way: copy(part, source, way, False).start(),
                    )
                copy(part, source, "core", False).start()

            when(inside, pass_on)
            for way in ways + ["core"]:
                sent.append((part, source, way, both(inside, spot.exists[way]), False))
    for part, source, way, condition, from_own in sent:
        when(condition, lambda: copy(part, source, way, from_own).wait_send())

    def await_core(source, carry):
        for part in range(PARTS):
            landed = out_ref.at[1 - spot.grp, source, pl.ds(*ranges[part])]
            pltpu.make_async_remote_copy(
                src_ref=landed,
                dst_ref=landed,
                send_sem=core_send.at[part, source],
                recv_sem=core_recv.at[part, source],
                device_id=spot.neighbour["core"],
                device_id_type=MESH,
            ).wait_recv()
        return carry

    lax.fori_loop(0, 16, await_core, 0)
    told()
    masked_out[...] = jnp.sum(tiles[...], axis=0)
    local.wait()


def gather_rows(master, masked):
    units = master.shape[0]
    dma = pltpu.SemaphoreType.DMA
    anywhere = pl.BlockSpec(memory_space=pl.ANY)
    vmem = pl.BlockSpec(memory_space=pltpu.VMEM)
    return pl.pallas_call(
        gather_kernel,
        out_shape=(
            jax.ShapeDtypeStruct((2, 16, units, 4, LANES), BF16),
            jax.ShapeDtypeStruct((8, LANES), F32),
        ),
        in_specs=[anywhere, vmem],
        out_specs=(anywhere, vmem),
        scratch_shapes=[
            pltpu.VMEM((units, 4, LANES), F32),
            pltpu.VMEM((units, 4, LANES), BF16),
            pltpu.VMEM((16, 8, LANES), F32),
            dma,
            dma((PARTS, 16, 4)),
            dma((PARTS, 16)),
            dma((PARTS, 16)),
            dma((PARTS, 16)),
            dma((16,)),
            dma((16,)),
        ],
        compiler_params=pltpu.CompilerParams(collective_id=0, has_side_effects=True),
        name="gather_rows",
    )(master, masked)


def slot_tables():
    tables = []
    for order in ORDERS:
        table = {}
        for way in WAYS:
            keys = []
            along = False
            for place in [(0, 0, 0)] + relatives():
                if way in onward(order, place):
                    if place[1:] not in keys:
                        keys.append(place[1:])
                    along = along or place[0] != 0
            table[way] = (keys, 3 if way in ("up", "down") else (4 if along else 1))
        tables.append(table)
    return tables


SLOTS = slot_tables()
STAGES = 3
RING = 28
MANY = 6


def wide_shards(units):
    shard = units * UNIT
    last_matrix = sum(math.prod(shape) for shape in ENC_LAYOUT[:-2])
    return ((last_matrix // shard, 16), (0, -(-NDEC // shard)))


def scatter_kernel(grad_ref, loss_ref, out_ref, sums_ref, *refs):
    ranges = part_ranges(grad_ref.shape[1])
    landing = {}
    for part in range(PARTS):
        for number, way in enumerate(WAYS):
            landing[part, way] = refs[part * 4 + number]
    stage, ring, total, tiles, send_sem, recv_sem, stage_sem, out_sem, tile_send, tile_recv = refs[
        4 * PARTS :
    ]
    spot = Spot()
    spot.greet(True)
    spot.await_all(True)
    bounds = wide_shards(grad_ref.shape[1])
    z_here = spot.z

    def is_wide(owner):
        low = jnp.where(spot.grp == 0, bounds[0][0], bounds[1][0])
        high = jnp.where(spot.grp == 0, bounds[0][1], bounds[1][1])
        return (owner >= low) & (owner < high)

    def is_split(part, way, z, owner):
        axis = way if way in ("x", "y") else "z"
        order = ORDERS[part]
        chips = math.prod(AXIS_SIZE[later] for later in order[order.index(axis) + 1 :])
        if axis != "z":
            return True if chips >= MANY else is_wide(owner)
        chips = chips * (z + 1 if way == "up" else DP_GRID[0] - z)
        return is_wide(owner) | (chips >= MANY)

    def slot(part, way, place, z):
        keys, depth = SLOTS[part][way]
        base = keys.index(place[1:]) * depth
        if way == "up":
            return base + z
        if way == "down":
            return base + z - 1
        return base + (z if depth == 4 else 0)

    def parent(part, place):
        axis = last_axis(ORDERS[part], place)
        if axis == "z":
            return "up" if place[0] > 0 else "down"
        return axis

    def seen_from_parent(part, place):
        way = parent(part, place)
        dz, dy, dx = place
        if way == "x":
            return (dz, dy, 0)
        if way == "y":
            return (dz, 0, dx)
        return (dz - 1 if way == "up" else dz + 1, dy, dx)

    def send(part, place, origin, half):
        z, owner, _ = spot.at(place)
        way = parent(part, place)
        back = OPPOSITE[way]
        place_there = slot(part, back, seen_from_parent(part, place), z)
        return pltpu.make_async_remote_copy(
            src_ref=origin.at[half],
            dst_ref=landing[part, back].at[place_there, half],
            send_sem=send_sem.at[part, owner, half],
            recv_sem=recv_sem.at[part, owner, WAYS.index(back), half],
            device_id=spot.neighbour[way],
            device_id_type=MESH,
        )

    nodes = []
    for place in relatives()[::-1] + [(0, 0, 0)]:
        for part in range(PARTS):
            z, owner, inside = spot.at(place)
            nodes.append((part, place, onward(ORDERS[part], place), z, owner, inside))

    def staged(number):
        part, _, _, _, owner, _ = nodes[number]
        return pltpu.make_async_copy(
            grad_ref.at[owner, pl.ds(*ranges[part])],
            stage.at[number % STAGES, pl.ds(0, ranges[part][1])],
            stage_sem.at[number % STAGES],
        )

    def ring_part(index, part):
        return ring.at[index % RING, :, pl.ds(0, ranges[part][1])]

    def finish_send(number):
        part, place, _, _, owner, inside = nodes[number]
        split = is_split(part, parent(part, place), spot.z, owner)

        def finish():
            source = ring_part(0, part)
            send(part, place, source, 0).wait_send()
            when(
                None if split is True else split,
                lambda: send(part, place, source, 1).wait_send(),
            )

        when(inside, finish)

    for number in range(STAGES - 1):
        when(nodes[number][5], lambda: staged(number).start())
    ringed = []
    for number, (part, place, ways, z, owner, inside) in enumerate(nodes):
        ahead = number + STAGES - 1
        if ahead < len(nodes):
            when(nodes[ahead][5], lambda: staged(ahead).start())
        length = ranges[part][1]
        root = place == (0, 0, 0)
        flat = [way for way in ways if way in ("x", "y")]
        along = [way for way in ways if way in ("up", "down")]
        if not flat:
            if len(ringed) >= RING:
                finish_send(ringed[-RING])
            ringed.append(number)
        ring_index = len(ringed) - 1

        def combine(arriving, number=number, part=part, place=place, z=z, owner=owner):
            slots = [landing[part, way].at[slot(part, way, place, z)] for way in arriving]
            target = slots[0] if slots else ring_part(ring_index, part)

            def arrived(way, item, half):
                pltpu.make_async_remote_copy(
                    src_ref=item.at[half],
                    dst_ref=item.at[half],
                    send_sem=send_sem.at[part, owner, half],
                    recv_sem=recv_sem.at[part, owner, WAYS.index(way), half],
                    device_id=spot.neighbour[way],
                    device_id_type=MESH,
                ).wait_recv()

            def lines(ref):
                return ref.reshape(ref.shape[0] * 4, LANES)

            mine = lines(stage.at[number % STAGES, pl.ds(0, length)])

            def every(action):
                count = 4 * length
                some = 4 * CHUNK

                def step(index, carry):
                    action(pl.ds(pl.multiple_of(index * some, some), some))
                    return carry

                lax.fori_loop(0, count // some, step, 0)
                if count % some:
                    action(pl.ds(count - count % some, count % some))

            def put(rows, value, split):
                if root:
                    lines(total.at[pl.ds(*ranges[part])])[rows] = value
                    return
                high = value.astype(BF16)
                lines(target.at[0])[rows] = high
                if split:
                    lines(target.at[1])[rows] = (value - high.astype(F32)).astype(BF16)

            def summed(rows):
                value = mine[rows]
                for item in slots:
                    value = value + lines(item.at[0])[rows].astype(F32)
                return value

            for way, item in zip(arriving, slots):
                arrived(way, item, 0)
            staged(number).wait()
            theirs = []
            for way in arriving:
                there = {"up": z_here + 1, "down": z_here - 1}.get(way, z_here)
                theirs.append(is_split(part, OPPOSITE[way], there, owner))
            ours = False if root else is_split(part, parent(part, place), z_here, owner)
            some_split = functools.reduce(lambda a, b: a | b, theirs + [ours])

            def short():
                every(lambda rows: put(rows, summed(rows), False))

            def long():
                def first(rows):
                    mine[rows] = summed(rows)

                if slots:
                    every(first)
                for way, item, split in zip(arriving, slots, theirs):

                    def rest(way=way, item=item):
                        arrived(way, item, 1)

                        def one(rows):
                            mine[rows] = mine[rows] + lines(item.at[1])[rows].astype(F32)

                        every(one)

                    when(None if split is True else split, rest)
                every(lambda rows: put(rows, mine[rows], True))

            if some_split is True:
                long()
            else:
                pl.when(some_split)(long)
                pl.when(jnp.logical_not(some_split))(short)
            if not root:
                send(part, place, target, 0).start()
                when(
                    None if ours is True else ours,
                    lambda: send(part, place, target, 1).start(),
                )

        def choose(flat=flat, along=along, combine=combine):
            if not along:
                combine(flat)
            elif len(along) == 1:
                there = spot.exists[along[0]]
                pl.when(there)(lambda: combine(flat + along))
                pl.when(jnp.logical_not(there))(lambda: combine(flat))
            else:
                up, down = spot.exists["up"], spot.exists["down"]
                pl.when(up & down)(lambda: combine(flat + ["up", "down"]))
                pl.when(jnp.logical_not(down))(lambda: combine(flat + ["up"]))
                pl.when(jnp.logical_not(up))(lambda: combine(flat + ["down"]))

        when(inside, choose)
    out = pltpu.make_async_copy(total, out_ref, out_sem)
    out.start()
    units = total.shape[0]

    def square(start, count, running):
        value = total[pl.ds(start, count)]
        return running + jnp.sum(value * value, axis=0)

    squares = lax.fori_loop(
        0,
        units // CHUNK,
        lambda index, running: square(index * CHUNK, CHUNK, running),
        jnp.zeros((4, LANES), F32),
    )
    if units % CHUNK:
        squares = square(units - units % CHUNK, units % CHUNK, squares)
    me = spot.grp * 16 + spot.dp
    tiles[me, pl.ds(0, 4)] = squares
    tiles[me, pl.ds(4, 4)] = loss_ref[pl.ds(4, 4)]
    tell, told = tell_all(spot, tiles, tile_send, tile_recv, True)
    tell()
    done = set(ringed[:-RING])
    for number, node in enumerate(nodes):
        if number not in done and node[1] != (0, 0, 0):
            finish_send(number)
    told()
    sums_ref[...] = jnp.sum(tiles[...], axis=0)
    out.wait()


def scatter_sums(grads, loss):
    units = grads.shape[1]
    ranges = part_ranges(units)
    scratch = []
    for part in range(PARTS):
        for way in WAYS:
            keys, depth = SLOTS[part][way]
            shape = (len(keys) * depth, 2, ranges[part][1], 4, LANES)
            scratch.append(pltpu.VMEM(shape, BF16))
    largest = max(length for _, length in ranges)
    dma = pltpu.SemaphoreType.DMA
    scratch += [
        pltpu.VMEM((STAGES, largest, 4, LANES), F32),
        pltpu.VMEM((RING, 2, largest, 4, LANES), BF16),
        pltpu.VMEM((units, 4, LANES), F32),
        pltpu.VMEM((32, 8, LANES), F32),
        dma((PARTS, 16, 2)),
        dma((PARTS, 16, 4, 2)),
        dma((STAGES,)),
        dma,
        dma((32,)),
        dma((32,)),
    ]
    anywhere = pl.BlockSpec(memory_space=pl.ANY)
    vmem = pl.BlockSpec(memory_space=pltpu.VMEM)
    return pl.pallas_call(
        scatter_kernel,
        out_shape=(
            jax.ShapeDtypeStruct((units, 4, LANES), F32),
            jax.ShapeDtypeStruct((8, LANES), F32),
        ),
        in_specs=[anywhere, vmem],
        out_specs=(anywhere, vmem),
        scratch_shapes=scratch,
        compiler_params=pltpu.CompilerParams(
            collective_id=1, has_side_effects=True, vmem_limit_bytes=63 * 2**20
        ),
        name="scatter_sums",
    )(grads, loss)


def update_values(owned, scale, params, first_moment, second_moment, average):
    clipped = owned * scale
    new_first = BETA_ONE * first_moment + (1.0 - BETA_ONE) * clipped
    new_second = BETA_TWO * second_moment + (1.0 - BETA_TWO) * clipped * clipped
    root = jnp.sqrt(new_second * (1.0 / (1.0 - BETA_TWO**STEP)))
    direction = new_first * (1.0 / (1.0 - BETA_ONE**STEP)) / (root + ADAM_EPS)
    new_params = params - RATE * (direction + DECAY_WEIGHT * params)
    new_average = AVERAGE_KEEP * average + (1.0 - AVERAGE_KEEP) * new_params
    return new_params, new_first, new_second, new_average


def update_kernel(sums_ref, masked_ref, *refs):
    squares = jnp.sum(sums_ref[pl.ds(0, 4)], axis=0, keepdims=True)
    norm = jnp.sqrt(jnp.sum(squares, axis=1, keepdims=True))
    scale = jnp.minimum(1.0, CLIP / norm)
    step = 31

    def one(index, carry):
        block = pl.ds(index * step, step)
        owned, params, first, second, average = [ref[block] for ref in refs[:5]]
        values = update_values(owned, scale[None], params, first, second, average)
        for out, value in zip(refs[5:9], values):
            out[block] = value
        return carry

    lax.fori_loop(0, refs[0].shape[0] // step, one, 0)
    loss_ref, total_ref, norm_ref = refs[9:]
    loss_ref[...] = sums_ref[pl.ds(4, 1), pl.ds(0, 1)]
    total_ref[...] = masked_ref[pl.ds(0, 1), pl.ds(0, 1)]
    norm_ref[...] = norm


def update(sums, masked, arrays):
    units = arrays[0].shape[0]
    depth = 155
    spec = pl.BlockSpec((depth, 4, LANES), lambda i: (i, 0, 0))
    tile = pl.BlockSpec((8, LANES), lambda i: (0, 0))
    scalar = pl.BlockSpec((1, 1), lambda i: (0, 0))
    return pl.pallas_call(
        update_kernel,
        grid=(units // depth,),
        out_shape=[jax.ShapeDtypeStruct((units, 4, LANES), F32)] * 4
        + [jax.ShapeDtypeStruct((1, 1), F32)] * 3,
        in_specs=[tile, tile] + [spec] * 5,
        out_specs=[spec] * 4 + [scalar] * 3,
        name="update",
    )(sums, masked, *arrays)


SLOTS_IN = 5


def sections(layout, base):
    matrices, vectors = [], []
    offset = base
    for shape in layout:
        (matrices if len(shape) == 2 else vectors).append((offset, shape))
        offset += math.prod(shape)
    return matrices, vectors


def matrix_plan(rows):
    enc_matrices, enc_vectors = sections(ENC_LAYOUT, 0)
    dec_matrices, dec_vectors = sections(DEC_LAYOUT, rows * LANES)
    lent = rows * LANES + NDEC
    matrices = enc_matrices + sections(LENT, lent)[0] + dec_matrices
    return matrices, enc_vectors, dec_vectors


def padded(columns):
    return -(-columns // LANES) * LANES


def block_depth(shape):
    if shape[1] % LANES:
        return shape[0]
    depth = shape[0]
    while depth * shape[1] > PIECE * LANES:
        depth //= 2
    return depth


def matrix_kernel(rows, flat_ref, *refs):
    matrices, enc_vectors, dec_vectors = matrix_plan(rows)
    count = len(matrices)
    out_refs = refs[:count]
    vector_refs = refs[count : count + 2]
    blocks = refs[count + 2 : 2 * count + 2]
    flat_in, wide, pairs, vector_in, in_sem, out_sem, vector_sem = refs[2 * count + 2 :]
    lane = lax.broadcasted_iota(jnp.int32, (1, LANES), 1)

    chunks = []
    for number, (offset, shape) in enumerate(matrices):
        depth = block_depth(shape)
        for start in range(0, shape[0], depth):
            place = offset + start * shape[1]
            chunks.append((number, start, depth, place // LANES, place % LANES))

    def load(index):
        number, _, depth, first, shift = chunks[index]
        length = depth * matrices[number][1][1] // LANES
        begin = first // 16 * 16
        end = -(-(first + length + (1 if shift else 0)) // 16) * 16
        copy = pltpu.make_async_copy(
            flat_ref.at[pl.ds(begin, end - begin)],
            flat_in.at[index % SLOTS_IN, pl.ds(0, end - begin)],
            in_sem.at[index % SLOTS_IN],
        )
        return copy, first - begin, end - begin

    def store(index):
        number, start, depth, _, _ = chunks[index]
        slot = start // depth % 2
        return pltpu.make_async_copy(
            blocks[number].at[slot], out_refs[number].at[pl.ds(start, depth)], out_sem.at[number, slot]
        )

    def widen(index, length):
        step = 256

        def one(start, size):
            wide[pl.ds(start, size)] = flat_in[index % SLOTS_IN, pl.ds(start, size)].astype(F32)

        def loop(i, carry):
            one(pl.multiple_of(i * step, step), step)
            return carry

        lax.fori_loop(0, length // step, loop, 0, unroll=2)
        if length % step:
            one(length - length % step, length % step)

    def turned(first, second):
        return pltpu.roll(jnp.where(lane < LANES // 2, second, first), LANES // 2, 1)

    def arrange(index, phase):
        number, start, depth, _, shift = chunks[index]
        columns = matrices[number][1][1]
        block = blocks[number].at[start // depth % 2]
        tiles = columns // LANES

        def plain(i, carry):
            row = pl.multiple_of(i * SUB, SUB)
            packed = wide[pl.ds(phase + row * tiles, SUB * tiles)].reshape(SUB, tiles, LANES)
            swapped = jnp.swapaxes(packed, 0, 1)
            for tile in range(tiles):
                value = swapped[tile]
                if shift:
                    after = wide[pl.ds(phase + row * tiles + tile + 1, SUB, stride=tiles)]
                    value = turned(value, after)
                block[pl.ds(row, SUB), pl.ds(tile * LANES, LANES)] = value.astype(BF16)
            return carry

        def paired(i, carry):
            stride = 2 * columns // LANES
            half = SUB // 2
            row = pl.multiple_of(i * half, half)
            for tile in range(tiles + 1):
                even = wide[pl.ds(phase + row * stride + tile, half, stride=stride)]
                odd = wide[pl.ds(phase + row * stride + tiles + tile, half, stride=stride)]
                if tile < tiles:
                    after = wide[pl.ds(phase + row * stride + tiles + tile + 1, half, stride=stride)]
                    odd = turned(odd, after)
                else:
                    even = jnp.where(lane < LANES // 2, even, 0.0)
                    odd = jnp.where(lane < LANES // 2, pltpu.roll(odd, LANES // 2, 1), 0.0)
                lanes = pl.ds(tile * LANES, LANES)
                pairs[tile, pl.ds(0, half, stride=2)] = even
                pairs[tile, pl.ds(1, half, stride=2)] = odd
                block[pl.ds(pl.multiple_of(i * SUB, SUB), SUB), lanes] = pairs[tile].astype(BF16)
            return carry

        lax.fori_loop(0, depth // SUB, paired if columns % LANES else plain, 0, unroll=4)

    windows = []
    wanted = [(0, n, v) for n, v in enumerate(enc_vectors)]
    wanted += [(1, n, v) for n, v in enumerate(dec_vectors)]
    for _, _, (offset, shape) in wanted:
        first = offset // LANES // 16 * 16
        end = -(-(offset // LANES + -(-shape[0] // LANES)) // 16) * 16
        if windows and first <= windows[-1][1]:
            windows[-1][1] = max(windows[-1][1], end)
        else:
            windows.append([first, end])
    bases = [sum(e - f for f, e in windows[:n]) for n in range(len(windows))]

    def vector_copy(n):
        first, end = windows[n]
        return pltpu.make_async_copy(
            flat_ref.at[pl.ds(first, end - first)],
            vector_in.at[pl.ds(bases[n], end - first)],
            vector_sem.at[n],
        )

    for index in range(SLOTS_IN - 1):
        load(index)[0].start()
    for n in range(len(windows)):
        vector_copy(n).start()
    for index, (number, start, depth, _, _) in enumerate(chunks):
        copy, phase, length = load(index)
        copy.wait()
        if index + SLOTS_IN - 1 < len(chunks):
            load(index + SLOTS_IN - 1)[0].start()
        widen(index, length)
        if start // depth >= 2:
            store(index - 2).wait()
        arrange(index, phase)
        store(index).start()
    for n in range(len(windows)):
        vector_copy(n).wait()
    total = bases[-1] + windows[-1][1] - windows[-1][0]
    wide[pl.ds(0, total)] = vector_in[...].astype(F32)
    for group, n, (offset, shape) in wanted:
        first = offset // LANES
        window = [k for k, (f, e) in enumerate(windows) if f <= first < e][0]
        base = bases[window] + first - windows[window][0]
        for tile in range(-(-shape[0] // LANES)):
            value = wide[pl.ds(base + tile, 1)]
            if shape[0] - tile * LANES < LANES:
                value = jnp.where(lane < shape[0] - tile * LANES, value, 0.0)
            vector_refs[group][pl.ds(n, 1), pl.ds(tile * LANES, LANES)] = value
    for index, (number, start, depth, _, _) in enumerate(chunks):
        if start + 2 * depth >= matrices[number][1][0]:
            store(index).wait()


def weight_matrices(flat):
    rows = flat.shape[0] // 2
    matrices, enc_vectors, dec_vectors = matrix_plan(rows)
    shapes = [(shape[0], padded(shape[1])) for _, shape in matrices]
    buffers = []
    for (_, shape), (_, columns) in zip(matrices, shapes):
        depth = block_depth(shape)
        buffers.append(pltpu.VMEM((min(2, shape[0] // depth), depth, columns), BF16))
    dma = pltpu.SemaphoreType.DMA
    windows = 0
    last = -1
    total = 0
    for offset, shape in enc_vectors + dec_vectors:
        first = offset // LANES // 16 * 16
        end = -(-(offset // LANES + -(-shape[0] // LANES)) // 16) * 16
        if first <= last:
            total += max(0, end - last)
            last = max(last, end)
        else:
            windows += 1
            total += end - first
            last = end
    anywhere = pl.BlockSpec(memory_space=pl.ANY)
    vmem = pl.BlockSpec(memory_space=pltpu.VMEM)
    return pl.pallas_call(
        functools.partial(matrix_kernel, rows),
        out_shape=[jax.ShapeDtypeStruct(shape, BF16) for shape in shapes]
        + [jax.ShapeDtypeStruct((VEC_ROWS, columns), F32) for columns in VEC_COLS],
        in_specs=[anywhere],
        out_specs=[anywhere] * len(shapes) + [vmem, vmem],
        scratch_shapes=buffers
        + [
            pltpu.VMEM((SLOTS_IN, PIECE + 32, LANES), BF16),
            pltpu.VMEM((PIECE + 32, LANES), F32),
            pltpu.VMEM((padded(HEAD) // LANES, SUB, LANES), F32),
            pltpu.VMEM((total, LANES), BF16),
            dma((SLOTS_IN,)),
            dma((len(shapes), 2)),
            dma((windows,)),
        ],
        compiler_params=pltpu.CompilerParams(vmem_limit_bytes=56 * 2**20),
        name="weight_matrices",
    )(flat)


def stream_items(layout, lent):
    items = []
    offset = 0
    numbers = [0, 0]
    for shape in layout + lent:
        matrix = len(shape) == 2
        number = numbers[matrix]
        numbers[matrix] += 1
        depth = block_depth(shape) if matrix else 0
        for start in range(0, shape[0] if matrix else 1, max(depth, 1)):
            items.append((matrix, number, shape, start, depth, offset))
            offset += depth * shape[1] if matrix else shape[0]
    return items, offset


ROLES = (
    (ENC_LAYOUT, [], (0, 1, 2, 3)),
    (DEC_LAYOUT, LENT, (6, 7, 8, 9, 10, 4, 5)),
)
PAIRS = 11
FLIGHTS = 4
DEPTH = 1024


def factor_buffers(shapes):
    sizes = []
    places = {}
    for role in (1, 0):
        taken = set()
        for number in ROLES[role][2]:
            for side in range(2):
                length, columns = shapes[2 * number + side]
                fits = [
                    n
                    for n, size in enumerate(sizes)
                    if n not in taken and size[0] == 2 * length and size[1] >= columns
                ]
                if fits:
                    place = min(fits, key=lambda n: sizes[n][1])
                else:
                    place = len(sizes)
                    sizes.append((2 * length, columns))
                taken.add(place)
                places[role, number, side] = place
    return sizes, places


def product_kernel(rows, shapes, *refs):
    factors, vectors, out_ref = refs[: 2 * PAIRS], refs[2 * PAIRS : 2 * PAIRS + 2], refs[24]
    sizes, places = factor_buffers(shapes)
    buffers = refs[25 : 25 + len(sizes)]
    refs = refs[25 + len(sizes) :]
    others = refs[:2]
    turned_left, tall, rows_out, own_sem, send_sem, recv_sem, out_sem = refs[2:]
    core = lax.axis_index("grp")
    sibling = (1 - core, lax.axis_index("dp"))
    barrier = pltpu.get_barrier_semaphore()
    pl.semaphore_signal(barrier, inc=1, device_id=sibling, device_id_type=MESH)
    pl.semaphore_wait(barrier, 1)

    def half_of(role, number, side, part):
        length, columns = shapes[2 * number + side]
        buffer = buffers[places[role, number, side]]
        return buffer.at[pl.ds(part * length, length), pl.ds(0, columns)]

    def local(role, number, side):
        return pltpu.make_async_copy(
            factors[2 * number + side], half_of(role, number, side, 0), own_sem.at[number, side]
        )

    def remote(role, number, side):
        return pltpu.make_async_remote_copy(
            src_ref=factors[2 * number + side],
            dst_ref=half_of(role, number, side, 1),
            send_sem=send_sem.at[number, side],
            recv_sem=recv_sem.at[number, side],
            device_id=sibling,
            device_id_type=MESH,
        )

    def remote_vectors(role):
        return pltpu.make_async_remote_copy(
            src_ref=vectors[role],
            dst_ref=others[role],
            send_sem=send_sem.at[PAIRS, role],
            recv_sem=recv_sem.at[PAIRS, role],
            device_id=sibling,
            device_id_type=MESH,
        )

    def act(role):
        remote_vectors(1 - role).start()
        pending = [(number, side) for number in ROLES[role][2] for side in range(2)]
        for number, side in pending:
            local(role, number, side).start()
        given = [(number, side) for number in ROLES[1 - role][2] for side in range(2)]
        for number, side in given:
            remote(1 - role, number, side).start()
        remote_vectors(role).wait_recv()

        def ready(number):
            for side in range(2):
                local(role, number, side).wait()
                remote(role, number, side).wait_recv()

        lefts, rights = [], []
        for number in ROLES[role][2]:
            for side, views in ((0, lefts), (1, rights)):
                length, columns = shapes[2 * number + side]
                buffer = buffers[places[role, number, side]]
                views.append(buffer.at[pl.ds(0, 2 * length), pl.ds(0, columns)])
        fill_row(
            rows,
            ROLES[role],
            ready,
            lefts,
            rights,
            vectors[role],
            others[role],
            turned_left,
            tall,
            rows_out,
            out_ref,
            out_sem,
        )
        for number, side in given:
            remote(1 - role, number, side).wait_send()
        remote_vectors(1 - role).wait_send()

    for role in range(2):
        pl.when(core == role)(functools.partial(act, role))


def fill_row(
    rows,
    role,
    ready,
    lefts,
    rights,
    mine_ref,
    other_ref,
    turned_left,
    tall,
    rows_out,
    out_ref,
    out_sem,
):
    layout, lent, numbers = role
    lane = lax.broadcasted_iota(jnp.int32, (1, LANES), 1)
    half = LANES // 2
    items, used = stream_items(layout, lent)
    groups = []
    current = []
    for item in items:
        current.append(item)
        if item[0]:
            groups.append(current)
            current = []
    groups.append(current)

    def vector(item, buffer, base):
        _, number, shape, _, _, _ = item
        for tile in range(-(-shape[0] // LANES)):
            lanes = pl.ds(tile * LANES, LANES)
            buffer[pl.ds(base + tile, 1)] = (
                mine_ref[pl.ds(number, 1), lanes] + other_ref[pl.ds(number, 1), lanes]
            )

    def matrix(item, buffer, base):
        _, number, shape, start, depth, offset = item
        columns = shape[1]
        shifted = offset % LANES
        tiles = -(-columns // LANES)
        width = min(WIDTH, columns)
        if start == 0:
            ready(numbers[number])
            if shifted:
                length = rights[number].shape[0]

                def turn(i, carry):
                    block = pl.ds(pl.multiple_of(i * 64, 64), 64)
                    value = rights[number][block].astype(F32)
                    rights[number][block] = pltpu.roll(value, half, 1).astype(BF16)
                    return carry

                lax.fori_loop(0, length // 64, turn, 0)
        length = lefts[number].shape[0]
        sub = min(DEPTH, depth)

        def loop(step, carry):
            k = pl.multiple_of(start + step * sub, sub)
            turned_left[pl.ds(0, sub), pl.ds(0, length)] = lefts[number][:, pl.ds(k, sub)].T

            def across(c, carry):
                column = pl.multiple_of(c * width, width)
                value = jnp.dot(
                    turned_left[pl.ds(0, sub), pl.ds(0, length)],
                    rights[number][:, pl.ds(column, width)],
                    preferred_element_type=F32,
                )
                row = base + step * sub * tiles
                for piece in range(width // LANES):
                    part = value[:, piece * LANES : (piece + 1) * LANES]
                    tile = c * (width // LANES) + piece
                    if columns % LANES:
                        tall[tile, pl.ds(step * sub, sub)] = part
                    elif shifted and piece == 0:
                        first = row + tile

                        @pl.when(c == 0)
                        def _():
                            before = pltpu.roll(part, 1, 0)
                            index = lax.broadcasted_iota(jnp.int32, (sub, LANES), 0)
                            held = buffer[pl.ds(row, 1)]
                            before = jnp.where(index == 0, held, before)
                            merged = jnp.where(lane < half, before, part)
                            buffer[pl.ds(row, sub, stride=tiles)] = merged
                            buffer[pl.ds(row + sub * tiles, 1)] = part[sub - 1 :]

                        @pl.when(c > 0)
                        def _():
                            buffer[pl.ds(first, sub, stride=tiles)] = part
                    else:
                        buffer[pl.ds(row + tile, sub, stride=tiles)] = part
                return carry

            count = tiles * LANES // width
            lax.fori_loop(0, count, across, 0, unroll=2 if count % 2 == 0 else 1)
            return carry

        lax.fori_loop(0, depth // sub, loop, 0)
        if columns % LANES:
            stride = 2 * columns // LANES
            pair = 64

            def weave(i, carry):
                k = pl.multiple_of(i * 2 * pair, 2 * pair)
                row = base + i * pair * stride
                evens = [tall[t, pl.ds(k, pair, stride=2)] for t in range(tiles)]
                odds = [tall[t, pl.ds(k + 1, pair, stride=2)] for t in range(tiles)]
                for t in range(tiles - 1):
                    buffer[pl.ds(row + t, pair, stride=stride)] = evens[t]
                middle = jnp.where(lane < half, evens[-1], pltpu.roll(odds[0], half, 1))
                buffer[pl.ds(row + tiles - 1, pair, stride=stride)] = middle
                for t in range(1, tiles):
                    both_halves = jnp.where(lane < half, odds[t], odds[t - 1])
                    buffer[pl.ds(row + tiles - 1 + t, pair, stride=stride)] = pltpu.roll(
                        both_halves, half, 1
                    )
                return carry

            lax.fori_loop(0, depth // 2 // pair, weave, 0)

    flights = []
    tail = None
    for number, group in enumerate(groups):
        slot = number % 2
        buffer = rows_out.at[slot]
        if number >= 2:
            for copy in flights[number - 2]:
                copy.wait()
        first = group[0][5] // LANES if group else used // LANES
        begin = first // 8 * 8
        if tail is not None:
            buffer[pl.ds(0, 8)] = rows_out[1 - slot, pl.ds(tail, 8)]
        for item in group:
            (matrix if item[0] else vector)(item, buffer, item[5] // LANES - begin)
        last = number == len(groups) - 1
        if last:
            at = used // LANES - begin
            if used % LANES:
                buffer[pl.ds(at, 1)] = jnp.where(lane < used % LANES, buffer[pl.ds(at, 1)], 0.0)
                at += 1
            length = rows - begin
            if length > at:
                buffer[pl.ds(at, length - at)] = jnp.zeros((length - at, LANES), F32)
        else:
            end = groups[number + 1][0][5] if groups[number + 1] else used
            tail = (end // LANES - begin) // 8 * 8
            length = tail
        cuts = [length * n // FLIGHTS // 8 * 8 for n in range(FLIGHTS)] + [length]
        flight = [
            pltpu.make_async_copy(
                buffer.at[pl.ds(lower, upper - lower)],
                out_ref.at[pl.ds(begin + lower, upper - lower)],
                out_sem.at[slot, n],
            )
            for n, (lower, upper) in enumerate(zip(cuts, cuts[1:]))
            if upper > lower
        ]
        for copy in flight:
            copy.start()
        flights.append(flight)
    for flight in flights[-2:]:
        for copy in flight:
            copy.wait()


def flat_gradient(rows, factors, enc_vectors, dec_vectors):
    shapes = [factor.shape for factor in factors]
    sizes, _ = factor_buffers(shapes)
    longest = max(length for length, _ in sizes)
    dma = pltpu.SemaphoreType.DMA
    anywhere = pl.BlockSpec(memory_space=pl.ANY)
    vmem = pl.BlockSpec(memory_space=pltpu.VMEM)
    return pl.pallas_call(
        functools.partial(product_kernel, rows, shapes),
        out_shape=jax.ShapeDtypeStruct((rows, LANES), F32),
        in_specs=[anywhere] * (2 * PAIRS) + [vmem, vmem],
        out_specs=anywhere,
        scratch_shapes=[pltpu.VMEM(size, BF16) for size in sizes]
        + [
            pltpu.VMEM(enc_vectors.shape, F32),
            pltpu.VMEM(dec_vectors.shape, F32),
            pltpu.VMEM((DEPTH, longest), BF16),
            pltpu.VMEM((padded(HEAD) // LANES, DD, LANES), F32),
            pltpu.VMEM((2, PIECE + 128, LANES), F32),
            dma((PAIRS, 2)),
            dma((PAIRS + 1, 2)),
            dma((PAIRS + 1, 2)),
            dma((2, FLIGHTS)),
        ],
        compiler_params=pltpu.CompilerParams(
            collective_id=2, has_side_effects=True, vmem_limit_bytes=63 * 2**20
        ),
        name="flat_gradient",
    )(*factors, enc_vectors, dec_vectors)


LN1_G, LN1_B, LN2_G, LN2_B, FC1_B, FC2_B, LNF_G, LNF_B, LAST_B = range(1, 10)
GROUP = 256
TURNS = 16
BATCH = 2


def dot(left, right):
    return jnp.dot(left, right, preferred_element_type=F32)


def dot_nt(left, right):
    return lax.dot_general(left, right, (((1,), (1,)), ((), ())), preferred_element_type=F32)


def dot_tn(left, right):
    return lax.dot_general(left, right, (((0,), (0,)), ((), ())), preferred_element_type=F32)


def blocks(length, size, action):
    def step(index, carry):
        action(pl.ds(pl.multiple_of(index * size, size), size))
        return carry

    count = length // size
    unroll = 4 if count % 4 == 0 else 2 if count % 2 == 0 else 1
    lax.fori_loop(0, count, step, 0, unroll=unroll)


def row_step(length):
    return 208 if length % 208 == 0 else 128


def score_step(length):
    return 832 if length % 208 == 0 else 256


def normed(state):
    centered = state - jnp.mean(state, axis=-1, keepdims=True)
    inverse = lax.rsqrt(jnp.mean(centered * centered, axis=-1, keepdims=True) + NORM_EPS)
    return centered * inverse, inverse


def norm_rows(source, target, vectors, gain):
    width = source.shape[1]

    def one(rows):
        unit, _ = normed(source[rows])
        value = unit * vectors[pl.ds(gain, 1), pl.ds(0, width)]
        target[rows] = (value + vectors[pl.ds(gain + 1, 1), pl.ds(0, width)]).astype(BF16)

    blocks(source.shape[0], row_step(source.shape[0]), one)


def norm_rows_back(source, grad, vectors, sums, gain, finish):
    width = source.shape[1]
    lanes = pl.ds(0, width)

    def one(rows):
        unit, inverse = normed(source[rows])
        out = grad[rows]
        sums[pl.ds(gain, 1), lanes] += jnp.sum(out * unit, axis=0, keepdims=True)
        sums[pl.ds(gain + 1, 1), lanes] += jnp.sum(out, axis=0, keepdims=True)
        scaled = out * vectors[pl.ds(gain, 1), lanes]
        mean = jnp.mean(scaled, axis=-1, keepdims=True)
        along = jnp.mean(scaled * unit, axis=-1, keepdims=True)
        finish(rows, inverse * (scaled - mean - unit * along))

    blocks(source.shape[0], row_step(source.shape[0]), one)


def gelu_parts(value):
    below = 0.5 * (1.0 + lax.erf(value * math.sqrt(0.5)))
    return below, value * below


def head_masks(depth):
    lane = lax.broadcasted_iota(jnp.int32, (1, GROUP), 1)
    return [
        ((lane >= head * depth) & (lane < (head + 1) * depth)).astype(F32).astype(BF16)
        for head in range(GROUP // depth)
    ]


def stack_heads(target, value, masks):
    length = value.shape[0]
    for head, mask in enumerate(masks):
        target[pl.ds(head * length, length)] = value * mask


def attention_forward(images, length, heads, qkv, bias, attend, attend_low, stacked, mixed):
    width = mixed.shape[1]
    depth = width // heads
    masks = head_masks(depth)
    groups = width // GROUP
    scale = depth**-0.5

    def one(index, carry):
        image, group = index // groups, index % groups
        rows = pl.ds(pl.multiple_of(image * length, length), length)

        def lanes(part):
            return pl.ds(pl.multiple_of(part * width + group * GROUP, GROUP), GROUP)

        stack_heads(stacked, qkv[rows, lanes(0)], masks)
        attend[index] = dot_nt(stacked[...], qkv[rows, lanes(1)])
        shift = bias[pl.ds(image, 1)]

        def softmax(block):
            scores = attend[index, block] * scale + shift
            raised = jnp.exp(scores - jnp.max(scores, axis=-1, keepdims=True))
            value = raised / jnp.sum(raised, axis=-1, keepdims=True)
            attend[index, block] = value
            attend_low[block] = value.astype(BF16)

        blocks(len(masks) * length, score_step(length), softmax)
        value = qkv[rows, lanes(2)]
        total = jnp.zeros((length, GROUP), F32)
        for head, mask in enumerate(masks):
            total += dot(attend_low[pl.ds(head * length, length)], value * mask)
        mixed[rows, lanes(0)] = total.astype(BF16)
        return carry

    lax.fori_loop(0, images * groups, one, 0, unroll=4)


def attention_backward(
    images, length, heads, qkv, grad_mixed, attend, attend_low, grad_low, grads, stacked, other, out
):
    width = grad_mixed.shape[1]
    depth = width // heads
    masks = head_masks(depth)
    groups = width // GROUP
    scale = depth**-0.5

    def one(index, carry):
        image, group = index // groups, index % groups
        rows = pl.ds(pl.multiple_of(image * length, length), length)

        def lanes(part):
            return pl.ds(pl.multiple_of(part * width + group * GROUP, GROUP), GROUP)

        stack_heads(stacked, qkv[rows, lanes(0)], masks)
        stack_heads(other, grad_mixed[rows, lanes(0)], masks)
        grads[...] = dot_nt(other[...], qkv[rows, lanes(2)])

        def scores(block):
            value = attend[index, block]
            grad = grads[block]
            total = jnp.sum(grad * value, axis=-1, keepdims=True)
            grad_low[block] = (value * (grad - total)).astype(BF16)
            attend_low[block] = value.astype(BF16)

        blocks(len(masks) * length, score_step(length), scores)
        out[rows, lanes(2)] = dot_tn(attend_low[...], other[...]).astype(BF16)
        out[rows, lanes(1)] = (dot_tn(grad_low[...], stacked[...]) * scale).astype(BF16)
        key = qkv[rows, lanes(1)]
        total = jnp.zeros((length, GROUP), F32)
        for head, mask in enumerate(masks):
            total += dot(grad_low[pl.ds(head * length, length)], key * mask)
        out[rows, lanes(0)] = (total * scale).astype(BF16)
        return carry

    lax.fori_loop(0, images * groups, one, 0, unroll=4)


def columns_loop(columns, size, action):
    blocks(columns, min(2 * size, columns), action)


def feed_forward(normed_two, fc1_w, fc2_w, vectors, middle, pre, active, state):
    bias = pl.ds(FC1_B, 1)

    def up(lanes):
        value = dot(normed_two[...], fc1_w[:, lanes]) + vectors[bias, lanes]
        pre[:, lanes] = value
        active[:, lanes] = gelu_parts(value)[1].astype(BF16)

    columns_loop(pre.shape[1], 256, up)

    def down(lanes):
        value = dot(active[...], fc2_w[:, lanes])
        state[:, lanes] = middle[:, lanes] + value + vectors[pl.ds(FC2_B, 1), lanes]

    columns_loop(state.shape[1], 256, down)


def feed_backward(grad_low, fc1_w, fc2_w, pre, sums, grad_pre, out):
    def up(lanes):
        value = pre[:, lanes]
        below, _ = gelu_parts(value)
        slope = below + value * (jnp.exp(-0.5 * value * value) * (1.0 / math.sqrt(2.0 * math.pi)))
        grad = dot_nt(grad_low[...], fc2_w[lanes]) * slope
        sums[pl.ds(FC1_B, 1), lanes] += jnp.sum(grad, axis=0, keepdims=True)
        grad_pre[:, lanes] = grad.astype(BF16)

    columns_loop(pre.shape[1], 256, up)

    def down(lanes):
        out[:, lanes] = dot_nt(grad_pre[...], fc1_w[lanes])

    columns_loop(out.shape[1], 256, down)


def turn_code(places, table):
    lane = lax.broadcasted_iota(jnp.int32, (places.shape[0], TURNS), 1)
    passed = (lane > 0) & (lane < TURNS - 1) & (places >= lane * GSIDE)
    row = jnp.sum(passed.astype(F32), axis=1, keepdims=True).astype(jnp.int32)
    parts = []
    for pick in (row, places - row * GSIDE):
        chosen = (lane == pick).astype(F32)
        parts.append(jnp.dot(chosen, table, precision=HIGHEST, preferred_element_type=F32))
    return jnp.concatenate(parts, axis=1)


def decoder_kernel(
    sent,
    pixels,
    spot_rows,
    spot_columns,
    table,
    masked_ref,
    bands_w,
    vectors,
    qkv_w,
    out_w,
    fc1_w,
    fc2_w,
    head_w,
    normed_one,
    grad_qkv,
    mixed,
    grad_middle_low,
    normed_two,
    grad_pre,
    active,
    grad_out_low,
    normed_last,
    grad_predicted,
    grad_sent,
    sums,
    loss,
    seen,
    bias,
    state,
    middle,
    last,
    grad,
    spare,
    qkv,
    pre,
    attend,
    attend_low,
    scores_low,
    scores_grad,
    stacked,
    other,
    grad_mixed,
):
    width = state.shape[1]
    lanes = pl.ds(0, width)

    @pl.when(pl.program_id(0) == 0)
    def _():
        sums[...] = jnp.zeros_like(sums)
        loss[...] = jnp.zeros_like(loss)

    grid = lax.broadcasted_iota(jnp.int32, (GPAD, 1), 0)
    key = lax.broadcasted_iota(jnp.int32, (1, GPAD), 1)
    token = vectors[pl.ds(0, 1), lanes]
    for image in range(BATCH):
        rows = pl.ds(image * GPAD, GPAD)
        chosen = (grid == spot_rows[image]).astype(F32)
        shown = jnp.sum(chosen, axis=1, keepdims=True)
        placed = dot(chosen.astype(BF16), sent[pl.ds(image * VMAX, VMAX)])
        seen[rows] = jnp.where(grid < GRID, shown, 1.0)
        code = turn_code(grid, table[image])
        state[rows] = jnp.where(shown > 0.5, placed, token) + code
        bias[pl.ds(image, 1)] = jnp.where(key < GRID, 0.0, MASK_FILL)

    norm_rows(state, normed_one, vectors, LN1_G)

    def project(part):
        qkv[:, part] = dot(normed_one[...], qkv_w[:, part]).astype(BF16)

    columns_loop(qkv.shape[1], 256, project)
    attention_forward(
        BATCH, GPAD, HD, qkv, bias, attend, attend_low, stacked, mixed
    )

    def output(part):
        middle[:, part] = state[:, part] + dot(mixed[...], out_w[:, part])

    columns_loop(width, 256, output)
    norm_rows(middle, normed_two, vectors, LN2_G)
    feed_forward(normed_two, fc1_w, fc2_w, vectors, middle, pre, active, last)
    norm_rows(last, normed_last, vectors, LNF_G)

    weight = 1.0 / masked_ref[pl.ds(0, 1), pl.ds(0, 1)]

    def predict(part):
        value = dot(normed_last[...], head_w[:, part]) + vectors[pl.ds(LAST_B, 1), part]
        miss = value - dot(pixels[...], bands_w[:, part])
        index = lax.broadcasted_iota(jnp.int32, (1, GROUP), 1) + part.start
        low = index < LOWPIX
        square = miss * miss
        root = jnp.sqrt(square + 1.0)
        unseen = 1.0 - seen[...]
        loss[...] += jnp.sum(jnp.where(low, square, root - 1.0) * unseen)
        slope = jnp.where(low, 2.0 * miss, miss / root) * (unseen * weight)
        rounded = slope.astype(BF16)
        grad_predicted[:, part] = rounded
        sums[pl.ds(LAST_B, 1), part] += jnp.sum(rounded.astype(F32), axis=0, keepdims=True)

    blocks(head_w.shape[1], GROUP, predict)

    def head_back(part):
        spare[:, part] = dot_nt(grad_predicted[...], head_w[part])

    columns_loop(width, 256, head_back)

    def last_back(rows, value):
        grad[rows] = value
        grad_out_low[rows] = value.astype(BF16)
        sums[pl.ds(FC2_B, 1), lanes] += jnp.sum(value, axis=0, keepdims=True)

    norm_rows_back(last, spare, vectors, sums, LNF_G, last_back)
    block_backward(
        BATCH,
        GPAD,
        HD,
        (qkv_w, out_w, fc1_w, fc2_w),
        vectors,
        sums,
        (state, middle, grad, spare, pre, qkv),
        (grad_out_low, grad_pre, grad_middle_low, grad_mixed, grad_qkv),
        (attend, attend_low, scores_low, scores_grad, stacked, other),
    )
    unseen = 1.0 - seen[...]
    sums[pl.ds(0, 1), lanes] += jnp.sum(grad[...] * unseen, axis=0, keepdims=True)
    for image in range(BATCH):
        chosen = (spot_columns[pl.ds(image * VMAX, VMAX)] == key).astype(F32).astype(BF16)
        value = dot(chosen, grad[pl.ds(image * GPAD, GPAD)].astype(BF16))
        grad_sent[pl.ds(image * VMAX, VMAX)] = value.astype(BF16)


def block_backward(images, length, heads, weights, vectors, sums, states, lows, scratch):
    qkv_w, out_w, fc1_w, fc2_w = weights
    state, middle, grad, spare, pre, qkv = states
    grad_out_low, grad_pre, grad_middle_low, grad_mixed, grad_qkv = lows
    attend, attend_low, scores_low, scores_grad, stacked, other = scratch
    width = state.shape[1]
    feed_backward(grad_out_low, fc1_w, fc2_w, pre, sums, grad_pre, spare)

    def middle_back(rows, value):
        total = grad[rows] + value
        grad[rows] = total
        grad_middle_low[rows] = total.astype(BF16)

    norm_rows_back(middle, spare, vectors, sums, LN2_G, middle_back)

    def mixed_back(part):
        grad_mixed[:, part] = dot_nt(grad_middle_low[...], out_w[part]).astype(BF16)

    columns_loop(width, 256, mixed_back)
    attention_backward(
        images,
        length,
        heads,
        qkv,
        grad_mixed,
        attend,
        attend_low,
        scores_low,
        scores_grad,
        stacked,
        other,
        grad_qkv,
    )

    def first_back(part):
        spare[:, part] = dot_nt(grad_qkv[...], qkv_w[part])

    columns_loop(width, 256, first_back)

    def state_back(rows, value):
        grad[rows] = grad[rows] + value

    norm_rows_back(state, spare, vectors, sums, LN1_G, state_back)


def decoder(sent, pixels, spots, tables, masked_tile, vectors, weights):
    images = spots.shape[0]
    rows = BATCH * GPAD
    shown = BATCH * VMAX
    stack = GROUP // (DD // HD) * GPAD
    widths = [DD, 3 * DD, DD, DD, DD, FD, FD, DD, DD, padded(HEAD)]
    whole = lambda array: pl.BlockSpec(array.shape, lambda i: (0,) * array.ndim)
    by_rows = lambda length, columns: pl.BlockSpec((length, columns), lambda i: (i, 0))
    bands_w = band_matrix()
    out_shape = [jax.ShapeDtypeStruct((images * GPAD, columns), BF16) for columns in widths]
    out_shape.append(jax.ShapeDtypeStruct((images * VMAX, DD), BF16))
    out_shape.append(jax.ShapeDtypeStruct((VEC_ROWS, VEC_COLS[1]), F32))
    out_shape.append(jax.ShapeDtypeStruct((8, LANES), F32))
    operands = [masked_tile, bands_w, vectors, *weights]
    f32 = lambda *shape: pltpu.VMEM(shape, F32)
    b16 = lambda *shape: pltpu.VMEM(shape, BF16)
    return pl.pallas_call(
        decoder_kernel,
        grid=(images // BATCH,),
        out_shape=out_shape,
        in_specs=[
            by_rows(shown, DD),
            by_rows(rows, PIX),
            pl.BlockSpec((BATCH, 1, VMAX), lambda i: (i, 0, 0)),
            by_rows(shown, 1),
            pl.BlockSpec((BATCH, TURNS, DD // 2), lambda i: (i, 0, 0)),
        ]
        + [whole(operand) for operand in operands],
        out_specs=[by_rows(rows, columns) for columns in widths]
        + [by_rows(shown, DD)]
        + [pl.BlockSpec(shape.shape, lambda i: (0, 0)) for shape in out_shape[-2:]],
        scratch_shapes=[
            f32(rows, 1),
            f32(BATCH, GPAD),
            f32(rows, DD),
            f32(rows, DD),
            f32(rows, DD),
            f32(rows, DD),
            f32(rows, DD),
            b16(rows, 3 * DD),
            f32(rows, FD),
            f32(BATCH * DD // GROUP, stack, GPAD),
            b16(stack, GPAD),
            b16(stack, GPAD),
            f32(stack, GPAD),
            b16(stack, GROUP),
            b16(stack, GROUP),
            b16(rows, DD),
        ],
        compiler_params=pltpu.CompilerParams(vmem_limit_bytes=62 * 2**20),
        name="decoder",
    )(sent, pixels, spots.reshape(images, 1, VMAX), spots.reshape(-1, 1), tables, *operands)


def encoder_forward_kernel(
    pixels,
    spot_rows,
    spot_columns,
    table,
    vectors,
    pe_hbm,
    qkv_hbm,
    out_hbm,
    fc1_hbm,
    fc2_hbm,
    emb_hbm,
    sent,
    patches,
    state,
    normed_one,
    qkv,
    mixed,
    middle,
    normed_two,
    pre,
    active,
    last,
    normed_last,
    attend,
    pe_w,
    qkv_w,
    out_w,
    fc1_w,
    fc2_w,
    emb_w,
    bias,
    attend_low,
    stacked,
    sems,
):
    pairs = [
        (pe_hbm, pe_w),
        (qkv_hbm, qkv_w),
        (out_hbm, out_w),
        (fc1_hbm, fc1_w),
        (fc2_hbm, fc2_w),
        (emb_hbm, emb_w),
    ]
    copies = [pltpu.make_async_copy(*pair, sems.at[n]) for n, pair in enumerate(pairs)]
    for copy in copies:
        copy.start()
    images = spot_rows.shape[0]
    key = lax.broadcasted_iota(jnp.int32, (1, GPAD), 1)
    for image in range(images):
        rows = pl.ds(image * VMAX, VMAX)
        place = spot_columns[rows]
        chosen = (place == key).astype(F32).astype(BF16)
        patches[rows] = dot(chosen, pixels[pl.ds(image * GPAD, GPAD)]).astype(BF16)
        code = turn_code(jnp.maximum(place, 0), table[image])
        state[rows] = code + vectors[pl.ds(0, 1), pl.ds(0, DE)]
        bias[pl.ds(image, 1)] = jnp.where(spot_rows[image] < 0, MASK_FILL, 0.0)
    copies[0].wait()

    def embed(part):
        state[:, part] += dot(patches[...], pe_w[:, part])

    columns_loop(DE, 256, embed)
    norm_rows(state, normed_one, vectors, LN1_G)
    copies[1].wait()

    def project(part):
        qkv[:, part] = dot(normed_one[...], qkv_w[:, part]).astype(BF16)

    columns_loop(3 * DE, 256, project)
    attention_forward(images, VMAX, HE, qkv, bias, attend, attend_low, stacked, mixed)
    copies[2].wait()

    def output(part):
        middle[:, part] = state[:, part] + dot(mixed[...], out_w[:, part])

    columns_loop(DE, 256, output)
    norm_rows(middle, normed_two, vectors, LN2_G)
    copies[3].wait()
    copies[4].wait()
    feed_forward(normed_two, fc1_w, fc2_w, vectors, middle, pre, active, last)
    norm_rows(last, normed_last, vectors, LNF_G)
    copies[5].wait()
    value = dot(normed_last[...], emb_w[...]) + vectors[pl.ds(LAST_B, 1), pl.ds(0, DD)]
    sent[...] = value.astype(BF16)


def encoder_forward(pixels, spots, tables, vectors, weights):
    images = spots.shape[0]
    rows = images * VMAX
    stack = GROUP // (DE // HE) * VMAX
    anywhere = pl.BlockSpec(memory_space=pl.ANY)
    vmem = pl.BlockSpec(memory_space=pltpu.VMEM)
    kept = [
        (DD, BF16),
        (PIX, BF16),
        (DE, F32),
        (DE, BF16),
        (3 * DE, BF16),
        (DE, BF16),
        (DE, F32),
        (DE, BF16),
        (FE, F32),
        (FE, BF16),
        (DE, F32),
        (DE, BF16),
    ]
    out_shape = [jax.ShapeDtypeStruct((rows, columns), kind) for columns, kind in kept]
    out_shape.append(jax.ShapeDtypeStruct((images * DE // GROUP, stack, VMAX), F32))
    return pl.pallas_call(
        encoder_forward_kernel,
        out_shape=out_shape,
        in_specs=[vmem] * 5 + [anywhere] * 6,
        out_specs=[vmem] * len(out_shape),
        scratch_shapes=[pltpu.VMEM(weight.shape, BF16) for weight in weights]
        + [
            pltpu.VMEM((images, VMAX), F32),
            pltpu.VMEM((stack, VMAX), BF16),
            pltpu.VMEM((stack, GROUP), BF16),
            pltpu.SemaphoreType.DMA((6,)),
        ],
        compiler_params=pltpu.CompilerParams(vmem_limit_bytes=60 * 2**20),
        name="encoder_forward",
    )(pixels, spots.reshape(images, 1, VMAX), spots.reshape(-1, 1), tables, vectors, *weights)


def encoder_backward_kernel(
    grad_sent,
    vectors,
    state,
    qkv,
    middle,
    pre,
    last,
    attend,
    qkv_hbm,
    out_hbm,
    fc1_hbm,
    fc2_hbm,
    emb_hbm,
    grad_state_low,
    grad_qkv,
    grad_middle_low,
    grad_pre,
    grad_out_low,
    sums,
    qkv_w,
    out_w,
    fc1_w,
    fc2_w,
    emb_w,
    grad,
    spare,
    grad_mixed,
    attend_low,
    scores_low,
    scores_grad,
    stacked,
    other,
    sems,
):
    pairs = [
        (emb_hbm, emb_w),
        (fc2_hbm, fc2_w),
        (fc1_hbm, fc1_w),
        (out_hbm, out_w),
        (qkv_hbm, qkv_w),
    ]
    copies = [pltpu.make_async_copy(*pair, sems.at[n]) for n, pair in enumerate(pairs)]
    for copy in copies:
        copy.start()
    lanes = pl.ds(0, DE)
    sums[...] = jnp.zeros_like(sums)
    summed = jnp.sum(grad_sent[...].astype(F32), axis=0, keepdims=True)
    sums[pl.ds(LAST_B, 1), pl.ds(0, DD)] = summed
    copies[0].wait()

    def sent_back(part):
        spare[:, part] = dot_nt(grad_sent[...], emb_w[part])

    columns_loop(DE, 256, sent_back)

    def last_back(rows, value):
        grad[rows] = value
        grad_out_low[rows] = value.astype(BF16)
        sums[pl.ds(FC2_B, 1), lanes] += jnp.sum(value, axis=0, keepdims=True)

    norm_rows_back(last, spare, vectors, sums, LNF_G, last_back)
    for copy in copies[1:]:
        copy.wait()
    block_backward(
        state.shape[0] // VMAX,
        VMAX,
        HE,
        (qkv_w, out_w, fc1_w, fc2_w),
        vectors,
        sums,
        (state, middle, grad, spare, pre, qkv),
        (grad_out_low, grad_pre, grad_middle_low, grad_mixed, grad_qkv),
        (attend, attend_low, scores_low, scores_grad, stacked, other),
    )

    def first(rows):
        value = grad[rows]
        sums[pl.ds(0, 1), lanes] += jnp.sum(value, axis=0, keepdims=True)
        grad_state_low[rows] = value.astype(BF16)

    blocks(grad.shape[0], row_step(grad.shape[0]), first)


def encoder_backward(grad_sent, vectors, kept, weights):
    state, qkv, middle, pre, last, attend = kept
    rows = state.shape[0]
    stack = attend.shape[1]
    anywhere = pl.BlockSpec(memory_space=pl.ANY)
    vmem = pl.BlockSpec(memory_space=pltpu.VMEM)
    out_shape = [
        jax.ShapeDtypeStruct((rows, columns), BF16) for columns in (DE, 3 * DE, DE, FE, DE)
    ]
    out_shape.append(jax.ShapeDtypeStruct((VEC_ROWS, VEC_COLS[0]), F32))
    f32 = lambda *shape: pltpu.VMEM(shape, F32)
    b16 = lambda *shape: pltpu.VMEM(shape, BF16)
    return pl.pallas_call(
        encoder_backward_kernel,
        out_shape=out_shape,
        in_specs=[vmem] * 8 + [anywhere] * 5,
        out_specs=[vmem] * len(out_shape),
        scratch_shapes=[pltpu.VMEM(weight.shape, BF16) for weight in weights]
        + [
            f32(rows, DE),
            f32(rows, DE),
            b16(rows, DE),
            b16(stack, VMAX),
            b16(stack, VMAX),
            f32(stack, VMAX),
            b16(stack, GROUP),
            b16(stack, GROUP),
            pltpu.SemaphoreType.DMA((5,)),
        ],
        compiler_params=pltpu.CompilerParams(vmem_limit_bytes=60 * 2**20),
        name="encoder_backward",
    )(grad_sent, vectors, state, qkv, middle, pre, last, attend, *weights)


def band_matrix():
    ids = np.arange(PIX)
    coarse = (ids // (3 * PSIDE) // 2 * (PSIDE // 2) + ids // 3 % PSIDE // 2) * 3 + ids % 3
    low = np.where(coarse[:, None] == np.arange(LOWPIX)[None], 0.25, 0.0)
    high = np.eye(PIX) - np.where(coarse[:, None] == coarse[None], 0.25, 0.0)
    rest = np.zeros((PIX, padded(HEAD) - HEAD))
    return jnp.asarray(np.concatenate([low, high, rest], axis=1).astype(ml_dtypes.bfloat16))


def turn_table(scales, width):
    quarter = width // 4
    frequency = jnp.exp(jnp.arange(quarter, dtype=F32) * (-math.log(10000.0) / quarter))
    angle = (jnp.arange(TURNS, dtype=F32)[None] * scales[:, None])[..., None] * frequency
    return jnp.concatenate([jnp.sin(angle), jnp.cos(angle)], axis=-1)


def forward_backward(parts, pixels, index_rows, counts, scales, masked_tile):
    pe_w, qkv_w, fc1_w, emb_w, out_w, fc2_w = parts[:6]
    dec_weights = parts[6:11]
    enc_vectors, dec_vectors = parts[11:]
    images = counts.shape[0]
    valid = jnp.arange(VMAX, dtype=jnp.int32)[None, :] < counts[:, None]
    spots = jnp.where(valid, index_rows, -1)
    pixels = jnp.pad(pixels.reshape(images, GRID, PIX), ((0, 0), (0, GPAD - GRID), (0, 0)))
    pixels = pixels.reshape(images * GPAD, PIX)
    (
        sent,
        patches,
        state,
        normed_one,
        qkv,
        mixed,
        middle,
        normed_two,
        pre,
        active,
        last,
        normed_last,
        attend,
    ) = encoder_forward(
        pixels,
        spots,
        turn_table(scales, DE),
        enc_vectors,
        [pe_w, qkv_w, out_w, fc1_w, fc2_w, emb_w],
    )
    *dec_factors, grad_sent, dec_sums, loss = decoder(
        sent, pixels, spots, turn_table(scales, DD), masked_tile, dec_vectors, dec_weights
    )
    grad_state, grad_qkv, grad_middle, grad_pre, grad_out, enc_sums = encoder_backward(
        grad_sent,
        enc_vectors,
        [state, qkv, middle, pre, last, attend],
        [qkv_w, out_w, fc1_w, fc2_w, emb_w],
    )
    factors = [patches, grad_state, normed_one, grad_qkv, normed_two, grad_pre]
    factors += [normed_last, grad_sent, mixed, grad_middle, active, grad_out]
    return factors + dec_factors, enc_sums, dec_sums, loss


def body(
    params, first_moment, second_moment, average, pixels, visible_index, visible_count, gsd_id
):
    chips = lax.axis_size("dp")
    rows = params.shape[1] // LANES
    special = chips == math.prod(DP_GRID) and rows % 4 == 0
    masked = jnp.sum(GRID - visible_count).astype(F32)
    if special:
        shards = [a.reshape(-1, 4, LANES) for a in (params, first_moment, second_moment, average)]
        copies, masked_tile = gather_rows(shards[0], jnp.full((8, LANES), masked))
    else:
        copies = lax.all_gather(params.astype(BF16).reshape(-1, LANES), "dp", axis=0, tiled=True)
        copies = lax.all_gather(copies, "grp", axis=0, tiled=True)
        masked_tile = jnp.full((8, LANES), lax.psum(masked, "dp"))
    parts = weight_matrices(copies.reshape(-1, LANES))

    half = visible_count.shape[0] // 2
    core = lax.axis_index("grp")

    def mine(array, count):
        return lax.dynamic_slice_in_dim(array, core * count, count, 0)

    scales = 0.5 + 0.25 * mine(gsd_id, half).astype(F32)
    factors, enc_sums, dec_sums, loss_tile = forward_backward(
        parts,
        mine(pixels, half * GRID),
        mine(visible_index, half),
        mine(visible_count, half),
        scales,
        masked_tile,
    )
    gradient = flat_gradient(chips * rows, factors, enc_sums, dec_sums)
    if special:
        owned, sums = scatter_sums(gradient.reshape(chips, rows // 4, 4, LANES), loss_tile)
        outs = update(sums, masked_tile, [owned] + shards)
        outs = [out.reshape(params.shape) for out in outs[:4]] + [out.reshape(()) for out in outs[4:]]
        return tuple(outs)
    owned = lax.psum_scatter(gradient, "dp", scatter_dimension=0, tiled=True)
    owned = owned.reshape(params.shape)
    squares, loss_sum = lax.psum((jnp.sum(owned * owned), loss_tile[0, 0]), ("grp", "dp"))
    norm = jnp.sqrt(squares)
    scale = jnp.minimum(1.0, CLIP / norm)
    outs = update_values(owned, scale, params, first_moment, second_moment, average)
    return (*outs, loss_sum, masked_tile[0, 0], norm)


def solution(mesh):
    return jax.shard_map(
        body,
        mesh=mesh,
        in_specs=(P("grp", "dp"),) * 4 + (P("dp", None), P("dp", None), P("dp"), P("dp")),
        out_specs=(P("grp", "dp"),) * 4 + (P(), P(), P()),
        check_vma=False,
    )
```

```python
import functools
import math

import jax
import jax.numpy as jnp
import ml_dtypes
import numpy as np
from jax import lax
from jax.experimental import pallas as pl
from jax.experimental.pallas import tpu as pltpu
from jax.sharding import PartitionSpec as P

DE = 1024
HE = 16
FE = 4096
DD = 512
HD = 16
FD = 2048
PSIDE = 16
GSIDE = 14
VMAX = 64
STEP = 10
PIX = 768
LOWPIX = 192
GRID = 196
GPAD = 208
NENC = 8662528
NDEC = 3644352
LANES = 128
UNIT = 4 * LANES

HIGHEST = lax.Precision.HIGHEST
CLIP = 0.05
RATE = 0.01
BETA_ONE = 0.5
BETA_TWO = 0.5
ADAM_EPS = 1e-08
DECAY_WEIGHT = 0.05
AVERAGE_KEEP = 0.9
NORM_EPS = 1e-06
MASK_FILL = -1000000000.0
F32 = jnp.float32
BF16 = jnp.bfloat16
MESH = pl.DeviceIdType.MESH

WIDTH = 512
SUB = 64
PIECE = 8192
VEC_ROWS = 16
VEC_COLS = (FE, FD)
HEAD = LOWPIX + PIX

ENC_LAYOUT = [
    (PIX, DE),
    (DE,),
    (DE,),
    (DE,),
    (DE, 3 * DE),
    (DE,),
    (DE,),
    (DE, FE),
    (FE,),
    (DE,),
    (DE,),
    (DE,),
    (DE, DD),
    (DD,),
]
DEC_LAYOUT = [
    (DD,),
    (DD,),
    (DD,),
    (DD, 3 * DD),
    (DD, DD),
    (DD,),
    (DD,),
    (DD, FD),
    (FD,),
    (FD, DD),
    (DD,),
    (DD,),
    (DD,),
    (DD, HEAD),
    (HEAD,),
]
LENT = [(DE, DE), (FE, DE)]


DP_GRID = (4, 2, 2)
YZX, XZY, ZXY = ("y", "z", "x"), ("x", "z", "y"), ("z", "x", "y")
SPLIT = 2
ORDERS = (YZX,) * SPLIT + (XZY,) * SPLIT + (ZXY,) * SPLIT
PARTS = len(ORDERS)
OWN_FIRST = tuple(range(2 * SPLIT, 3 * SPLIT)) + tuple(range(2 * SPLIT))
SHARES = (0.41, 0.26, 0.33)
WAYS = ("x", "y", "up", "down")
CHUNK = 64
AXIS_SIZE = {"z": 4, "y": 2, "x": 2}
OPPOSITE = {"x": "x", "y": "y", "up": "down", "down": "up"}


def part_ranges(units):
    ends = [0]
    for share in SHARES:
        for _ in range(SPLIT):
            ends.append(ends[-1] + share / SPLIT)
    ends = [round(end * units) for end in ends[:-1]] + [units]
    return [(start, end - start) for start, end in zip(ends, ends[1:])]


def relatives():
    places = [(dz, dy, dx) for dz in range(-3, 4) for dy in (0, 1) for dx in (0, 1)]
    places.remove((0, 0, 0))
    return sorted(places, key=lambda r: abs(r[0]) + r[1] + r[2])


def last_axis(order, place):
    differs = {"z": place[0] != 0, "y": place[1] != 0, "x": place[2] != 0}
    return [axis for axis in order if differs[axis]][-1]


def onward(order, place):
    if place == (0, 0, 0):
        return ["up", "down", "x", "y"]
    axis = last_axis(order, place)
    ways = []
    if axis == "z":
        ways.append("up" if place[0] < 0 else "down")
    for later in order[order.index(axis) + 1 :]:
        ways += ["up", "down"] if later == "z" else [later]
    return ways


def when(condition, action):
    if condition is None:
        action()
    else:
        pl.when(condition)(action)


def both(left, right):
    if left is None:
        return right
    return left if right is None else left & right


class Spot:
    def __init__(self):
        self.grp = lax.axis_index("grp")
        self.dp = lax.axis_index("dp")
        self.x = self.dp % 2
        self.y = (self.dp // 2) % 2
        self.z = self.dp // 4
        self.neighbour = {
            "x": (self.grp, self.index(self.z, self.y, 1 - self.x)),
            "y": (self.grp, self.index(self.z, 1 - self.y, self.x)),
            "up": (self.grp, self.index(jnp.minimum(self.z + 1, 3), self.y, self.x)),
            "down": (self.grp, self.index(jnp.maximum(self.z - 1, 0), self.y, self.x)),
            "core": (1 - self.grp, self.dp),
        }
        self.exists = {"x": None, "y": None, "up": self.z < 3, "down": self.z > 0, "core": None}

    def index(self, z, y, x):
        return z * 4 + y * 2 + x

    def at(self, place):
        z = self.z + place[0]
        y = 1 - self.y if place[1] else self.y
        x = 1 - self.x if place[2] else self.x
        inside = None if place[0] == 0 else (z >= 0) & (z <= 3)
        return z, self.index(z, y, x), inside

    def greet(self, everyone):
        barrier = pltpu.get_barrier_semaphore()

        def signal(step, carry):
            pl.semaphore_signal(
                barrier, inc=1, device_id=self.partner(step, everyone), device_id_type=MESH
            )
            return carry

        lax.fori_loop(1, 32 if everyone else 16, signal, 0)
        if not everyone:
            sibling = self.neighbour["core"]
            pl.semaphore_signal(barrier, inc=1, device_id=sibling, device_id_type=MESH)

    def await_all(self, everyone):
        pl.semaphore_wait(pltpu.get_barrier_semaphore(), 31 if everyone else 16)

    def number(self, everyone):
        return self.grp * 16 + self.dp if everyone else self.dp

    def partner(self, step, everyone):
        if everyone:
            other = (self.number(True) + step) % 32
            return (other // 16, other % 16)
        return (self.grp, (self.dp + step) % 16)


def tell_all(spot, tiles, send_sem, recv_sem, everyone):
    me = spot.number(everyone)
    count = 32 if everyone else 16

    def copy(number, other, target):
        return pltpu.make_async_remote_copy(
            src_ref=tiles.at[number],
            dst_ref=tiles.at[number],
            send_sem=send_sem.at[other],
            recv_sem=recv_sem.at[number],
            device_id=target,
            device_id_type=MESH,
        )

    def start(step, carry):
        copy(me, (me + step) % count, spot.partner(step, everyone)).start()
        return carry

    def finish(step, carry):
        other = (me + step) % count
        copy(other, other, spot.partner(step, everyone)).wait_recv()
        copy(me, other, spot.partner(step, everyone)).wait_send()
        return carry

    return (
        lambda: lax.fori_loop(1, count, start, 0),
        lambda: lax.fori_loop(1, count, finish, 0),
    )


def gather_kernel(
    master_ref,
    masked_ref,
    out_ref,
    masked_out,
    master,
    own_ref,
    tiles,
    local_sem,
    send_sem,
    recv_sem,
    core_send,
    core_recv,
    tile_send,
    tile_recv,
):
    spot = Spot()
    read = pltpu.make_async_copy(master_ref, master, local_sem)
    read.start()
    tiles[spot.dp] = masked_ref[...]
    spot.greet(False)
    tell, told = tell_all(spot, tiles, tile_send, tile_recv, False)
    ranges = part_ranges(own_ref.shape[0])
    read.wait()

    def round_off(start, length):
        def one(first, count):
            block = pl.ds(first, count)
            own_ref[block] = master[block].astype(BF16)

        def step(index, carry):
            one(start + index * CHUNK, CHUNK)
            return carry

        lax.fori_loop(0, length // CHUNK, step, 0)
        if length % CHUNK:
            one(start + length - length % CHUNK, length % CHUNK)

    def copy(part, source, way, from_own):
        target = out_ref.at[spot.grp, source, pl.ds(*ranges[part])]
        origin = own_ref.at[pl.ds(*ranges[part])] if from_own else target
        if way == "core":
            sems = (core_send.at[part, source], core_recv.at[part, source])
        else:
            sems = (send_sem.at[part, source, WAYS.index(way)], recv_sem.at[part, source])
        return pltpu.make_async_remote_copy(
            src_ref=origin,
            dst_ref=target,
            send_sem=sems[0],
            recv_sem=sems[1],
            device_id=spot.neighbour[way],
            device_id_type=MESH,
        )

    sent = []
    for part in OWN_FIRST:
        round_off(*ranges[part])
        if part == OWN_FIRST[0]:
            spot.await_all(False)
        for way in onward(ORDERS[part], (0, 0, 0)):
            when(
                spot.exists[way],
                lambda part=part, way=way: copy(part, spot.dp, way, True).start(),
            )
            sent.append((part, spot.dp, way, spot.exists[way], True))
    local = pltpu.make_async_copy(own_ref, out_ref.at[spot.grp, spot.dp], local_sem)
    local.start()
    tell()
    for part in range(PARTS):
        copy(part, spot.dp, "core", True).start()
        sent.append((part, spot.dp, "core", None, True))
    for place in relatives():
        _, source, inside = spot.at(place)
        for part in range(PARTS):
            ways = onward(ORDERS[part], place)

            def pass_on(part=part, source=source, ways=ways):
                copy(part, source, "x", False).wait_recv()
                for way in ways:
                    when(
                        spot.exists[way],
                        lambda way=way: copy(part, source, way, False).start(),
                    )
                copy(part, source, "core", False).start()

            when(inside, pass_on)
            for way in ways + ["core"]:
                sent.append((part, source, way, both(inside, spot.exists[way]), False))
    for part, source, way, condition, from_own in sent:
        when(condition, lambda: copy(part, source, way, from_own).wait_send())

    def await_core(source, carry):
        for part in range(PARTS):
            landed = out_ref.at[1 - spot.grp, source, pl.ds(*ranges[part])]
            pltpu.make_async_remote_copy(
                src_ref=landed,
                dst_ref=landed,
                send_sem=core_send.at[part, source],
                recv_sem=core_recv.at[part, source],
                device_id=spot.neighbour["core"],
                device_id_type=MESH,
            ).wait_recv()
        return carry

    lax.fori_loop(0, 16, await_core, 0)
    told()
    masked_out[...] = jnp.sum(tiles[...], axis=0)
    local.wait()


def gather_rows(master, masked):
    units = master.shape[0]
    dma = pltpu.SemaphoreType.DMA
    anywhere = pl.BlockSpec(memory_space=pl.ANY)
    vmem = pl.BlockSpec(memory_space=pltpu.VMEM)
    return pl.pallas_call(
        gather_kernel,
        out_shape=(
            jax.ShapeDtypeStruct((2, 16, units, 4, LANES), BF16),
            jax.ShapeDtypeStruct((8, LANES), F32),
        ),
        in_specs=[anywhere, vmem],
        out_specs=(anywhere, vmem),
        scratch_shapes=[
            pltpu.VMEM((units, 4, LANES), F32),
            pltpu.VMEM((units, 4, LANES), BF16),
            pltpu.VMEM((16, 8, LANES), F32),
            dma,
            dma((PARTS, 16, 4)),
            dma((PARTS, 16)),
            dma((PARTS, 16)),
            dma((PARTS, 16)),
            dma((16,)),
            dma((16,)),
        ],
        compiler_params=pltpu.CompilerParams(collective_id=0, has_side_effects=True),
        name="gather_rows",
    )(master, masked)


def slot_tables():
    tables = []
    for order in ORDERS:
        table = {}
        for way in WAYS:
            keys = []
            along = False
            for place in [(0, 0, 0)] + relatives():
                if way in onward(order, place):
                    if place[1:] not in keys:
                        keys.append(place[1:])
                    along = along or place[0] != 0
            table[way] = (keys, 3 if way in ("up", "down") else (4 if along else 1))
        tables.append(table)
    return tables


SLOTS = slot_tables()
STAGES = 3
RING = 30
MANY = 6


def wide_shards(units):
    shard = units * UNIT
    last_matrix = sum(math.prod(shape) for shape in ENC_LAYOUT[:-2])
    return ((last_matrix // shard, 16), (0, -(-NDEC // shard)))


def scatter_kernel(grad_ref, loss_ref, out_ref, sums_ref, *refs):
    ranges = part_ranges(grad_ref.shape[1])
    landing = {}
    for part in range(PARTS):
        for number, way in enumerate(WAYS):
            landing[part, way] = refs[part * 4 + number]
    stage, ring, total, tiles, send_sem, recv_sem, stage_sem, out_sem, tile_send, tile_recv = refs[
        4 * PARTS :
    ]
    spot = Spot()
    spot.greet(True)
    spot.await_all(True)
    bounds = wide_shards(grad_ref.shape[1])
    z_here = spot.z

    def is_wide(owner):
        low = jnp.where(spot.grp == 0, bounds[0][0], bounds[1][0])
        high = jnp.where(spot.grp == 0, bounds[0][1], bounds[1][1])
        return (owner >= low) & (owner < high)

    def is_split(part, way, z, owner):
        axis = way if way in ("x", "y") else "z"
        order = ORDERS[part]
        chips = math.prod(AXIS_SIZE[later] for later in order[order.index(axis) + 1 :])
        if axis != "z":
            return True if chips >= MANY else is_wide(owner)
        chips = chips * (z + 1 if way == "up" else DP_GRID[0] - z)
        return is_wide(owner) | (chips >= MANY)

    def slot(part, way, place, z):
        keys, depth = SLOTS[part][way]
        base = keys.index(place[1:]) * depth
        if way == "up":
            return base + z
        if way == "down":
            return base + z - 1
        return base + (z if depth == 4 else 0)

    def parent(part, place):
        axis = last_axis(ORDERS[part], place)
        if axis == "z":
            return "up" if place[0] > 0 else "down"
        return axis

    def seen_from_parent(part, place):
        way = parent(part, place)
        dz, dy, dx = place
        if way == "x":
            return (dz, dy, 0)
        if way == "y":
            return (dz, 0, dx)
        return (dz - 1 if way == "up" else dz + 1, dy, dx)

    def send(part, place, origin, half):
        z, owner, _ = spot.at(place)
        way = parent(part, place)
        back = OPPOSITE[way]
        place_there = slot(part, back, seen_from_parent(part, place), z)
        return pltpu.make_async_remote_copy(
            src_ref=origin.at[half],
            dst_ref=landing[part, back].at[place_there, half],
            send_sem=send_sem.at[part, owner, half],
            recv_sem=recv_sem.at[part, owner, WAYS.index(back), half],
            device_id=spot.neighbour[way],
            device_id_type=MESH,
        )

    nodes = []
    for place in relatives()[::-1] + [(0, 0, 0)]:
        for part in range(PARTS):
            z, owner, inside = spot.at(place)
            nodes.append((part, place, onward(ORDERS[part], place), z, owner, inside))

    def staged(number):
        part, _, _, _, owner, _ = nodes[number]
        return pltpu.make_async_copy(
            grad_ref.at[owner, pl.ds(*ranges[part])],
            stage.at[number % STAGES, pl.ds(0, ranges[part][1])],
            stage_sem.at[number % STAGES],
        )

    def ring_part(index, part):
        return ring.at[index % RING, :, pl.ds(0, ranges[part][1])]

    def finish_send(number):
        part, place, _, _, owner, inside = nodes[number]
        split = is_split(part, parent(part, place), spot.z, owner)

        def finish():
            source = ring_part(0, part)
            send(part, place, source, 0).wait_send()
            when(
                None if split is True else split,
                lambda: send(part, place, source, 1).wait_send(),
            )

        when(inside, finish)

    for number in range(STAGES - 1):
        when(nodes[number][5], lambda: staged(number).start())
    ringed = []
    for number, (part, place, ways, z, owner, inside) in enumerate(nodes):
        ahead = number + STAGES - 1
        if ahead < len(nodes):
            when(nodes[ahead][5], lambda: staged(ahead).start())
        length = ranges[part][1]
        root = place == (0, 0, 0)
        flat = [way for way in ways if way in ("x", "y")]
        along = [way for way in ways if way in ("up", "down")]
        if not flat:
            if len(ringed) >= RING:
                finish_send(ringed[-RING])
            ringed.append(number)
        ring_index = len(ringed) - 1

        def combine(arriving, number=number, part=part, place=place, z=z, owner=owner):
            slots = [landing[part, way].at[slot(part, way, place, z)] for way in arriving]
            target = slots[0] if slots else ring_part(ring_index, part)

            def arrived(way, item, half):
                pltpu.make_async_remote_copy(
                    src_ref=item.at[half],
                    dst_ref=item.at[half],
                    send_sem=send_sem.at[part, owner, half],
                    recv_sem=recv_sem.at[part, owner, WAYS.index(way), half],
                    device_id=spot.neighbour[way],
                    device_id_type=MESH,
                ).wait_recv()

            def lines(ref):
                return ref.reshape(ref.shape[0] * 4, LANES)

            mine = lines(stage.at[number % STAGES, pl.ds(0, length)])

            def every(action):
                count = 4 * length
                some = 4 * CHUNK

                def step(index, carry):
                    action(pl.ds(pl.multiple_of(index * some, some), some))
                    return carry

                lax.fori_loop(0, count // some, step, 0)
                if count % some:
                    action(pl.ds(count - count % some, count % some))

            def put(rows, value, split):
                if root:
                    lines(total.at[pl.ds(*ranges[part])])[rows] = value
                    return
                high = value.astype(BF16)
                lines(target.at[0])[rows] = high
                if split:
                    lines(target.at[1])[rows] = (value - high.astype(F32)).astype(BF16)

            def summed(rows):
                value = mine[rows]
                for item in slots:
                    value = value + lines(item.at[0])[rows].astype(F32)
                return value

            for way, item in zip(arriving, slots):
                arrived(way, item, 0)
            staged(number).wait()
            theirs = []
            for way in arriving:
                there = {"up": z_here + 1, "down": z_here - 1}.get(way, z_here)
                theirs.append(is_split(part, OPPOSITE[way], there, owner))
            ours = False if root else is_split(part, parent(part, place), z_here, owner)
            some_split = functools.reduce(lambda a, b: a | b, theirs + [ours])

            def short():
                every(lambda rows: put(rows, summed(rows), False))

            def long():
                def first(rows):
                    mine[rows] = summed(rows)

                if slots:
                    every(first)
                for way, item, split in zip(arriving, slots, theirs):

                    def rest(way=way, item=item):
                        arrived(way, item, 1)

                        def one(rows):
                            mine[rows] = mine[rows] + lines(item.at[1])[rows].astype(F32)

                        every(one)

                    when(None if split is True else split, rest)
                every(lambda rows: put(rows, mine[rows], True))

            if some_split is True:
                long()
            else:
                pl.when(some_split)(long)
                pl.when(jnp.logical_not(some_split))(short)
            if not root:
                send(part, place, target, 0).start()
                when(
                    None if ours is True else ours,
                    lambda: send(part, place, target, 1).start(),
                )

        def choose(flat=flat, along=along, combine=combine):
            if not along:
                combine(flat)
            elif len(along) == 1:
                there = spot.exists[along[0]]
                pl.when(there)(lambda: combine(flat + along))
                pl.when(jnp.logical_not(there))(lambda: combine(flat))
            else:
                up, down = spot.exists["up"], spot.exists["down"]
                pl.when(up & down)(lambda: combine(flat + ["up", "down"]))
                pl.when(jnp.logical_not(down))(lambda: combine(flat + ["up"]))
                pl.when(jnp.logical_not(up))(lambda: combine(flat + ["down"]))

        when(inside, choose)
    out = pltpu.make_async_copy(total, out_ref, out_sem)
    out.start()
    units = total.shape[0]

    def square(start, count, running):
        value = total[pl.ds(start, count)]
        return running + jnp.sum(value * value, axis=0)

    squares = lax.fori_loop(
        0,
        units // CHUNK,
        lambda index, running: square(index * CHUNK, CHUNK, running),
        jnp.zeros((4, LANES), F32),
    )
    if units % CHUNK:
        squares = square(units - units % CHUNK, units % CHUNK, squares)
    me = spot.grp * 16 + spot.dp
    tiles[me, pl.ds(0, 4)] = squares
    tiles[me, pl.ds(4, 4)] = loss_ref[pl.ds(4, 4)]
    tell, told = tell_all(spot, tiles, tile_send, tile_recv, True)
    tell()
    done = set(ringed[:-RING])
    for number, node in enumerate(nodes):
        if number not in done and node[1] != (0, 0, 0):
            finish_send(number)
    told()
    sums_ref[...] = jnp.sum(tiles[...], axis=0)
    out.wait()


def scatter_sums(grads, loss):
    units = grads.shape[1]
    ranges = part_ranges(units)
    scratch = []
    for part in range(PARTS):
        for way in WAYS:
            keys, depth = SLOTS[part][way]
            shape = (len(keys) * depth, 2, ranges[part][1], 4, LANES)
            scratch.append(pltpu.VMEM(shape, BF16))
    largest = max(length for _, length in ranges)
    dma = pltpu.SemaphoreType.DMA
    scratch += [
        pltpu.VMEM((STAGES, largest, 4, LANES), F32),
        pltpu.VMEM((RING, 2, largest, 4, LANES), BF16),
        pltpu.VMEM((units, 4, LANES), F32),
        pltpu.VMEM((32, 8, LANES), F32),
        dma((PARTS, 16, 2)),
        dma((PARTS, 16, 4, 2)),
        dma((STAGES,)),
        dma,
        dma((32,)),
        dma((32,)),
    ]
    anywhere = pl.BlockSpec(memory_space=pl.ANY)
    vmem = pl.BlockSpec(memory_space=pltpu.VMEM)
    return pl.pallas_call(
        scatter_kernel,
        out_shape=(
            jax.ShapeDtypeStruct((units, 4, LANES), F32),
            jax.ShapeDtypeStruct((8, LANES), F32),
        ),
        in_specs=[anywhere, vmem],
        out_specs=(anywhere, vmem),
        scratch_shapes=scratch,
        compiler_params=pltpu.CompilerParams(
            collective_id=1, has_side_effects=True, vmem_limit_bytes=63 * 2**20
        ),
        name="scatter_sums",
    )(grads, loss)


def update_values(owned, scale, params, first_moment, second_moment, average):
    clipped = owned * scale
    new_first = BETA_ONE * first_moment + (1.0 - BETA_ONE) * clipped
    new_second = BETA_TWO * second_moment + (1.0 - BETA_TWO) * clipped * clipped
    root = jnp.sqrt(new_second * (1.0 / (1.0 - BETA_TWO**STEP)))
    direction = new_first * (1.0 / (1.0 - BETA_ONE**STEP)) / (root + ADAM_EPS)
    new_params = params - RATE * (direction + DECAY_WEIGHT * params)
    new_average = AVERAGE_KEEP * average + (1.0 - AVERAGE_KEEP) * new_params
    return new_params, new_first, new_second, new_average


def update_kernel(sums_ref, masked_ref, *refs):
    squares = jnp.sum(sums_ref[pl.ds(0, 4)], axis=0, keepdims=True)
    norm = jnp.sqrt(jnp.sum(squares, axis=1, keepdims=True))
    scale = jnp.minimum(1.0, CLIP / norm)
    step = 31

    def one(index, carry):
        block = pl.ds(index * step, step)
        owned, params, first, second, average = [ref[block] for ref in refs[:5]]
        values = update_values(owned, scale[None], params, first, second, average)
        for out, value in zip(refs[5:9], values):
            out[block] = value
        return carry

    lax.fori_loop(0, refs[0].shape[0] // step, one, 0)
    loss_ref, total_ref, norm_ref = refs[9:]
    loss_ref[...] = sums_ref[pl.ds(4, 1), pl.ds(0, 1)]
    total_ref[...] = masked_ref[pl.ds(0, 1), pl.ds(0, 1)]
    norm_ref[...] = norm


def update(sums, masked, arrays):
    units = arrays[0].shape[0]
    depth = 217
    spec = pl.BlockSpec((depth, 4, LANES), lambda i: (i, 0, 0))
    tile = pl.BlockSpec((8, LANES), lambda i: (0, 0))
    scalar = pl.BlockSpec((1, 1), lambda i: (0, 0))
    return pl.pallas_call(
        update_kernel,
        grid=(units // depth,),
        out_shape=[jax.ShapeDtypeStruct((units, 4, LANES), F32)] * 4
        + [jax.ShapeDtypeStruct((1, 1), F32)] * 3,
        in_specs=[tile, tile] + [spec] * 5,
        out_specs=[spec] * 4 + [scalar] * 3,
        name="update",
    )(sums, masked, *arrays)


SLOTS_IN = 5


def sections(layout, base):
    matrices, vectors = [], []
    offset = base
    for shape in layout:
        (matrices if len(shape) == 2 else vectors).append((offset, shape))
        offset += math.prod(shape)
    return matrices, vectors


def matrix_plan(rows):
    enc_matrices, enc_vectors = sections(ENC_LAYOUT, 0)
    dec_matrices, dec_vectors = sections(DEC_LAYOUT, rows * LANES)
    lent = rows * LANES + NDEC
    matrices = enc_matrices + sections(LENT, lent)[0] + dec_matrices
    return matrices, enc_vectors, dec_vectors


def padded(columns):
    return -(-columns // LANES) * LANES


def block_depth(shape):
    if shape[1] % LANES:
        return shape[0]
    depth = shape[0]
    while depth * shape[1] > PIECE * LANES:
        depth //= 2
    return depth


def matrix_kernel(rows, flat_ref, *refs):
    matrices, enc_vectors, dec_vectors = matrix_plan(rows)
    count = len(matrices)
    out_refs = refs[:count]
    vector_refs = refs[count : count + 2]
    blocks = refs[count + 2 : 2 * count + 2]
    flat_in, wide, pairs, vector_in, in_sem, out_sem, vector_sem = refs[2 * count + 2 :]
    lane = lax.broadcasted_iota(jnp.int32, (1, LANES), 1)

    chunks = []
    for number, (offset, shape) in enumerate(matrices):
        depth = block_depth(shape)
        for start in range(0, shape[0], depth):
            place = offset + start * shape[1]
            chunks.append((number, start, depth, place // LANES, place % LANES))

    def load(index):
        number, _, depth, first, shift = chunks[index]
        length = depth * matrices[number][1][1] // LANES
        begin = first // 16 * 16
        end = -(-(first + length + (1 if shift else 0)) // 16) * 16
        copy = pltpu.make_async_copy(
            flat_ref.at[pl.ds(begin, end - begin)],
            flat_in.at[index % SLOTS_IN, pl.ds(0, end - begin)],
            in_sem.at[index % SLOTS_IN],
        )
        return copy, first - begin, end - begin

    def store(index):
        number, start, depth, _, _ = chunks[index]
        slot = start // depth % 2
        return pltpu.make_async_copy(
            blocks[number].at[slot], out_refs[number].at[pl.ds(start, depth)], out_sem.at[number, slot]
        )

    def widen(index, length):
        step = 256

        def one(start, size):
            wide[pl.ds(start, size)] = flat_in[index % SLOTS_IN, pl.ds(start, size)].astype(F32)

        def loop(i, carry):
            one(pl.multiple_of(i * step, step), step)
            return carry

        lax.fori_loop(0, length // step, loop, 0, unroll=2)
        if length % step:
            one(length - length % step, length % step)

    def turned(first, second):
        return pltpu.roll(jnp.where(lane < LANES // 2, second, first), LANES // 2, 1)

    def arrange(index, phase):
        number, start, depth, _, shift = chunks[index]
        columns = matrices[number][1][1]
        block = blocks[number].at[start // depth % 2]
        tiles = columns // LANES

        def plain(i, carry):
            row = pl.multiple_of(i * SUB, SUB)
            packed = wide[pl.ds(phase + row * tiles, SUB * tiles)].reshape(SUB, tiles, LANES)
            swapped = jnp.swapaxes(packed, 0, 1)
            for tile in range(tiles):
                value = swapped[tile]
                if shift:
                    after = wide[pl.ds(phase + row * tiles + tile + 1, SUB, stride=tiles)]
                    value = turned(value, after)
                block[pl.ds(row, SUB), pl.ds(tile * LANES, LANES)] = value.astype(BF16)
            return carry

        def paired(i, carry):
            stride = 2 * columns // LANES
            half = SUB // 2
            row = pl.multiple_of(i * half, half)
            for tile in range(tiles + 1):
                even = wide[pl.ds(phase + row * stride + tile, half, stride=stride)]
                odd = wide[pl.ds(phase + row * stride + tiles + tile, half, stride=stride)]
                if tile < tiles:
                    after = wide[pl.ds(phase + row * stride + tiles + tile + 1, half, stride=stride)]
                    odd = turned(odd, after)
                else:
                    even = jnp.where(lane < LANES // 2, even, 0.0)
                    odd = jnp.where(lane < LANES // 2, pltpu.roll(odd, LANES // 2, 1), 0.0)
                lanes = pl.ds(tile * LANES, LANES)
                pairs[tile, pl.ds(0, half, stride=2)] = even
                pairs[tile, pl.ds(1, half, stride=2)] = odd
                block[pl.ds(pl.multiple_of(i * SUB, SUB), SUB), lanes] = pairs[tile].astype(BF16)
            return carry

        lax.fori_loop(0, depth // SUB, paired if columns % LANES else plain, 0, unroll=4)

    windows = []
    wanted = [(0, n, v) for n, v in enumerate(enc_vectors)]
    wanted += [(1, n, v) for n, v in enumerate(dec_vectors)]
    for _, _, (offset, shape) in wanted:
        first = offset // LANES // 16 * 16
        end = -(-(offset // LANES + -(-shape[0] // LANES)) // 16) * 16
        if windows and first <= windows[-1][1]:
            windows[-1][1] = max(windows[-1][1], end)
        else:
            windows.append([first, end])
    bases = [sum(e - f for f, e in windows[:n]) for n in range(len(windows))]

    def vector_copy(n):
        first, end = windows[n]
        return pltpu.make_async_copy(
            flat_ref.at[pl.ds(first, end - first)],
            vector_in.at[pl.ds(bases[n], end - first)],
            vector_sem.at[n],
        )

    for index in range(SLOTS_IN - 1):
        load(index)[0].start()
    for n in range(len(windows)):
        vector_copy(n).start()
    for index, (number, start, depth, _, _) in enumerate(chunks):
        copy, phase, length = load(index)
        copy.wait()
        if index + SLOTS_IN - 1 < len(chunks):
            load(index + SLOTS_IN - 1)[0].start()
        widen(index, length)
        if start // depth >= 2:
            store(index - 2).wait()
        arrange(index, phase)
        store(index).start()
    for n in range(len(windows)):
        vector_copy(n).wait()
    total = bases[-1] + windows[-1][1] - windows[-1][0]
    wide[pl.ds(0, total)] = vector_in[...].astype(F32)
    for group, n, (offset, shape) in wanted:
        first = offset // LANES
        window = [k for k, (f, e) in enumerate(windows) if f <= first < e][0]
        base = bases[window] + first - windows[window][0]
        for tile in range(-(-shape[0] // LANES)):
            value = wide[pl.ds(base + tile, 1)]
            if shape[0] - tile * LANES < LANES:
                value = jnp.where(lane < shape[0] - tile * LANES, value, 0.0)
            vector_refs[group][pl.ds(n, 1), pl.ds(tile * LANES, LANES)] = value
    for index, (number, start, depth, _, _) in enumerate(chunks):
        if start + 2 * depth >= matrices[number][1][0]:
            store(index).wait()


def weight_matrices(flat):
    rows = flat.shape[0] // 2
    matrices, enc_vectors, dec_vectors = matrix_plan(rows)
    shapes = [(shape[0], padded(shape[1])) for _, shape in matrices]
    buffers = []
    for (_, shape), (_, columns) in zip(matrices, shapes):
        depth = block_depth(shape)
        buffers.append(pltpu.VMEM((min(2, shape[0] // depth), depth, columns), BF16))
    dma = pltpu.SemaphoreType.DMA
    windows = 0
    last = -1
    total = 0
    for offset, shape in enc_vectors + dec_vectors:
        first = offset // LANES // 16 * 16
        end = -(-(offset // LANES + -(-shape[0] // LANES)) // 16) * 16
        if first <= last:
            total += max(0, end - last)
            last = max(last, end)
        else:
            windows += 1
            total += end - first
            last = end
    anywhere = pl.BlockSpec(memory_space=pl.ANY)
    vmem = pl.BlockSpec(memory_space=pltpu.VMEM)
    return pl.pallas_call(
        functools.partial(matrix_kernel, rows),
        out_shape=[jax.ShapeDtypeStruct(shape, BF16) for shape in shapes]
        + [jax.ShapeDtypeStruct((VEC_ROWS, columns), F32) for columns in VEC_COLS],
        in_specs=[anywhere],
        out_specs=[anywhere] * len(shapes) + [vmem, vmem],
        scratch_shapes=buffers
        + [
            pltpu.VMEM((SLOTS_IN, PIECE + 32, LANES), BF16),
            pltpu.VMEM((PIECE + 32, LANES), F32),
            pltpu.VMEM((padded(HEAD) // LANES, SUB, LANES), F32),
            pltpu.VMEM((total, LANES), BF16),
            dma((SLOTS_IN,)),
            dma((len(shapes), 2)),
            dma((windows,)),
        ],
        compiler_params=pltpu.CompilerParams(vmem_limit_bytes=56 * 2**20),
        name="weight_matrices",
    )(flat)


def stream_items(layout, lent):
    items = []
    offset = 0
    numbers = [0, 0]
    for shape in layout + lent:
        matrix = len(shape) == 2
        number = numbers[matrix]
        numbers[matrix] += 1
        depth = block_depth(shape) if matrix else 0
        for start in range(0, shape[0] if matrix else 1, max(depth, 1)):
            items.append((matrix, number, shape, start, depth, offset))
            offset += depth * shape[1] if matrix else shape[0]
    return items, offset


ROLES = (
    (ENC_LAYOUT, [], (0, 1, 2, 3)),
    (DEC_LAYOUT, LENT, (6, 7, 8, 9, 10, 4, 5)),
)
PAIRS = 11
FLIGHTS = 4
DEPTH = 1024


def factor_buffers(shapes):
    sizes = []
    places = {}
    for role in (1, 0):
        taken = set()
        for number in ROLES[role][2]:
            for side in range(2):
                length, columns = shapes[2 * number + side]
                fits = [
                    n
                    for n, size in enumerate(sizes)
                    if n not in taken and size[0] == 2 * length and size[1] >= columns
                ]
                if fits:
                    place = min(fits, key=lambda n: sizes[n][1])
                else:
                    place = len(sizes)
                    sizes.append((2 * length, columns))
                taken.add(place)
                places[role, number, side] = place
    return sizes, places


def product_kernel(rows, shapes, *refs):
    factors, vectors, out_ref = refs[: 2 * PAIRS], refs[2 * PAIRS : 2 * PAIRS + 2], refs[24]
    sizes, places = factor_buffers(shapes)
    buffers = refs[25 : 25 + len(sizes)]
    refs = refs[25 + len(sizes) :]
    others = refs[:2]
    turned_left, tall, rows_out, own_sem, send_sem, recv_sem, out_sem = refs[2:]
    core = lax.axis_index("grp")
    sibling = (1 - core, lax.axis_index("dp"))
    barrier = pltpu.get_barrier_semaphore()
    pl.semaphore_signal(barrier, inc=1, device_id=sibling, device_id_type=MESH)
    pl.semaphore_wait(barrier, 1)

    def half_of(role, number, side, part):
        length, columns = shapes[2 * number + side]
        buffer = buffers[places[role, number, side]]
        return buffer.at[pl.ds(part * length, length), pl.ds(0, columns)]

    def local(role, number, side):
        return pltpu.make_async_copy(
            factors[2 * number + side], half_of(role, number, side, 0), own_sem.at[number, side]
        )

    def remote(role, number, side):
        return pltpu.make_async_remote_copy(
            src_ref=factors[2 * number + side],
            dst_ref=half_of(role, number, side, 1),
            send_sem=send_sem.at[number, side],
            recv_sem=recv_sem.at[number, side],
            device_id=sibling,
            device_id_type=MESH,
        )

    def remote_vectors(role):
        return pltpu.make_async_remote_copy(
            src_ref=vectors[role],
            dst_ref=others[role],
            send_sem=send_sem.at[PAIRS, role],
            recv_sem=recv_sem.at[PAIRS, role],
            device_id=sibling,
            device_id_type=MESH,
        )

    def act(role):
        remote_vectors(1 - role).start()
        pending = [(number, side) for number in ROLES[role][2] for side in range(2)]
        given = [(number, side) for number in ROLES[1 - role][2] for side in range(2)]
        for number, side in given:
            remote(1 - role, number, side).start()
        for number, side in pending:
            local(role, number, side).start()
        remote_vectors(role).wait_recv()

        def ready(number):
            for side in range(2):
                local(role, number, side).wait()
                remote(role, number, side).wait_recv()

        lefts, rights = [], []
        for number in ROLES[role][2]:
            for side, views in ((0, lefts), (1, rights)):
                length, columns = shapes[2 * number + side]
                buffer = buffers[places[role, number, side]]
                views.append(buffer.at[pl.ds(0, 2 * length), pl.ds(0, columns)])
        fill_row(
            rows,
            ROLES[role],
            ready,
            lefts,
            rights,
            vectors[role],
            others[role],
            turned_left,
            tall,
            rows_out,
            out_ref,
            out_sem,
        )
        for number, side in given:
            remote(1 - role, number, side).wait_send()
        remote_vectors(1 - role).wait_send()

    for role in range(2):
        pl.when(core == role)(functools.partial(act, role))


def fill_row(
    rows,
    role,
    ready,
    lefts,
    rights,
    mine_ref,
    other_ref,
    turned_left,
    tall,
    rows_out,
    out_ref,
    out_sem,
):
    layout, lent, numbers = role
    lane = lax.broadcasted_iota(jnp.int32, (1, LANES), 1)
    half = LANES // 2
    items, used = stream_items(layout, lent)
    groups = []
    current = []
    for item in items:
        current.append(item)
        if item[0]:
            groups.append(current)
            current = []
    groups.append(current)

    def vector(item, buffer, base):
        _, number, shape, _, _, _ = item
        for tile in range(-(-shape[0] // LANES)):
            lanes = pl.ds(tile * LANES, LANES)
            buffer[pl.ds(base + tile, 1)] = (
                mine_ref[pl.ds(number, 1), lanes] + other_ref[pl.ds(number, 1), lanes]
            )

    def matrix(item, buffer, base):
        _, number, shape, start, depth, offset = item
        columns = shape[1]
        shifted = offset % LANES
        tiles = -(-columns // LANES)
        width = min(WIDTH, columns)
        if start == 0:
            ready(numbers[number])
            if shifted:
                length = rights[number].shape[0]

                def turn(i, carry):
                    block = pl.ds(pl.multiple_of(i * 64, 64), 64)
                    value = rights[number][block].astype(F32)
                    rights[number][block] = pltpu.roll(value, half, 1).astype(BF16)
                    return carry

                lax.fori_loop(0, length // 64, turn, 0)
        length = lefts[number].shape[0]
        sub = min(DEPTH, depth)

        def loop(step, carry):
            k = pl.multiple_of(start + step * sub, sub)
            turned_left[pl.ds(0, sub), pl.ds(0, length)] = lefts[number][:, pl.ds(k, sub)].T

            def across(c, carry):
                column = pl.multiple_of(c * width, width)
                value = jnp.dot(
                    turned_left[pl.ds(0, sub), pl.ds(0, length)],
                    rights[number][:, pl.ds(column, width)],
                    preferred_element_type=F32,
                )
                row = base + step * sub * tiles
                for piece in range(width // LANES):
                    part = value[:, piece * LANES : (piece + 1) * LANES]
                    tile = c * (width // LANES) + piece
                    if columns % LANES:
                        tall[tile, pl.ds(step * sub, sub)] = part
                    elif shifted and piece == 0:
                        first = row + tile

                        @pl.when(c == 0)
                        def _():
                            before = pltpu.roll(part, 1, 0)
                            index = lax.broadcasted_iota(jnp.int32, (sub, LANES), 0)
                            held = buffer[pl.ds(row, 1)]
                            before = jnp.where(index == 0, held, before)
                            merged = jnp.where(lane < half, before, part)
                            buffer[pl.ds(row, sub, stride=tiles)] = merged
                            buffer[pl.ds(row + sub * tiles, 1)] = part[sub - 1 :]

                        @pl.when(c > 0)
                        def _():
                            buffer[pl.ds(first, sub, stride=tiles)] = part
                    else:
                        buffer[pl.ds(row + tile, sub, stride=tiles)] = part
                return carry

            count = tiles * LANES // width
            lax.fori_loop(0, count, across, 0, unroll=2 if count % 2 == 0 else 1)
            return carry

        lax.fori_loop(0, depth // sub, loop, 0)
        if columns % LANES:
            stride = 2 * columns // LANES
            pair = 64

            def weave(i, carry):
                k = pl.multiple_of(i * 2 * pair, 2 * pair)
                row = base + i * pair * stride
                evens = [tall[t, pl.ds(k, pair, stride=2)] for t in range(tiles)]
                odds = [tall[t, pl.ds(k + 1, pair, stride=2)] for t in range(tiles)]
                for t in range(tiles - 1):
                    buffer[pl.ds(row + t, pair, stride=stride)] = evens[t]
                middle = jnp.where(lane < half, evens[-1], pltpu.roll(odds[0], half, 1))
                buffer[pl.ds(row + tiles - 1, pair, stride=stride)] = middle
                for t in range(1, tiles):
                    both_halves = jnp.where(lane < half, odds[t], odds[t - 1])
                    buffer[pl.ds(row + tiles - 1 + t, pair, stride=stride)] = pltpu.roll(
                        both_halves, half, 1
                    )
                return carry

            lax.fori_loop(0, depth // 2 // pair, weave, 0)

    flights = []
    tail = None
    for number, group in enumerate(groups):
        slot = number % 2
        buffer = rows_out.at[slot]
        if number >= 2:
            for copy in flights[number - 2]:
                copy.wait()
        first = group[0][5] // LANES if group else used // LANES
        begin = first // 8 * 8
        if tail is not None:
            buffer[pl.ds(0, 8)] = rows_out[1 - slot, pl.ds(tail, 8)]
        for item in group:
            (matrix if item[0] else vector)(item, buffer, item[5] // LANES - begin)
        last = number == len(groups) - 1
        if last:
            at = used // LANES - begin
            if used % LANES:
                buffer[pl.ds(at, 1)] = jnp.where(lane < used % LANES, buffer[pl.ds(at, 1)], 0.0)
                at += 1
            length = rows - begin
            if length > at:
                buffer[pl.ds(at, length - at)] = jnp.zeros((length - at, LANES), F32)
        else:
            end = groups[number + 1][0][5] if groups[number + 1] else used
            tail = (end // LANES - begin) // 8 * 8
            length = tail
        cuts = [length * n // FLIGHTS // 8 * 8 for n in range(FLIGHTS)] + [length]
        flight = [
            pltpu.make_async_copy(
                buffer.at[pl.ds(lower, upper - lower)],
                out_ref.at[pl.ds(begin + lower, upper - lower)],
                out_sem.at[slot, n],
            )
            for n, (lower, upper) in enumerate(zip(cuts, cuts[1:]))
            if upper > lower
        ]
        for copy in flight:
            copy.start()
        flights.append(flight)
    for flight in flights[-2:]:
        for copy in flight:
            copy.wait()


def flat_gradient(rows, factors, enc_vectors, dec_vectors):
    shapes = [factor.shape for factor in factors]
    sizes, _ = factor_buffers(shapes)
    longest = max(length for length, _ in sizes)
    dma = pltpu.SemaphoreType.DMA
    anywhere = pl.BlockSpec(memory_space=pl.ANY)
    vmem = pl.BlockSpec(memory_space=pltpu.VMEM)
    return pl.pallas_call(
        functools.partial(product_kernel, rows, shapes),
        out_shape=jax.ShapeDtypeStruct((rows, LANES), F32),
        in_specs=[anywhere] * (2 * PAIRS) + [vmem, vmem],
        out_specs=anywhere,
        scratch_shapes=[pltpu.VMEM(size, BF16) for size in sizes]
        + [
            pltpu.VMEM(enc_vectors.shape, F32),
            pltpu.VMEM(dec_vectors.shape, F32),
            pltpu.VMEM((DEPTH, longest), BF16),
            pltpu.VMEM((padded(HEAD) // LANES, DD, LANES), F32),
            pltpu.VMEM((2, PIECE + 128, LANES), F32),
            dma((PAIRS, 2)),
            dma((PAIRS + 1, 2)),
            dma((PAIRS + 1, 2)),
            dma((2, FLIGHTS)),
        ],
        compiler_params=pltpu.CompilerParams(
            collective_id=2, has_side_effects=True, vmem_limit_bytes=63 * 2**20
        ),
        name="flat_gradient",
    )(*factors, enc_vectors, dec_vectors)


LN1_G, LN1_B, LN2_G, LN2_B, FC1_B, FC2_B, LNF_G, LNF_B, LAST_B = range(1, 10)
GROUP = 256
TURNS = 16
BATCH = 2


def dot(left, right):
    return jnp.dot(left, right, preferred_element_type=F32)


def dot_nt(left, right):
    return lax.dot_general(left, right, (((1,), (1,)), ((), ())), preferred_element_type=F32)


def dot_tn(left, right):
    return lax.dot_general(left, right, (((0,), (0,)), ((), ())), preferred_element_type=F32)


def blocks(length, size, action):
    def step(index, carry):
        action(pl.ds(pl.multiple_of(index * size, size), size))
        return carry

    count = length // size
    unroll = 4 if count % 4 == 0 else 2 if count % 2 == 0 else 1
    lax.fori_loop(0, count, step, 0, unroll=unroll)


def row_step(length):
    return 208 if length % 208 == 0 else 128


def score_step(length):
    return 832 if length % 208 == 0 else 256


def normed(state):
    centered = state - jnp.mean(state, axis=-1, keepdims=True)
    inverse = lax.rsqrt(jnp.mean(centered * centered, axis=-1, keepdims=True) + NORM_EPS)
    return centered * inverse, inverse


def norm_rows(source, target, vectors, gain):
    width = source.shape[1]

    def one(rows):
        unit, _ = normed(source[rows])
        value = unit * vectors[pl.ds(gain, 1), pl.ds(0, width)]
        target[rows] = (value + vectors[pl.ds(gain + 1, 1), pl.ds(0, width)]).astype(BF16)

    blocks(source.shape[0], row_step(source.shape[0]), one)


def norm_rows_back(source, grad, vectors, sums, gain, finish):
    width = source.shape[1]
    lanes = pl.ds(0, width)

    def one(rows):
        unit, inverse = normed(source[rows])
        out = grad[rows]
        sums[pl.ds(gain, 1), lanes] += jnp.sum(out * unit, axis=0, keepdims=True)
        sums[pl.ds(gain + 1, 1), lanes] += jnp.sum(out, axis=0, keepdims=True)
        scaled = out * vectors[pl.ds(gain, 1), lanes]
        mean = jnp.mean(scaled, axis=-1, keepdims=True)
        along = jnp.mean(scaled * unit, axis=-1, keepdims=True)
        finish(rows, inverse * (scaled - mean - unit * along))

    blocks(source.shape[0], row_step(source.shape[0]), one)


def gelu_parts(value):
    below = 0.5 * (1.0 + lax.erf(value * math.sqrt(0.5)))
    return below, value * below


def head_masks(depth):
    lane = lax.broadcasted_iota(jnp.int32, (1, GROUP), 1)
    return [
        ((lane >= head * depth) & (lane < (head + 1) * depth)).astype(F32).astype(BF16)
        for head in range(GROUP // depth)
    ]


def stack_heads(target, value, masks):
    length = value.shape[0]
    for head, mask in enumerate(masks):
        target[pl.ds(head * length, length)] = value * mask


def attention_forward(images, length, heads, qkv, bias, attend, attend_low, stacked, mixed):
    width = mixed.shape[1]
    depth = width // heads
    masks = head_masks(depth)
    groups = width // GROUP
    scale = depth**-0.5

    def one(index, carry):
        image, group = index // groups, index % groups
        rows = pl.ds(pl.multiple_of(image * length, length), length)

        def lanes(part):
            return pl.ds(pl.multiple_of(part * width + group * GROUP, GROUP), GROUP)

        stack_heads(stacked, qkv[rows, lanes(0)], masks)
        attend[index] = dot_nt(stacked[...], qkv[rows, lanes(1)])
        shift = bias[pl.ds(image, 1)]

        def softmax(block):
            scores = attend[index, block] * scale + shift
            raised = jnp.exp(scores - jnp.max(scores, axis=-1, keepdims=True))
            value = raised / jnp.sum(raised, axis=-1, keepdims=True)
            attend[index, block] = value
            attend_low[block] = value.astype(BF16)

        blocks(len(masks) * length, score_step(length), softmax)
        value = qkv[rows, lanes(2)]
        total = jnp.zeros((length, GROUP), F32)
        for head, mask in enumerate(masks):
            total += dot(attend_low[pl.ds(head * length, length)], value * mask)
        mixed[rows, lanes(0)] = total.astype(BF16)
        return carry

    lax.fori_loop(0, images * groups, one, 0, unroll=4)


def attention_backward(
    images, length, heads, qkv, grad_mixed, attend, attend_low, grad_low, grads, stacked, other, out
):
    width = grad_mixed.shape[1]
    depth = width // heads
    masks = head_masks(depth)
    groups = width // GROUP
    scale = depth**-0.5

    def one(index, carry):
        image, group = index // groups, index % groups
        rows = pl.ds(pl.multiple_of(image * length, length), length)

        def lanes(part):
            return pl.ds(pl.multiple_of(part * width + group * GROUP, GROUP), GROUP)

        stack_heads(stacked, qkv[rows, lanes(0)], masks)
        stack_heads(other, grad_mixed[rows, lanes(0)], masks)
        grads[...] = dot_nt(other[...], qkv[rows, lanes(2)])

        def scores(block):
            value = attend[index, block]
            grad = grads[block]
            total = jnp.sum(grad * value, axis=-1, keepdims=True)
            grad_low[block] = (value * (grad - total)).astype(BF16)
            attend_low[block] = value.astype(BF16)

        blocks(len(masks) * length, score_step(length), scores)
        out[rows, lanes(2)] = dot_tn(attend_low[...], other[...]).astype(BF16)
        out[rows, lanes(1)] = (dot_tn(grad_low[...], stacked[...]) * scale).astype(BF16)
        key = qkv[rows, lanes(1)]
        total = jnp.zeros((length, GROUP), F32)
        for head, mask in enumerate(masks):
            total += dot(grad_low[pl.ds(head * length, length)], key * mask)
        out[rows, lanes(0)] = (total * scale).astype(BF16)
        return carry

    lax.fori_loop(0, images * groups, one, 0, unroll=4)


def columns_loop(columns, size, action):
    blocks(columns, min(2 * size, columns), action)


def feed_forward(normed_two, fc1_w, fc2_w, vectors, middle, pre, active, state):
    bias = pl.ds(FC1_B, 1)

    def up(lanes):
        value = dot(normed_two[...], fc1_w[:, lanes]) + vectors[bias, lanes]
        pre[:, lanes] = value
        active[:, lanes] = gelu_parts(value)[1].astype(BF16)

    columns_loop(pre.shape[1], 256, up)

    def down(lanes):
        value = dot(active[...], fc2_w[:, lanes])
        state[:, lanes] = middle[:, lanes] + value + vectors[pl.ds(FC2_B, 1), lanes]

    columns_loop(state.shape[1], 256, down)


def feed_backward(grad_low, fc1_w, fc2_w, pre, sums, grad_pre, out):
    def up(lanes):
        value = pre[:, lanes]
        below, _ = gelu_parts(value)
        slope = below + value * (jnp.exp(-0.5 * value * value) * (1.0 / math.sqrt(2.0 * math.pi)))
        grad = dot_nt(grad_low[...], fc2_w[lanes]) * slope
        sums[pl.ds(FC1_B, 1), lanes] += jnp.sum(grad, axis=0, keepdims=True)
        grad_pre[:, lanes] = grad.astype(BF16)

    columns_loop(pre.shape[1], 256, up)

    def down(lanes):
        out[:, lanes] = dot_nt(grad_pre[...], fc1_w[lanes])

    columns_loop(out.shape[1], 256, down)


def turn_code(places, table):
    lane = lax.broadcasted_iota(jnp.int32, (places.shape[0], TURNS), 1)
    passed = (lane > 0) & (lane < TURNS - 1) & (places >= lane * GSIDE)
    row = jnp.sum(passed.astype(F32), axis=1, keepdims=True).astype(jnp.int32)
    parts = []
    for pick in (row, places - row * GSIDE):
        chosen = (lane == pick).astype(F32)
        parts.append(jnp.dot(chosen, table, precision=HIGHEST, preferred_element_type=F32))
    return jnp.concatenate(parts, axis=1)


def decoder_kernel(
    sent,
    pixels,
    spot_rows,
    spot_columns,
    table,
    masked_ref,
    bands_w,
    vectors,
    qkv_w,
    out_w,
    fc1_w,
    fc2_w,
    head_w,
    normed_one,
    grad_qkv,
    mixed,
    grad_middle_low,
    normed_two,
    grad_pre,
    active,
    grad_out_low,
    normed_last,
    grad_predicted,
    grad_sent,
    sums,
    loss,
    seen,
    bias,
    state,
    middle,
    last,
    grad,
    spare,
    qkv,
    pre,
    attend,
    attend_low,
    scores_low,
    scores_grad,
    stacked,
    other,
    grad_mixed,
):
    width = state.shape[1]
    lanes = pl.ds(0, width)

    @pl.when(pl.program_id(0) == 0)
    def _():
        sums[...] = jnp.zeros_like(sums)
        loss[...] = jnp.zeros_like(loss)

    grid = lax.broadcasted_iota(jnp.int32, (GPAD, 1), 0)
    key = lax.broadcasted_iota(jnp.int32, (1, GPAD), 1)
    token = vectors[pl.ds(0, 1), lanes]
    for image in range(BATCH):
        rows = pl.ds(image * GPAD, GPAD)
        chosen = (grid == spot_rows[image]).astype(F32)
        shown = jnp.sum(chosen, axis=1, keepdims=True)
        placed = dot(chosen.astype(BF16), sent[pl.ds(image * VMAX, VMAX)])
        seen[rows] = jnp.where(grid < GRID, shown, 1.0)
        code = turn_code(grid, table[image])
        state[rows] = jnp.where(shown > 0.5, placed, token) + code
        bias[pl.ds(image, 1)] = jnp.where(key < GRID, 0.0, MASK_FILL)

    norm_rows(state, normed_one, vectors, LN1_G)

    def project(part):
        qkv[:, part] = dot(normed_one[...], qkv_w[:, part]).astype(BF16)

    columns_loop(qkv.shape[1], 256, project)
    attention_forward(
        BATCH, GPAD, HD, qkv, bias, attend, attend_low, stacked, mixed
    )

    def output(part):
        middle[:, part] = state[:, part] + dot(mixed[...], out_w[:, part])

    columns_loop(width, 256, output)
    norm_rows(middle, normed_two, vectors, LN2_G)
    feed_forward(normed_two, fc1_w, fc2_w, vectors, middle, pre, active, last)
    norm_rows(last, normed_last, vectors, LNF_G)

    weight = 1.0 / masked_ref[pl.ds(0, 1), pl.ds(0, 1)]

    def predict(part):
        value = dot(normed_last[...], head_w[:, part]) + vectors[pl.ds(LAST_B, 1), part]
        miss = value - dot(pixels[...], bands_w[:, part])
        index = lax.broadcasted_iota(jnp.int32, (1, GROUP), 1) + part.start
        low = index < LOWPIX
        square = miss * miss
        root = jnp.sqrt(square + 1.0)
        unseen = 1.0 - seen[...]
        loss[...] += jnp.sum(jnp.where(low, square, root - 1.0) * unseen)
        slope = jnp.where(low, 2.0 * miss, miss / root) * (unseen * weight)
        rounded = slope.astype(BF16)
        grad_predicted[:, part] = rounded
        sums[pl.ds(LAST_B, 1), part] += jnp.sum(rounded.astype(F32), axis=0, keepdims=True)

    blocks(head_w.shape[1], GROUP, predict)

    def head_back(part):
        spare[:, part] = dot_nt(grad_predicted[...], head_w[part])

    columns_loop(width, 256, head_back)

    def last_back(rows, value):
        grad[rows] = value
        grad_out_low[rows] = value.astype(BF16)
        sums[pl.ds(FC2_B, 1), lanes] += jnp.sum(value, axis=0, keepdims=True)

    norm_rows_back(last, spare, vectors, sums, LNF_G, last_back)
    block_backward(
        BATCH,
        GPAD,
        HD,
        (qkv_w, out_w, fc1_w, fc2_w),
        vectors,
        sums,
        (state, middle, grad, spare, pre, qkv),
        (grad_out_low, grad_pre, grad_middle_low, grad_mixed, grad_qkv),
        (attend, attend_low, scores_low, scores_grad, stacked, other),
    )
    unseen = 1.0 - seen[...]
    sums[pl.ds(0, 1), lanes] += jnp.sum(grad[...] * unseen, axis=0, keepdims=True)
    for image in range(BATCH):
        chosen = (spot_columns[pl.ds(image * VMAX, VMAX)] == key).astype(F32).astype(BF16)
        value = dot(chosen, grad[pl.ds(image * GPAD, GPAD)].astype(BF16))
        grad_sent[pl.ds(image * VMAX, VMAX)] = value.astype(BF16)


def block_backward(images, length, heads, weights, vectors, sums, states, lows, scratch):
    qkv_w, out_w, fc1_w, fc2_w = weights
    state, middle, grad, spare, pre, qkv = states
    grad_out_low, grad_pre, grad_middle_low, grad_mixed, grad_qkv = lows
    attend, attend_low, scores_low, scores_grad, stacked, other = scratch
    width = state.shape[1]
    feed_backward(grad_out_low, fc1_w, fc2_w, pre, sums, grad_pre, spare)

    def middle_back(rows, value):
        total = grad[rows] + value
        grad[rows] = total
        grad_middle_low[rows] = total.astype(BF16)

    norm_rows_back(middle, spare, vectors, sums, LN2_G, middle_back)

    def mixed_back(part):
        grad_mixed[:, part] = dot_nt(grad_middle_low[...], out_w[part]).astype(BF16)

    columns_loop(width, 256, mixed_back)
    attention_backward(
        images,
        length,
        heads,
        qkv,
        grad_mixed,
        attend,
        attend_low,
        scores_low,
        scores_grad,
        stacked,
        other,
        grad_qkv,
    )

    def first_back(part):
        spare[:, part] = dot_nt(grad_qkv[...], qkv_w[part])

    columns_loop(width, 256, first_back)

    def state_back(rows, value):
        grad[rows] = grad[rows] + value

    norm_rows_back(state, spare, vectors, sums, LN1_G, state_back)


def decoder(sent, pixels, spots, tables, masked_tile, vectors, weights):
    images = spots.shape[0]
    rows = BATCH * GPAD
    shown = BATCH * VMAX
    stack = GROUP // (DD // HD) * GPAD
    widths = [DD, 3 * DD, DD, DD, DD, FD, FD, DD, DD, padded(HEAD)]
    whole = lambda array: pl.BlockSpec(array.shape, lambda i: (0,) * array.ndim)
    by_rows = lambda length, columns: pl.BlockSpec((length, columns), lambda i: (i, 0))
    bands_w = band_matrix()
    out_shape = [jax.ShapeDtypeStruct((images * GPAD, columns), BF16) for columns in widths]
    out_shape.append(jax.ShapeDtypeStruct((images * VMAX, DD), BF16))
    out_shape.append(jax.ShapeDtypeStruct((VEC_ROWS, VEC_COLS[1]), F32))
    out_shape.append(jax.ShapeDtypeStruct((8, LANES), F32))
    operands = [masked_tile, bands_w, vectors, *weights]
    f32 = lambda *shape: pltpu.VMEM(shape, F32)
    b16 = lambda *shape: pltpu.VMEM(shape, BF16)
    return pl.pallas_call(
        decoder_kernel,
        grid=(images // BATCH,),
        out_shape=out_shape,
        in_specs=[
            by_rows(shown, DD),
            by_rows(rows, PIX),
            pl.BlockSpec((BATCH, 1, VMAX), lambda i: (i, 0, 0)),
            by_rows(shown, 1),
            pl.BlockSpec((BATCH, TURNS, DD // 2), lambda i: (i, 0, 0)),
        ]
        + [whole(operand) for operand in operands],
        out_specs=[by_rows(rows, columns) for columns in widths]
        + [by_rows(shown, DD)]
        + [pl.BlockSpec(shape.shape, lambda i: (0, 0)) for shape in out_shape[-2:]],
        scratch_shapes=[
            f32(rows, 1),
            f32(BATCH, GPAD),
            f32(rows, DD),
            f32(rows, DD),
            f32(rows, DD),
            f32(rows, DD),
            f32(rows, DD),
            b16(rows, 3 * DD),
            f32(rows, FD),
            f32(BATCH * DD // GROUP, stack, GPAD),
            b16(stack, GPAD),
            b16(stack, GPAD),
            f32(stack, GPAD),
            b16(stack, GROUP),
            b16(stack, GROUP),
            b16(rows, DD),
        ],
        compiler_params=pltpu.CompilerParams(vmem_limit_bytes=62 * 2**20),
        name="decoder",
    )(sent, pixels, spots.reshape(images, 1, VMAX), spots.reshape(-1, 1), tables, *operands)


def encoder_forward_kernel(
    pixels,
    spot_rows,
    spot_columns,
    table,
    vectors,
    pe_hbm,
    qkv_hbm,
    out_hbm,
    fc1_hbm,
    fc2_hbm,
    emb_hbm,
    sent,
    patches,
    state,
    normed_one,
    qkv,
    mixed,
    middle,
    normed_two,
    pre,
    active,
    last,
    normed_last,
    attend,
    pe_w,
    qkv_w,
    out_w,
    fc1_w,
    fc2_w,
    emb_w,
    bias,
    attend_low,
    stacked,
    sems,
):
    pairs = [
        (pe_hbm, pe_w),
        (qkv_hbm, qkv_w),
        (out_hbm, out_w),
        (fc1_hbm, fc1_w),
        (fc2_hbm, fc2_w),
        (emb_hbm, emb_w),
    ]
    copies = [pltpu.make_async_copy(*pair, sems.at[n]) for n, pair in enumerate(pairs)]
    for copy in copies:
        copy.start()
    images = spot_rows.shape[0]
    key = lax.broadcasted_iota(jnp.int32, (1, GPAD), 1)
    for image in range(images):
        rows = pl.ds(image * VMAX, VMAX)
        place = spot_columns[rows]
        chosen = (place == key).astype(F32).astype(BF16)
        patches[rows] = dot(chosen, pixels[pl.ds(image * GPAD, GPAD)]).astype(BF16)
        code = turn_code(jnp.maximum(place, 0), table[image])
        state[rows] = code + vectors[pl.ds(0, 1), pl.ds(0, DE)]
        bias[pl.ds(image, 1)] = jnp.where(spot_rows[image] < 0, MASK_FILL, 0.0)
    copies[0].wait()

    def embed(part):
        state[:, part] += dot(patches[...], pe_w[:, part])

    columns_loop(DE, 256, embed)
    norm_rows(state, normed_one, vectors, LN1_G)
    copies[1].wait()

    def project(part):
        qkv[:, part] = dot(normed_one[...], qkv_w[:, part]).astype(BF16)

    columns_loop(3 * DE, 256, project)
    attention_forward(images, VMAX, HE, qkv, bias, attend, attend_low, stacked, mixed)
    copies[2].wait()

    def output(part):
        middle[:, part] = state[:, part] + dot(mixed[...], out_w[:, part])

    columns_loop(DE, 256, output)
    norm_rows(middle, normed_two, vectors, LN2_G)
    copies[3].wait()
    copies[4].wait()
    feed_forward(normed_two, fc1_w, fc2_w, vectors, middle, pre, active, last)
    norm_rows(last, normed_last, vectors, LNF_G)
    copies[5].wait()
    value = dot(normed_last[...], emb_w[...]) + vectors[pl.ds(LAST_B, 1), pl.ds(0, DD)]
    sent[...] = value.astype(BF16)


def encoder_forward(pixels, spots, tables, vectors, weights):
    images = spots.shape[0]
    rows = images * VMAX
    stack = GROUP // (DE // HE) * VMAX
    anywhere = pl.BlockSpec(memory_space=pl.ANY)
    vmem = pl.BlockSpec(memory_space=pltpu.VMEM)
    kept = [
        (DD, BF16),
        (PIX, BF16),
        (DE, F32),
        (DE, BF16),
        (3 * DE, BF16),
        (DE, BF16),
        (DE, F32),
        (DE, BF16),
        (FE, F32),
        (FE, BF16),
        (DE, F32),
        (DE, BF16),
    ]
    out_shape = [jax.ShapeDtypeStruct((rows, columns), kind) for columns, kind in kept]
    out_shape.append(jax.ShapeDtypeStruct((images * DE // GROUP, stack, VMAX), F32))
    return pl.pallas_call(
        encoder_forward_kernel,
        out_shape=out_shape,
        in_specs=[vmem] * 5 + [anywhere] * 6,
        out_specs=[vmem] * len(out_shape),
        scratch_shapes=[pltpu.VMEM(weight.shape, BF16) for weight in weights]
        + [
            pltpu.VMEM((images, VMAX), F32),
            pltpu.VMEM((stack, VMAX), BF16),
            pltpu.VMEM((stack, GROUP), BF16),
            pltpu.SemaphoreType.DMA((6,)),
        ],
        compiler_params=pltpu.CompilerParams(vmem_limit_bytes=60 * 2**20),
        name="encoder_forward",
    )(pixels, spots.reshape(images, 1, VMAX), spots.reshape(-1, 1), tables, vectors, *weights)


def encoder_backward_kernel(
    grad_sent,
    vectors,
    state,
    qkv,
    middle,
    pre,
    last,
    attend,
    qkv_hbm,
    out_hbm,
    fc1_hbm,
    fc2_hbm,
    emb_hbm,
    grad_state_low,
    grad_qkv,
    grad_middle_low,
    grad_pre,
    grad_out_low,
    sums,
    qkv_w,
    out_w,
    fc1_w,
    fc2_w,
    emb_w,
    grad,
    spare,
    grad_mixed,
    attend_low,
    scores_low,
    scores_grad,
    stacked,
    other,
    sems,
):
    pairs = [
        (emb_hbm, emb_w),
        (fc2_hbm, fc2_w),
        (fc1_hbm, fc1_w),
        (out_hbm, out_w),
        (qkv_hbm, qkv_w),
    ]
    copies = [pltpu.make_async_copy(*pair, sems.at[n]) for n, pair in enumerate(pairs)]
    for copy in copies:
        copy.start()
    lanes = pl.ds(0, DE)
    sums[...] = jnp.zeros_like(sums)
    summed = jnp.sum(grad_sent[...].astype(F32), axis=0, keepdims=True)
    sums[pl.ds(LAST_B, 1), pl.ds(0, DD)] = summed
    copies[0].wait()

    def sent_back(part):
        spare[:, part] = dot_nt(grad_sent[...], emb_w[part])

    columns_loop(DE, 256, sent_back)

    def last_back(rows, value):
        grad[rows] = value
        grad_out_low[rows] = value.astype(BF16)
        sums[pl.ds(FC2_B, 1), lanes] += jnp.sum(value, axis=0, keepdims=True)

    norm_rows_back(last, spare, vectors, sums, LNF_G, last_back)
    for copy in copies[1:]:
        copy.wait()
    block_backward(
        state.shape[0] // VMAX,
        VMAX,
        HE,
        (qkv_w, out_w, fc1_w, fc2_w),
        vectors,
        sums,
        (state, middle, grad, spare, pre, qkv),
        (grad_out_low, grad_pre, grad_middle_low, grad_mixed, grad_qkv),
        (attend, attend_low, scores_low, scores_grad, stacked, other),
    )

    def first(rows):
        value = grad[rows]
        sums[pl.ds(0, 1), lanes] += jnp.sum(value, axis=0, keepdims=True)
        grad_state_low[rows] = value.astype(BF16)

    blocks(grad.shape[0], row_step(grad.shape[0]), first)


def encoder_backward(grad_sent, vectors, kept, weights):
    state, qkv, middle, pre, last, attend = kept
    rows = state.shape[0]
    stack = attend.shape[1]
    anywhere = pl.BlockSpec(memory_space=pl.ANY)
    vmem = pl.BlockSpec(memory_space=pltpu.VMEM)
    out_shape = [
        jax.ShapeDtypeStruct((rows, columns), BF16) for columns in (DE, 3 * DE, DE, FE, DE)
    ]
    out_shape.append(jax.ShapeDtypeStruct((VEC_ROWS, VEC_COLS[0]), F32))
    f32 = lambda *shape: pltpu.VMEM(shape, F32)
    b16 = lambda *shape: pltpu.VMEM(shape, BF16)
    return pl.pallas_call(
        encoder_backward_kernel,
        out_shape=out_shape,
        in_specs=[vmem] * 8 + [anywhere] * 5,
        out_specs=[vmem] * len(out_shape),
        scratch_shapes=[pltpu.VMEM(weight.shape, BF16) for weight in weights]
        + [
            f32(rows, DE),
            f32(rows, DE),
            b16(rows, DE),
            b16(stack, VMAX),
            b16(stack, VMAX),
            f32(stack, VMAX),
            b16(stack, GROUP),
            b16(stack, GROUP),
            pltpu.SemaphoreType.DMA((5,)),
        ],
        compiler_params=pltpu.CompilerParams(vmem_limit_bytes=60 * 2**20),
        name="encoder_backward",
    )(grad_sent, vectors, state, qkv, middle, pre, last, attend, *weights)


def band_matrix():
    ids = np.arange(PIX)
    coarse = (ids // (3 * PSIDE) // 2 * (PSIDE // 2) + ids // 3 % PSIDE // 2) * 3 + ids % 3
    low = np.where(coarse[:, None] == np.arange(LOWPIX)[None], 0.25, 0.0)
    high = np.eye(PIX) - np.where(coarse[:, None] == coarse[None], 0.25, 0.0)
    rest = np.zeros((PIX, padded(HEAD) - HEAD))
    return jnp.asarray(np.concatenate([low, high, rest], axis=1).astype(ml_dtypes.bfloat16))


def turn_table(scales, width):
    quarter = width // 4
    frequency = jnp.exp(jnp.arange(quarter, dtype=F32) * (-math.log(10000.0) / quarter))
    angle = (jnp.arange(TURNS, dtype=F32)[None] * scales[:, None])[..., None] * frequency
    return jnp.concatenate([jnp.sin(angle), jnp.cos(angle)], axis=-1)


def forward_backward(parts, pixels, index_rows, counts, scales, masked_tile):
    pe_w, qkv_w, fc1_w, emb_w, out_w, fc2_w = parts[:6]
    dec_weights = parts[6:11]
    enc_vectors, dec_vectors = parts[11:]
    images = counts.shape[0]
    valid = jnp.arange(VMAX, dtype=jnp.int32)[None, :] < counts[:, None]
    spots = jnp.where(valid, index_rows, -1)
    pixels = jnp.pad(pixels.reshape(images, GRID, PIX), ((0, 0), (0, GPAD - GRID), (0, 0)))
    pixels = pixels.reshape(images * GPAD, PIX)
    (
        sent,
        patches,
        state,
        normed_one,
        qkv,
        mixed,
        middle,
        normed_two,
        pre,
        active,
        last,
        normed_last,
        attend,
    ) = encoder_forward(
        pixels,
        spots,
        turn_table(scales, DE),
        enc_vectors,
        [pe_w, qkv_w, out_w, fc1_w, fc2_w, emb_w],
    )
    *dec_factors, grad_sent, dec_sums, loss = decoder(
        sent, pixels, spots, turn_table(scales, DD), masked_tile, dec_vectors, dec_weights
    )
    grad_state, grad_qkv, grad_middle, grad_pre, grad_out, enc_sums = encoder_backward(
        grad_sent,
        enc_vectors,
        [state, qkv, middle, pre, last, attend],
        [qkv_w, out_w, fc1_w, fc2_w, emb_w],
    )
    factors = [patches, grad_state, normed_one, grad_qkv, normed_two, grad_pre]
    factors += [normed_last, grad_sent, mixed, grad_middle, active, grad_out]
    return factors + dec_factors, enc_sums, dec_sums, loss


def body(
    params, first_moment, second_moment, average, pixels, visible_index, visible_count, gsd_id
):
    chips = lax.axis_size("dp")
    rows = params.shape[1] // LANES
    special = chips == math.prod(DP_GRID) and rows % 4 == 0
    masked = jnp.sum(GRID - visible_count).astype(F32)
    if special:
        shards = [a.reshape(-1, 4, LANES) for a in (params, first_moment, second_moment, average)]
        copies, masked_tile = gather_rows(shards[0], jnp.full((8, LANES), masked))
    else:
        copies = lax.all_gather(params.astype(BF16).reshape(-1, LANES), "dp", axis=0, tiled=True)
        copies = lax.all_gather(copies, "grp", axis=0, tiled=True)
        masked_tile = jnp.full((8, LANES), lax.psum(masked, "dp"))
    parts = weight_matrices(copies.reshape(-1, LANES))

    half = visible_count.shape[0] // 2
    core = lax.axis_index("grp")

    def mine(array, count):
        return lax.dynamic_slice_in_dim(array, core * count, count, 0)

    scales = 0.5 + 0.25 * mine(gsd_id, half).astype(F32)
    factors, enc_sums, dec_sums, loss_tile = forward_backward(
        parts,
        mine(pixels, half * GRID),
        mine(visible_index, half),
        mine(visible_count, half),
        scales,
        masked_tile,
    )
    gradient = flat_gradient(chips * rows, factors, enc_sums, dec_sums)
    if special:
        owned, sums = scatter_sums(gradient.reshape(chips, rows // 4, 4, LANES), loss_tile)
        outs = update(sums, masked_tile, [owned] + shards)
        outs = [out.reshape(params.shape) for out in outs[:4]] + [out.reshape(()) for out in outs[4:]]
        return tuple(outs)
    owned = lax.psum_scatter(gradient, "dp", scatter_dimension=0, tiled=True)
    owned = owned.reshape(params.shape)
    squares, loss_sum = lax.psum((jnp.sum(owned * owned), loss_tile[0, 0]), ("grp", "dp"))
    norm = jnp.sqrt(squares)
    scale = jnp.minimum(1.0, CLIP / norm)
    outs = update_values(owned, scale, params, first_moment, second_moment, average)
    return (*outs, loss_sum, masked_tile[0, 0], norm)


def solution(mesh):
    return jax.shard_map(
        body,
        mesh=mesh,
        in_specs=(P("grp", "dp"),) * 4 + (P("dp", None), P("dp", None), P("dp"), P("dp")),
        out_specs=(P("grp", "dp"),) * 4 + (P(), P(), P()),
        check_vma=False,
    )
```
